32 devices in a mesh: groups: 2 (over y), tm: 4 (over z), chan: 2 (over x), pol: 2 (over core).
Axes of the slice: x: 2, y: 2, z: 4, core: 2. Of those that a mesh axis runs over, the one named last changes fastest.
Arguments:
- voltages: bfloat16 [1024, 2, 8, 2, 512], P(('groups', 'tm'), 'pol', 'chan'), parts along dimension 0, may hold values from -60 to 60
- start_block: float32 [2, 8, 2, 8, 512], P('pol', 'chan'), may hold values from -6 to 6
- flags: int32 [16], P(('groups', 'chan')), parts along dimension 0, may hold values 0 or 1
- ranks: int32 [16], P(('groups', 'chan')), parts along dimension 0, may hold values from 1 to 8
- phase_index: int32 [256, 512], replicated, may hold values from 0 to 1023
Outputs:
- power: float32 [1024, 8, 256], P(('groups', 'tm'), 'chan', 'pol'), parts along dimension 0
The draws below stay inside these ranges and needn't reach their ends.
There are 2 independent parts, one for each index of `groups`. The reference program is written for one: setup_inputs(seed, part) draws one part's arguments, and reference() takes and returns one part's arrays. A program takes and returns all parts, laid end to end along the dimension named above; an argument that names none is the same for every part. Nothing has to cross between parts.
All inputs are finite; a program needn't handle non-finite values. No bound on the sum of `flags` on one device may be relied on, other than what follows from the above.
Results may differ from the reference program's by a relative error of at most 0.008.
Values may be sent and summed in bfloat16 or wider, within the bound.
No kernel may reach another device: no remote copies, remote signals or barrier semaphores. Data moves between devices by JAX's collectives and lax.ppermute only.
A program may use at most 128 MiB of HBM per device.

```python
import jax
import jax.numpy as jnp
from jax import lax

A = 512
BEAMS = 256
K = 8
ITERS = 4
PHASES = 1024
NS = 6
TS = 128
NPOL = 2
TIMES = 512
CH = 8
N_TM = 4


def draw_voltages(key, part):
    key = jax.random.fold_in(key, 11)
    noise_key, phase_key, amp_key, signal_key = jax.random.split(key, 4)
    noise = jax.random.truncated_normal(noise_key, -5.0, 5.0, (TIMES, NPOL, CH, 2, A), jnp.float32)
    phases = jax.random.uniform(phase_key, (NS, CH, A), jnp.float32, -jnp.pi, jnp.pi)
    amplitude = jnp.exp(jax.random.uniform(amp_key, (NS, CH), jnp.float32, jnp.log(0.05), jnp.log(1.5)))
    real_sum = noise[:, :, :, 0]
    imag_sum = noise[:, :, :, 1]
    for source in range(NS):
        signal = jax.random.truncated_normal(jax.random.fold_in(signal_key, source), -4.0, 4.0, (TIMES, NPOL, CH, 2), jnp.float32)
        sig_real = (signal[..., 0] * amplitude[source])[..., None]
        sig_imag = (signal[..., 1] * amplitude[source])[..., None]
        cosine = jnp.cos(phases[source])
        sine = jnp.sin(phases[source])
        real_sum = real_sum + sig_real * cosine - sig_imag * sine
        imag_sum = imag_sum + sig_real * sine + sig_imag * cosine
    return jnp.stack([real_sum, imag_sum], axis=3).astype(jnp.bfloat16)


def plant(values, key, low, top_value):
    spot = [jax.random.randint(jax.random.fold_in(key, axis), (), 0, length) for axis, length in enumerate(values.shape)]
    longest = values.shape.index(max(values.shape))
    next_to = spot[:longest] + [(spot[longest] + 1) % values.shape[longest]] + spot[longest + 1:]
    return values.at[tuple(spot)].set(low).at[tuple(next_to)].set(top_value)


def steps_of(own_key, shape, cuts, least, high):
    level, own = 1.0, jax.random.fold_in(own_key, 6)
    for axis_at, shards_of in cuts:
        heights = jnp.exp(jax.random.uniform(jax.random.fold_in(own, axis_at), (shards_of,), jnp.float32, least / len(cuts), high / len(cuts)))
        level = level * jnp.repeat(heights, shape[axis_at] // shards_of).reshape([-1 if axis == axis_at else 1 for axis in range(len(shape))])
    return level


def bell_draw(stream_key, dims, scale, most, cuts=(), held_as=jnp.bfloat16):
    loudness = steps_of(stream_key, dims, cuts, -0.22, 0.18) if cuts else 1.0
    array = jax.random.normal(stream_key, dims, jnp.float32) * scale * loudness
    return jnp.minimum(jnp.maximum(array, -most), most).astype(held_as)


def setup_inputs(seed: int = 0, part: int = 0) -> dict:
    key_of = jax.random.split(jax.random.key(seed), 6)
    part_keys = jax.random.split(jax.random.fold_in(key_of[5], part), 6)
    return {
        "voltages": draw_voltages(jax.random.fold_in(jax.random.fold_in(key_of[5], part), 71), part),
        "start_block": bell_draw(key_of[1], (NPOL, CH, 2, K, A), 1.0, 6.0, ((0, 2), (1, 2)), jnp.float32),
        "flags": plant((jax.random.randint(part_keys[2], (CH,), 0, 4) < 3).astype(jnp.int32), jax.random.fold_in(part_keys[2], 1), 0, 1),
        "ranks": plant(jax.random.randint(part_keys[3], (CH,), 1, K + 1), jax.random.fold_in(part_keys[3], 1), 1, K).astype(jnp.int32),
        "phase_index": plant(jax.random.randint(key_of[4], (BEAMS, A), 0, PHASES), jax.random.fold_in(key_of[4], 1), 0, PHASES - 1).astype(jnp.int32),
    }


HIGH = lax.Precision.HIGHEST

def block_terms(piece, factor):
    real_part = piece[:, 0]
    imag_part = piece[:, 1]
    stacked = jnp.concatenate([real_part, imag_part], axis=0)
    rotated = jnp.concatenate([imag_part, -real_part], axis=0)
    left_side = jnp.concatenate([stacked, rotated], axis=1)
    product = jnp.dot(left_side.T, stacked, preferred_element_type=jnp.float32) * factor
    return product.reshape(2, stacked.shape[1], stacked.shape[1])

def apply_cov(cov, real_q, imag_q):

    def times_matrix(vectors, matrix):
        return jnp.einsum('cmk,cjk->cmj', vectors, matrix, precision=HIGH)
    cov_real = cov[:, 0]
    cov_imag = cov[:, 1]
    new_real = times_matrix(real_q, cov_real) - times_matrix(imag_q, cov_imag)
    new_imag = times_matrix(imag_q, cov_real) + times_matrix(real_q, cov_imag)
    return (new_real, new_imag)

def orthonormalize(real_z, imag_z):
    done_real = []
    done_imag = []
    for column in range(real_z.shape[1]):
        vec_real = real_z[:, column]
        vec_imag = imag_z[:, column]
        if column > 0:
            base_real = jnp.stack(done_real, axis=1)
            base_imag = jnp.stack(done_imag, axis=1)
            dot_real = lax.optimization_barrier(jnp.sum(base_real * vec_real[:, None] + base_imag * vec_imag[:, None], axis=-1, keepdims=True))
            dot_imag = lax.optimization_barrier(jnp.sum(base_real * vec_imag[:, None] - base_imag * vec_real[:, None], axis=-1, keepdims=True))
            vec_real = vec_real - lax.optimization_barrier(jnp.sum(dot_real * base_real - dot_imag * base_imag, axis=1))
            vec_imag = vec_imag - lax.optimization_barrier(jnp.sum(dot_real * base_imag + dot_imag * base_real, axis=1))
        factor = 1.0 / jnp.sqrt(lax.optimization_barrier(jnp.sum(vec_real * vec_real + vec_imag * vec_imag, axis=-1, keepdims=True)) + 1e-06)
        done_real.append(vec_real * factor)
        done_imag.append(vec_imag * factor)
    return (jnp.stack(done_real, axis=1), jnp.stack(done_imag, axis=1))

def subspace(cov, real_q, imag_q):
    for sweep in range(ITERS):
        real_z, imag_z = apply_cov(cov, real_q, imag_q)
        real_q, imag_q = orthonormalize(real_z, imag_z)
    return (real_q, imag_q)

def projector(real_u, imag_u):

    def outer_sum(left_vec, right_vec):
        return jnp.einsum('cmj,cmk->cjk', left_vec, right_vec, precision=HIGH)
    identity = jnp.eye(real_u.shape[2], dtype=jnp.float32)[None]
    proj_real = identity - (outer_sum(real_u, real_u) + outer_sum(imag_u, imag_u))
    proj_imag = outer_sum(real_u, imag_u) - outer_sum(imag_u, real_u)
    return jnp.stack([proj_real, proj_imag], axis=1).astype(jnp.bfloat16)

def project(series, proj):

    def apply_one(vectors, matrix):
        return jnp.einsum('sck,cjk->scj', vectors.astype(jnp.float32), matrix.astype(jnp.float32))
    in_real = series[:, :, 0]
    in_imag = series[:, :, 1]
    proj_real = proj[:, 0]
    proj_imag = proj[:, 1]
    out_real = apply_one(in_real, proj_real) - apply_one(in_imag, proj_imag)
    out_imag = apply_one(in_imag, proj_real) + apply_one(in_real, proj_imag)
    return jnp.stack([out_real, out_imag], axis=2).astype(jnp.bfloat16)

def steering(chan_ids, phase_index):
    turn = phase_index[None] * (chan_ids[:, None, None] + 1) % PHASES
    angle = turn.astype(jnp.float32) * (2.0 * jnp.pi / PHASES)
    norm_factor = 1.0 / jnp.sqrt(jnp.float32(phase_index.shape[1]))
    return ((jnp.cos(angle) * norm_factor).astype(jnp.bfloat16), (jnp.sin(angle) * norm_factor).astype(jnp.bfloat16))

def beam_power(cleaned, weight_real, weight_imag):

    def form(vectors, weights):
        return jnp.einsum('sca,cba->scb', vectors.astype(jnp.float32), weights.astype(jnp.float32))
    out_real = cleaned[:, :, 0]
    out_imag = cleaned[:, :, 1]
    beam_real = form(out_real, weight_real) - form(out_imag, weight_imag)
    beam_imag = form(out_real, weight_imag) + form(out_imag, weight_real)
    return beam_real * beam_real + beam_imag * beam_imag

def reference(voltages, start_block, flags, ranks, phase_index):

    def one_channel(channel):
        column = lax.dynamic_index_in_dim(voltages, channel, 2, keepdims=False)
        starts = lax.dynamic_index_in_dim(start_block, channel, 1, keepdims=False)
        rank_now = flags[channel] * ranks[channel]
        keep = (jnp.arange(K, dtype=jnp.int32) < rank_now).astype(jnp.float32)[None, :, None]
        weight_real, weight_imag = steering(channel.reshape(1), phase_index)
        total = jnp.zeros((TIMES, 1, BEAMS), jnp.float32)
        for polar in range(NPOL):
            series = column[:, polar]
            blocks = series.reshape(N_TM, TS, 2, A)

            def add_block(carry, piece):
                rounded = lax.optimization_barrier(block_terms(piece, 1.0 / TIMES).astype(jnp.bfloat16))
                return (carry + rounded.astype(jnp.float32), None)
            cov, unused = lax.scan(add_block, jnp.zeros((2, A, A), jnp.float32), blocks)
            real_q, imag_q = subspace(cov[None], starts[polar, 0][None], starts[polar, 1][None])
            proj = projector(real_q * keep, imag_q * keep)
            cleaned = project(series[:, None], proj)
            total = total + beam_power(cleaned, weight_real, weight_imag)
        return total[:, 0]
    result = lax.map(one_channel, jnp.arange(CH, dtype=jnp.int32))
    return jnp.transpose(result, (1, 0, 2))
```

```python
import functools

import jax
import jax.numpy as jnp
from jax import lax
from jax.experimental import pallas as pl
from jax.experimental.pallas import tpu as pltpu
from jax.sharding import PartitionSpec as P

ITERS = 4
PHASES = 1024
QUARTER = PHASES // 4
EPS = 1e-06
F32 = jnp.float32
BF16 = jnp.bfloat16
NT = (((1,), (1,)), ((), ()))
NN = (((1,), (0,)), ((), ()))
TN = (((0,), (0,)), ((), ()))
VMEM_LIMIT = 48 * 1024 * 1024


def dot(left, right, dims):
    return lax.dot_general(left, right, dims, preferred_element_type=F32)


def split(values):
    high = values.astype(BF16)
    low = (values - high.astype(F32)).astype(BF16)
    return high, low


def steer(phase, step, norm):
    turn = (phase * step) & (PHASES - 1)
    quadrant = (turn + QUARTER // 2) // QUARTER
    angle = (turn - quadrant * QUARTER).astype(F32) * (2.0 * jnp.pi / PHASES)
    sq = angle * angle
    sine = angle * (1.0 + sq * (-1.0 / 6 + sq * (1.0 / 120 + sq * (-1.0 / 5040 + sq / 362880))))
    cosine = 1.0 + sq * (-0.5 + sq * (1.0 / 24 + sq * (-1.0 / 720 + sq / 40320)))
    odd = (quadrant & 1) == 1
    real = jnp.where(odd, sine, cosine) * norm
    imag = jnp.where(odd, cosine, sine) * norm
    real = jnp.where(((quadrant + 1) & 2) == 2, -real, real)
    imag = jnp.where((quadrant & 2) == 2, -imag, imag)
    return real.astype(BF16), imag.astype(BF16)


def fill_weights(phase_ref, first, rows, step, out):
    norm = 1.0 / (phase_ref.shape[1] ** 0.5)
    chunk = 32

    def body(i, carry):
        at = pl.multiple_of(i * chunk, chunk)
        real, imag = steer(phase_ref[pl.ds(first + at, chunk), :], step, norm)
        out[pl.ds(at, chunk), :] = real
        out[pl.ds(rows + at, chunk), :] = imag
        return carry

    lax.fori_loop(0, rows // chunk, body, 0)


def own_weights_kernel(own, chan_dev, phase_ref, out_ref):
    beams = phase_ref.shape[0]
    first = lax.axis_index("chan") * chan_dev + lax.axis_index("tm") * own
    for o in range(own):
        fill_weights(phase_ref, 0, beams, first + o + 1, out_ref.at[o])


def raw_beams_kernel(chan_dev, phase_ref, mine_ref, other_ref, out_ref, weights):
    half = phase_ref.shape[0] // 2
    width = phase_ref.shape[1]
    chan_id = lax.axis_index("chan") * chan_dev + pl.program_id(0)
    first = pl.multiple_of(lax.axis_index("pol") * half, half)
    fill_weights(phase_ref, first, half, chan_id + 1, weights)
    for slot, ref in enumerate((mine_ref, other_ref)):
        by_real = dot(ref[0, :, :width], weights[...], NT)
        by_imag = dot(ref[0, :, width:], weights[...], NT)
        out_ref[0, slot, :, :half] = by_real[:, :half] - by_imag[:, half:]
        out_ref[0, slot, :, half:] = by_real[:, half:] + by_imag[:, :half]


def correlate(real, imag, x_ref):
    rows = jnp.concatenate(
        [jnp.concatenate([real, imag], axis=1), jnp.concatenate([imag, -real], axis=1)], axis=0
    )
    count = rows.shape[0]
    product = dot(jnp.concatenate(split(rows), axis=0), x_ref[...], NT)
    return product[:count] + product[count:]


def cov_times(real, imag, x_ref, factor):
    vectors, width = real.shape
    series = correlate(real, imag, x_ref)
    count = series.shape[0]
    product = dot(jnp.concatenate(split(series), axis=0), x_ref[...], NN)
    product = (product[:count] + product[count:]) * factor
    real_z = product[:vectors, :width] - product[vectors:, width:]
    imag_z = product[vectors:, :width] + product[:vectors, width:]
    return real_z, imag_z


def orthonormalize(real_z, imag_z):
    vectors = real_z.shape[0]
    row = lax.broadcasted_iota(jnp.int32, real_z.shape, 0)
    real_v, imag_v = real_z, imag_z
    scale = jnp.zeros((vectors, 1), F32)
    for n in range(vectors):
        here = row == n
        real_a, imag_a = real_v[n : n + 1], imag_v[n : n + 1]
        real_z = jnp.where(here, real_v, real_z)
        imag_z = jnp.where(here, imag_v, imag_z)
        real_d = jnp.sum(real_a * real_z + imag_a * imag_z, axis=1, keepdims=True)
        norm = real_d[n : n + 1] + EPS
        scale = jnp.where(row[:, :1] == n, norm, scale)
        if n + 1 < vectors:
            imag_d = jnp.sum(real_a * imag_z - imag_a * real_z, axis=1, keepdims=True)
            inverse = 1.0 / norm
            later = row[:, :1] > n
            real_c = jnp.where(later, real_d * inverse, 0.0)
            imag_c = jnp.where(later, imag_d * inverse, 0.0)
            real_v = real_v - (real_c * real_a - imag_c * imag_a)
            imag_v = imag_v - (real_c * imag_a + imag_c * real_a)
    factor = 1.0 / jnp.sqrt(scale)
    return real_v * factor, imag_v * factor


def subspace_kernel(tm, own, samples, factor, x_ref, start_ref, flags_ref, ranks_ref, weights_ref, *rest):
    outs, series_ref, steered_ref = rest[:-2], rest[-2], rest[-1]
    vectors, width = start_ref.shape[3], start_ref.shape[4]
    tm_index = lax.axis_index("tm")
    pol_index = lax.axis_index("pol")
    half = steered_ref.shape[1] // 2
    for o in range(own):
        chan = tm_index * own + o
        real_q = start_ref[0, chan, 0]
        imag_q = start_ref[0, chan, 1]
        x = x_ref.at[o]
        for sweep in range(ITERS):
            real_z, imag_z = cov_times(real_q, imag_q, x, factor)
            real_q, imag_q = orthonormalize(real_z, imag_z)
        rank = flags_ref[chan] * ranks_ref[chan]
        keep = lax.broadcasted_iota(jnp.int32, (vectors, width), 0) < rank
        real_u = jnp.where(keep, real_q, 0.0)
        imag_u = jnp.where(keep, imag_q, 0.0)
        series = correlate(real_u, imag_u, x)
        series_ref[:vectors] = series[:vectors]
        series_ref[vectors:] = -series[vectors:]
        rows = jnp.concatenate([real_u, imag_u], axis=0)
        product = dot(jnp.concatenate(split(rows), axis=0), weights_ref[o], NT)
        product = product[: 2 * vectors] + product[2 * vectors :]
        beams = product.shape[1] // 2
        steered_ref[:vectors] = product[:vectors, :beams] - product[vectors:, beams:]
        steered_ref[vectors:] = product[:vectors, beams:] + product[vectors:, :beams]
        for d in range(tm):
            to = lax.rem(tm_index + d, tm)
            part = series_ref[:, pl.ds(pl.multiple_of(to * samples, samples), samples)]
            for swap in range(2):
                core = lax.rem(pol_index + swap, 2)
                out = outs[2 * d + swap]
                out[o, :, :samples] = part
                out[o, :, samples:] = steered_ref[:, pl.ds(pl.multiple_of(core * half, half), half)]


def finish_kernel(tm, own, raw_ref, *rest):
    arrived, out_ref, powers = rest[:-2], rest[-2], rest[-1]
    samples = raw_ref.shape[2]
    half = raw_ref.shape[3] // 2
    tm_index = lax.axis_index("tm")
    for d in range(tm):
        source = lax.rem(tm_index + tm - d, tm)
        for o in range(own):
            chan = source * own + o
            total = jnp.zeros((samples, half), F32)
            for swap in range(2):
                ref = arrived[2 * d + swap]
                series = ref[o, :, :samples]
                steered = ref[o, :, samples:]
                vectors = steered.shape[0] // 2
                real_w, imag_w = steered[:vectors], steered[vectors:]
                right = jnp.concatenate(
                    [
                        jnp.concatenate([real_w, imag_w], axis=1),
                        jnp.concatenate([-imag_w, real_w], axis=1),
                    ],
                    axis=0,
                )
                high_s, low_s = split(series)
                high_w, low_w = split(right)
                left = jnp.concatenate([high_s, high_s, low_s], axis=0)
                right = jnp.concatenate([high_w, low_w, high_w], axis=0)
                beam = raw_ref[chan, swap] - dot(left, right, TN)
                total = total + beam[:, :half] * beam[:, :half] + beam[:, half:] * beam[:, half:]
            powers[chan] = total
    for chan in range(powers.shape[0]):
        out_ref[:, chan, :] = powers[chan]


def local(voltages, start_block, flags, ranks, phase_index):
    tm = lax.axis_size("tm")
    samples, chan_dev, width = voltages.shape[0], voltages.shape[2], voltages.shape[4]
    own = chan_dev // tm
    vectors = start_block.shape[3]
    beams = phase_index.shape[0]
    half = beams // 2
    factor = 1.0 / (samples * tm)
    params = pltpu.CompilerParams(vmem_limit_bytes=VMEM_LIMIT)
    whole = pl.BlockSpec(memory_space=pltpu.VMEM)
    scalars = pl.BlockSpec(memory_space=pltpu.SMEM)

    series = voltages[:, 0].transpose(1, 0, 2, 3).reshape(chan_dev, samples, 2 * width)
    moved = lax.all_to_all(series, "tm", split_axis=0, concat_axis=0, tiled=True)
    other = lax.ppermute(series, "pol", [(0, 1), (1, 0)])

    own_weights = pl.pallas_call(
        functools.partial(own_weights_kernel, own, chan_dev),
        out_shape=jax.ShapeDtypeStruct((own, 2 * beams, width), BF16),
        in_specs=[whole],
        out_specs=whole,
        compiler_params=params,
        cost_estimate=pl.CostEstimate(
            flops=40 * own * beams * width, bytes_accessed=8 * own * beams * width, transcendentals=0
        ),
    )(phase_index)

    raw = pl.pallas_call(
        functools.partial(raw_beams_kernel, chan_dev),
        grid=(chan_dev,),
        out_shape=jax.ShapeDtypeStruct((chan_dev, 2, samples, beams), F32),
        in_specs=[
            pl.BlockSpec((beams, width), lambda c: (0, 0)),
            pl.BlockSpec((1, samples, 2 * width), lambda c: (c, 0, 0)),
            pl.BlockSpec((1, samples, 2 * width), lambda c: (c, 0, 0)),
        ],
        out_specs=pl.BlockSpec((1, 2, samples, beams), lambda c: (c, 0, 0, 0)),
        scratch_shapes=[pltpu.VMEM((beams, width), BF16)],
        compiler_params=params,
        cost_estimate=pl.CostEstimate(
            flops=8 * chan_dev * samples * 2 * width * beams,
            bytes_accessed=8 * chan_dev * samples * width,
            transcendentals=0,
        ),
    )(phase_index, series, other)

    blocks = moved.reshape(tm, own, samples, 2 * width)
    blocks = blocks.transpose(1, 0, 2, 3).reshape(own, tm * samples, 2 * width)
    packet = jax.ShapeDtypeStruct((own, 2 * vectors, samples + half), F32)
    packets = pl.pallas_call(
        functools.partial(subspace_kernel, tm, own, samples, factor),
        out_shape=[packet] * (2 * tm),
        in_specs=[whole, whole, scalars, scalars, whole],
        out_specs=[whole] * (2 * tm),
        scratch_shapes=[
            pltpu.VMEM((2 * vectors, tm * samples), F32),
            pltpu.VMEM((2 * vectors, beams), F32),
        ],
        compiler_params=params,
        cost_estimate=pl.CostEstimate(
            flops=64 * own * vectors * tm * samples * width * ITERS,
            bytes_accessed=4 * own * tm * samples * width,
            transcendentals=0,
        ),
    )(blocks, start_block, flags, ranks, own_weights)

    arrived = []
    for d in range(tm):
        for swap in range(2):
            packet = packets[2 * d + swap]
            if d or swap:
                route = [
                    (z * 2 + p, (z + d) % tm * 2 + (p + swap) % 2) for z in range(tm) for p in range(2)
                ]
                packet = lax.ppermute(packet, ("tm", "pol"), route)
            arrived.append(packet)

    return pl.pallas_call(
        functools.partial(finish_kernel, tm, own),
        out_shape=jax.ShapeDtypeStruct((samples, chan_dev, half), F32),
        in_specs=[whole] * (1 + 2 * tm),
        out_specs=whole,
        scratch_shapes=[pltpu.VMEM((chan_dev, samples, half), F32)],
        compiler_params=params,
    )(raw, *arrived)


def solution(mesh):
    placed = (
        P(("groups", "tm"), "pol", "chan", None, None),
        P("pol", "chan", None, None, None),
        P(("groups", "chan")),
        P(("groups", "chan")),
        P(),
    )
    return jax.shard_map(
        local,
        mesh=mesh,
        in_specs=placed,
        out_specs=P(("groups", "tm"), "chan", "pol"),
        check_vma=False,
    )
```

```python
import functools

import jax
import jax.numpy as jnp
from jax import lax
from jax.experimental import pallas as pl
from jax.experimental.pallas import tpu as pltpu
from jax.sharding import PartitionSpec as P

ITERS = 4
PHASES = 1024
QUARTER = PHASES // 4
EPS = 1e-06
F32 = jnp.float32
BF16 = jnp.bfloat16
NT = (((1,), (1,)), ((), ()))
NN = (((1,), (0,)), ((), ()))
TN = (((0,), (0,)), ((), ()))
VMEM_LIMIT = 48 * 1024 * 1024


def dot(left, right, dims):
    return lax.dot_general(left, right, dims, preferred_element_type=F32)


def split(values):
    high = values.astype(BF16)
    low = (values - high.astype(F32)).astype(BF16)
    return high, low


def steer(phase, step, norm):
    turn = (phase * step) & (PHASES - 1)
    quadrant = (turn + QUARTER // 2) // QUARTER
    angle = (turn - quadrant * QUARTER).astype(F32) * (2.0 * jnp.pi / PHASES)
    sq = angle * angle
    sine = angle * (1.0 + sq * (-1.0 / 6 + sq * (1.0 / 120 + sq * (-1.0 / 5040 + sq / 362880))))
    cosine = 1.0 + sq * (-0.5 + sq * (1.0 / 24 + sq * (-1.0 / 720 + sq / 40320)))
    odd = (quadrant & 1) == 1
    real = jnp.where(odd, sine, cosine) * norm
    imag = jnp.where(odd, cosine, sine) * norm
    real = jnp.where(((quadrant + 1) & 2) == 2, -real, real)
    imag = jnp.where((quadrant & 2) == 2, -imag, imag)
    return real.astype(BF16), imag.astype(BF16)


def fill_weights(phase_ref, first, rows, step, out):
    norm = 1.0 / (phase_ref.shape[1] ** 0.5)
    chunk = 32

    def body(i, carry):
        at = pl.multiple_of(i * chunk, chunk)
        real, imag = steer(phase_ref[pl.ds(first + at, chunk), :], step, norm)
        out[pl.ds(at, chunk), :] = real
        out[pl.ds(rows + at, chunk), :] = imag
        return carry

    lax.fori_loop(0, rows // chunk, body, 0)


def own_weights_kernel(own, chan_dev, phase_ref, out_ref):
    beams = phase_ref.shape[0]
    first = lax.axis_index("chan") * chan_dev + lax.axis_index("tm") * own
    for o in range(own):
        fill_weights(phase_ref, 0, beams, first + o + 1, out_ref.at[o])


def turned(values, axis):
    size = values.shape[axis]
    at = lax.broadcasted_iota(jnp.int32, values.shape, axis)
    after = pltpu.roll(values, size - 1, axis)
    before = pltpu.roll(values, 1, axis)
    return jnp.where((at & 1) == 0, after, -before)


def raw_beams_kernel(chan_dev, phase_ref, series_ref, mine_ref, other_ref, weights):
    half = phase_ref.shape[0] // 2
    rows = series_ref.shape[1]
    chan_id = lax.axis_index("chan") * chan_dev + pl.program_id(0)
    for swap, out_ref in enumerate((mine_ref, other_ref)):
        first = pl.multiple_of((lax.axis_index("pol") ^ swap) * half, half)
        fill_weights(phase_ref, first, half, chan_id + 1, weights)
        product = dot(series_ref[0], weights[...], NT)
        by_imag = turned(product[:, half:].reshape(rows // 8, 8, half), 1).reshape(rows, half)
        out_ref[0] = product[:, :half] - by_imag


def correlate(real, imag, x):
    vectors = real.shape[0]
    rows = jnp.concatenate([real, imag], axis=0)
    product = dot(jnp.concatenate(split(rows), axis=0), x, NT)
    product = product[: 2 * vectors] + product[2 * vectors :]
    other = turned(product, 1)
    return product[:vectors] + other[vectors:], product[vectors:] - other[:vectors]


def cov_times(real, imag, blocks, factor):
    vectors = real.shape[0]
    total = None
    for x in blocks:
        pair = jnp.concatenate(correlate(real, imag, x), axis=0)
        term = dot(jnp.concatenate(split(pair), axis=0), x, NN)
        total = term if total is None else total + term
    total = (total[: 2 * vectors] + total[2 * vectors :]) * factor
    return total[:vectors], total[vectors:]


def orthonormalize(real_z, imag_z):
    vectors = real_z.shape[0]
    row = lax.broadcasted_iota(jnp.int32, real_z.shape, 0)
    real_v, imag_v = real_z, imag_z
    scale = jnp.zeros((vectors, 1), F32)
    for n in range(vectors):
        here = row == n
        real_a, imag_a = real_v[n : n + 1], imag_v[n : n + 1]
        real_z = jnp.where(here, real_v, real_z)
        imag_z = jnp.where(here, imag_v, imag_z)
        real_d = jnp.sum(real_a * real_z + imag_a * imag_z, axis=1, keepdims=True)
        norm = real_d[n : n + 1] + EPS
        scale = jnp.where(row[:, :1] == n, norm, scale)
        if n + 1 < vectors:
            imag_d = jnp.sum(real_a * imag_z - imag_a * real_z, axis=1, keepdims=True)
            inverse = 1.0 / norm
            later = row[:, :1] > n
            real_c = jnp.where(later, real_d * inverse, 0.0)
            imag_c = jnp.where(later, imag_d * inverse, 0.0)
            real_v = real_v - (real_c * real_a - imag_c * imag_a)
            imag_v = imag_v - (real_c * imag_a + imag_c * real_a)
    factor = 1.0 / jnp.sqrt(scale)
    return real_v * factor, imag_v * factor


def subspace_kernel(tm, own, factor, start_ref, flags_ref, ranks_ref, weights_ref, beams_ref, *rest):
    blocks_ref, outs = rest[:tm], rest[tm + 1 :]
    vectors, width = start_ref.shape[3], start_ref.shape[4]
    rows = blocks_ref[0].shape[1]
    tm_index = lax.axis_index("tm")
    beams = weights_ref.shape[1] // 2
    for o in range(own):
        chan = tm_index * own + o
        real_q = start_ref[0, chan, 0]
        imag_q = start_ref[0, chan, 1]
        blocks = [ref[o] for ref in blocks_ref]
        for sweep in range(ITERS):
            real_z, imag_z = cov_times(real_q, imag_q, blocks, factor)
            real_q, imag_q = orthonormalize(real_z, imag_z)
        rank = flags_ref[chan] * ranks_ref[chan]
        keep = lax.broadcasted_iota(jnp.int32, (vectors, width), 0) < rank
        real_u = jnp.where(keep, real_q, 0.0)
        imag_u = jnp.where(keep, imag_q, 0.0)
        both = jnp.concatenate([real_u, imag_u], axis=0)
        product = dot(jnp.concatenate(split(both), axis=0), weights_ref[o], NT)
        product = product[: 2 * vectors] + product[2 * vectors :]
        real_w = product[:vectors, :beams] - product[vectors:, beams:]
        imag_w = product[:vectors, beams:] + product[vectors:, :beams]
        for x in range(tm):
            outs[x][o, :, :rows] = correlate(real_u, imag_u, blocks[x])[0]
            outs[x][o, :, rows : rows + beams] = real_w
            outs[x][o, :, rows + beams :] = imag_w


def finish_kernel(tm, own, mine_ref, theirs_ref, *rest):
    arrived, out_ref, squares, powers = rest[:-3], rest[-3], rest[-2], rest[-1]
    rows, half = mine_ref.shape[1], mine_ref.shape[2]
    samples = rows // 2
    tm_index = lax.axis_index("tm")
    real_at = pl.multiple_of(rows + lax.axis_index("pol") * half, half)
    imag_at = pl.multiple_of(real_at + 2 * half, half)
    for x in range(tm):
        for o in range(own):
            chan = (tm_index ^ x) * own + o
            total = None
            for raw_ref, ref in ((mine_ref, arrived[x]), (theirs_ref, arrived[tm + x])):
                series = ref[o, :, :rows]
                left = jnp.concatenate([series, -turned(series, 1)], axis=0)
                right = jnp.concatenate(
                    [ref[o, :, pl.ds(real_at, half)], ref[o, :, pl.ds(imag_at, half)]], axis=0
                )
                high_s, low_s = split(left)
                high_w, low_w = split(right)
                left = jnp.concatenate([high_s, high_s, low_s], axis=0)
                right = jnp.concatenate([high_w, low_w, high_w], axis=0)
                beam = raw_ref[chan] - dot(left, right, TN)
                total = beam * beam if total is None else total + beam * beam
            squares[...] = total
            powers[chan] = squares[pl.ds(0, samples, 2), :] + squares[pl.ds(1, samples, 2), :]
    for chan in range(powers.shape[0]):
        out_ref[:, chan, :] = powers[chan]


def local(voltages, start_block, flags, ranks, phase_index):
    tm = lax.axis_size("tm")
    tm_index = lax.axis_index("tm")
    samples, chan_dev, width = voltages.shape[0], voltages.shape[2], voltages.shape[4]
    own = chan_dev // tm
    vectors = start_block.shape[3]
    beams = phase_index.shape[0]
    half = beams // 2
    rows = 2 * samples
    factor = 1.0 / (samples * tm)
    params = pltpu.CompilerParams(vmem_limit_bytes=VMEM_LIMIT)
    whole = pl.BlockSpec(memory_space=pltpu.VMEM)
    scalars = pl.BlockSpec(memory_space=pltpu.SMEM)
    unread = pl.BlockSpec(memory_space=pl.ANY)

    series = voltages[:, 0].transpose(1, 0, 2, 3).reshape(chan_dev, rows, width)

    blocks = [None] * tm
    for x in [*range(2, tm), 1, 0]:
        piece = lax.dynamic_slice_in_dim(series, (tm_index ^ x) * own, own, 0)
        blocks[x] = lax.ppermute(piece, "tm", [(z, z ^ x) for z in range(tm)]) if x else piece

    own_weights = pl.pallas_call(
        functools.partial(own_weights_kernel, own, chan_dev),
        out_shape=jax.ShapeDtypeStruct((own, 2 * beams, width), BF16),
        in_specs=[whole],
        out_specs=whole,
        compiler_params=params,
        cost_estimate=pl.CostEstimate(
            flops=40 * own * beams * width, bytes_accessed=8 * own * beams * width, transcendentals=0
        ),
    )(phase_index)

    raw = jax.ShapeDtypeStruct((chan_dev, rows, half), F32)
    mine, other = pl.pallas_call(
        functools.partial(raw_beams_kernel, chan_dev),
        grid=(chan_dev,),
        out_shape=[raw] * 2,
        in_specs=[
            pl.BlockSpec((beams, width), lambda c: (0, 0)),
            pl.BlockSpec((1, rows, width), lambda c: (c, 0, 0)),
        ],
        out_specs=[pl.BlockSpec((1, rows, half), lambda c: (c, 0, 0))] * 2,
        scratch_shapes=[pltpu.VMEM((beams, width), BF16)],
        compiler_params=params,
        cost_estimate=pl.CostEstimate(
            flops=8 * chan_dev * samples * width * beams,
            bytes_accessed=8 * chan_dev * samples * width,
            transcendentals=0,
        ),
    )(phase_index, series)
    cores = [(0, 1), (1, 0)]

    packet = jax.ShapeDtypeStruct((own, vectors, rows + 2 * beams), F32)
    other, *packets = pl.pallas_call(
        functools.partial(subspace_kernel, tm, own, factor),
        out_shape=[raw] + [packet] * tm,
        in_specs=[whole, scalars, scalars, whole, unread] + [whole] * tm,
        out_specs=[unread] + [whole] * tm,
        input_output_aliases={4: 0},
        compiler_params=params,
        cost_estimate=pl.CostEstimate(
            flops=64 * own * vectors * tm * samples * width * ITERS,
            bytes_accessed=4 * own * tm * samples * width,
            transcendentals=0,
        ),
    )(start_block, flags, ranks, own_weights, other, *blocks)

    theirs = lax.ppermute(other, "pol", cores)
    arrived = list(packets)
    for x in range(1, tm):
        arrived[x] = lax.ppermute(packets[x], "tm", [(z, z ^ x) for z in range(tm)])
    arrived += [lax.ppermute(packet, "pol", cores) for packet in arrived]

    return pl.pallas_call(
        functools.partial(finish_kernel, tm, own),
        out_shape=jax.ShapeDtypeStruct((samples, chan_dev, half), F32),
        in_specs=[whole] * (2 + 2 * tm),
        out_specs=whole,
        scratch_shapes=[
            pltpu.VMEM((rows, half), F32),
            pltpu.VMEM((chan_dev, samples, half), F32),
        ],
        compiler_params=params,
    )(mine, theirs, *arrived)


def solution(mesh):
    placed = (
        P(("groups", "tm"), "pol", "chan", None, None),
        P("pol", "chan", None, None, None),
        P(("groups", "chan")),
        P(("groups", "chan")),
        P(),
    )
    return jax.shard_map(
        local,
        mesh=mesh,
        in_specs=placed,
        out_specs=P(("groups", "tm"), "chan", "pol"),
        check_vma=False,
    )
```

```python
import functools

import jax
import jax.numpy as jnp
from jax import lax
from jax.experimental import pallas as pl
from jax.experimental.pallas import tpu as pltpu
from jax.sharding import PartitionSpec as P

ITERS = 4
PHASES = 1024
QUARTER = PHASES // 4
EPS = 1e-06
F32 = jnp.float32
BF16 = jnp.bfloat16
NT = (((1,), (1,)), ((), ()))
NN = (((1,), (0,)), ((), ()))
TN = (((0,), (0,)), ((), ()))
VMEM_LIMIT = 48 * 1024 * 1024


def dot(left, right, dims):
    return lax.dot_general(left, right, dims, preferred_element_type=F32)


def split(values):
    high = values.astype(BF16)
    low = (values - high.astype(F32)).astype(BF16)
    return high, low


def steer(phase, step, norm):
    turn = (phase * step) & (PHASES - 1)
    quadrant = (turn + QUARTER // 2) // QUARTER
    angle = (turn - quadrant * QUARTER).astype(F32) * (2.0 * jnp.pi / PHASES)
    sq = angle * angle
    sine = angle * (1.0 + sq * (-1.0 / 6 + sq * (1.0 / 120 + sq * (-1.0 / 5040 + sq / 362880))))
    cosine = 1.0 + sq * (-0.5 + sq * (1.0 / 24 + sq * (-1.0 / 720 + sq / 40320)))
    odd = (quadrant & 1) == 1
    real = jnp.where(odd, sine, cosine) * norm
    imag = jnp.where(odd, cosine, sine) * norm
    real = jnp.where(((quadrant + 1) & 2) == 2, -real, real)
    imag = jnp.where((quadrant & 2) == 2, -imag, imag)
    return real.astype(BF16), imag.astype(BF16)


def fill_weights(phase_ref, first, rows, step, out):
    norm = 1.0 / (phase_ref.shape[1] ** 0.5)
    chunk = 32

    def body(i, carry):
        at = pl.multiple_of(i * chunk, chunk)
        real, imag = steer(phase_ref[pl.ds(first + at, chunk), :], step, norm)
        out[pl.ds(at, chunk), :] = real
        out[pl.ds(rows + at, chunk), :] = imag
        return carry

    lax.fori_loop(0, rows // chunk, body, 0)


def shifts(tm, pol):
    first = [*range(2, tm), 1]
    second = [1, *range(2, tm)]
    return [0] + [jnp.where(pol == 0, a, b) for a, b in zip(first, second)]


def routes(tm):
    first = [*range(2, tm), 1]
    second = [1, *range(2, tm)]
    return [
        [(2 * z + p, 2 * (z ^ x[p]) + p) for z in range(tm) for p in range(2)]
        for x in zip(first, second)
    ]


def own_weights_kernel(own, chan_dev, phase_ref, beams_ref, out_ref, beams_out_ref):
    beams = phase_ref.shape[0]
    first = lax.axis_index("chan") * chan_dev + lax.axis_index("tm") * own
    for o in range(own):
        fill_weights(phase_ref, 0, beams, first + o + 1, out_ref.at[o])


def turned(values, axis):
    size = values.shape[axis]
    at = lax.broadcasted_iota(jnp.int32, values.shape, axis)
    after = pltpu.roll(values, size - 1, axis)
    before = pltpu.roll(values, 1, axis)
    return jnp.where((at & 1) == 0, after, -before)


def raw_beams_kernel(tm, own, phase_ref, *rest):
    pieces, (mine_ref, other_ref, weights) = rest[:tm], rest[tm:]
    half = phase_ref.shape[0] // 2
    rows = pieces[0].shape[1]
    pol = lax.axis_index("pol")
    start = lax.axis_index("chan") * tm * own
    for x, piece in zip(shifts(tm, pol), pieces):
        for o in range(own):
            chan = (lax.axis_index("tm") ^ x) * own + o
            for swap, out_ref in enumerate((mine_ref, other_ref)):
                first = pl.multiple_of((pol ^ swap) * half, half)
                fill_weights(phase_ref, first, half, start + chan + 1, weights)
                product = dot(piece[o], weights[...], NT)
                by_imag = turned(product[:, half:].reshape(rows // 8, 8, half), 1).reshape(rows, half)
                out_ref[chan] = product[:, :half] - by_imag


def cov_terms(x):
    rotated = -turned(x.astype(F32), 0)
    return dot(x, x, TN), dot(x, rotated.astype(BF16), TN)


def cov_kernel(*refs):
    blocks, out_ref = refs[:-1], refs[-1]
    for o in range(out_ref.shape[0]):
        for i, ref in enumerate(blocks):
            real, imag = cov_terms(ref[o])
            out_ref[o, 0] = real if i == 0 else out_ref[o, 0] + real
            out_ref[o, 1] = imag if i == 0 else out_ref[o, 1] + imag


def correlate(real, imag, x):
    vectors = real.shape[0]
    rows = jnp.concatenate([real, imag], axis=0)
    product = dot(jnp.concatenate(split(rows), axis=0), x, NT)
    product = product[: 2 * vectors] + product[2 * vectors :]
    return product[:vectors] + turned(product[vectors:], 1)


def cov_times(real, imag, high_ref, low_ref):
    vectors = real.shape[0]
    rows = jnp.concatenate(
        [jnp.concatenate([real, imag], axis=1), jnp.concatenate([imag, -real], axis=1)], axis=0
    )
    high, low = split(rows)
    product = dot(jnp.concatenate([high, low], axis=0), high_ref[...], NN)
    product = product[: 2 * vectors] + product[2 * vectors :] + dot(high, low_ref[...], NN)
    return product[:vectors], product[vectors:]


def orthonormalize(real_z, imag_z):
    vectors = real_z.shape[0]
    row = lax.broadcasted_iota(jnp.int32, real_z.shape, 0)
    real_v, imag_v = real_z, imag_z
    scale = jnp.zeros((vectors, 1), F32)
    for n in range(vectors):
        here = row == n
        real_a, imag_a = real_v[n : n + 1], imag_v[n : n + 1]
        real_z = jnp.where(here, real_v, real_z)
        imag_z = jnp.where(here, imag_v, imag_z)
        real_d = jnp.sum(real_a * real_z + imag_a * imag_z, axis=1, keepdims=True)
        norm = real_d[n : n + 1] + EPS
        scale = jnp.where(row[:, :1] == n, norm, scale)
        if n + 1 < vectors:
            imag_d = jnp.sum(real_a * imag_z - imag_a * real_z, axis=1, keepdims=True)
            inverse = 1.0 / norm
            later = row[:, :1] > n
            real_c = jnp.where(later, real_d * inverse, 0.0)
            imag_c = jnp.where(later, imag_d * inverse, 0.0)
            real_v = real_v - (real_c * real_a - imag_c * imag_a)
            imag_v = imag_v - (real_c * imag_a + imag_c * real_a)
    factor = 1.0 / jnp.sqrt(scale)
    return real_v * factor, imag_v * factor


def subspace_kernel(tm, own, factor, start_ref, flags_ref, ranks_ref, weights_ref, cov_ref, *rest):
    blocks, (out_ref, high_ref, low_ref) = rest[:tm], rest[tm:]
    vectors, width = start_ref.shape[3], start_ref.shape[4]
    rows = blocks[0].shape[1]
    tm_index = lax.axis_index("tm")
    beams = weights_ref.shape[1] // 2
    half = beams // 2
    for o in range(own):
        chan = tm_index * own + o
        for part, term in enumerate(cov_terms(blocks[-1][o])):
            high, low = split((cov_ref[o, part] + term) * factor)
            high_ref[part * width : (part + 1) * width] = high
            low_ref[part * width : (part + 1) * width] = low
        real_q = start_ref[0, chan, 0]
        imag_q = start_ref[0, chan, 1]
        for sweep in range(ITERS):
            real_z, imag_z = cov_times(real_q, imag_q, high_ref, low_ref)
            real_q, imag_q = orthonormalize(real_z, imag_z)
        rank = flags_ref[chan] * ranks_ref[chan]
        keep = lax.broadcasted_iota(jnp.int32, (vectors, width), 0) < rank
        real_u = jnp.where(keep, real_q, 0.0)
        imag_u = jnp.where(keep, imag_q, 0.0)
        both = jnp.concatenate([real_u, imag_u], axis=0)
        product = dot(jnp.concatenate(split(both), axis=0), weights_ref[o], NT)
        product = product[: 2 * vectors] + product[2 * vectors :]
        real_w = product[:vectors, :beams] - product[vectors:, beams:]
        imag_w = product[:vectors, beams:] + product[vectors:, :beams]
        for x, block in zip(shifts(tm, lax.axis_index("pol")), blocks):
            series = correlate(real_u, imag_u, block[o])
            for core in range(2):
                to = (tm_index ^ x) * 2 + core
                out_ref[to, o, :, :rows] = series
                out_ref[to, o, :, rows : rows + half] = real_w[:, core * half : (core + 1) * half]
                out_ref[to, o, :, rows + half :] = imag_w[:, core * half : (core + 1) * half]


def finish_kernel(tm, own, mine_ref, theirs_ref, arrived_ref, out_ref, squares, powers):
    rows, half = mine_ref.shape[1], mine_ref.shape[2]
    samples = rows // 2
    pol = lax.axis_index("pol")
    for chan in range(tm * own):
        total = None
        for swap, raw_ref in enumerate((mine_ref, theirs_ref)):
            packet = arrived_ref[chan // own * 2 + (pol ^ swap), chan % own]
            series = packet[:, :rows]
            left = jnp.concatenate([series, -turned(series, 1)], axis=0)
            right = jnp.concatenate([packet[:, rows : rows + half], packet[:, rows + half :]], axis=0)
            high_s, low_s = split(left)
            high_w, low_w = split(right)
            left = jnp.concatenate([high_s, high_s, low_s], axis=0)
            right = jnp.concatenate([high_w, low_w, high_w], axis=0)
            beam = raw_ref[chan] - dot(left, right, TN)
            total = beam * beam if total is None else total + beam * beam
        squares[...] = total
        powers[chan] = squares[pl.ds(0, samples, 2), :] + squares[pl.ds(1, samples, 2), :]
    for chan in range(powers.shape[0]):
        out_ref[:, chan, :] = powers[chan]


def local(voltages, start_block, flags, ranks, phase_index):
    tm = lax.axis_size("tm")
    tm_index = lax.axis_index("tm")
    samples, chan_dev, width = voltages.shape[0], voltages.shape[2], voltages.shape[4]
    own = chan_dev // tm
    vectors = start_block.shape[3]
    beams = phase_index.shape[0]
    half = beams // 2
    rows = 2 * samples
    factor = 1.0 / (samples * tm)
    params = pltpu.CompilerParams(vmem_limit_bytes=VMEM_LIMIT)
    whole = pl.BlockSpec(memory_space=pltpu.VMEM)
    scalars = pl.BlockSpec(memory_space=pltpu.SMEM)
    unread = pl.BlockSpec(memory_space=pl.ANY)

    def cost(multiplies, moved):
        return pl.CostEstimate(flops=2 * multiplies, bytes_accessed=moved, transcendentals=0)

    pieces = [
        lax.dynamic_slice_in_dim(voltages[:, 0], (tm_index ^ x) * own, own, 1)
        .transpose(1, 0, 2, 3)
        .reshape(own, rows, width)
        for x in shifts(tm, lax.axis_index("pol"))
    ]
    blocks = pieces[:1] + [
        lax.ppermute(piece, ("tm", "pol"), route) for piece, route in zip(pieces[1:], routes(tm))
    ]

    raw = jax.ShapeDtypeStruct((chan_dev, rows, half), F32)
    mine, other = pl.pallas_call(
        functools.partial(raw_beams_kernel, tm, own),
        out_shape=[raw] * 2,
        in_specs=[whole] * (1 + tm),
        out_specs=[whole] * 2,
        scratch_shapes=[pltpu.VMEM((beams, width), BF16)],
        compiler_params=params,
        cost_estimate=cost(4 * chan_dev * samples * width * beams, 8 * chan_dev * samples * width),
    )(phase_index, *pieces)

    own_weights, other = pl.pallas_call(
        functools.partial(own_weights_kernel, own, chan_dev),
        out_shape=[jax.ShapeDtypeStruct((own, 2 * beams, width), BF16), raw],
        in_specs=[whole, unread],
        out_specs=[whole, unread],
        input_output_aliases={1: 1},
        compiler_params=params,
        cost_estimate=cost(20 * own * beams * width, 8 * own * beams * width),
    )(phase_index, other)
    theirs = lax.ppermute(other, "pol", [(0, 1), (1, 0)])

    cov = pl.pallas_call(
        cov_kernel,
        out_shape=jax.ShapeDtypeStruct((own, 2, width, width), F32),
        in_specs=[whole] * (tm - 1),
        out_specs=whole,
        compiler_params=params,
        cost_estimate=cost(4 * (tm - 1) * own * samples * width * width, 8 * own * width * width),
    )(*blocks[:-1])

    packets = pl.pallas_call(
        functools.partial(subspace_kernel, tm, own, factor),
        out_shape=jax.ShapeDtypeStruct((2 * tm, own, vectors, rows + beams), F32),
        in_specs=[whole, scalars, scalars, whole, whole] + [whole] * tm,
        out_specs=whole,
        scratch_shapes=[pltpu.VMEM((2 * width, width), BF16)] * 2,
        compiler_params=params,
        cost_estimate=cost(32 * own * vectors * tm * samples * width, 8 * own * width * width),
    )(start_block, flags, ranks, own_weights, cov, *blocks)
    arrived = lax.all_to_all(packets, ("tm", "pol"), split_axis=0, concat_axis=0, tiled=True)

    return pl.pallas_call(
        functools.partial(finish_kernel, tm, own),
        out_shape=jax.ShapeDtypeStruct((samples, chan_dev, half), F32),
        in_specs=[whole] * 3,
        out_specs=whole,
        scratch_shapes=[
            pltpu.VMEM((rows, half), F32),
            pltpu.VMEM((chan_dev, samples, half), F32),
        ],
        compiler_params=params,
    )(mine, theirs, arrived)


def solution(mesh):
    placed = (
        P(("groups", "tm"), "pol", "chan", None, None),
        P("pol", "chan", None, None, None),
        P(("groups", "chan")),
        P(("groups", "chan")),
        P(),
    )
    return jax.shard_map(
        local,
        mesh=mesh,
        in_specs=placed,
        out_specs=P(("groups", "tm"), "chan", "pol"),
        check_vma=False,
    )
```

```python
import functools

import jax
import jax.numpy as jnp
from jax import lax
from jax.experimental import pallas as pl
from jax.experimental.pallas import tpu as pltpu
from jax.sharding import PartitionSpec as P

ITERS = 4
PHASES = 1024
QUARTER = PHASES // 4
EPS = 1e-06
F32 = jnp.float32
BF16 = jnp.bfloat16
NT = (((1,), (1,)), ((), ()))
NN = (((1,), (0,)), ((), ()))
TN = (((0,), (0,)), ((), ()))
VMEM_LIMIT = 48 * 1024 * 1024


def dot(left, right, dims):
    return lax.dot_general(left, right, dims, preferred_element_type=F32)


def split(values):
    high = values.astype(BF16)
    low = (values - high.astype(F32)).astype(BF16)
    return high, low


def steer(phase, step, norm):
    turn = (phase * step) & (PHASES - 1)
    quadrant = (turn + QUARTER // 2) // QUARTER
    angle = (turn - quadrant * QUARTER).astype(F32) * (2.0 * jnp.pi / PHASES)
    sq = angle * angle
    sine = angle * (1.0 + sq * (-1.0 / 6 + sq * (1.0 / 120 + sq * (-1.0 / 5040 + sq / 362880))))
    cosine = 1.0 + sq * (-0.5 + sq * (1.0 / 24 + sq * (-1.0 / 720 + sq / 40320)))
    odd = (quadrant & 1) == 1
    real = jnp.where(odd, sine, cosine) * norm
    imag = jnp.where(odd, cosine, sine) * norm
    real = jnp.where(((quadrant + 1) & 2) == 2, -real, real)
    imag = jnp.where((quadrant & 2) == 2, -imag, imag)
    return real.astype(BF16), imag.astype(BF16)


def fill_weights(phase_ref, first, rows, step, out):
    norm = 1.0 / (phase_ref.shape[1] ** 0.5)
    chunk = 32

    def body(i, carry):
        at = pl.multiple_of(i * chunk, chunk)
        real, imag = steer(phase_ref[pl.ds(first + at, chunk), :], step, norm)
        out[pl.ds(at, chunk), :] = real
        out[pl.ds(rows + at, chunk), :] = imag
        return carry

    lax.fori_loop(0, rows // chunk, body, 0)


def orders(tm):
    far = [*range(2, tm)]
    return [0, *far[:1], 1, *far[1:]], [0, *far, 1]


def shifts(tm, pol):
    return [jnp.where(pol == 0, a, b) for a, b in zip(*orders(tm))]


def routes(tm):
    return [
        [(2 * z + p, 2 * (z ^ x[p]) + p) for z in range(tm) for p in range(2)]
        for x in zip(*orders(tm))
    ]


def cut_kernel(tm, own, voltages_ref, *rest):
    pieces, done = rest[:tm], rest[tm]
    copies = []
    for i, x in enumerate(shifts(tm, lax.axis_index("pol"))):
        first = (lax.axis_index("tm") ^ x) * own
        copy = pltpu.make_async_copy(voltages_ref.at[:, 0, pl.ds(first, own)], pieces[i], done.at[i])
        copy.start()
        copies.append(copy)
    for copy in copies:
        copy.wait()


def turned(values, axis):
    size = values.shape[axis]
    at = lax.broadcasted_iota(jnp.int32, values.shape, axis)
    after = pltpu.roll(values, size - 1, axis)
    before = pltpu.roll(values, 1, axis)
    return jnp.where((at & 1) == 0, after, -before)


def raw_beams_kernel(tm, own, phase_ref, *rest):
    pieces, (mine_ref, other_ref, weights) = rest[:tm], rest[tm:]
    half = phase_ref.shape[0] // 2
    rows = pieces[0].shape[1]
    pol = lax.axis_index("pol")
    start = lax.axis_index("chan") * tm * own
    for x, piece in zip(shifts(tm, pol), pieces):
        for o in range(own):
            chan = (lax.axis_index("tm") ^ x) * own + o
            for swap, out_ref in enumerate((mine_ref, other_ref)):
                first = pl.multiple_of((pol ^ swap) * half, half)
                fill_weights(phase_ref, first, half, start + chan + 1, weights)
                product = dot(piece[o], weights[...], NT)
                by_imag = turned(product[:, half:].reshape(rows // 8, 8, half), 1).reshape(rows, half)
                out_ref[chan] = product[:, :half] - by_imag


def cov_terms(x):
    rotated = -turned(x.astype(F32), 0)
    return dot(x, x, TN), dot(x, rotated.astype(BF16), TN)


def own_kernel(own, chan_dev, phase_ref, block_ref, weights_ref, cov_ref):
    beams = phase_ref.shape[0]
    first = lax.axis_index("chan") * chan_dev + lax.axis_index("tm") * own
    for o in range(own):
        fill_weights(phase_ref, 0, beams, first + o + 1, weights_ref.at[o])
        cov_ref[o, 0], cov_ref[o, 1] = cov_terms(block_ref[o])


def cov_kernel(factor, cov_ref, *rest):
    blocks, (high_ref, low_ref) = rest[:-2], rest[-2:]
    width = cov_ref.shape[2]
    for o in range(cov_ref.shape[0]):
        sums = cov_ref[o, 0], cov_ref[o, 1]
        for block in blocks:
            sums = [total + term for total, term in zip(sums, cov_terms(block[o]))]
        for part, total in enumerate(sums):
            high, low = split(total * factor)
            high_ref[o, part * width : (part + 1) * width] = high
            low_ref[o, part * width : (part + 1) * width] = low


def correlate(real, imag, x):
    vectors = real.shape[0]
    rows = jnp.concatenate([real, imag], axis=0)
    product = dot(jnp.concatenate(split(rows), axis=0), x, NT)
    product = product[: 2 * vectors] + product[2 * vectors :]
    return product[:vectors] + turned(product[vectors:], 1)


def cov_times(real, imag, high_ref, low_ref):
    vectors = real.shape[0]
    rows = jnp.concatenate(
        [jnp.concatenate([real, imag], axis=1), jnp.concatenate([imag, -real], axis=1)], axis=0
    )
    high, low = split(rows)
    product = dot(jnp.concatenate([high, low], axis=0), high_ref[...], NN)
    product = product[: 2 * vectors] + product[2 * vectors :] + dot(high, low_ref[...], NN)
    return product[:vectors], product[vectors:]


def orthonormalize(real_z, imag_z):
    vectors = real_z.shape[0]
    row = lax.broadcasted_iota(jnp.int32, real_z.shape, 0)
    real_v, imag_v = real_z, imag_z
    scale = jnp.zeros((vectors, 1), F32)
    for n in range(vectors):
        here = row == n
        real_a, imag_a = real_v[n : n + 1], imag_v[n : n + 1]
        real_z = jnp.where(here, real_v, real_z)
        imag_z = jnp.where(here, imag_v, imag_z)
        real_d = jnp.sum(real_a * real_z + imag_a * imag_z, axis=1, keepdims=True)
        norm = real_d[n : n + 1] + EPS
        scale = jnp.where(row[:, :1] == n, norm, scale)
        if n + 1 < vectors:
            imag_d = jnp.sum(real_a * imag_z - imag_a * real_z, axis=1, keepdims=True)
            inverse = 1.0 / norm
            later = row[:, :1] > n
            real_c = jnp.where(later, real_d * inverse, 0.0)
            imag_c = jnp.where(later, imag_d * inverse, 0.0)
            real_v = real_v - (real_c * real_a - imag_c * imag_a)
            imag_v = imag_v - (real_c * imag_a + imag_c * real_a)
    factor = 1.0 / jnp.sqrt(scale)
    return real_v * factor, imag_v * factor


def subspace_kernel(tm, own, beams_ref, start_ref, flags_ref, ranks_ref, weights_ref, high_ref, low_ref, *rest):
    blocks, outs = rest[:tm], rest[tm + 1 :]
    vectors, width = start_ref.shape[3], start_ref.shape[4]
    rows = blocks[0].shape[1]
    tm_index = lax.axis_index("tm")
    beams = weights_ref.shape[1] // 2
    for o in range(own):
        chan = tm_index * own + o
        real_q = start_ref[0, chan, 0]
        imag_q = start_ref[0, chan, 1]
        for sweep in range(ITERS):
            real_z, imag_z = cov_times(real_q, imag_q, high_ref.at[o], low_ref.at[o])
            real_q, imag_q = orthonormalize(real_z, imag_z)
        rank = flags_ref[chan] * ranks_ref[chan]
        keep = lax.broadcasted_iota(jnp.int32, (vectors, width), 0) < rank
        real_u = jnp.where(keep, real_q, 0.0)
        imag_u = jnp.where(keep, imag_q, 0.0)
        both = jnp.concatenate([real_u, imag_u], axis=0)
        product = dot(jnp.concatenate(split(both), axis=0), weights_ref[o], NT)
        product = product[: 2 * vectors] + product[2 * vectors :]
        real_w = product[:vectors, :beams] - product[vectors:, beams:]
        imag_w = product[:vectors, beams:] + product[vectors:, :beams]
        series = [correlate(real_u, imag_u, block[o]) for block in blocks]
        first, second = orders(tm)
        for x, out in enumerate(outs):
            a, b = first.index(x), second.index(x)
            out[o, :, :rows] = jnp.where(lax.axis_index("pol") == 0, series[a], series[b])
            out[o, :, rows : rows + beams] = real_w
            out[o, :, rows + beams :] = imag_w


def nulled_squares(raw, packet_ref):
    rows, half = raw.shape
    at = pl.multiple_of(rows + lax.axis_index("pol") * half, half)
    series = packet_ref[:, :rows]
    left = jnp.concatenate([series, -turned(series, 1)], axis=0)
    right = jnp.concatenate(
        [packet_ref[:, pl.ds(at, half)], packet_ref[:, pl.ds(pl.multiple_of(at + 2 * half, half), half)]],
        axis=0,
    )
    high_s, low_s = split(left)
    high_w, low_w = split(right)
    left = jnp.concatenate([high_s, high_s, low_s], axis=0)
    right = jnp.concatenate([high_w, low_w, high_w], axis=0)
    beam = raw - dot(left, right, TN)
    return beam * beam


def first_kernel(own, raw_ref, *rest):
    packets, out_ref = rest[:-1], rest[-1]
    for x, ref in enumerate(packets):
        for o in range(own):
            chan = (lax.axis_index("tm") ^ x) * own + o
            out_ref[chan] = nulled_squares(raw_ref[chan], ref.at[o])


def second_kernel(own, first_ref, raw_ref, *rest):
    packets, (out_ref, squares, powers) = rest[:-3], rest[-3:]
    samples = out_ref.shape[0]
    for x, ref in enumerate(packets):
        for o in range(own):
            chan = (lax.axis_index("tm") ^ x) * own + o
            squares[...] = first_ref[chan] + nulled_squares(raw_ref[chan], ref.at[o])
            powers[chan] = squares[pl.ds(0, samples, 2), :] + squares[pl.ds(1, samples, 2), :]
    for chan in range(powers.shape[0]):
        out_ref[:, chan, :] = powers[chan]


def local(voltages, start_block, flags, ranks, phase_index):
    tm = lax.axis_size("tm")
    tm_index = lax.axis_index("tm")
    samples, chan_dev, width = voltages.shape[0], voltages.shape[2], voltages.shape[4]
    own = chan_dev // tm
    vectors = start_block.shape[3]
    beams = phase_index.shape[0]
    half = beams // 2
    rows = 2 * samples
    factor = 1.0 / (samples * tm)
    params = pltpu.CompilerParams(vmem_limit_bytes=VMEM_LIMIT)
    whole = pl.BlockSpec(memory_space=pltpu.VMEM)
    scalars = pl.BlockSpec(memory_space=pltpu.SMEM)
    unread = pl.BlockSpec(memory_space=pl.ANY)

    def cost(multiplies, moved):
        return pl.CostEstimate(flops=2 * multiplies, bytes_accessed=moved, transcendentals=0)

    cut = pl.pallas_call(
        functools.partial(cut_kernel, tm, own),
        out_shape=[jax.ShapeDtypeStruct((samples, own, 2, width), BF16)] * tm,
        in_specs=[unread],
        out_specs=[whole] * tm,
        scratch_shapes=[pltpu.SemaphoreType.DMA((tm,))],
        compiler_params=params,
    )(voltages)
    pieces = [piece.transpose(1, 0, 2, 3).reshape(own, rows, width) for piece in cut]
    blocks = pieces[:1] + [
        lax.ppermute(piece, ("tm", "pol"), route) for piece, route in zip(pieces[1:], routes(tm)[1:])
    ]

    raw = jax.ShapeDtypeStruct((chan_dev, rows, half), F32)
    mine, other = pl.pallas_call(
        functools.partial(raw_beams_kernel, tm, own),
        out_shape=[raw] * 2,
        in_specs=[whole] * (1 + tm),
        out_specs=[whole] * 2,
        scratch_shapes=[pltpu.VMEM((beams, width), BF16)],
        compiler_params=params,
        cost_estimate=cost(4 * chan_dev * samples * width * beams, 8 * chan_dev * samples * width),
    )(phase_index, *pieces)

    cov = jax.ShapeDtypeStruct((own, 2, width, width), F32)
    own_weights, cov = pl.pallas_call(
        functools.partial(own_kernel, own, chan_dev),
        out_shape=[jax.ShapeDtypeStruct((own, 2 * beams, width), BF16), cov],
        in_specs=[whole] * 2,
        out_specs=[whole] * 2,
        compiler_params=params,
        cost_estimate=cost(
            own * width * (20 * beams + 4 * samples * width), 8 * own * width * (beams + width)
        ),
    )(phase_index, pieces[0])
    high, low = pl.pallas_call(
        functools.partial(cov_kernel, factor),
        out_shape=[jax.ShapeDtypeStruct((own, 2 * width, width), BF16)] * 2,
        in_specs=[whole] * tm,
        out_specs=[whole] * 2,
        compiler_params=params,
        cost_estimate=cost(4 * (tm - 1) * own * samples * width * width, 16 * own * width * width),
    )(cov, *blocks[1:])

    other, *packets = pl.pallas_call(
        functools.partial(subspace_kernel, tm, own),
        out_shape=[raw] + [jax.ShapeDtypeStruct((own, vectors, rows + 2 * beams), F32)] * tm,
        in_specs=[unread, whole, scalars, scalars] + [whole] * (3 + tm),
        out_specs=[unread] + [whole] * tm,
        input_output_aliases={0: 0},
        compiler_params=params,
        cost_estimate=cost(32 * own * vectors * tm * samples * width, 8 * own * width * width),
    )(other, start_block, flags, ranks, own_weights, high, low, *blocks)
    cores = [(0, 1), (1, 0)]
    theirs = lax.ppermute(other, "pol", cores)
    arrived = list(packets)
    for x in reversed(range(1, tm)):
        arrived[x] = lax.ppermute(packets[x], "tm", [(z, z ^ x) for z in range(tm)])
    swapped = [lax.ppermute(packet, "pol", cores) for packet in arrived]

    finish = cost(2 * chan_dev * rows * 6 * vectors * half, 8 * chan_dev * rows * half)
    part = pl.pallas_call(
        functools.partial(first_kernel, own),
        out_shape=raw,
        in_specs=[whole] * (1 + tm),
        out_specs=whole,
        compiler_params=params,
        cost_estimate=finish,
    )(mine, *arrived)
    return pl.pallas_call(
        functools.partial(second_kernel, own),
        out_shape=jax.ShapeDtypeStruct((samples, chan_dev, half), F32),
        in_specs=[whole] * (2 + tm),
        out_specs=whole,
        scratch_shapes=[
            pltpu.VMEM((rows, half), F32),
            pltpu.VMEM((chan_dev, samples, half), F32),
        ],
        compiler_params=params,
        cost_estimate=finish,
    )(part, theirs, *swapped)


def solution(mesh):
    placed = (
        P(("groups", "tm"), "pol", "chan", None, None),
        P("pol", "chan", None, None, None),
        P(("groups", "chan")),
        P(("groups", "chan")),
        P(),
    )
    return jax.shard_map(
        local,
        mesh=mesh,
        in_specs=placed,
        out_specs=P(("groups", "tm"), "chan", "pol"),
        check_vma=False,
    )
```

```python
import functools

import jax
import jax.numpy as jnp
from jax import lax
from jax.experimental import pallas as pl
from jax.experimental.pallas import tpu as pltpu
from jax.sharding import PartitionSpec as P

ITERS = 4
PHASES = 1024
QUARTER = PHASES // 4
EPS = 1e-06
F32 = jnp.float32
BF16 = jnp.bfloat16
NT = (((1,), (1,)), ((), ()))
NN = (((1,), (0,)), ((), ()))
TN = (((0,), (0,)), ((), ()))
VMEM_LIMIT = 48 * 1024 * 1024


def dot(left, right, dims):
    return lax.dot_general(left, right, dims, preferred_element_type=F32)


def split(values):
    high = values.astype(BF16)
    low = (values - high.astype(F32)).astype(BF16)
    return high, low


def steer(phase, step, norm):
    turn = (phase * step) & (PHASES - 1)
    quadrant = (turn + QUARTER // 2) // QUARTER
    angle = (turn - quadrant * QUARTER).astype(F32) * (2.0 * jnp.pi / PHASES)
    sq = angle * angle
    sine = angle * (1.0 + sq * (-1.0 / 6 + sq * (1.0 / 120 + sq * (-1.0 / 5040 + sq / 362880))))
    cosine = 1.0 + sq * (-0.5 + sq * (1.0 / 24 + sq * (-1.0 / 720 + sq / 40320)))
    odd = (quadrant & 1) == 1
    real = jnp.where(odd, sine, cosine) * norm
    imag = jnp.where(odd, cosine, sine) * norm
    real = jnp.where(((quadrant + 1) & 2) == 2, -real, real)
    imag = jnp.where((quadrant & 2) == 2, -imag, imag)
    return real.astype(BF16), imag.astype(BF16)


def fill_weights(phase_ref, first, rows, step, out):
    norm = 1.0 / (phase_ref.shape[1] ** 0.5)
    chunk = 32

    def body(i, carry):
        at = pl.multiple_of(i * chunk, chunk)
        real, imag = steer(phase_ref[pl.ds(first + at, chunk), :], step, norm)
        out[pl.ds(at, chunk), :] = real
        out[pl.ds(rows + at, chunk), :] = imag
        return carry

    lax.fori_loop(0, rows // chunk, body, 0)


def orders(tm):
    far = [*range(2, tm)]
    return [0, *far[:1], 1, *far[1:]], [0, *far, 1]


def shifts(tm, pol):
    return [jnp.where(pol == 0, a, b) for a, b in zip(*orders(tm))]


def routes(tm):
    return [
        [(2 * z + p, 2 * (z ^ x[p]) + p) for z in range(tm) for p in range(2)]
        for x in zip(*orders(tm))
    ]


def cut_kernel(tm, own, voltages_ref, *rest):
    pieces, done = rest[:tm], rest[tm]
    copies = []
    for i, x in enumerate(shifts(tm, lax.axis_index("pol"))):
        first = (lax.axis_index("tm") ^ x) * own
        copy = pltpu.make_async_copy(voltages_ref.at[:, 0, pl.ds(first, own)], pieces[i], done.at[i])
        copy.start()
        copies.append(copy)
    for copy in copies:
        copy.wait()


def turned(values, axis):
    size = values.shape[axis]
    at = lax.broadcasted_iota(jnp.int32, values.shape, axis)
    after = pltpu.roll(values, size - 1, axis)
    before = pltpu.roll(values, 1, axis)
    return jnp.where((at & 1) == 0, after, -before)


def raw_beams_kernel(tm, own, phase_ref, *rest):
    pieces, (mine_ref, other_ref, weights) = rest[:tm], rest[tm:]
    half = phase_ref.shape[0] // 2
    rows = pieces[0].shape[1]
    pol = lax.axis_index("pol")
    start = lax.axis_index("chan") * tm * own
    for x, piece in zip(shifts(tm, pol), pieces):
        for o in range(own):
            chan = (lax.axis_index("tm") ^ x) * own + o
            for swap, out_ref in enumerate((mine_ref, other_ref)):
                first = pl.multiple_of((pol ^ swap) * half, half)
                fill_weights(phase_ref, first, half, start + chan + 1, weights)
                product = dot(piece[o], weights[...], NT)
                by_imag = turned(product[:, half:].reshape(rows // 8, 8, half), 1).reshape(rows, half)
                out_ref[chan] = product[:, :half] - by_imag


def own_weights_kernel(own, chan_dev, phase_ref, out_ref):
    beams = phase_ref.shape[0]
    first = lax.axis_index("chan") * chan_dev + lax.axis_index("tm") * own
    for o in range(own):
        fill_weights(phase_ref, 0, beams, first + o + 1, out_ref.at[o])


def fill_cov(factor, blocks, own_at, across_ref, along_ref, rotated_ref, high_ref, low_ref):
    rows, width = blocks[0].shape[1:]
    for i, block in enumerate(blocks):
        x = block[own_at]
        at = slice(i * rows, (i + 1) * rows)
        along_ref[at] = x
        rotated_ref[at] = -turned(x.astype(F32), 0).astype(BF16)
        across_ref[:, at] = x.T
    step = width // 2
    for part, right in enumerate((along_ref, rotated_ref)):
        for first in range(0, width, step):
            total = dot(across_ref[first : first + step], right[...], NN) * factor
            at = slice(part * width + first, part * width + first + step)
            high_ref[at], low_ref[at] = split(total)


def cov_times(real, imag, high_ref, low_ref):
    vectors = real.shape[0]
    rows = jnp.concatenate(
        [jnp.concatenate([real, imag], axis=1), jnp.concatenate([imag, -real], axis=1)], axis=0
    )
    high, low = split(rows)
    product = dot(jnp.concatenate([high, low], axis=0), high_ref[...], NN)
    product = product[: 2 * vectors] + product[2 * vectors :] + dot(high, low_ref[...], NN)
    return product[:vectors], product[vectors:]


def orthonormalize(real_z, imag_z):
    vectors, width = real_z.shape
    row = lax.broadcasted_iota(jnp.int32, (vectors, 1), 0)
    real_v, imag_v = real_z, imag_z
    scale = jnp.zeros((vectors, 1), F32)
    for n in range(vectors):
        real_a = jnp.broadcast_to(real_v[n : n + 1], real_z.shape)
        imag_a = jnp.broadcast_to(imag_v[n : n + 1], real_z.shape)
        norm = jnp.sum(real_a * real_a + imag_a * imag_a, axis=1, keepdims=True) + EPS
        scale = jnp.where(row == n, norm, scale)
        if n + 1 < vectors:
            real_d = jnp.sum(real_a * real_z + imag_a * imag_z, axis=1, keepdims=True)
            imag_d = jnp.sum(real_a * imag_z - imag_a * real_z, axis=1, keepdims=True)
            inverse = jnp.where(row > n, 1.0 / norm, 0.0)
            real_c = real_d * inverse
            imag_c = imag_d * inverse
            real_v = real_v - (real_c * real_a - imag_c * imag_a)
            imag_v = imag_v - (real_c * imag_a + imag_c * real_a)
    factor = 1.0 / jnp.sqrt(scale)
    return real_v * factor, imag_v * factor


def subspace_kernel(tm, own, factor, beams_ref, start_ref, flags_ref, ranks_ref, weights_ref, *rest):
    blocks, outs, scratch = rest[:tm], rest[tm + 1 : 2 * tm + 1], rest[2 * tm + 1 :]
    across_ref, along_ref, rotated_ref, high_ref, low_ref = scratch
    vectors, width = start_ref.shape[3], start_ref.shape[4]
    rows = blocks[0].shape[1]
    tm_index = lax.axis_index("tm")
    beams = weights_ref.shape[1] // 2
    for o in range(own):
        chan = tm_index * own + o
        fill_cov(factor, blocks, o, *scratch)
        real_q = start_ref[0, chan, 0]
        imag_q = start_ref[0, chan, 1]
        for sweep in range(ITERS):
            real_z, imag_z = cov_times(real_q, imag_q, high_ref, low_ref)
            real_q, imag_q = orthonormalize(real_z, imag_z)
        rank = flags_ref[chan] * ranks_ref[chan]
        keep = lax.broadcasted_iota(jnp.int32, (vectors, width), 0) < rank
        real_u = jnp.where(keep, real_q, 0.0)
        imag_u = jnp.where(keep, imag_q, 0.0)
        both = jnp.concatenate(split(jnp.concatenate([real_u, imag_u], axis=0)), axis=0)
        product = dot(both, weights_ref[o], NT)
        product = product[: 2 * vectors] + product[2 * vectors :]
        real_w = product[:vectors, :beams] - product[vectors:, beams:]
        imag_w = product[:vectors, beams:] + product[vectors:, :beams]
        product = dot(both, across_ref[...], NN)
        product = product[: 2 * vectors] + product[2 * vectors :]
        series = [
            product[:vectors, i * rows : (i + 1) * rows]
            + turned(product[vectors:, i * rows : (i + 1) * rows], 1)
            for i in range(tm)
        ]
        first, second = orders(tm)
        for x, out in enumerate(outs):
            a, b = first.index(x), second.index(x)
            out[o, :, :rows] = jnp.where(lax.axis_index("pol") == 0, series[a], series[b])
            out[o, :, rows : rows + beams] = real_w
            out[o, :, rows + beams :] = imag_w


def nulled_squares(raw, packet_ref):
    rows, half = raw.shape
    at = pl.multiple_of(rows + lax.axis_index("pol") * half, half)
    series = packet_ref[:, :rows]
    left = jnp.concatenate([series, -turned(series, 1)], axis=0)
    right = jnp.concatenate(
        [packet_ref[:, pl.ds(at, half)], packet_ref[:, pl.ds(pl.multiple_of(at + 2 * half, half), half)]],
        axis=0,
    )
    high_s, low_s = split(left)
    high_w, low_w = split(right)
    left = jnp.concatenate([high_s, high_s, low_s], axis=0)
    right = jnp.concatenate([high_w, low_w, high_w], axis=0)
    beam = raw - dot(left, right, TN)
    return beam * beam


def pair_sums(squares):
    samples = squares.shape[0] // 2
    return squares[pl.ds(0, samples, 2), :] + squares[pl.ds(1, samples, 2), :]


def first_kernel(own, raw_ref, *rest):
    packets, (out_ref, squares) = rest[:-2], rest[-2:]
    for x, ref in enumerate(packets):
        for o in range(own):
            chan = (lax.axis_index("tm") ^ x) * own + o
            squares[...] = nulled_squares(raw_ref[chan], ref.at[o])
            out_ref[chan] = pair_sums(squares)


def second_kernel(own, first_ref, raw_ref, *rest):
    packets, (out_ref, squares, powers) = rest[:-3], rest[-3:]
    for x, ref in enumerate(packets):
        for o in range(own):
            chan = (lax.axis_index("tm") ^ x) * own + o
            squares[...] = nulled_squares(raw_ref[chan], ref.at[o])
            powers[chan] = first_ref[chan] + pair_sums(squares)
    for chan in range(powers.shape[0]):
        out_ref[:, chan, :] = powers[chan]


def local(voltages, start_block, flags, ranks, phase_index):
    tm = lax.axis_size("tm")
    tm_index = lax.axis_index("tm")
    samples, chan_dev, width = voltages.shape[0], voltages.shape[2], voltages.shape[4]
    own = chan_dev // tm
    vectors = start_block.shape[3]
    beams = phase_index.shape[0]
    half = beams // 2
    rows = 2 * samples
    factor = 1.0 / (samples * tm)
    params = pltpu.CompilerParams(vmem_limit_bytes=VMEM_LIMIT)
    whole = pl.BlockSpec(memory_space=pltpu.VMEM)
    scalars = pl.BlockSpec(memory_space=pltpu.SMEM)
    unread = pl.BlockSpec(memory_space=pl.ANY)

    def cost(multiplies, moved):
        return pl.CostEstimate(flops=2 * multiplies, bytes_accessed=moved, transcendentals=0)

    cut = pl.pallas_call(
        functools.partial(cut_kernel, tm, own),
        out_shape=[jax.ShapeDtypeStruct((samples, own, 2, width), BF16)] * tm,
        in_specs=[pl.BlockSpec(memory_space=pltpu.HBM)],
        out_specs=[whole] * tm,
        scratch_shapes=[pltpu.SemaphoreType.DMA((tm,))],
        compiler_params=params,
    )(voltages)
    pieces = [piece.transpose(1, 0, 2, 3).reshape(own, rows, width) for piece in cut]
    blocks = pieces[:1] + [
        lax.ppermute(piece, ("tm", "pol"), route) for piece, route in zip(pieces[1:], routes(tm)[1:])
    ]

    raw = jax.ShapeDtypeStruct((chan_dev, rows, half), F32)
    mine, other = pl.pallas_call(
        functools.partial(raw_beams_kernel, tm, own),
        out_shape=[raw] * 2,
        in_specs=[whole] * (1 + tm),
        out_specs=[whole] * 2,
        scratch_shapes=[pltpu.VMEM((beams, width), BF16)],
        compiler_params=params,
        cost_estimate=cost(4 * chan_dev * samples * width * beams, 8 * chan_dev * samples * width),
    )(phase_index, *pieces)

    own_weights = pl.pallas_call(
        functools.partial(own_weights_kernel, own, chan_dev),
        out_shape=jax.ShapeDtypeStruct((own, 2 * beams, width), BF16),
        in_specs=[whole],
        out_specs=whole,
        compiler_params=params,
        cost_estimate=cost(20 * own * beams * width, 8 * own * beams * width),
    )(phase_index)

    other, *packets = pl.pallas_call(
        functools.partial(subspace_kernel, tm, own, factor),
        out_shape=[raw] + [jax.ShapeDtypeStruct((own, vectors, rows + 2 * beams), F32)] * tm,
        in_specs=[unread, whole, scalars, scalars] + [whole] * (1 + tm),
        out_specs=[unread] + [whole] * tm,
        input_output_aliases={0: 0},
        scratch_shapes=[
            pltpu.VMEM((width, tm * rows), BF16),
            pltpu.VMEM((tm * rows, width), BF16),
            pltpu.VMEM((tm * rows, width), BF16),
            pltpu.VMEM((2 * width, width), BF16),
            pltpu.VMEM((2 * width, width), BF16),
        ],
        compiler_params=params,
        cost_estimate=cost(32 * own * vectors * tm * samples * width, 8 * own * width * width),
    )(other, start_block, flags, ranks, own_weights, *blocks)
    cores = [(0, 1), (1, 0)]
    theirs = lax.ppermute(other, "pol", cores)
    arrived = list(packets)
    for x in reversed(range(1, tm)):
        arrived[x] = lax.ppermute(packets[x], "tm", [(z, z ^ x) for z in range(tm)])
    swapped = [lax.ppermute(packet, "pol", cores) for packet in arrived]

    finish = cost(2 * chan_dev * rows * 6 * vectors * half, 8 * chan_dev * rows * half)
    part = pl.pallas_call(
        functools.partial(first_kernel, own),
        out_shape=jax.ShapeDtypeStruct((chan_dev, samples, half), F32),
        in_specs=[whole] * (1 + tm),
        out_specs=whole,
        scratch_shapes=[pltpu.VMEM((rows, half), F32)],
        compiler_params=params,
        cost_estimate=finish,
    )(mine, *arrived)
    return pl.pallas_call(
        functools.partial(second_kernel, own),
        out_shape=jax.ShapeDtypeStruct((samples, chan_dev, half), F32),
        in_specs=[whole] * (2 + tm),
        out_specs=whole,
        scratch_shapes=[
            pltpu.VMEM((rows, half), F32),
            pltpu.VMEM((chan_dev, samples, half), F32),
        ],
        compiler_params=params,
        cost_estimate=finish,
    )(part, theirs, *swapped)


def solution(mesh):
    placed = (
        P(("groups", "tm"), "pol", "chan", None, None),
        P("pol", "chan", None, None, None),
        P(("groups", "chan")),
        P(("groups", "chan")),
        P(),
    )
    return jax.shard_map(
        local,
        mesh=mesh,
        in_specs=placed,
        out_specs=P(("groups", "tm"), "chan", "pol"),
        check_vma=False,
    )
```

```python
import functools

import jax
import jax.numpy as jnp
from jax import lax
from jax.experimental import pallas as pl
from jax.experimental.pallas import tpu as pltpu
from jax.sharding import PartitionSpec as P

ITERS = 4
PHASES = 1024
QUARTER = PHASES // 4
EPS = 1e-06
F32 = jnp.float32
BF16 = jnp.bfloat16
NT = (((1,), (1,)), ((), ()))
NN = (((1,), (0,)), ((), ()))
TN = (((0,), (0,)), ((), ()))
VMEM_LIMIT = 48 * 1024 * 1024
CUT_LIMIT = (64 * 1024 - 768) * 1024


def dot(left, right, dims):
    return lax.dot_general(left, right, dims, preferred_element_type=F32)


def split(values):
    high = values.astype(BF16)
    low = (values - high.astype(F32)).astype(BF16)
    return high, low


def steer(phase, step, norm):
    turn = (phase * step) & (PHASES - 1)
    quadrant = (turn + QUARTER // 2) // QUARTER
    angle = (turn - quadrant * QUARTER).astype(F32) * (2.0 * jnp.pi / PHASES)
    sq = angle * angle
    sine = angle * (1.0 + sq * (-1.0 / 6 + sq * (1.0 / 120 + sq * (-1.0 / 5040 + sq / 362880))))
    cosine = 1.0 + sq * (-0.5 + sq * (1.0 / 24 + sq * (-1.0 / 720 + sq / 40320)))
    odd = (quadrant & 1) == 1
    real = jnp.where(odd, sine, cosine) * norm
    imag = jnp.where(odd, cosine, sine) * norm
    real = jnp.where(((quadrant + 1) & 2) == 2, -real, real)
    imag = jnp.where((quadrant & 2) == 2, -imag, imag)
    return real.astype(BF16), imag.astype(BF16)


def fill_weights(phase_ref, first, rows, step, out):
    norm = 1.0 / (phase_ref.shape[1] ** 0.5)
    chunk = 32

    def body(i, carry):
        at = pl.multiple_of(i * chunk, chunk)
        real, imag = steer(phase_ref[pl.ds(first + at, chunk), :], step, norm)
        out[pl.ds(at, chunk), :] = real
        out[pl.ds(rows + at, chunk), :] = imag
        return carry

    lax.fori_loop(0, rows // chunk, body, 0)


def orders(tm):
    far = [*range(2, tm)]
    return [0, *far[:1], 1, *far[1:]], [0, *far, 1]


def shifts(tm, pol):
    return [jnp.where(pol == 0, a, b) for a, b in zip(*orders(tm))]


def routes(tm):
    return [
        [(2 * z + p, 2 * (z ^ x[p]) + p) for z in range(tm) for p in range(2)]
        for x in zip(*orders(tm))
    ]


def cut_kernel(tm, own, voltages_ref, *rest):
    pieces, done = rest[:tm], rest[tm]
    copies = []
    for i, x in enumerate(shifts(tm, lax.axis_index("pol"))):
        first = (lax.axis_index("tm") ^ x) * own
        copy = pltpu.make_async_copy(voltages_ref.at[:, 0, pl.ds(first, own)], pieces[i], done.at[i])
        copy.start()
        copies.append(copy)
    for copy in copies:
        copy.wait()


def turned(values, axis):
    size = values.shape[axis]
    at = lax.broadcasted_iota(jnp.int32, values.shape, axis)
    after = pltpu.roll(values, size - 1, axis)
    before = pltpu.roll(values, 1, axis)
    return jnp.where((at & 1) == 0, after, -before)


def raw_beams_kernel(tm, own, phase_ref, *rest):
    pieces, (mine_ref, other_ref, weights) = rest[:tm], rest[tm:]
    half = phase_ref.shape[0] // 2
    rows = pieces[0].shape[1]
    pol = lax.axis_index("pol")
    start = lax.axis_index("chan") * tm * own
    for x, piece in zip(shifts(tm, pol), pieces):
        for o in range(own):
            chan = (lax.axis_index("tm") ^ x) * own + o
            for swap, out_ref in enumerate((mine_ref, other_ref)):
                first = pl.multiple_of((pol ^ swap) * half, half)
                fill_weights(phase_ref, first, half, start + chan + 1, weights)
                product = dot(piece[o], weights[...], NT)
                by_imag = turned(product[:, half:].reshape(rows // 8, 8, half), 1).reshape(rows, half)
                out_ref[chan] = product[:, :half] - by_imag


def own_weights_kernel(own, chan_dev, phase_ref, out_ref):
    beams = phase_ref.shape[0]
    first = lax.axis_index("chan") * chan_dev + lax.axis_index("tm") * own
    for o in range(own):
        fill_weights(phase_ref, 0, beams, first + o + 1, out_ref.at[o])


def cov_terms(x, across):
    rotated = -turned(x.astype(F32), 0)
    return dot(across, x, NN), dot(across, rotated.astype(BF16), NN)


def early_cov_kernel(*refs):
    blocks, (cov_ref, across_ref, along_ref, rotated_ref) = refs[:-4], refs[-4:]
    rows, width = blocks[0].shape[1:]
    for o in range(cov_ref.shape[0]):
        for i, block in enumerate(blocks):
            x = block[o]
            at = slice(i * rows, (i + 1) * rows)
            along_ref[at] = x
            rotated_ref[at] = -turned(x.astype(F32), 0).astype(BF16)
            across_ref[o, :, at] = x.T
        cov_ref[o, 0] = dot(across_ref[o], along_ref[...], NN)
        cov_ref[o, 1] = dot(across_ref[o], rotated_ref[...], NN)


def cov_times(real, imag, high_ref, low_ref):
    vectors = real.shape[0]
    rows = jnp.concatenate(
        [jnp.concatenate([real, imag], axis=1), jnp.concatenate([imag, -real], axis=1)], axis=0
    )
    high, low = split(rows)
    product = dot(jnp.concatenate([high, low], axis=0), high_ref[...], NN)
    product = product[: 2 * vectors] + product[2 * vectors :] + dot(high, low_ref[...], NN)
    return product[:vectors], product[vectors:]


def orthonormalize(real_z, imag_z):
    vectors, width = real_z.shape
    row = lax.broadcasted_iota(jnp.int32, (vectors, 1), 0)
    real_v, imag_v = real_z, imag_z
    scale = jnp.zeros((vectors, 1), F32)
    for n in range(vectors):
        real_a = jnp.broadcast_to(real_v[n : n + 1], real_z.shape)
        imag_a = jnp.broadcast_to(imag_v[n : n + 1], real_z.shape)
        norm = jnp.sum(real_a * real_a + imag_a * imag_a, axis=1, keepdims=True) + EPS
        scale = jnp.where(row == n, norm, scale)
        if n + 1 < vectors:
            real_d = jnp.sum(real_a * real_z + imag_a * imag_z, axis=1, keepdims=True)
            imag_d = jnp.sum(real_a * imag_z - imag_a * real_z, axis=1, keepdims=True)
            inverse = jnp.where(row > n, 1.0 / norm, 0.0)
            real_c = real_d * inverse
            imag_c = imag_d * inverse
            real_v = real_v - (real_c * real_a - imag_c * imag_a)
            imag_v = imag_v - (real_c * imag_a + imag_c * real_a)
    factor = 1.0 / jnp.sqrt(scale)
    return real_v * factor, imag_v * factor


def subspace_kernel(
    tm, own, factor, beams_ref, start_ref, flags_ref, ranks_ref, weights_ref, cov_ref, across_ref, last_ref, *rest
):
    outs, (high_ref, low_ref) = rest[1 : tm + 1], rest[tm + 1 :]
    vectors, width = start_ref.shape[3], start_ref.shape[4]
    rows = last_ref.shape[1]
    tm_index = lax.axis_index("tm")
    beams = weights_ref.shape[1] // 2
    for o in range(own):
        chan = tm_index * own + o
        across = last_ref[o].T
        for part, term in enumerate(cov_terms(last_ref[o], across)):
            at = slice(part * width, (part + 1) * width)
            high_ref[at], low_ref[at] = split((cov_ref[o, part] + term) * factor)
        real_q = start_ref[0, chan, 0]
        imag_q = start_ref[0, chan, 1]
        for sweep in range(ITERS):
            real_z, imag_z = cov_times(real_q, imag_q, high_ref, low_ref)
            real_q, imag_q = orthonormalize(real_z, imag_z)
        rank = flags_ref[chan] * ranks_ref[chan]
        keep = lax.broadcasted_iota(jnp.int32, (vectors, width), 0) < rank
        real_u = jnp.where(keep, real_q, 0.0)
        imag_u = jnp.where(keep, imag_q, 0.0)
        both = jnp.concatenate(split(jnp.concatenate([real_u, imag_u], axis=0)), axis=0)
        product = dot(both, weights_ref[o], NT)
        product = product[: 2 * vectors] + product[2 * vectors :]
        real_w = product[:vectors, :beams] - product[vectors:, beams:]
        imag_w = product[:vectors, beams:] + product[vectors:, :beams]
        series = []
        for i in range(tm):
            block = across_ref[o, :, i * rows : (i + 1) * rows] if i < tm - 1 else across
            product = dot(both, block, NN)
            product = product[: 2 * vectors] + product[2 * vectors :]
            series.append(product[:vectors] + turned(product[vectors:], 1))
        first, second = orders(tm)
        for x, out in enumerate(outs):
            a, b = first.index(x), second.index(x)
            out[o, :, :rows] = jnp.where(lax.axis_index("pol") == 0, series[a], series[b])
            out[o, :, rows : rows + beams] = real_w
            out[o, :, rows + beams :] = imag_w


def nulled_squares(raw, packet_ref):
    rows, half = raw.shape
    at = pl.multiple_of(rows + lax.axis_index("pol") * half, half)
    series = packet_ref[:, :rows]
    left = jnp.concatenate([series, -turned(series, 1)], axis=0)
    right = jnp.concatenate(
        [packet_ref[:, pl.ds(at, half)], packet_ref[:, pl.ds(pl.multiple_of(at + 2 * half, half), half)]],
        axis=0,
    )
    high_s, low_s = split(left)
    high_w, low_w = split(right)
    left = jnp.concatenate([high_s, high_s, low_s], axis=0)
    right = jnp.concatenate([high_w, low_w, high_w], axis=0)
    beam = raw - dot(left, right, TN)
    return beam * beam


def pair_sums(squares):
    samples = squares.shape[0] // 2
    return squares[pl.ds(0, samples, 2), :] + squares[pl.ds(1, samples, 2), :]


def first_kernel(own, xs, raw_ref, *rest):
    packets, outs, squares = rest[: len(xs)], rest[-1 - len(xs) : -1], rest[-1]
    for x, ref, out_ref in zip(xs, packets, outs):
        for o in range(own):
            squares[...] = nulled_squares(raw_ref[(lax.axis_index("tm") ^ x) * own + o], ref.at[o])
            out_ref[o] = pair_sums(squares)


def second_kernel(tm, own, raw_ref, *rest):
    firsts, packets, (out_ref, squares, powers) = rest[:tm], rest[tm : 2 * tm], rest[2 * tm :]
    for x, (first_ref, ref) in enumerate(zip(firsts, packets)):
        for o in range(own):
            chan = (lax.axis_index("tm") ^ x) * own + o
            squares[...] = nulled_squares(raw_ref[chan], ref.at[o])
            powers[chan] = first_ref[o] + pair_sums(squares)
    for chan in range(powers.shape[0]):
        out_ref[:, chan, :] = powers[chan]


def local(voltages, start_block, flags, ranks, phase_index):
    tm = lax.axis_size("tm")
    tm_index = lax.axis_index("tm")
    samples, chan_dev, width = voltages.shape[0], voltages.shape[2], voltages.shape[4]
    own = chan_dev // tm
    vectors = start_block.shape[3]
    beams = phase_index.shape[0]
    half = beams // 2
    rows = 2 * samples
    factor = 1.0 / (samples * tm)
    params = pltpu.CompilerParams(vmem_limit_bytes=VMEM_LIMIT)
    whole = pl.BlockSpec(memory_space=pltpu.VMEM)
    scalars = pl.BlockSpec(memory_space=pltpu.SMEM)
    unread = pl.BlockSpec(memory_space=pl.ANY)

    def cost(multiplies, moved):
        return pl.CostEstimate(flops=2 * multiplies, bytes_accessed=moved, transcendentals=0)

    cut = pl.pallas_call(
        functools.partial(cut_kernel, tm, own),
        out_shape=[jax.ShapeDtypeStruct((samples, own, 2, width), BF16)] * tm,
        in_specs=[pl.BlockSpec(memory_space=pltpu.HBM)],
        out_specs=[whole] * tm,
        scratch_shapes=[pltpu.SemaphoreType.DMA((tm,))],
        compiler_params=pltpu.CompilerParams(vmem_limit_bytes=CUT_LIMIT),
    )(voltages)
    pieces = [piece.transpose(1, 0, 2, 3).reshape(own, rows, width) for piece in cut]
    blocks = pieces[:1] + [
        lax.ppermute(piece, ("tm", "pol"), route) for piece, route in zip(pieces[1:], routes(tm)[1:])
    ]

    raw = jax.ShapeDtypeStruct((chan_dev, rows, half), F32)
    mine, other = pl.pallas_call(
        functools.partial(raw_beams_kernel, tm, own),
        out_shape=[raw] * 2,
        in_specs=[whole] * (1 + tm),
        out_specs=[whole] * 2,
        scratch_shapes=[pltpu.VMEM((beams, width), BF16)],
        compiler_params=params,
        cost_estimate=cost(4 * chan_dev * samples * width * beams, 8 * chan_dev * samples * width),
    )(phase_index, *pieces)

    own_weights = pl.pallas_call(
        functools.partial(own_weights_kernel, own, chan_dev),
        out_shape=jax.ShapeDtypeStruct((own, 2 * beams, width), BF16),
        in_specs=[whole],
        out_specs=whole,
        compiler_params=params,
        cost_estimate=cost(20 * own * beams * width, 8 * own * beams * width),
    )(phase_index)

    early = (tm - 1) * rows
    cov, across = pl.pallas_call(
        early_cov_kernel,
        out_shape=[
            jax.ShapeDtypeStruct((own, 2, width, width), F32),
            jax.ShapeDtypeStruct((own, width, early), BF16),
        ],
        in_specs=[whole] * (tm - 1),
        out_specs=[whole] * 2,
        scratch_shapes=[pltpu.VMEM((early, width), BF16)] * 2,
        compiler_params=params,
        cost_estimate=cost(2 * own * early * width * width, 8 * own * width * width),
    )(*blocks[:-1])

    other, *packets = pl.pallas_call(
        functools.partial(subspace_kernel, tm, own, factor),
        out_shape=[raw] + [jax.ShapeDtypeStruct((own, vectors, rows + 2 * beams), F32)] * tm,
        in_specs=[unread, whole, scalars, scalars] + [whole] * 4,
        out_specs=[unread] + [whole] * tm,
        input_output_aliases={0: 0},
        scratch_shapes=[pltpu.VMEM((2 * width, width), BF16)] * 2,
        compiler_params=params,
        cost_estimate=cost(32 * own * vectors * tm * samples * width, 8 * own * width * width),
    )(other, start_block, flags, ranks, own_weights, cov, across, blocks[-1])
    cores = [(0, 1), (1, 0)]
    theirs = lax.ppermute(other, "pol", cores)

    def first(xs, *before):
        return pl.pallas_call(
            functools.partial(first_kernel, own, xs),
            out_shape=[jax.ShapeDtypeStruct((own, samples, half), F32)] * len(xs),
            in_specs=[whole] * (1 + len(xs)) + [unread] * len(before),
            out_specs=[whole] * len(xs),
            scratch_shapes=[pltpu.VMEM((rows, half), F32)],
            compiler_params=params,
            cost_estimate=cost(len(xs) * own * rows * 6 * vectors * half, 8 * own * rows * half),
        )(mine, *[arrived[x] for x in xs], *before)

    arrived = list(packets)
    for x in reversed(range(1, tm)):
        arrived[x] = lax.ppermute(packets[x], "tm", [(z, z ^ x) for z in range(tm)])
    swapped = [lax.ppermute(packet, "pol", cores) for packet in arrived]
    firsts = [None] * tm
    firsts[0], firsts[-1] = first([0, tm - 1])
    for x in reversed(range(1, tm - 1)):
        (firsts[x],) = first([x], firsts[x + 1])

    return pl.pallas_call(
        functools.partial(second_kernel, tm, own),
        out_shape=jax.ShapeDtypeStruct((samples, chan_dev, half), F32),
        in_specs=[whole] * (1 + 2 * tm),
        out_specs=whole,
        scratch_shapes=[
            pltpu.VMEM((rows, half), F32),
            pltpu.VMEM((chan_dev, samples, half), F32),
        ],
        compiler_params=params,
        cost_estimate=cost(2 * chan_dev * rows * 6 * vectors * half, 8 * chan_dev * rows * half),
    )(theirs, *firsts, *swapped)


def solution(mesh):
    placed = (
        P(("groups", "tm"), "pol", "chan", None, None),
        P("pol", "chan", None, None, None),
        P(("groups", "chan")),
        P(("groups", "chan")),
        P(),
    )
    return jax.shard_map(
        local,
        mesh=mesh,
        in_specs=placed,
        out_specs=P(("groups", "tm"), "chan", "pol"),
        check_vma=False,
    )
```

```python
import functools

import jax
import jax.numpy as jnp
from jax import lax
from jax.experimental import pallas as pl
from jax.experimental.pallas import tpu as pltpu
from jax.sharding import PartitionSpec as P

ITERS = 4
PHASES = 1024
QUARTER = PHASES // 4
EPS = 1e-06
F32 = jnp.float32
BF16 = jnp.bfloat16
NT = (((1,), (1,)), ((), ()))
NN = (((1,), (0,)), ((), ()))
TN = (((0,), (0,)), ((), ()))
VMEM_LIMIT = 48 * 1024 * 1024


def dot(left, right, dims):
    return lax.dot_general(left, right, dims, preferred_element_type=F32)


def split(values):
    high = values.astype(BF16)
    low = (values - high.astype(F32)).astype(BF16)
    return high, low


def steer(phase, step, norm):
    turn = (phase * step) & (PHASES - 1)
    quadrant = (turn + QUARTER // 2) // QUARTER
    angle = (turn - quadrant * QUARTER).astype(F32) * (2.0 * jnp.pi / PHASES)
    sq = angle * angle
    sine = angle * (1.0 + sq * (-1.0 / 6 + sq * (1.0 / 120 + sq * (-1.0 / 5040 + sq / 362880))))
    cosine = 1.0 + sq * (-0.5 + sq * (1.0 / 24 + sq * (-1.0 / 720 + sq / 40320)))
    odd = (quadrant & 1) == 1
    real = jnp.where(odd, sine, cosine) * norm
    imag = jnp.where(odd, cosine, sine) * norm
    real = jnp.where(((quadrant + 1) & 2) == 2, -real, real)
    imag = jnp.where((quadrant & 2) == 2, -imag, imag)
    return real.astype(BF16), imag.astype(BF16)


def fill_weights(phase_ref, first, rows, step, out):
    norm = 1.0 / (phase_ref.shape[1] ** 0.5)
    chunk = 32

    def body(i, carry):
        at = pl.multiple_of(i * chunk, chunk)
        real, imag = steer(phase_ref[pl.ds(first + at, chunk), :], step, norm)
        out[pl.ds(at, chunk), :] = real
        out[pl.ds(rows + at, chunk), :] = imag
        return carry

    lax.fori_loop(0, rows // chunk, body, 0)


def shifted(by):
    tm = lax.axis_size("tm")
    return lax.rem(lax.axis_index("tm") + tm + by, tm)


def cut_kernel(tm, own, voltages_ref, *rest):
    pieces, done = rest[:tm], rest[tm]
    copies = []
    for i, piece in enumerate(pieces):
        channels = pl.ds(shifted(i) * own, own)
        copy = pltpu.make_async_copy(voltages_ref.at[:, 0, channels], piece, done.at[i])
        copy.start()
        copies.append(copy)
    for copy in copies:
        copy.wait()


def turned(values, axis):
    size = values.shape[axis]
    at = lax.broadcasted_iota(jnp.int32, values.shape, axis)
    after = pltpu.roll(values, size - 1, axis)
    before = pltpu.roll(values, 1, axis)
    return jnp.where((at & 1) == 0, after, -before)


def raw_beams_kernel(tm, own, phase_ref, *rest):
    pieces, (mine_ref, other_ref, weights) = rest[:tm], rest[tm:]
    half = phase_ref.shape[0] // 2
    rows = pieces[0].shape[1]
    pol = lax.axis_index("pol")
    start = lax.axis_index("chan") * tm * own
    for i, piece in enumerate(pieces):
        for o in range(own):
            chan = shifted(i) * own + o
            for swap, out_ref in enumerate((mine_ref, other_ref)):
                first = pl.multiple_of((pol ^ swap) * half, half)
                fill_weights(phase_ref, first, half, start + chan + 1, weights)
                product = dot(piece[o], weights[...], NT)
                by_imag = turned(product[:, half:].reshape(rows // 8, 8, half), 1).reshape(rows, half)
                out_ref[chan] = product[:, :half] - by_imag


def own_weights_kernel(own, chan_dev, phase_ref, out_ref):
    beams = phase_ref.shape[0]
    first = lax.axis_index("chan") * chan_dev + lax.axis_index("tm") * own
    for o in range(own):
        fill_weights(phase_ref, 0, beams, first + o + 1, out_ref.at[o])


def cov_terms(x, across):
    rotated = -turned(x.astype(F32), 0)
    return dot(across, x, NN), dot(across, rotated.astype(BF16), NN)


def early_cov_kernel(*refs):
    blocks, (cov_ref, across_ref, along_ref, rotated_ref) = refs[:-4], refs[-4:]
    rows, width = blocks[0].shape[1:]
    for o in range(cov_ref.shape[0]):
        for i, block in enumerate(blocks):
            x = block[o]
            at = slice(i * rows, (i + 1) * rows)
            along_ref[at] = x
            rotated_ref[at] = -turned(x.astype(F32), 0).astype(BF16)
            across_ref[o, :, at] = x.T
        cov_ref[o, 0] = dot(across_ref[o], along_ref[...], NN)
        cov_ref[o, 1] = dot(across_ref[o], rotated_ref[...], NN)


def cov_times(real, imag, high_ref, low_ref):
    vectors = real.shape[0]
    rows = jnp.concatenate(
        [jnp.concatenate([real, imag], axis=1), jnp.concatenate([imag, -real], axis=1)], axis=0
    )
    high, low = split(rows)
    product = dot(jnp.concatenate([high, low], axis=0), high_ref[...], NN)
    product = product[: 2 * vectors] + product[2 * vectors :] + dot(high, low_ref[...], NN)
    return product[:vectors], product[vectors:]


def orthonormalize(real_z, imag_z):
    vectors, width = real_z.shape
    row = lax.broadcasted_iota(jnp.int32, (vectors, 1), 0)
    real_v, imag_v = real_z, imag_z
    scale = jnp.zeros((vectors, 1), F32)
    for n in range(vectors):
        real_a = jnp.broadcast_to(real_v[n : n + 1], real_z.shape)
        imag_a = jnp.broadcast_to(imag_v[n : n + 1], real_z.shape)
        norm = jnp.sum(real_a * real_a + imag_a * imag_a, axis=1, keepdims=True) + EPS
        scale = jnp.where(row == n, norm, scale)
        if n + 1 < vectors:
            real_d = jnp.sum(real_a * real_z + imag_a * imag_z, axis=1, keepdims=True)
            imag_d = jnp.sum(real_a * imag_z - imag_a * real_z, axis=1, keepdims=True)
            inverse = jnp.where(row > n, 1.0 / norm, 0.0)
            real_c = real_d * inverse
            imag_c = imag_d * inverse
            real_v = real_v - (real_c * real_a - imag_c * imag_a)
            imag_v = imag_v - (real_c * imag_a + imag_c * real_a)
    factor = 1.0 / jnp.sqrt(scale)
    return real_v * factor, imag_v * factor


def subspace_kernel(
    tm, own, factor, beams_ref, start_ref, flags_ref, ranks_ref, weights_ref, cov_ref, across_ref, last_ref, *rest
):
    outs, (high_ref, low_ref, series_ref) = rest[1 : tm + 1], rest[tm + 1 :]
    vectors, width = start_ref.shape[3], start_ref.shape[4]
    rows = last_ref.shape[1]
    tm_index = lax.axis_index("tm")
    beams = weights_ref.shape[1] // 2
    for o in range(own):
        chan = tm_index * own + o
        across = last_ref[o].T
        for part, term in enumerate(cov_terms(last_ref[o], across)):
            at = slice(part * width, (part + 1) * width)
            high_ref[at], low_ref[at] = split((cov_ref[o, part] + term) * factor)
        real_q = start_ref[0, chan, 0]
        imag_q = start_ref[0, chan, 1]
        for sweep in range(ITERS):
            real_z, imag_z = cov_times(real_q, imag_q, high_ref, low_ref)
            real_q, imag_q = orthonormalize(real_z, imag_z)
        rank = flags_ref[chan] * ranks_ref[chan]
        keep = lax.broadcasted_iota(jnp.int32, (vectors, width), 0) < rank
        real_u = jnp.where(keep, real_q, 0.0)
        imag_u = jnp.where(keep, imag_q, 0.0)
        both = jnp.concatenate(split(jnp.concatenate([real_u, imag_u], axis=0)), axis=0)
        product = dot(both, weights_ref[o], NT)
        product = product[: 2 * vectors] + product[2 * vectors :]
        real_w = product[:vectors, :beams] - product[vectors:, beams:]
        imag_w = product[:vectors, beams:] + product[vectors:, :beams]
        for i in range(tm):
            block = across_ref[o, :, i * rows : (i + 1) * rows] if i < tm - 1 else across
            product = dot(both, block, NN)
            product = product[: 2 * vectors] + product[2 * vectors :]
            series = product[:vectors] + turned(product[vectors:], 1)
            series_ref[tm_index ^ shifted(-i)] = series
        for x, out in enumerate(outs):
            out[o, :, :rows] = series_ref[x]
            out[o, :, rows : rows + beams] = real_w
            out[o, :, rows + beams :] = imag_w


def nulled_squares(raw, packet_ref):
    rows, half = raw.shape
    at = pl.multiple_of(rows + lax.axis_index("pol") * half, half)
    series = packet_ref[:, :rows]
    left = jnp.concatenate([series, -turned(series, 1)], axis=0)
    right = jnp.concatenate(
        [packet_ref[:, pl.ds(at, half)], packet_ref[:, pl.ds(pl.multiple_of(at + 2 * half, half), half)]],
        axis=0,
    )
    high_s, low_s = split(left)
    high_w, low_w = split(right)
    left = jnp.concatenate([high_s, high_s, low_s], axis=0)
    right = jnp.concatenate([high_w, low_w, high_w], axis=0)
    beam = raw - dot(left, right, TN)
    return beam * beam


def pair_sums(squares):
    samples = squares.shape[0] // 2
    return squares[pl.ds(0, samples, 2), :] + squares[pl.ds(1, samples, 2), :]


def first_kernel(own, xs, raw_ref, *rest):
    packets, outs, squares = rest[: len(xs)], rest[-1 - len(xs) : -1], rest[-1]
    for x, ref, out_ref in zip(xs, packets, outs):
        for o in range(own):
            squares[...] = nulled_squares(raw_ref[(lax.axis_index("tm") ^ x) * own + o], ref.at[o])
            out_ref[o] = pair_sums(squares)


def second_kernel(tm, own, raw_ref, *rest):
    firsts, packets, (out_ref, squares, powers) = rest[:tm], rest[tm : 2 * tm], rest[2 * tm :]
    for x, (first_ref, ref) in enumerate(zip(firsts, packets)):
        for o in range(own):
            chan = (lax.axis_index("tm") ^ x) * own + o
            squares[...] = nulled_squares(raw_ref[chan], ref.at[o])
            powers[chan] = first_ref[o] + pair_sums(squares)
    for chan in range(powers.shape[0]):
        out_ref[:, chan, :] = powers[chan]


def local(voltages, start_block, flags, ranks, phase_index):
    tm = lax.axis_size("tm")
    tm_index = lax.axis_index("tm")
    samples, chan_dev, width = voltages.shape[0], voltages.shape[2], voltages.shape[4]
    own = chan_dev // tm
    vectors = start_block.shape[3]
    beams = phase_index.shape[0]
    half = beams // 2
    rows = 2 * samples
    factor = 1.0 / (samples * tm)
    params = pltpu.CompilerParams(vmem_limit_bytes=VMEM_LIMIT)
    whole = pl.BlockSpec(memory_space=pltpu.VMEM)
    scalars = pl.BlockSpec(memory_space=pltpu.SMEM)
    unread = pl.BlockSpec(memory_space=pl.ANY)

    def cost(multiplies, moved):
        return pl.CostEstimate(flops=2 * multiplies, bytes_accessed=moved, transcendentals=0)

    cut = pl.pallas_call(
        functools.partial(cut_kernel, tm, own),
        out_shape=[jax.ShapeDtypeStruct((samples, own, 2, width), BF16)] * tm,
        in_specs=[pl.BlockSpec(memory_space=pltpu.HBM)],
        out_specs=[whole] * tm,
        scratch_shapes=[pltpu.SemaphoreType.DMA((tm,))],
        compiler_params=params,
    )(voltages)
    pieces = [piece.transpose(1, 0, 2, 3).reshape(own, rows, width) for piece in cut]
    blocks = pieces[:1] + [
        lax.ppermute(pieces[i], "tm", [(z, (z + i) % tm) for z in range(tm)]) for i in range(1, tm)
    ]

    raw = jax.ShapeDtypeStruct((chan_dev, rows, half), F32)
    mine, other = pl.pallas_call(
        functools.partial(raw_beams_kernel, tm, own),
        out_shape=[raw] * 2,
        in_specs=[whole] * (1 + tm),
        out_specs=[whole] * 2,
        scratch_shapes=[pltpu.VMEM((beams, width), BF16)],
        compiler_params=params,
        cost_estimate=cost(4 * chan_dev * samples * width * beams, 8 * chan_dev * samples * width),
    )(phase_index, *pieces)

    own_weights = pl.pallas_call(
        functools.partial(own_weights_kernel, own, chan_dev),
        out_shape=jax.ShapeDtypeStruct((own, 2 * beams, width), BF16),
        in_specs=[whole],
        out_specs=whole,
        compiler_params=params,
        cost_estimate=cost(20 * own * beams * width, 8 * own * beams * width),
    )(phase_index)

    early = (tm - 1) * rows
    cov, across = pl.pallas_call(
        early_cov_kernel,
        out_shape=[
            jax.ShapeDtypeStruct((own, 2, width, width), F32),
            jax.ShapeDtypeStruct((own, width, early), BF16),
        ],
        in_specs=[whole] * (tm - 1),
        out_specs=[whole] * 2,
        scratch_shapes=[pltpu.VMEM((early, width), BF16)] * 2,
        compiler_params=params,
        cost_estimate=cost(2 * own * early * width * width, 8 * own * width * width),
    )(*blocks[:-1])

    other, *packets = pl.pallas_call(
        functools.partial(subspace_kernel, tm, own, factor),
        out_shape=[raw] + [jax.ShapeDtypeStruct((own, vectors, rows + 2 * beams), F32)] * tm,
        in_specs=[unread, whole, scalars, scalars] + [whole] * 4,
        out_specs=[unread] + [whole] * tm,
        input_output_aliases={0: 0},
        scratch_shapes=[pltpu.VMEM((2 * width, width), BF16)] * 2
        + [pltpu.VMEM((tm, vectors, rows), F32)],
        compiler_params=params,
        cost_estimate=cost(32 * own * vectors * tm * samples * width, 8 * own * width * width),
    )(other, start_block, flags, ranks, own_weights, cov, across, blocks[-1])
    cores = [(0, 1), (1, 0)]
    theirs = lax.ppermute(other, "pol", cores)

    def first(xs, *before):
        return pl.pallas_call(
            functools.partial(first_kernel, own, xs),
            out_shape=[jax.ShapeDtypeStruct((own, samples, half), F32)] * len(xs),
            in_specs=[whole] * (1 + len(xs)) + [unread] * len(before),
            out_specs=[whole] * len(xs),
            scratch_shapes=[pltpu.VMEM((rows, half), F32)],
            compiler_params=params,
            cost_estimate=cost(len(xs) * own * rows * 6 * vectors * half, 8 * own * rows * half),
        )(mine, *[arrived[x] for x in xs], *before)

    arrived = list(packets)
    for x in reversed(range(1, tm)):
        arrived[x] = lax.ppermute(packets[x], "tm", [(z, z ^ x) for z in range(tm)])
    swapped = [lax.ppermute(packet, "pol", cores) for packet in arrived]
    firsts = [None] * tm
    firsts[0], firsts[-1] = first([0, tm - 1])
    for x in reversed(range(1, tm - 1)):
        (firsts[x],) = first([x], firsts[x + 1])

    return pl.pallas_call(
        functools.partial(second_kernel, tm, own),
        out_shape=jax.ShapeDtypeStruct((samples, chan_dev, half), F32),
        in_specs=[whole] * (1 + 2 * tm),
        out_specs=whole,
        scratch_shapes=[
            pltpu.VMEM((rows, half), F32),
            pltpu.VMEM((chan_dev, samples, half), F32),
        ],
        compiler_params=params,
        cost_estimate=cost(2 * chan_dev * rows * 6 * vectors * half, 8 * chan_dev * rows * half),
    )(theirs, *firsts, *swapped)


def solution(mesh):
    placed = (
        P(("groups", "tm"), "pol", "chan", None, None),
        P("pol", "chan", None, None, None),
        P(("groups", "chan")),
        P(("groups", "chan")),
        P(),
    )
    return jax.shard_map(
        local,
        mesh=mesh,
        in_specs=placed,
        out_specs=P(("groups", "tm"), "chan", "pol"),
        check_vma=False,
    )
```

```python
import functools

import jax
import jax.numpy as jnp
from jax import lax
from jax.experimental import pallas as pl
from jax.experimental.pallas import tpu as pltpu
from jax.sharding import PartitionSpec as P

ITERS = 4
PHASES = 1024
QUARTER = PHASES // 4
EPS = 1e-06
F32 = jnp.float32
BF16 = jnp.bfloat16
NT = (((1,), (1,)), ((), ()))
NN = (((1,), (0,)), ((), ()))
TN = (((0,), (0,)), ((), ()))
VMEM_LIMIT = 48 * 1024 * 1024


def dot(left, right, dims):
    return lax.dot_general(left, right, dims, preferred_element_type=F32)


def split(values):
    high = values.astype(BF16)
    low = (values - high.astype(F32)).astype(BF16)
    return high, low


def steer(phase, step, norm):
    turn = (phase * step) & (PHASES - 1)
    quadrant = (turn + QUARTER // 2) // QUARTER
    angle = (turn - quadrant * QUARTER).astype(F32) * (2.0 * jnp.pi / PHASES)
    sq = angle * angle
    sine = angle * (1.0 + sq * (-1.0 / 6 + sq * (1.0 / 120 + sq * (-1.0 / 5040 + sq / 362880))))
    cosine = 1.0 + sq * (-0.5 + sq * (1.0 / 24 + sq * (-1.0 / 720 + sq / 40320)))
    odd = (quadrant & 1) == 1
    real = jnp.where(odd, sine, cosine) * norm
    imag = jnp.where(odd, cosine, sine) * norm
    real = jnp.where(((quadrant + 1) & 2) == 2, -real, real)
    imag = jnp.where((quadrant & 2) == 2, -imag, imag)
    return real.astype(BF16), imag.astype(BF16)


def fill_weights(phase_ref, first, rows, step, out):
    norm = 1.0 / (phase_ref.shape[1] ** 0.5)
    chunk = 32

    def body(i, carry):
        at = pl.multiple_of(i * chunk, chunk)
        real, imag = steer(phase_ref[pl.ds(first + at, chunk), :], step, norm)
        out[pl.ds(at, chunk), :] = real
        out[pl.ds(rows + at, chunk), :] = imag
        return carry

    lax.fori_loop(0, rows // chunk, body, 0)


def steps(tm):
    return [0, *[by for by in range(1, tm) if by != tm // 2], tm // 2]


def shifted(by):
    tm = lax.axis_size("tm")
    return lax.rem(lax.axis_index("tm") + tm + by, tm)


def cut_kernel(tm, own, voltages_ref, *rest):
    pieces, done = rest[:tm], rest[tm]
    copies = []
    for i, (by, piece) in enumerate(zip(steps(tm), pieces)):
        channels = pl.ds(shifted(by) * own, own)
        copy = pltpu.make_async_copy(voltages_ref.at[:, 0, channels], piece, done.at[i])
        copy.start()
        copies.append(copy)
    for copy in copies:
        copy.wait()


def turned(values, axis):
    size = values.shape[axis]
    at = lax.broadcasted_iota(jnp.int32, values.shape, axis)
    after = pltpu.roll(values, size - 1, axis)
    before = pltpu.roll(values, 1, axis)
    return jnp.where((at & 1) == 0, after, -before)


def raw_beams_kernel(tm, own, phase_ref, *rest):
    pieces, (mine_ref, other_ref, weights) = rest[:tm], rest[tm:]
    half = phase_ref.shape[0] // 2
    rows = pieces[0].shape[1]
    pol = lax.axis_index("pol")
    start = lax.axis_index("chan") * tm * own
    for by, piece in zip(steps(tm), pieces):
        for o in range(own):
            chan = shifted(by) * own + o
            for swap, out_ref in enumerate((mine_ref, other_ref)):
                first = pl.multiple_of((pol ^ swap) * half, half)
                fill_weights(phase_ref, first, half, start + chan + 1, weights)
                product = dot(piece[o], weights[...], NT)
                by_imag = turned(product[:, half:].reshape(rows // 8, 8, half), 1).reshape(rows, half)
                out_ref[chan] = product[:, :half] - by_imag


def own_weights_kernel(own, chan_dev, phase_ref, out_ref):
    beams = phase_ref.shape[0]
    first = lax.axis_index("chan") * chan_dev + lax.axis_index("tm") * own
    for o in range(own):
        fill_weights(phase_ref, 0, beams, first + o + 1, out_ref.at[o])


def cov_terms(x, across):
    rotated = -turned(x.astype(F32), 0)
    return dot(across, x, NN), dot(across, rotated.astype(BF16), NN)


def early_cov_kernel(*refs):
    blocks, (cov_ref, across_ref, along_ref, rotated_ref) = refs[:-4], refs[-4:]
    rows, width = blocks[0].shape[1:]
    for o in range(cov_ref.shape[0]):
        for i, block in enumerate(blocks):
            x = block[o]
            at = slice(i * rows, (i + 1) * rows)
            along_ref[at] = x
            rotated_ref[at] = -turned(x.astype(F32), 0).astype(BF16)
            across_ref[o, :, at] = x.T
        cov_ref[o, 0] = dot(across_ref[o], along_ref[...], NN)
        cov_ref[o, 1] = dot(across_ref[o], rotated_ref[...], NN)


def cov_times(real, imag, high_ref, low_ref):
    vectors = real.shape[0]
    rows = jnp.concatenate(
        [jnp.concatenate([real, imag], axis=1), jnp.concatenate([imag, -real], axis=1)], axis=0
    )
    high, low = split(rows)
    product = dot(jnp.concatenate([high, low], axis=0), high_ref[...], NN)
    product = product[: 2 * vectors] + product[2 * vectors :] + dot(high, low_ref[...], NN)
    return product[:vectors], product[vectors:]


def orthonormalize(real_z, imag_z):
    vectors, width = real_z.shape
    row = lax.broadcasted_iota(jnp.int32, (vectors, 1), 0)
    real_v, imag_v = real_z, imag_z
    scale = jnp.zeros((vectors, 1), F32)
    for n in range(vectors):
        real_a = jnp.broadcast_to(real_v[n : n + 1], real_z.shape)
        imag_a = jnp.broadcast_to(imag_v[n : n + 1], real_z.shape)
        norm = jnp.sum(real_a * real_a + imag_a * imag_a, axis=1, keepdims=True) + EPS
        scale = jnp.where(row == n, norm, scale)
        if n + 1 < vectors:
            real_d = jnp.sum(real_a * real_z + imag_a * imag_z, axis=1, keepdims=True)
            imag_d = jnp.sum(real_a * imag_z - imag_a * real_z, axis=1, keepdims=True)
            inverse = jnp.where(row > n, 1.0 / norm, 0.0)
            real_c = real_d * inverse
            imag_c = imag_d * inverse
            real_v = real_v - (real_c * real_a - imag_c * imag_a)
            imag_v = imag_v - (real_c * imag_a + imag_c * real_a)
    factor = 1.0 / jnp.sqrt(scale)
    return real_v * factor, imag_v * factor


def subspace_kernel(
    tm, own, factor, beams_ref, start_ref, flags_ref, ranks_ref, weights_ref, cov_ref, across_ref, last_ref, *rest
):
    outs, (high_ref, low_ref, series_ref) = rest[:tm], rest[tm:]
    vectors, width = start_ref.shape[3], start_ref.shape[4]
    rows = last_ref.shape[1]
    tm_index = lax.axis_index("tm")
    beams = weights_ref.shape[1] // 2
    for o in range(own):
        chan = tm_index * own + o
        across = last_ref[o].T
        for part, term in enumerate(cov_terms(last_ref[o], across)):
            at = slice(part * width, (part + 1) * width)
            high_ref[at], low_ref[at] = split((cov_ref[o, part] + term) * factor)
        real_q = start_ref[0, chan, 0]
        imag_q = start_ref[0, chan, 1]
        for sweep in range(ITERS):
            real_z, imag_z = cov_times(real_q, imag_q, high_ref, low_ref)
            real_q, imag_q = orthonormalize(real_z, imag_z)
        rank = flags_ref[chan] * ranks_ref[chan]
        keep = lax.broadcasted_iota(jnp.int32, (vectors, width), 0) < rank
        real_u = jnp.where(keep, real_q, 0.0)
        imag_u = jnp.where(keep, imag_q, 0.0)
        both = jnp.concatenate(split(jnp.concatenate([real_u, imag_u], axis=0)), axis=0)
        product = dot(both, weights_ref[o], NT)
        product = product[: 2 * vectors] + product[2 * vectors :]
        real_w = product[:vectors, :beams] - product[vectors:, beams:]
        imag_w = product[:vectors, beams:] + product[vectors:, :beams]
        for i, by in enumerate(steps(tm)):
            block = across_ref[o, :, i * rows : (i + 1) * rows] if i < tm - 1 else across
            product = dot(both, block, NN)
            product = product[: 2 * vectors] + product[2 * vectors :]
            series = product[:vectors] + turned(product[vectors:], 1)
            series_ref[tm_index ^ shifted(-by)] = series
        for x, out in enumerate(outs):
            out[o, :, :rows] = series_ref[x]
            out[o, :, rows : rows + beams] = real_w
            out[o, :, rows + beams :] = imag_w


def first_kernel(own, xs, mine_ref, other_ref, *rest):
    packets, (mine_out, other_out, squares) = rest[: len(xs)], rest[-3:]
    rows, half = mine_ref.shape[1:]
    samples = rows // 2
    for x, ref in zip(xs, packets):
        for o in range(own):
            chan = (lax.axis_index("tm") ^ x) * own + o
            series = ref[o, :, :rows]
            left = jnp.concatenate([series, -turned(series, 1)], axis=0)
            high_s, low_s = split(left)
            left = jnp.concatenate([high_s, high_s, low_s], axis=0)
            for swap, (raw_ref, out_ref) in enumerate(((mine_ref, mine_out), (other_ref, other_out))):
                at = rows + (lax.axis_index("pol") ^ swap) * half
                real_at = pl.ds(pl.multiple_of(at, half), half)
                imag_at = pl.ds(pl.multiple_of(at + 2 * half, half), half)
                right = jnp.concatenate([ref[o, :, real_at], ref[o, :, imag_at]], axis=0)
                high_w, low_w = split(right)
                right = jnp.concatenate([high_w, low_w, high_w], axis=0)
                beam = raw_ref[chan] - dot(left, right, TN)
                squares[...] = beam * beam
                out_ref[chan] = squares[pl.ds(0, samples, 2), :] + squares[pl.ds(1, samples, 2), :]


def second_kernel(mine_ref, theirs_ref, out_ref):
    for chan in range(out_ref.shape[1]):
        out_ref[:, chan, :] = mine_ref[chan] + theirs_ref[chan]


def local(voltages, start_block, flags, ranks, phase_index):
    tm = lax.axis_size("tm")
    tm_index = lax.axis_index("tm")
    samples, chan_dev, width = voltages.shape[0], voltages.shape[2], voltages.shape[4]
    own = chan_dev // tm
    vectors = start_block.shape[3]
    beams = phase_index.shape[0]
    half = beams // 2
    rows = 2 * samples
    factor = 1.0 / (samples * tm)
    params = pltpu.CompilerParams(vmem_limit_bytes=VMEM_LIMIT)
    whole = pl.BlockSpec(memory_space=pltpu.VMEM)
    scalars = pl.BlockSpec(memory_space=pltpu.SMEM)
    unread = pl.BlockSpec(memory_space=pl.ANY)

    def cost(multiplies, moved):
        return pl.CostEstimate(flops=2 * multiplies, bytes_accessed=moved, transcendentals=0)

    cut = pl.pallas_call(
        functools.partial(cut_kernel, tm, own),
        out_shape=[jax.ShapeDtypeStruct((samples, own, 2, width), BF16)] * tm,
        in_specs=[pl.BlockSpec(memory_space=pltpu.HBM)],
        out_specs=[whole] * tm,
        scratch_shapes=[pltpu.SemaphoreType.DMA((tm,))],
        compiler_params=params,
    )(voltages)
    pieces = [piece.transpose(1, 0, 2, 3).reshape(own, rows, width) for piece in cut]
    blocks = pieces[:1] + [
        lax.ppermute(piece, "tm", [(z, (z + by) % tm) for z in range(tm)])
        for by, piece in zip(steps(tm)[1:], pieces[1:])
    ]

    raw = jax.ShapeDtypeStruct((chan_dev, rows, half), F32)
    mine, other = pl.pallas_call(
        functools.partial(raw_beams_kernel, tm, own),
        out_shape=[raw] * 2,
        in_specs=[whole] * (1 + tm),
        out_specs=[whole] * 2,
        scratch_shapes=[pltpu.VMEM((beams, width), BF16)],
        compiler_params=params,
        cost_estimate=cost(4 * chan_dev * samples * width * beams, 8 * chan_dev * samples * width),
    )(phase_index, *pieces)

    own_weights = pl.pallas_call(
        functools.partial(own_weights_kernel, own, chan_dev),
        out_shape=jax.ShapeDtypeStruct((own, 2 * beams, width), BF16),
        in_specs=[whole],
        out_specs=whole,
        compiler_params=params,
        cost_estimate=cost(20 * own * beams * width, 8 * own * beams * width),
    )(phase_index)

    early = (tm - 1) * rows
    cov, across = pl.pallas_call(
        early_cov_kernel,
        out_shape=[
            jax.ShapeDtypeStruct((own, 2, width, width), F32),
            jax.ShapeDtypeStruct((own, width, early), BF16),
        ],
        in_specs=[whole] * (tm - 1),
        out_specs=[whole] * 2,
        scratch_shapes=[pltpu.VMEM((early, width), BF16)] * 2,
        compiler_params=params,
        cost_estimate=cost(2 * own * early * width * width, 8 * own * width * width),
    )(*blocks[:-1])

    packets = pl.pallas_call(
        functools.partial(subspace_kernel, tm, own, factor),
        out_shape=[jax.ShapeDtypeStruct((own, vectors, rows + 2 * beams), F32)] * tm,
        in_specs=[unread, whole, scalars, scalars] + [whole] * 4,
        out_specs=[whole] * tm,
        scratch_shapes=[pltpu.VMEM((2 * width, width), BF16)] * 2
        + [pltpu.VMEM((tm, vectors, rows), F32)],
        compiler_params=params,
        cost_estimate=cost(32 * own * vectors * tm * samples * width, 8 * own * width * width),
    )(mine, start_block, flags, ranks, own_weights, cov, across, blocks[-1])

    arrived = list(packets)
    for x in reversed(range(1, tm)):
        arrived[x] = lax.ppermute(packets[x], "tm", [(z, z ^ x) for z in range(tm)])
    groups = [[0, tm - 1], *[[x] for x in reversed(range(1, tm - 1))]]
    shape = jax.ShapeDtypeStruct((chan_dev, samples, half), F32)
    powers = []
    for xs in groups:
        powers = pl.pallas_call(
            functools.partial(first_kernel, own, xs),
            out_shape=[shape] * 2,
            in_specs=[whole] * (2 + len(xs) + len(powers)),
            out_specs=[whole] * 2,
            input_output_aliases={2 + len(xs) + i: i for i in range(len(powers))},
            scratch_shapes=[pltpu.VMEM((rows, half), F32)],
            compiler_params=params,
            cost_estimate=cost(len(xs) * own * rows * 6 * vectors * beams, 8 * own * rows * beams),
        )(mine, other, *[arrived[x] for x in xs], *powers)
    theirs = lax.ppermute(powers[1], "pol", [(0, 1), (1, 0)])

    return pl.pallas_call(
        second_kernel,
        out_shape=jax.ShapeDtypeStruct((samples, chan_dev, half), F32),
        in_specs=[whole] * 2,
        out_specs=whole,
        compiler_params=params,
        cost_estimate=cost(chan_dev * samples * half, 12 * chan_dev * samples * half),
    )(powers[0], theirs)


def solution(mesh):
    placed = (
        P(("groups", "tm"), "pol", "chan", None, None),
        P("pol", "chan", None, None, None),
        P(("groups", "chan")),
        P(("groups", "chan")),
        P(),
    )
    return jax.shard_map(
        local,
        mesh=mesh,
        in_specs=placed,
        out_specs=P(("groups", "tm"), "chan", "pol"),
        check_vma=False,
    )
```

```python
import functools

import jax
import jax.numpy as jnp
from jax import lax
from jax.experimental import pallas as pl
from jax.experimental.pallas import tpu as pltpu
from jax.sharding import PartitionSpec as P

ITERS = 4
PHASES = 1024
QUARTER = PHASES // 4
EPS = 1e-06
F32 = jnp.float32
BF16 = jnp.bfloat16
NT = (((1,), (1,)), ((), ()))
NN = (((1,), (0,)), ((), ()))
TN = (((0,), (0,)), ((), ()))
VMEM_LIMIT = 48 * 1024 * 1024
CHUNK = 128


def dot(left, right, dims):
    return lax.dot_general(left, right, dims, preferred_element_type=F32)


def split(values):
    high = values.astype(BF16)
    low = (values - high.astype(F32)).astype(BF16)
    return high, low


def steer(phase, step, norm):
    turn = (phase * step) & (PHASES - 1)
    quadrant = (turn + QUARTER // 2) // QUARTER
    angle = (turn - quadrant * QUARTER).astype(F32) * (2.0 * jnp.pi / PHASES)
    sq = angle * angle
    sine = angle * (1.0 + sq * (-1.0 / 6 + sq * (1.0 / 120 + sq * (-1.0 / 5040 + sq / 362880))))
    cosine = 1.0 + sq * (-0.5 + sq * (1.0 / 24 + sq * (-1.0 / 720 + sq / 40320)))
    odd = (quadrant & 1) == 1
    real = jnp.where(odd, sine, cosine) * norm
    imag = jnp.where(odd, cosine, sine) * norm
    real = jnp.where(((quadrant + 1) & 2) == 2, -real, real)
    imag = jnp.where((quadrant & 2) == 2, -imag, imag)
    return real.astype(BF16), imag.astype(BF16)


def fill_weights(phase_ref, first, rows, step, out):
    norm = 1.0 / (phase_ref.shape[1] ** 0.5)
    chunk = 32

    def body(i, carry):
        at = pl.multiple_of(i * chunk, chunk)
        real, imag = steer(phase_ref[pl.ds(first + at, chunk), :], step, norm)
        out[pl.ds(at, chunk), :] = real
        out[pl.ds(rows + at, chunk), :] = imag
        return carry

    lax.fori_loop(0, rows // chunk, body, 0)


def steps(tm):
    return [0, *[by for by in range(1, tm) if by != tm // 2], tm // 2]


def shifted(by):
    tm = lax.axis_size("tm")
    return lax.rem(lax.axis_index("tm") + tm + by, tm)


def cut_kernel(own, bys, voltages_ref, *rest):
    pieces, done = rest[:-1], rest[-1]
    copies = []
    for i, (by, piece) in enumerate(zip(bys, pieces)):
        channels = pl.ds(shifted(by) * own, own)
        copy = pltpu.make_async_copy(voltages_ref.at[:, 0, channels], piece, done.at[i])
        copy.start()
        copies.append(copy)
    for copy in copies:
        copy.wait()


def turned(values, axis):
    size = values.shape[axis]
    at = lax.broadcasted_iota(jnp.int32, values.shape, axis)
    after = pltpu.roll(values, size - 1, axis)
    before = pltpu.roll(values, 1, axis)
    return jnp.where((at & 1) == 0, after, -before)


def raw_beams_kernel(tm, own, phase_ref, *rest):
    pieces, (mine_ref, other_ref, weights) = rest[:tm], rest[tm:]
    half = phase_ref.shape[0] // 2
    rows = pieces[0].shape[1]
    pol = lax.axis_index("pol")
    start = lax.axis_index("chan") * tm * own
    for by, piece in zip(steps(tm), pieces):
        for o in range(own):
            chan = shifted(by) * own + o
            for swap, out_ref in enumerate((mine_ref, other_ref)):
                first = pl.multiple_of((pol ^ swap) * half, half)
                fill_weights(phase_ref, first, half, start + chan + 1, weights)
                product = dot(piece[o], weights[...], NT)
                by_imag = turned(product[:, half:].reshape(rows // 8, 8, half), 1).reshape(rows, half)
                out_ref[chan] = product[:, :half] - by_imag


def own_weights_kernel(own, chan_dev, phase_ref, out_ref):
    beams = phase_ref.shape[0]
    first = lax.axis_index("chan") * chan_dev + lax.axis_index("tm") * own
    for o in range(own):
        fill_weights(phase_ref, 0, beams, first + o + 1, out_ref.at[o])


def rotate(x):
    return (-turned(x.astype(F32), 0)).astype(BF16)


def early_kernel(start_ref, *refs):
    blocks, (cov_ref, first_ref, across_ref, along_ref, rotated_ref) = refs[:-5], refs[-5:]
    rows, width = blocks[0].shape[1:]
    own = cov_ref.shape[0]
    for o in range(own):
        for i, block in enumerate(blocks):
            x = block[o]
            at = slice(i * rows, (i + 1) * rows)
            along_ref[at] = x
            rotated_ref[at] = rotate(x)
            across_ref[o, :, at] = x.T
        cov_ref[o, 0] = dot(across_ref[o], along_ref[...], NN)
        cov_ref[o, 1] = dot(across_ref[o], rotated_ref[...], NN)
        chan = lax.axis_index("tm") * own + o
        first_ref[o] = block_times(start_ref[0, chan, 0], start_ref[0, chan, 1], across_ref[o], along_ref[...])


def project(real, imag, across):
    vectors = real.shape[0]
    both = jnp.concatenate(split(jnp.concatenate([real, imag], axis=0)), axis=0)
    product = dot(both, across, NN)
    product = product[: 2 * vectors] + product[2 * vectors :]
    other = turned(product, 1)
    return product[:vectors] + other[vectors:], product[vectors:] - other[:vectors]


def block_times(real, imag, across, along):
    pair = jnp.concatenate(project(real, imag, across), axis=0)
    product = dot(jnp.concatenate(split(pair), axis=0), along, NN)
    return product[: pair.shape[0]] + product[pair.shape[0] :]


def cov_times(real, imag, high_ref, low_ref):
    vectors = real.shape[0]
    rows = jnp.concatenate(
        [jnp.concatenate([real, imag], axis=1), jnp.concatenate([imag, -real], axis=1)], axis=0
    )
    high, low = split(rows)
    product = dot(jnp.concatenate([high, low], axis=0), high_ref[...], NN)
    product = product[: 2 * vectors] + product[2 * vectors :] + dot(high, low_ref[...], NN)
    return product[:vectors], product[vectors:]


def orthonormalize(real_z, imag_z, beside=()):
    beside = list(beside)
    vectors, width = real_z.shape
    row = lax.broadcasted_iota(jnp.int32, (vectors, 1), 0)
    real_v, imag_v = real_z, imag_z
    scale = jnp.zeros((vectors, 1), F32)
    for n in range(vectors):
        real_a = jnp.broadcast_to(real_v[n : n + 1], real_z.shape)
        imag_a = jnp.broadcast_to(imag_v[n : n + 1], real_z.shape)
        norm = jnp.sum(real_a * real_a + imag_a * imag_a, axis=1, keepdims=True) + EPS
        scale = jnp.where(row == n, norm, scale)
        if n + 1 < vectors:
            real_d = jnp.sum(real_a * real_z + imag_a * imag_z, axis=1, keepdims=True)
            imag_d = jnp.sum(real_a * imag_z - imag_a * real_z, axis=1, keepdims=True)
            inverse = jnp.where(row > n, 1.0 / norm, 0.0)
            real_c = real_d * inverse
            imag_c = imag_d * inverse
            real_v = real_v - (real_c * real_a - imag_c * imag_a)
            imag_v = imag_v - (real_c * imag_a + imag_c * real_a)
        for work in beside[n::vectors]:
            work()
    factor = 1.0 / jnp.sqrt(scale)
    return real_v * factor, imag_v * factor


def subspace_kernel(
    tm, own, factor, beams_ref, start_ref, flags_ref, ranks_ref, weights_ref, cov_ref, first_ref, across_ref, last_ref, *rest
):
    outs, (high_ref, low_ref, series_ref) = rest[:tm], rest[tm:]
    vectors, width = start_ref.shape[3], start_ref.shape[4]
    rows = last_ref.shape[1]
    tm_index = lax.axis_index("tm")
    beams = weights_ref.shape[1] // 2
    for o in range(own):
        chan = tm_index * own + o
        across = last_ref[o].T
        rotated = rotate(last_ref[o])

        def add_last(part, first):
            right = last_ref[o] if part == 0 else rotated
            term = dot(across[first : first + CHUNK], right, NN)
            at = slice(part * width + first, part * width + first + CHUNK)
            high_ref[at], low_ref[at] = split((cov_ref[o, part, first : first + CHUNK] + term) * factor)

        chunks = [
            functools.partial(add_last, part, first) for part in range(2) for first in range(0, width, CHUNK)
        ]
        last = block_times(start_ref[0, chan, 0], start_ref[0, chan, 1], across, last_ref[o])
        both = (first_ref[o] + last) * factor
        real_q, imag_q = orthonormalize(both[:vectors], both[vectors:], chunks)
        for sweep in range(1, ITERS):
            real_z, imag_z = cov_times(real_q, imag_q, high_ref, low_ref)
            real_q, imag_q = orthonormalize(real_z, imag_z)
        rank = flags_ref[chan] * ranks_ref[chan]
        keep = lax.broadcasted_iota(jnp.int32, (vectors, width), 0) < rank
        real_u = jnp.where(keep, real_q, 0.0)
        imag_u = jnp.where(keep, imag_q, 0.0)
        both = jnp.concatenate(split(jnp.concatenate([real_u, imag_u], axis=0)), axis=0)
        product = dot(both, weights_ref[o], NT)
        product = product[: 2 * vectors] + product[2 * vectors :]
        real_w = product[:vectors, :beams] - product[vectors:, beams:]
        imag_w = product[:vectors, beams:] + product[vectors:, :beams]
        for i, by in enumerate(steps(tm)):
            block = across_ref[o, :, i * rows : (i + 1) * rows] if i < tm - 1 else across
            series = project(real_u, imag_u, block)[0]
            series_ref[tm_index ^ shifted(-by)] = series
        for x, out in enumerate(outs):
            out[o, :, :rows] = series_ref[x]
            out[o, :, rows : rows + beams] = real_w
            out[o, :, rows + beams :] = imag_w


def first_kernel(own, xs, mine_ref, other_ref, *rest):
    packets, (mine_out, other_out, squares) = rest[: len(xs)], rest[-3:]
    rows, half = mine_ref.shape[1:]
    samples = rows // 2
    for x, ref in zip(xs, packets):
        for o in range(own):
            chan = (lax.axis_index("tm") ^ x) * own + o
            series = ref[o, :, :rows]
            left = jnp.concatenate([series, -turned(series, 1)], axis=0)
            high_s, low_s = split(left)
            left = jnp.concatenate([high_s, high_s, low_s], axis=0)
            for swap, (raw_ref, out_ref) in enumerate(((mine_ref, mine_out), (other_ref, other_out))):
                at = rows + (lax.axis_index("pol") ^ swap) * half
                real_at = pl.ds(pl.multiple_of(at, half), half)
                imag_at = pl.ds(pl.multiple_of(at + 2 * half, half), half)
                right = jnp.concatenate([ref[o, :, real_at], ref[o, :, imag_at]], axis=0)
                high_w, low_w = split(right)
                right = jnp.concatenate([high_w, low_w, high_w], axis=0)
                beam = raw_ref[chan] - dot(left, right, TN)
                squares[...] = beam * beam
                out_ref[chan] = squares[pl.ds(0, samples, 2), :] + squares[pl.ds(1, samples, 2), :]


def second_kernel(mine_ref, theirs_ref, out_ref):
    for chan in range(out_ref.shape[1]):
        out_ref[:, chan, :] = mine_ref[chan] + theirs_ref[chan]


def local(voltages, start_block, flags, ranks, phase_index):
    tm = lax.axis_size("tm")
    tm_index = lax.axis_index("tm")
    samples, chan_dev, width = voltages.shape[0], voltages.shape[2], voltages.shape[4]
    own = chan_dev // tm
    vectors = start_block.shape[3]
    beams = phase_index.shape[0]
    half = beams // 2
    rows = 2 * samples
    factor = 1.0 / (samples * tm)
    params = pltpu.CompilerParams(vmem_limit_bytes=VMEM_LIMIT)
    whole = pl.BlockSpec(memory_space=pltpu.VMEM)
    scalars = pl.BlockSpec(memory_space=pltpu.SMEM)
    unread = pl.BlockSpec(memory_space=pl.ANY)

    def cost(multiplies, moved):
        return pl.CostEstimate(flops=2 * multiplies, bytes_accessed=moved, transcendentals=0)

    by = steps(tm)
    later = pl.pallas_call(
        functools.partial(cut_kernel, own, [by[0], *by[2:]]),
        out_shape=[jax.ShapeDtypeStruct((samples, own, 2, width), BF16)] * (tm - 1),
        in_specs=[pl.BlockSpec(memory_space=pltpu.HBM)],
        out_specs=[whole] * (tm - 1),
        scratch_shapes=[pltpu.SemaphoreType.DMA((tm - 1,))],
        compiler_params=params,
    )(voltages)
    urgent = lax.dynamic_slice_in_dim(voltages[:, 0], shifted(by[1]) * own, own, 1)
    cut = [later[0], urgent, *later[1:]]
    pieces = [piece.transpose(1, 0, 2, 3).reshape(own, rows, width) for piece in cut]
    blocks = pieces[:1] + [
        lax.ppermute(piece, "tm", [(z, (z + by) % tm) for z in range(tm)])
        for by, piece in zip(steps(tm)[1:], pieces[1:])
    ]

    raw = jax.ShapeDtypeStruct((chan_dev, rows, half), F32)
    mine, other = pl.pallas_call(
        functools.partial(raw_beams_kernel, tm, own),
        out_shape=[raw] * 2,
        in_specs=[whole] * (1 + tm),
        out_specs=[whole] * 2,
        scratch_shapes=[pltpu.VMEM((beams, width), BF16)],
        compiler_params=params,
        cost_estimate=cost(4 * chan_dev * samples * width * beams, 8 * chan_dev * samples * width),
    )(phase_index, *pieces)

    own_weights = pl.pallas_call(
        functools.partial(own_weights_kernel, own, chan_dev),
        out_shape=jax.ShapeDtypeStruct((own, 2 * beams, width), BF16),
        in_specs=[whole],
        out_specs=whole,
        compiler_params=params,
        cost_estimate=cost(20 * own * beams * width, 8 * own * beams * width),
    )(phase_index)

    early = (tm - 1) * rows
    cov, first, across = pl.pallas_call(
        early_kernel,
        out_shape=[
            jax.ShapeDtypeStruct((own, 2, width, width), F32),
            jax.ShapeDtypeStruct((own, 2 * vectors, width), F32),
            jax.ShapeDtypeStruct((own, width, early), BF16),
        ],
        in_specs=[whole] * tm,
        out_specs=[whole] * 3,
        scratch_shapes=[pltpu.VMEM((early, width), BF16)] * 2,
        compiler_params=params,
        cost_estimate=cost(2 * own * early * width * width, 8 * own * width * width),
    )(start_block, *blocks[:-1])

    packets = pl.pallas_call(
        functools.partial(subspace_kernel, tm, own, factor),
        out_shape=[jax.ShapeDtypeStruct((own, vectors, rows + 2 * beams), F32)] * tm,
        in_specs=[unread, whole, scalars, scalars] + [whole] * 5,
        out_specs=[whole] * tm,
        scratch_shapes=[pltpu.VMEM((2 * width, width), BF16)] * 2
        + [pltpu.VMEM((tm, vectors, rows), F32)],
        compiler_params=params,
        cost_estimate=cost(32 * own * vectors * tm * samples * width, 8 * own * width * width),
    )(mine, start_block, flags, ranks, own_weights, cov, first, across, blocks[-1])

    arrived = list(packets)
    for x in reversed(range(1, tm)):
        arrived[x] = lax.ppermute(packets[x], "tm", [(z, z ^ x) for z in range(tm)])
    groups = [[0, tm - 1], *[[x] for x in reversed(range(1, tm - 1))]]
    shape = jax.ShapeDtypeStruct((chan_dev, samples, half), F32)
    powers = []
    for xs in groups:
        powers = pl.pallas_call(
            functools.partial(first_kernel, own, xs),
            out_shape=[shape] * 2,
            in_specs=[whole] * (2 + len(xs) + len(powers)),
            out_specs=[whole] * 2,
            input_output_aliases={2 + len(xs) + i: i for i in range(len(powers))},
            scratch_shapes=[pltpu.VMEM((rows, half), F32)],
            compiler_params=params,
            cost_estimate=cost(len(xs) * own * rows * 6 * vectors * beams, 8 * own * rows * beams),
        )(mine, other, *[arrived[x] for x in xs], *powers)
    theirs = lax.ppermute(powers[1], "pol", [(0, 1), (1, 0)])

    return pl.pallas_call(
        second_kernel,
        out_shape=jax.ShapeDtypeStruct((samples, chan_dev, half), F32),
        in_specs=[whole] * 2,
        out_specs=whole,
        compiler_params=params,
        cost_estimate=cost(chan_dev * samples * half, 12 * chan_dev * samples * half),
    )(powers[0], theirs)


def solution(mesh):
    placed = (
        P(("groups", "tm"), "pol", "chan", None, None),
        P("pol", "chan", None, None, None),
        P(("groups", "chan")),
        P(("groups", "chan")),
        P(),
    )
    return jax.shard_map(
        local,
        mesh=mesh,
        in_specs=placed,
        out_specs=P(("groups", "tm"), "chan", "pol"),
        check_vma=False,
    )
```

```python
import functools

import jax
import jax.numpy as jnp
from jax import lax
from jax.experimental import pallas as pl
from jax.experimental.pallas import tpu as pltpu
from jax.sharding import PartitionSpec as P

ITERS = 4
PHASES = 1024
QUARTER = PHASES // 4
EPS = 1e-06
F32 = jnp.float32
BF16 = jnp.bfloat16
NT = (((1,), (1,)), ((), ()))
NN = (((1,), (0,)), ((), ()))
TN = (((0,), (0,)), ((), ()))
VMEM_LIMIT = 48 * 1024 * 1024
CHUNK = 128


def dot(left, right, dims):
    return lax.dot_general(left, right, dims, preferred_element_type=F32)


def split(values):
    high = values.astype(BF16)
    low = (values - high.astype(F32)).astype(BF16)
    return high, low


def steer(phase, step, norm):
    turn = (phase * step) & (PHASES - 1)
    quadrant = (turn + QUARTER // 2) // QUARTER
    angle = (turn - quadrant * QUARTER).astype(F32) * (2.0 * jnp.pi / PHASES)
    sq = angle * angle
    sine = angle * (1.0 + sq * (-1.0 / 6 + sq * (1.0 / 120 + sq * (-1.0 / 5040 + sq / 362880))))
    cosine = 1.0 + sq * (-0.5 + sq * (1.0 / 24 + sq * (-1.0 / 720 + sq / 40320)))
    odd = (quadrant & 1) == 1
    real = jnp.where(odd, sine, cosine) * norm
    imag = jnp.where(odd, cosine, sine) * norm
    real = jnp.where(((quadrant + 1) & 2) == 2, -real, real)
    imag = jnp.where((quadrant & 2) == 2, -imag, imag)
    return real.astype(BF16), imag.astype(BF16)


def fill_weights(phase_ref, first, rows, step, out):
    norm = 1.0 / (phase_ref.shape[1] ** 0.5)
    chunk = 32

    def body(i, carry):
        at = pl.multiple_of(i * chunk, chunk)
        real, imag = steer(phase_ref[pl.ds(first + at, chunk), :], step, norm)
        out[pl.ds(at, chunk), :] = real
        out[pl.ds(rows + at, chunk), :] = imag
        return carry

    lax.fori_loop(0, rows // chunk, body, 0)


def steps(tm):
    return [0, *[by for by in range(1, tm) if by != tm // 2], tm // 2]


def shifted(by):
    tm = lax.axis_size("tm")
    return lax.rem(lax.axis_index("tm") + tm + by, tm)


def cut_kernel(own, bys, voltages_ref, *rest):
    pieces, done = rest[:-1], rest[-1]
    copies = []
    for i, (by, piece) in enumerate(zip(bys, pieces)):
        channels = pl.ds(shifted(by) * own, own)
        copy = pltpu.make_async_copy(voltages_ref.at[:, 0, channels], piece, done.at[i])
        copy.start()
        copies.append(copy)
    for copy in copies:
        copy.wait()


def turned(values, axis):
    size = values.shape[axis]
    at = lax.broadcasted_iota(jnp.int32, values.shape, axis)
    after = pltpu.roll(values, size - 1, axis)
    before = pltpu.roll(values, 1, axis)
    return jnp.where((at & 1) == 0, after, -before)


def raw_beams_kernel(tm, own, phase_ref, *rest):
    pieces, (mine_ref, other_ref, weights) = rest[:tm], rest[tm:]
    half = phase_ref.shape[0] // 2
    rows = pieces[0].shape[1]
    pol = lax.axis_index("pol")
    start = lax.axis_index("chan") * tm * own
    for by, piece in zip(steps(tm), pieces):
        for o in range(own):
            chan = shifted(by) * own + o
            for swap, out_ref in enumerate((mine_ref, other_ref)):
                first = pl.multiple_of((pol ^ swap) * half, half)
                fill_weights(phase_ref, first, half, start + chan + 1, weights)
                product = dot(piece[o], weights[...], NT)
                by_imag = turned(product[:, half:].reshape(rows // 8, 8, half), 1).reshape(rows, half)
                out_ref[chan] = product[:, :half] - by_imag


def own_weights_kernel(own, chan_dev, phase_ref, out_ref):
    beams = phase_ref.shape[0]
    first = lax.axis_index("chan") * chan_dev + lax.axis_index("tm") * own
    for o in range(own):
        fill_weights(phase_ref, 0, beams, first + o + 1, out_ref.at[o])


def rotate(x):
    return (-turned(x.astype(F32), 0)).astype(BF16)


def early_kernel(start_ref, *refs):
    blocks, (cov_ref, first_ref, across_ref, along_ref, rotated_ref) = refs[:-5], refs[-5:]
    rows, width = blocks[0].shape[1:]
    own = cov_ref.shape[0]
    for o in range(own):
        for i, block in enumerate(blocks):
            x = block[o]
            at = slice(i * rows, (i + 1) * rows)
            along_ref[at] = x
            rotated_ref[at] = rotate(x)
            across_ref[o, :, at] = x.T
        cov_ref[o, 0] = dot(across_ref[o], along_ref[...], NN)
        cov_ref[o, 1] = dot(across_ref[o], rotated_ref[...], NN)
        chan = lax.axis_index("tm") * own + o
        first_ref[o] = block_times(start_ref[0, chan, 0], start_ref[0, chan, 1], across_ref[o], along_ref[...])


def project(real, imag, across):
    vectors = real.shape[0]
    both = jnp.concatenate(split(jnp.concatenate([real, imag], axis=0)), axis=0)
    product = dot(both, across, NN)
    product = product[: 2 * vectors] + product[2 * vectors :]
    other = turned(product, 1)
    return product[:vectors] + other[vectors:], product[vectors:] - other[:vectors]


def block_times(real, imag, across, along):
    pair = jnp.concatenate(project(real, imag, across), axis=0)
    product = dot(jnp.concatenate(split(pair), axis=0), along, NN)
    return product[: pair.shape[0]] + product[pair.shape[0] :]


def cov_times(real, imag, high_ref, low_ref):
    vectors = real.shape[0]
    rows = jnp.concatenate(
        [jnp.concatenate([real, imag], axis=1), jnp.concatenate([imag, -real], axis=1)], axis=0
    )
    high, low = split(rows)
    product = dot(jnp.concatenate([high, low], axis=0), high_ref[...], NN)
    product = product[: 2 * vectors] + product[2 * vectors :] + dot(high, low_ref[...], NN)
    return product[:vectors], product[vectors:]


def orthonormalize(real_z, imag_z, beside=()):
    beside = list(beside)
    vectors, width = real_z.shape
    row = lax.broadcasted_iota(jnp.int32, (vectors, 1), 0)
    real_v, imag_v = real_z, imag_z
    scale = jnp.zeros((vectors, 1), F32)
    for n in range(vectors):
        real_a = jnp.broadcast_to(real_v[n : n + 1], real_z.shape)
        imag_a = jnp.broadcast_to(imag_v[n : n + 1], real_z.shape)
        norm = jnp.sum(real_a * real_a + imag_a * imag_a, axis=1, keepdims=True) + EPS
        scale = jnp.where(row == n, norm, scale)
        if n + 1 < vectors:
            real_d = jnp.sum(real_a * real_z + imag_a * imag_z, axis=1, keepdims=True)
            imag_d = jnp.sum(real_a * imag_z - imag_a * real_z, axis=1, keepdims=True)
            inverse = jnp.where(row > n, 1.0 / norm, 0.0)
            real_c = real_d * inverse
            imag_c = imag_d * inverse
            real_v = real_v - (real_c * real_a - imag_c * imag_a)
            imag_v = imag_v - (real_c * imag_a + imag_c * real_a)
        for work in beside[n::vectors]:
            work()
    factor = 1.0 / jnp.sqrt(scale)
    return real_v * factor, imag_v * factor


def orthonormalize_by_gram(real_z, imag_z):
    vectors = real_z.shape[0]
    row = lax.broadcasted_iota(jnp.int32, (vectors, 1), 0)
    by_z = []
    for n in range(vectors):
        real_a = jnp.broadcast_to(real_z[n : n + 1], real_z.shape)
        imag_a = jnp.broadcast_to(imag_z[n : n + 1], real_z.shape)
        by_z.append(
            (
                jnp.sum(real_a * real_z + imag_a * imag_z, axis=1, keepdims=True),
                jnp.sum(real_a * imag_z - imag_a * real_z, axis=1, keepdims=True),
            )
        )
    by_v = list(by_z)
    real_v, imag_v = real_z, imag_z
    for n in range(vectors - 1):
        (real_d, imag_d), (real_p, imag_p) = by_z[n], by_v[n]
        square = jnp.maximum(real_p[n : n + 1], 0.0)
        inverse = jnp.where(row > n, 1.0 / (square + EPS), 0.0)
        real_c, imag_c = real_d * inverse, imag_d * inverse
        real_b, imag_b = real_p - real_c * square, imag_p - imag_c * square
        for j in range(n + 1, vectors):
            real_s, imag_s = real_c[j : j + 1], imag_c[j : j + 1]
            real_q, imag_q = real_p[j : j + 1], -imag_p[j : j + 1]
            real, imag = by_v[j]
            by_v[j] = (
                real - (real_c * real_q - imag_c * imag_q) - (real_s * real_b + imag_s * imag_b),
                imag - (real_c * imag_q + imag_c * real_q) - (real_s * imag_b - imag_s * real_b),
            )
            real, imag = by_z[j]
            by_z[j] = (
                real - (real_s * real_d + imag_s * imag_d),
                imag - (real_s * imag_d - imag_s * real_d),
            )
        real_a, imag_a = real_v[n : n + 1], imag_v[n : n + 1]
        real_v = real_v - (real_c * real_a - imag_c * imag_a)
        imag_v = imag_v - (real_c * imag_a + imag_c * real_a)
    factor = 1.0 / jnp.sqrt(jnp.sum(real_v * real_v + imag_v * imag_v, axis=1, keepdims=True) + EPS)
    return real_v * factor, imag_v * factor


def subspace_kernel(
    tm, own, factor, beams_ref, start_ref, flags_ref, ranks_ref, weights_ref, cov_ref, first_ref, across_ref, last_ref, *rest
):
    outs, (high_ref, low_ref, series_ref) = rest[:tm], rest[tm:]
    vectors, width = start_ref.shape[3], start_ref.shape[4]
    rows = last_ref.shape[1]
    tm_index = lax.axis_index("tm")
    beams = weights_ref.shape[1] // 2
    for o in range(own):
        chan = tm_index * own + o
        across = last_ref[o].T
        rotated = rotate(last_ref[o])

        def add_last(part, first):
            right = last_ref[o] if part == 0 else rotated
            term = dot(across[first : first + CHUNK], right, NN)
            at = slice(part * width + first, part * width + first + CHUNK)
            high_ref[at], low_ref[at] = split((cov_ref[o, part, first : first + CHUNK] + term) * factor)

        chunks = [
            functools.partial(add_last, part, first) for part in range(2) for first in range(0, width, CHUNK)
        ]
        last = block_times(start_ref[0, chan, 0], start_ref[0, chan, 1], across, last_ref[o])
        both = (first_ref[o] + last) * factor
        real_q, imag_q = orthonormalize(both[:vectors], both[vectors:], chunks)
        for sweep in range(1, ITERS):
            real_z, imag_z = cov_times(real_q, imag_q, high_ref, low_ref)
            real_q, imag_q = orthonormalize_by_gram(real_z, imag_z)
        rank = flags_ref[chan] * ranks_ref[chan]
        keep = lax.broadcasted_iota(jnp.int32, (vectors, width), 0) < rank
        real_u = jnp.where(keep, real_q, 0.0)
        imag_u = jnp.where(keep, imag_q, 0.0)
        both = jnp.concatenate(split(jnp.concatenate([real_u, imag_u], axis=0)), axis=0)
        product = dot(both, weights_ref[o], NT)
        product = product[: 2 * vectors] + product[2 * vectors :]
        real_w = product[:vectors, :beams] - product[vectors:, beams:]
        imag_w = product[:vectors, beams:] + product[vectors:, :beams]
        for i, by in enumerate(steps(tm)):
            block = across_ref[o, :, i * rows : (i + 1) * rows] if i < tm - 1 else across
            series = project(real_u, imag_u, block)[0]
            series_ref[tm_index ^ shifted(-by)] = series
        for x, out in enumerate(outs):
            out[o, :, :rows] = series_ref[x]
            out[o, :, rows : rows + beams] = real_w
            out[o, :, rows + beams :] = imag_w


def first_kernel(own, xs, mine_ref, other_ref, *rest):
    packets, (mine_out, other_out, squares) = rest[: len(xs)], rest[-3:]
    rows, half = mine_ref.shape[1:]
    samples = rows // 2
    for x, ref in zip(xs, packets):
        for o in range(own):
            chan = (lax.axis_index("tm") ^ x) * own + o
            series = ref[o, :, :rows]
            left = jnp.concatenate([series, -turned(series, 1)], axis=0)
            high_s, low_s = split(left)
            left = jnp.concatenate([high_s, high_s, low_s], axis=0)
            for swap, (raw_ref, out_ref) in enumerate(((mine_ref, mine_out), (other_ref, other_out))):
                at = rows + (lax.axis_index("pol") ^ swap) * half
                real_at = pl.ds(pl.multiple_of(at, half), half)
                imag_at = pl.ds(pl.multiple_of(at + 2 * half, half), half)
                right = jnp.concatenate([ref[o, :, real_at], ref[o, :, imag_at]], axis=0)
                high_w, low_w = split(right)
                right = jnp.concatenate([high_w, low_w, high_w], axis=0)
                beam = raw_ref[chan] - dot(left, right, TN)
                squares[...] = beam * beam
                out_ref[chan] = squares[pl.ds(0, samples, 2), :] + squares[pl.ds(1, samples, 2), :]


def second_kernel(mine_ref, theirs_ref, out_ref):
    for chan in range(out_ref.shape[1]):
        out_ref[:, chan, :] = mine_ref[chan] + theirs_ref[chan]


def local(voltages, start_block, flags, ranks, phase_index):
    tm = lax.axis_size("tm")
    tm_index = lax.axis_index("tm")
    samples, chan_dev, width = voltages.shape[0], voltages.shape[2], voltages.shape[4]
    own = chan_dev // tm
    vectors = start_block.shape[3]
    beams = phase_index.shape[0]
    half = beams // 2
    rows = 2 * samples
    factor = 1.0 / (samples * tm)
    params = pltpu.CompilerParams(vmem_limit_bytes=VMEM_LIMIT)
    whole = pl.BlockSpec(memory_space=pltpu.VMEM)
    scalars = pl.BlockSpec(memory_space=pltpu.SMEM)
    unread = pl.BlockSpec(memory_space=pl.ANY)

    def cost(multiplies, moved):
        return pl.CostEstimate(flops=2 * multiplies, bytes_accessed=moved, transcendentals=0)

    by = steps(tm)
    later = pl.pallas_call(
        functools.partial(cut_kernel, own, [by[0], *by[2:]]),
        out_shape=[jax.ShapeDtypeStruct((samples, own, 2, width), BF16)] * (tm - 1),
        in_specs=[pl.BlockSpec(memory_space=pltpu.HBM)],
        out_specs=[whole] * (tm - 1),
        scratch_shapes=[pltpu.SemaphoreType.DMA((tm - 1,))],
        compiler_params=params,
    )(voltages)
    urgent = lax.dynamic_slice_in_dim(voltages[:, 0], shifted(by[1]) * own, own, 1)
    cut = [later[0], urgent, *later[1:]]
    pieces = [piece.transpose(1, 0, 2, 3).reshape(own, rows, width) for piece in cut]
    blocks = pieces[:1] + [
        lax.ppermute(piece, "tm", [(z, (z + by) % tm) for z in range(tm)])
        for by, piece in zip(steps(tm)[1:], pieces[1:])
    ]

    raw = jax.ShapeDtypeStruct((chan_dev, rows, half), F32)
    mine, other = pl.pallas_call(
        functools.partial(raw_beams_kernel, tm, own),
        out_shape=[raw] * 2,
        in_specs=[whole] * (1 + tm),
        out_specs=[whole] * 2,
        scratch_shapes=[pltpu.VMEM((beams, width), BF16)],
        compiler_params=params,
        cost_estimate=cost(4 * chan_dev * samples * width * beams, 8 * chan_dev * samples * width),
    )(phase_index, *pieces)

    own_weights = pl.pallas_call(
        functools.partial(own_weights_kernel, own, chan_dev),
        out_shape=jax.ShapeDtypeStruct((own, 2 * beams, width), BF16),
        in_specs=[whole],
        out_specs=whole,
        compiler_params=params,
        cost_estimate=cost(20 * own * beams * width, 8 * own * beams * width),
    )(phase_index)

    early = (tm - 1) * rows
    cov, first, across = pl.pallas_call(
        early_kernel,
        out_shape=[
            jax.ShapeDtypeStruct((own, 2, width, width), F32),
            jax.ShapeDtypeStruct((own, 2 * vectors, width), F32),
            jax.ShapeDtypeStruct((own, width, early), BF16),
        ],
        in_specs=[whole] * tm,
        out_specs=[whole] * 3,
        scratch_shapes=[pltpu.VMEM((early, width), BF16)] * 2,
        compiler_params=params,
        cost_estimate=cost(2 * own * early * width * width, 8 * own * width * width),
    )(start_block, *blocks[:-1])

    packets = pl.pallas_call(
        functools.partial(subspace_kernel, tm, own, factor),
        out_shape=[jax.ShapeDtypeStruct((own, vectors, rows + 2 * beams), F32)] * tm,
        in_specs=[unread, whole, scalars, scalars] + [whole] * 5,
        out_specs=[whole] * tm,
        scratch_shapes=[pltpu.VMEM((2 * width, width), BF16)] * 2
        + [pltpu.VMEM((tm, vectors, rows), F32)],
        compiler_params=params,
        cost_estimate=cost(32 * own * vectors * tm * samples * width, 8 * own * width * width),
    )(mine, start_block, flags, ranks, own_weights, cov, first, across, blocks[-1])

    arrived = list(packets)
    for x in reversed(range(1, tm)):
        arrived[x] = lax.ppermute(packets[x], "tm", [(z, z ^ x) for z in range(tm)])
    groups = [[0, tm - 1], *[[x] for x in reversed(range(1, tm - 1))]]
    shape = jax.ShapeDtypeStruct((chan_dev, samples, half), F32)
    powers = []
    for xs in groups:
        powers = pl.pallas_call(
            functools.partial(first_kernel, own, xs),
            out_shape=[shape] * 2,
            in_specs=[whole] * (2 + len(xs) + len(powers)),
            out_specs=[whole] * 2,
            input_output_aliases={2 + len(xs) + i: i for i in range(len(powers))},
            scratch_shapes=[pltpu.VMEM((rows, half), F32)],
            compiler_params=params,
            cost_estimate=cost(len(xs) * own * rows * 6 * vectors * beams, 8 * own * rows * beams),
        )(mine, other, *[arrived[x] for x in xs], *powers)
    theirs = lax.ppermute(powers[1], "pol", [(0, 1), (1, 0)])

    return pl.pallas_call(
        second_kernel,
        out_shape=jax.ShapeDtypeStruct((samples, chan_dev, half), F32),
        in_specs=[whole] * 2,
        out_specs=whole,
        compiler_params=params,
        cost_estimate=cost(chan_dev * samples * half, 12 * chan_dev * samples * half),
    )(powers[0], theirs)


def solution(mesh):
    placed = (
        P(("groups", "tm"), "pol", "chan", None, None),
        P("pol", "chan", None, None, None),
        P(("groups", "chan")),
        P(("groups", "chan")),
        P(),
    )
    return jax.shard_map(
        local,
        mesh=mesh,
        in_specs=placed,
        out_specs=P(("groups", "tm"), "chan", "pol"),
        check_vma=False,
    )
```

```python
import functools

import jax
import jax.numpy as jnp
from jax import lax
from jax.experimental import pallas as pl
from jax.experimental.pallas import tpu as pltpu
from jax.sharding import PartitionSpec as P

ITERS = 4
PHASES = 1024
QUARTER = PHASES // 4
EPS = 1e-06
F32 = jnp.float32
BF16 = jnp.bfloat16
NT = (((1,), (1,)), ((), ()))
NN = (((1,), (0,)), ((), ()))
TN = (((0,), (0,)), ((), ()))
VMEM_LIMIT = 48 * 1024 * 1024
CHUNK = 128


def dot(left, right, dims):
    return lax.dot_general(left, right, dims, preferred_element_type=F32)


def split(values):
    high = values.astype(BF16)
    low = (values - high.astype(F32)).astype(BF16)
    return high, low


def steer(phase, step, norm):
    turn = (phase * step) & (PHASES - 1)
    quadrant = (turn + QUARTER // 2) // QUARTER
    angle = (turn - quadrant * QUARTER).astype(F32) * (2.0 * jnp.pi / PHASES)
    sq = angle * angle
    sine = angle * (1.0 + sq * (-1.0 / 6 + sq * (1.0 / 120 + sq * (-1.0 / 5040 + sq / 362880))))
    cosine = 1.0 + sq * (-0.5 + sq * (1.0 / 24 + sq * (-1.0 / 720 + sq / 40320)))
    odd = (quadrant & 1) == 1
    real = jnp.where(odd, sine, cosine) * norm
    imag = jnp.where(odd, cosine, sine) * norm
    real = jnp.where(((quadrant + 1) & 2) == 2, -real, real)
    imag = jnp.where((quadrant & 2) == 2, -imag, imag)
    return real.astype(BF16), imag.astype(BF16)


def fill_weights(phase_ref, first, rows, step, out):
    norm = 1.0 / (phase_ref.shape[1] ** 0.5)
    chunk = 32

    def body(i, carry):
        at = pl.multiple_of(i * chunk, chunk)
        real, imag = steer(phase_ref[pl.ds(first + at, chunk), :], step, norm)
        out[pl.ds(at, chunk), :] = real
        out[pl.ds(rows + at, chunk), :] = imag
        return carry

    lax.fori_loop(0, rows // chunk, body, 0)


def steps(tm):
    return [0, *[by for by in range(1, tm) if by != tm // 2], tm // 2]


def shifted(by):
    tm = lax.axis_size("tm")
    return lax.rem(lax.axis_index("tm") + tm + by, tm)


def cut_kernel(own, bys, voltages_ref, *rest):
    pieces, done = rest[:-1], rest[-1]
    copies = []
    for i, (by, piece) in enumerate(zip(bys, pieces)):
        channels = pl.ds(shifted(by) * own, own)
        copy = pltpu.make_async_copy(voltages_ref.at[:, 0, channels], piece, done.at[i])
        copy.start()
        copies.append(copy)
    for copy in copies:
        copy.wait()


def turned(values, axis):
    size = values.shape[axis]
    at = lax.broadcasted_iota(jnp.int32, values.shape, axis)
    after = pltpu.roll(values, size - 1, axis)
    before = pltpu.roll(values, 1, axis)
    return jnp.where((at & 1) == 0, after, -before)


def raw_beams_kernel(tm, own, phase_ref, *rest):
    pieces, (mine_ref, other_ref, weights) = rest[:tm], rest[tm:]
    half = phase_ref.shape[0] // 2
    rows = pieces[0].shape[1]
    pol = lax.axis_index("pol")
    start = lax.axis_index("chan") * tm * own
    for by, piece in zip(steps(tm), pieces):
        for o in range(own):
            chan = shifted(by) * own + o
            for swap, out_ref in enumerate((mine_ref, other_ref)):
                first = pl.multiple_of((pol ^ swap) * half, half)
                fill_weights(phase_ref, first, half, start + chan + 1, weights)
                product = dot(piece[o], weights[...], NT)
                by_imag = turned(product[:, half:].reshape(rows // 8, 8, half), 1).reshape(rows, half)
                out_ref[chan] = product[:, :half] - by_imag


def own_weights_kernel(own, chan_dev, phase_ref, out_ref, weights):
    beams = phase_ref.shape[0]
    first = lax.axis_index("chan") * chan_dev + lax.axis_index("tm") * own
    for o in range(own):
        fill_weights(phase_ref, 0, beams, first + o + 1, weights)
        out_ref[o] = weights[...].T


def rotate(x):
    return (-turned(x.astype(F32), 0)).astype(BF16)


def early_kernel(start_ref, *refs):
    blocks, (cov_ref, first_ref, across_ref, along_ref, rotated_ref) = refs[:-5], refs[-5:]
    rows, width = blocks[0].shape[1:]
    own = cov_ref.shape[0]
    for o in range(own):
        for i, block in enumerate(blocks):
            x = block[o]
            at = slice(i * rows, (i + 1) * rows)
            along_ref[at] = x
            rotated_ref[at] = rotate(x)
            across_ref[o, :, at] = x.T
        cov_ref[o, 0] = dot(across_ref[o], along_ref[...], NN)
        cov_ref[o, 1] = dot(across_ref[o], rotated_ref[...], NN)
        chan = lax.axis_index("tm") * own + o
        first_ref[o] = block_times(start_ref[0, chan, 0], start_ref[0, chan, 1], across_ref[o], along_ref[...])


def project(real, imag, across):
    vectors = real.shape[0]
    both = jnp.concatenate(split(jnp.concatenate([real, imag], axis=0)), axis=0)
    product = dot(both, across, NN)
    product = product[: 2 * vectors] + product[2 * vectors :]
    other = turned(product, 1)
    return product[:vectors] + other[vectors:], product[vectors:] - other[:vectors]


def block_times(real, imag, across, along):
    pair = jnp.concatenate(project(real, imag, across), axis=0)
    product = dot(jnp.concatenate(split(pair), axis=0), along, NN)
    return product[: pair.shape[0]] + product[pair.shape[0] :]


def cov_times(real, imag, high_ref, low_ref):
    vectors = real.shape[0]
    rows = jnp.concatenate(
        [jnp.concatenate([real, imag], axis=1), jnp.concatenate([imag, -real], axis=1)], axis=0
    )
    high, low = split(rows)
    product = dot(jnp.concatenate([high, low], axis=0), high_ref[...], NN)
    product = product[: 2 * vectors] + product[2 * vectors :] + dot(high, low_ref[...], NN)
    return product[:vectors], product[vectors:]


def orthonormalize(real_z, imag_z, beside=()):
    beside = list(beside)
    vectors, width = real_z.shape
    row = lax.broadcasted_iota(jnp.int32, (vectors, 1), 0)
    real_v, imag_v = real_z, imag_z
    scale = jnp.zeros((vectors, 1), F32)
    for n in range(vectors):
        real_a = jnp.broadcast_to(real_v[n : n + 1], real_z.shape)
        imag_a = jnp.broadcast_to(imag_v[n : n + 1], real_z.shape)
        norm = jnp.sum(real_a * real_a + imag_a * imag_a, axis=1, keepdims=True) + EPS
        scale = jnp.where(row == n, norm, scale)
        if n + 1 < vectors:
            real_d = jnp.sum(real_a * real_z + imag_a * imag_z, axis=1, keepdims=True)
            imag_d = jnp.sum(real_a * imag_z - imag_a * real_z, axis=1, keepdims=True)
            inverse = jnp.where(row > n, 1.0 / norm, 0.0)
            real_c = real_d * inverse
            imag_c = imag_d * inverse
            real_v = real_v - (real_c * real_a - imag_c * imag_a)
            imag_v = imag_v - (real_c * imag_a + imag_c * real_a)
        for work in beside[n::vectors]:
            work()
    factor = 1.0 / jnp.sqrt(scale)
    return real_v * factor, imag_v * factor


def orthonormalize_by_gram(real_z, imag_z):
    vectors = real_z.shape[0]
    row = lax.broadcasted_iota(jnp.int32, (vectors, 1), 0)
    by_z = []
    for n in range(vectors):
        real_a = jnp.broadcast_to(real_z[n : n + 1], real_z.shape)
        imag_a = jnp.broadcast_to(imag_z[n : n + 1], real_z.shape)
        by_z.append(
            (
                jnp.sum(real_a * real_z + imag_a * imag_z, axis=1, keepdims=True),
                jnp.sum(real_a * imag_z - imag_a * real_z, axis=1, keepdims=True),
            )
        )
    by_v = list(by_z)
    real_v, imag_v = real_z, imag_z
    for n in range(vectors - 1):
        (real_d, imag_d), (real_p, imag_p) = by_z[n], by_v[n]
        square = jnp.maximum(real_p[n : n + 1], 0.0)
        inverse = jnp.where(row > n, 1.0 / (square + EPS), 0.0)
        real_c, imag_c = real_d * inverse, imag_d * inverse
        real_b, imag_b = real_p - real_c * square, imag_p - imag_c * square
        for j in range(n + 1, vectors):
            real_s, imag_s = real_c[j : j + 1], imag_c[j : j + 1]
            real_q, imag_q = real_p[j : j + 1], -imag_p[j : j + 1]
            real, imag = by_v[j]
            by_v[j] = (
                real - (real_c * real_q - imag_c * imag_q) - (real_s * real_b + imag_s * imag_b),
                imag - (real_c * imag_q + imag_c * real_q) - (real_s * imag_b - imag_s * real_b),
            )
            real, imag = by_z[j]
            by_z[j] = (
                real - (real_s * real_d + imag_s * imag_d),
                imag - (real_s * imag_d - imag_s * real_d),
            )
        real_a, imag_a = real_v[n : n + 1], imag_v[n : n + 1]
        real_v = real_v - (real_c * real_a - imag_c * imag_a)
        imag_v = imag_v - (real_c * imag_a + imag_c * real_a)
    factor = 1.0 / jnp.sqrt(jnp.sum(real_v * real_v + imag_v * imag_v, axis=1, keepdims=True) + EPS)
    return real_v * factor, imag_v * factor


def subspace_kernel(
    tm, own, factor, beams_ref, start_ref, flags_ref, ranks_ref, weights_ref, cov_ref, first_ref, across_ref, last_ref, *rest
):
    outs, (high_ref, low_ref, series_ref) = rest[:tm], rest[tm:]
    vectors, width = start_ref.shape[3], start_ref.shape[4]
    rows = last_ref.shape[1]
    tm_index = lax.axis_index("tm")
    beams = weights_ref.shape[2] // 2
    for o in range(own):
        chan = tm_index * own + o
        across = last_ref[o].T
        rotated = rotate(last_ref[o])

        def add_last(part, first):
            right = last_ref[o] if part == 0 else rotated
            term = dot(across[first : first + CHUNK], right, NN)
            at = slice(part * width + first, part * width + first + CHUNK)
            high_ref[at], low_ref[at] = split((cov_ref[o, part, first : first + CHUNK] + term) * factor)

        chunks = [
            functools.partial(add_last, part, first) for part in range(2) for first in range(0, width, CHUNK)
        ]
        last = block_times(start_ref[0, chan, 0], start_ref[0, chan, 1], across, last_ref[o])
        both = (first_ref[o] + last) * factor
        real_q, imag_q = orthonormalize(both[:vectors], both[vectors:], chunks)
        for sweep in range(1, ITERS):
            real_z, imag_z = cov_times(real_q, imag_q, high_ref, low_ref)
            real_q, imag_q = orthonormalize_by_gram(real_z, imag_z)
        rank = flags_ref[chan] * ranks_ref[chan]
        keep = lax.broadcasted_iota(jnp.int32, (vectors, width), 0) < rank
        real_u = jnp.where(keep, real_q, 0.0)
        imag_u = jnp.where(keep, imag_q, 0.0)
        both = jnp.concatenate(split(jnp.concatenate([real_u, imag_u], axis=0)), axis=0)
        product = dot(both, weights_ref[o], NN)
        product = product[: 2 * vectors] + product[2 * vectors :]
        real_w = product[:vectors, :beams] - product[vectors:, beams:]
        imag_w = product[:vectors, beams:] + product[vectors:, :beams]
        for i, by in enumerate(steps(tm)):
            block = across_ref[o, :, i * rows : (i + 1) * rows] if i < tm - 1 else across
            series = project(real_u, imag_u, block)[0]
            series_ref[tm_index ^ shifted(-by)] = series
        for x, out in enumerate(outs):
            out[o, :, :rows] = series_ref[x]
            out[o, :, rows : rows + beams] = real_w
            out[o, :, rows + beams :] = imag_w


def first_kernel(own, xs, mine_ref, other_ref, *rest):
    packets, (mine_out, other_out, squares) = rest[: len(xs)], rest[-3:]
    rows, half = mine_ref.shape[1:]
    samples = rows // 2
    for x, ref in zip(xs, packets):
        for o in range(own):
            chan = (lax.axis_index("tm") ^ x) * own + o
            series = ref[o, :, :rows]
            left = jnp.concatenate([series, -turned(series, 1)], axis=0)
            high_s, low_s = split(left)
            left = jnp.concatenate([high_s, high_s, low_s], axis=0)
            for swap, (raw_ref, out_ref) in enumerate(((mine_ref, mine_out), (other_ref, other_out))):
                at = rows + (lax.axis_index("pol") ^ swap) * half
                real_at = pl.ds(pl.multiple_of(at, half), half)
                imag_at = pl.ds(pl.multiple_of(at + 2 * half, half), half)
                right = jnp.concatenate([ref[o, :, real_at], ref[o, :, imag_at]], axis=0)
                high_w, low_w = split(right)
                right = jnp.concatenate([high_w, low_w, high_w], axis=0)
                beam = raw_ref[chan] - dot(left, right, TN)
                squares[...] = beam * beam
                out_ref[chan] = squares[pl.ds(0, samples, 2), :] + squares[pl.ds(1, samples, 2), :]


def second_kernel(mine_ref, theirs_ref, out_ref):
    for chan in range(out_ref.shape[1]):
        out_ref[:, chan, :] = mine_ref[chan] + theirs_ref[chan]


def local(voltages, start_block, flags, ranks, phase_index):
    tm = lax.axis_size("tm")
    tm_index = lax.axis_index("tm")
    samples, chan_dev, width = voltages.shape[0], voltages.shape[2], voltages.shape[4]
    own = chan_dev // tm
    vectors = start_block.shape[3]
    beams = phase_index.shape[0]
    half = beams // 2
    rows = 2 * samples
    factor = 1.0 / (samples * tm)
    params = pltpu.CompilerParams(vmem_limit_bytes=VMEM_LIMIT)
    whole = pl.BlockSpec(memory_space=pltpu.VMEM)
    scalars = pl.BlockSpec(memory_space=pltpu.SMEM)
    unread = pl.BlockSpec(memory_space=pl.ANY)

    def cost(multiplies, moved):
        return pl.CostEstimate(flops=2 * multiplies, bytes_accessed=moved, transcendentals=0)

    by = steps(tm)
    later = pl.pallas_call(
        functools.partial(cut_kernel, own, [by[0], *by[2:]]),
        out_shape=[jax.ShapeDtypeStruct((samples, own, 2, width), BF16)] * (tm - 1),
        in_specs=[pl.BlockSpec(memory_space=pltpu.HBM)],
        out_specs=[whole] * (tm - 1),
        scratch_shapes=[pltpu.SemaphoreType.DMA((tm - 1,))],
        compiler_params=params,
    )(voltages)
    urgent = lax.dynamic_slice_in_dim(voltages[:, 0], shifted(by[1]) * own, own, 1)
    cut = [later[0], urgent, *later[1:]]
    pieces = [piece.transpose(1, 0, 2, 3).reshape(own, rows, width) for piece in cut]
    blocks = pieces[:1] + [
        lax.ppermute(piece, "tm", [(z, (z + by) % tm) for z in range(tm)])
        for by, piece in zip(steps(tm)[1:], pieces[1:])
    ]

    raw = jax.ShapeDtypeStruct((chan_dev, rows, half), F32)
    mine, other = pl.pallas_call(
        functools.partial(raw_beams_kernel, tm, own),
        out_shape=[raw] * 2,
        in_specs=[whole] * (1 + tm),
        out_specs=[whole] * 2,
        scratch_shapes=[pltpu.VMEM((beams, width), BF16)],
        compiler_params=params,
        cost_estimate=cost(4 * chan_dev * samples * width * beams, 8 * chan_dev * samples * width),
    )(phase_index, *pieces)

    own_weights = pl.pallas_call(
        functools.partial(own_weights_kernel, own, chan_dev),
        out_shape=jax.ShapeDtypeStruct((own, width, 2 * beams), BF16),
        in_specs=[whole],
        out_specs=whole,
        scratch_shapes=[pltpu.VMEM((2 * beams, width), BF16)],
        compiler_params=params,
        cost_estimate=cost(20 * own * beams * width, 8 * own * beams * width),
    )(phase_index)

    early = (tm - 1) * rows
    cov, first, across = pl.pallas_call(
        early_kernel,
        out_shape=[
            jax.ShapeDtypeStruct((own, 2, width, width), F32),
            jax.ShapeDtypeStruct((own, 2 * vectors, width), F32),
            jax.ShapeDtypeStruct((own, width, early), BF16),
        ],
        in_specs=[whole] * tm,
        out_specs=[whole] * 3,
        scratch_shapes=[pltpu.VMEM((early, width), BF16)] * 2,
        compiler_params=params,
        cost_estimate=cost(2 * own * early * width * width, 8 * own * width * width),
    )(start_block, *blocks[:-1])

    packets = pl.pallas_call(
        functools.partial(subspace_kernel, tm, own, factor),
        out_shape=[jax.ShapeDtypeStruct((own, vectors, rows + 2 * beams), F32)] * tm,
        in_specs=[unread, whole, scalars, scalars] + [whole] * 5,
        out_specs=[whole] * tm,
        scratch_shapes=[pltpu.VMEM((2 * width, width), BF16)] * 2
        + [pltpu.VMEM((tm, vectors, rows), F32)],
        compiler_params=params,
        cost_estimate=cost(32 * own * vectors * tm * samples * width, 8 * own * width * width),
    )(mine, start_block, flags, ranks, own_weights, cov, first, across, blocks[-1])

    order = [*range(2, tm), 1]
    arrived = list(packets)
    for x in order:
        arrived[x] = lax.ppermute(packets[x], "tm", [(z, z ^ x) for z in range(tm)])
    groups = [[0, order[0]], *[[x] for x in order[1:]]]
    shape = jax.ShapeDtypeStruct((chan_dev, samples, half), F32)
    powers = []
    for xs in groups:
        powers = pl.pallas_call(
            functools.partial(first_kernel, own, xs),
            out_shape=[shape] * 2,
            in_specs=[whole] * (2 + len(xs) + len(powers)),
            out_specs=[whole] * 2,
            input_output_aliases={2 + len(xs) + i: i for i in range(len(powers))},
            scratch_shapes=[pltpu.VMEM((rows, half), F32)],
            compiler_params=params,
            cost_estimate=cost(len(xs) * own * rows * 6 * vectors * beams, 8 * own * rows * beams),
        )(mine, other, *[arrived[x] for x in xs], *powers)
    theirs = lax.ppermute(powers[1], "pol", [(0, 1), (1, 0)])

    return pl.pallas_call(
        second_kernel,
        out_shape=jax.ShapeDtypeStruct((samples, chan_dev, half), F32),
        in_specs=[whole] * 2,
        out_specs=whole,
        compiler_params=params,
        cost_estimate=cost(chan_dev * samples * half, 12 * chan_dev * samples * half),
    )(powers[0], theirs)


def solution(mesh):
    placed = (
        P(("groups", "tm"), "pol", "chan", None, None),
        P("pol", "chan", None, None, None),
        P(("groups", "chan")),
        P(("groups", "chan")),
        P(),
    )
    return jax.shard_map(
        local,
        mesh=mesh,
        in_specs=placed,
        out_specs=P(("groups", "tm"), "chan", "pol"),
        check_vma=False,
    )
```

```python
import functools

import jax
import jax.numpy as jnp
from jax import lax
from jax.experimental import pallas as pl
from jax.experimental.pallas import tpu as pltpu
from jax.sharding import PartitionSpec as P

ITERS = 4
PHASES = 1024
QUARTER = PHASES // 4
EPS = 1e-06
F32 = jnp.float32
BF16 = jnp.bfloat16
NT = (((1,), (1,)), ((), ()))
NN = (((1,), (0,)), ((), ()))
TN = (((0,), (0,)), ((), ()))
VMEM_LIMIT = 48 * 1024 * 1024
CHUNK = 128


def dot(left, right, dims):
    return lax.dot_general(left, right, dims, preferred_element_type=F32)


def split(values):
    high = values.astype(BF16)
    low = (values - high.astype(F32)).astype(BF16)
    return high, low


def steer(phase, step, norm):
    turn = (phase * step) & (PHASES - 1)
    quadrant = (turn + QUARTER // 2) // QUARTER
    angle = (turn - quadrant * QUARTER).astype(F32) * (2.0 * jnp.pi / PHASES)
    sq = angle * angle
    sine = angle * (1.0 + sq * (-1.0 / 6 + sq * (1.0 / 120 + sq * (-1.0 / 5040 + sq / 362880))))
    cosine = 1.0 + sq * (-0.5 + sq * (1.0 / 24 + sq * (-1.0 / 720 + sq / 40320)))
    odd = (quadrant & 1) == 1
    real = jnp.where(odd, sine, cosine) * norm
    imag = jnp.where(odd, cosine, sine) * norm
    real = jnp.where(((quadrant + 1) & 2) == 2, -real, real)
    imag = jnp.where((quadrant & 2) == 2, -imag, imag)
    return real.astype(BF16), imag.astype(BF16)


def fill_weights(phase_ref, first, rows, step, out):
    norm = 1.0 / (phase_ref.shape[1] ** 0.5)
    chunk = 32

    def body(i, carry):
        at = pl.multiple_of(i * chunk, chunk)
        real, imag = steer(phase_ref[pl.ds(first + at, chunk), :], step, norm)
        out[pl.ds(at, chunk), :] = real
        out[pl.ds(rows + at, chunk), :] = imag
        return carry

    lax.fori_loop(0, rows // chunk, body, 0)


def steps(tm):
    return [0, *[by for by in range(1, tm) if by != tm // 2], tm // 2]


def shifted(by):
    tm = lax.axis_size("tm")
    return lax.rem(lax.axis_index("tm") + tm + by, tm)


def cut_kernel(own, bys, voltages_ref, *rest):
    pieces, done = rest[:-1], rest[-1]
    copies = []
    for i, (by, piece) in enumerate(zip(bys, pieces)):
        channels = pl.ds(shifted(by) * own, own)
        copy = pltpu.make_async_copy(voltages_ref.at[:, 0, channels], piece, done.at[i])
        copy.start()
        copies.append(copy)
    for copy in copies:
        copy.wait()


def turned(values, axis):
    size = values.shape[axis]
    at = lax.broadcasted_iota(jnp.int32, values.shape, axis)
    after = pltpu.roll(values, size - 1, axis)
    before = pltpu.roll(values, 1, axis)
    return jnp.where((at & 1) == 0, after, -before)


def raw_beams_kernel(tm, own, phase_ref, *rest):
    pieces, (mine_ref, other_ref, weights) = rest[:tm], rest[tm:]
    half = phase_ref.shape[0] // 2
    rows = pieces[0].shape[1]
    pol = lax.axis_index("pol")
    start = lax.axis_index("chan") * tm * own
    for by, piece in zip(steps(tm), pieces):
        for o in range(own):
            chan = shifted(by) * own + o
            for swap, out_ref in enumerate((mine_ref, other_ref)):
                first = pl.multiple_of((pol ^ swap) * half, half)
                fill_weights(phase_ref, first, half, start + chan + 1, weights)
                product = dot(piece[o], weights[...], NT)
                by_imag = turned(product[:, half:].reshape(rows // 8, 8, half), 1).reshape(rows, half)
                out_ref[chan] = product[:, :half] - by_imag


def own_weights_kernel(own, chan_dev, phase_ref, out_ref, weights):
    beams = phase_ref.shape[0]
    first = lax.axis_index("chan") * chan_dev + lax.axis_index("tm") * own
    for o in range(own):
        fill_weights(phase_ref, 0, beams, first + o + 1, weights)
        out_ref[o] = weights[...].T


def rotate(x):
    return (-turned(x.astype(F32), 0)).astype(BF16)


def early_kernel(start_ref, *refs):
    blocks, (cov_ref, first_ref, across_ref, along_ref, rotated_ref) = refs[:-5], refs[-5:]
    rows, width = blocks[0].shape[1:]
    own = cov_ref.shape[0]
    for o in range(own):
        for i, block in enumerate(blocks):
            x = block[o]
            at = slice(i * rows, (i + 1) * rows)
            along_ref[at] = x
            rotated_ref[at] = rotate(x)
            across_ref[o, :, at] = x.T
        cov_ref[o, 0] = dot(across_ref[o], along_ref[...], NN)
        cov_ref[o, 1] = dot(across_ref[o], rotated_ref[...], NN)
        chan = lax.axis_index("tm") * own + o
        first_ref[o] = block_times(start_ref[0, chan, 0], start_ref[0, chan, 1], across_ref[o], along_ref[...])


def project(real, imag, across):
    vectors = real.shape[0]
    both = jnp.concatenate(split(jnp.concatenate([real, imag], axis=0)), axis=0)
    product = dot(both, across, NN)
    product = product[: 2 * vectors] + product[2 * vectors :]
    other = turned(product, 1)
    return product[:vectors] + other[vectors:], product[vectors:] - other[:vectors]


def block_times(real, imag, across, along):
    pair = jnp.concatenate(project(real, imag, across), axis=0)
    product = dot(jnp.concatenate(split(pair), axis=0), along, NN)
    return product[: pair.shape[0]] + product[pair.shape[0] :]


def cov_times(real, imag, high_ref, low_ref):
    vectors = real.shape[0]
    rows = jnp.concatenate(
        [jnp.concatenate([real, imag], axis=1), jnp.concatenate([imag, -real], axis=1)], axis=0
    )
    high, low = split(rows)
    product = dot(jnp.concatenate([high, low], axis=0), high_ref[...], NN)
    product = product[: 2 * vectors] + product[2 * vectors :] + dot(high, low_ref[...], NN)
    return product[:vectors], product[vectors:]


def orthonormalize(real_z, imag_z, beside=()):
    beside = list(beside)
    vectors, width = real_z.shape
    row = lax.broadcasted_iota(jnp.int32, (vectors, 1), 0)
    real_v, imag_v = real_z, imag_z
    scale = jnp.zeros((vectors, 1), F32)
    for n in range(vectors):
        real_a = jnp.broadcast_to(real_v[n : n + 1], real_z.shape)
        imag_a = jnp.broadcast_to(imag_v[n : n + 1], real_z.shape)
        norm = jnp.sum(real_a * real_a + imag_a * imag_a, axis=1, keepdims=True) + EPS
        scale = jnp.where(row == n, norm, scale)
        if n + 1 < vectors:
            real_d = jnp.sum(real_a * real_z + imag_a * imag_z, axis=1, keepdims=True)
            imag_d = jnp.sum(real_a * imag_z - imag_a * real_z, axis=1, keepdims=True)
            inverse = jnp.where(row > n, 1.0 / norm, 0.0)
            real_c = real_d * inverse
            imag_c = imag_d * inverse
            real_v = real_v - (real_c * real_a - imag_c * imag_a)
            imag_v = imag_v - (real_c * imag_a + imag_c * real_a)
        for work in beside[n::vectors]:
            work()
    factor = 1.0 / jnp.sqrt(scale)
    return real_v * factor, imag_v * factor


def orthonormalize_by_gram(real_z, imag_z):
    vectors = real_z.shape[0]
    row = lax.broadcasted_iota(jnp.int32, (vectors, 1), 0)
    by_z = []
    for n in range(vectors):
        real_a = jnp.broadcast_to(real_z[n : n + 1], real_z.shape)
        imag_a = jnp.broadcast_to(imag_z[n : n + 1], real_z.shape)
        by_z.append(
            (
                jnp.sum(real_a * real_z + imag_a * imag_z, axis=1, keepdims=True),
                jnp.sum(real_a * imag_z - imag_a * real_z, axis=1, keepdims=True),
            )
        )
    by_v = list(by_z)
    real_v, imag_v = real_z, imag_z
    for n in range(vectors - 1):
        (real_d, imag_d), (real_p, imag_p) = by_z[n], by_v[n]
        square = jnp.maximum(real_p[n : n + 1], 0.0)
        inverse = jnp.where(row > n, 1.0 / (square + EPS), 0.0)
        real_c, imag_c = real_d * inverse, imag_d * inverse
        real_b, imag_b = real_p - real_c * square, imag_p - imag_c * square
        for j in range(n + 1, vectors):
            real_s, imag_s = real_c[j : j + 1], imag_c[j : j + 1]
            real_q, imag_q = real_p[j : j + 1], -imag_p[j : j + 1]
            real, imag = by_v[j]
            by_v[j] = (
                real - (real_c * real_q - imag_c * imag_q) - (real_s * real_b + imag_s * imag_b),
                imag - (real_c * imag_q + imag_c * real_q) - (real_s * imag_b - imag_s * real_b),
            )
            real, imag = by_z[j]
            by_z[j] = (
                real - (real_s * real_d + imag_s * imag_d),
                imag - (real_s * imag_d - imag_s * real_d),
            )
        real_a, imag_a = real_v[n : n + 1], imag_v[n : n + 1]
        real_v = real_v - (real_c * real_a - imag_c * imag_a)
        imag_v = imag_v - (real_c * imag_a + imag_c * real_a)
    factor = 1.0 / jnp.sqrt(jnp.sum(real_v * real_v + imag_v * imag_v, axis=1, keepdims=True) + EPS)
    return real_v * factor, imag_v * factor


def subspace_kernel(
    tm, own, factor, beams_ref, start_ref, flags_ref, ranks_ref, weights_ref, cov_ref, first_ref, across_ref, last_ref, *rest
):
    outs, (high_ref, low_ref, series_ref) = rest[:tm], rest[tm:]
    vectors, width = start_ref.shape[3], start_ref.shape[4]
    rows = last_ref.shape[1]
    tm_index = lax.axis_index("tm")
    beams = weights_ref.shape[2] // 2
    for o in range(own):
        chan = tm_index * own + o
        across = last_ref[o].T
        rotated = rotate(last_ref[o])

        def add_last(part, first):
            right = last_ref[o] if part == 0 else rotated
            term = dot(across[first : first + CHUNK], right, NN)
            at = slice(part * width + first, part * width + first + CHUNK)
            high_ref[at], low_ref[at] = split((cov_ref[o, part, first : first + CHUNK] + term) * factor)

        chunks = [
            functools.partial(add_last, part, first) for part in range(2) for first in range(0, width, CHUNK)
        ]
        last = block_times(start_ref[0, chan, 0], start_ref[0, chan, 1], across, last_ref[o])
        both = (first_ref[o] + last) * factor
        real_q, imag_q = orthonormalize(both[:vectors], both[vectors:], chunks)
        for sweep in range(1, ITERS):
            real_z, imag_z = cov_times(real_q, imag_q, high_ref, low_ref)
            real_q, imag_q = orthonormalize_by_gram(real_z, imag_z)
        rank = flags_ref[chan] * ranks_ref[chan]
        keep = lax.broadcasted_iota(jnp.int32, (vectors, width), 0) < rank
        real_u = jnp.where(keep, real_q, 0.0)
        imag_u = jnp.where(keep, imag_q, 0.0)
        both = jnp.concatenate(split(jnp.concatenate([real_u, imag_u], axis=0)), axis=0)
        product = dot(both, weights_ref[o], NN)
        product = product[: 2 * vectors] + product[2 * vectors :]
        real_w = product[:vectors, :beams] - product[vectors:, beams:]
        imag_w = product[:vectors, beams:] + product[vectors:, :beams]
        for i, by in enumerate(steps(tm)):
            block = across_ref[o, :, i * rows : (i + 1) * rows] if i < tm - 1 else across
            series = project(real_u, imag_u, block)[0]
            series_ref[tm_index ^ shifted(-by)] = series
        steered = jnp.concatenate([real_w, imag_w], axis=0).astype(BF16)
        for x, out in enumerate(outs):
            series = series_ref[x]
            series = jnp.concatenate([series[:, : rows // 2], series[:, rows // 2 :]], axis=0)
            out[o, :, :beams] = steered
            out[o, :, beams:] = series.astype(BF16)


def first_kernel(own, xs, mine_ref, other_ref, *rest):
    packets, (mine_out, other_out, squares) = rest[: len(xs)], rest[-3:]
    rows, half = mine_ref.shape[1:]
    samples = rows // 2
    for x, ref in zip(xs, packets):
        for o in range(own):
            chan = (lax.axis_index("tm") ^ x) * own + o
            series = ref[o, :, 2 * half :].astype(F32)
            vectors = series.shape[0] // 2
            series = jnp.concatenate([series[:vectors], series[vectors:]], axis=1)
            left = jnp.concatenate([series, -turned(series, 1)], axis=0).astype(BF16)
            for swap, (raw_ref, out_ref) in enumerate(((mine_ref, mine_out), (other_ref, other_out))):
                at = pl.multiple_of((lax.axis_index("pol") ^ swap) * half, half)
                right = ref[o, :, pl.ds(at, half)]
                beam = raw_ref[chan] - dot(left, right, TN)
                squares[...] = beam * beam
                out_ref[chan] = squares[pl.ds(0, samples, 2), :] + squares[pl.ds(1, samples, 2), :]


def second_kernel(mine_ref, theirs_ref, out_ref):
    for chan in range(out_ref.shape[1]):
        out_ref[:, chan, :] = mine_ref[chan] + theirs_ref[chan]


def local(voltages, start_block, flags, ranks, phase_index):
    tm = lax.axis_size("tm")
    tm_index = lax.axis_index("tm")
    samples, chan_dev, width = voltages.shape[0], voltages.shape[2], voltages.shape[4]
    own = chan_dev // tm
    vectors = start_block.shape[3]
    beams = phase_index.shape[0]
    half = beams // 2
    rows = 2 * samples
    factor = 1.0 / (samples * tm)
    params = pltpu.CompilerParams(vmem_limit_bytes=VMEM_LIMIT)
    whole = pl.BlockSpec(memory_space=pltpu.VMEM)
    scalars = pl.BlockSpec(memory_space=pltpu.SMEM)
    unread = pl.BlockSpec(memory_space=pl.ANY)

    def cost(multiplies, moved):
        return pl.CostEstimate(flops=2 * multiplies, bytes_accessed=moved, transcendentals=0)

    by = steps(tm)
    later = pl.pallas_call(
        functools.partial(cut_kernel, own, [by[0], *by[2:]]),
        out_shape=[jax.ShapeDtypeStruct((samples, own, 2, width), BF16)] * (tm - 1),
        in_specs=[pl.BlockSpec(memory_space=pltpu.HBM)],
        out_specs=[whole] * (tm - 1),
        scratch_shapes=[pltpu.SemaphoreType.DMA((tm - 1,))],
        compiler_params=params,
    )(voltages)
    urgent = lax.dynamic_slice_in_dim(voltages[:, 0], shifted(by[1]) * own, own, 1)
    cut = [later[0], urgent, *later[1:]]
    pieces = [piece.transpose(1, 0, 2, 3).reshape(own, rows, width) for piece in cut]
    blocks = pieces[:1] + [
        lax.ppermute(piece, "tm", [(z, (z + by) % tm) for z in range(tm)])
        for by, piece in zip(steps(tm)[1:], pieces[1:])
    ]

    raw = jax.ShapeDtypeStruct((chan_dev, rows, half), F32)
    mine, other = pl.pallas_call(
        functools.partial(raw_beams_kernel, tm, own),
        out_shape=[raw] * 2,
        in_specs=[whole] * (1 + tm),
        out_specs=[whole] * 2,
        scratch_shapes=[pltpu.VMEM((beams, width), BF16)],
        compiler_params=params,
        cost_estimate=cost(4 * chan_dev * samples * width * beams, 8 * chan_dev * samples * width),
    )(phase_index, *pieces)

    own_weights = pl.pallas_call(
        functools.partial(own_weights_kernel, own, chan_dev),
        out_shape=jax.ShapeDtypeStruct((own, width, 2 * beams), BF16),
        in_specs=[whole],
        out_specs=whole,
        scratch_shapes=[pltpu.VMEM((2 * beams, width), BF16)],
        compiler_params=params,
        cost_estimate=cost(20 * own * beams * width, 8 * own * beams * width),
    )(phase_index)

    early = (tm - 1) * rows
    cov, first, across = pl.pallas_call(
        early_kernel,
        out_shape=[
            jax.ShapeDtypeStruct((own, 2, width, width), F32),
            jax.ShapeDtypeStruct((own, 2 * vectors, width), F32),
            jax.ShapeDtypeStruct((own, width, early), BF16),
        ],
        in_specs=[whole] * tm,
        out_specs=[whole] * 3,
        scratch_shapes=[pltpu.VMEM((early, width), BF16)] * 2,
        compiler_params=params,
        cost_estimate=cost(2 * own * early * width * width, 8 * own * width * width),
    )(start_block, *blocks[:-1])

    packets = pl.pallas_call(
        functools.partial(subspace_kernel, tm, own, factor),
        out_shape=[jax.ShapeDtypeStruct((own, 2 * vectors, beams + samples), BF16)] * tm,
        in_specs=[unread, whole, scalars, scalars] + [whole] * 5,
        out_specs=[whole] * tm,
        scratch_shapes=[pltpu.VMEM((2 * width, width), BF16)] * 2
        + [pltpu.VMEM((tm, vectors, rows), F32)],
        compiler_params=params,
        cost_estimate=cost(32 * own * vectors * tm * samples * width, 8 * own * width * width),
    )(mine, start_block, flags, ranks, own_weights, cov, first, across, blocks[-1])

    order = [*range(2, tm), 1]
    arrived = list(packets)
    for x in order:
        arrived[x] = lax.ppermute(packets[x], "tm", [(z, z ^ x) for z in range(tm)])
    groups = [[0, order[0]], *[[x] for x in order[1:]]]
    shape = jax.ShapeDtypeStruct((chan_dev, samples, half), F32)
    powers = []
    for xs in groups:
        powers = pl.pallas_call(
            functools.partial(first_kernel, own, xs),
            out_shape=[shape] * 2,
            in_specs=[whole] * (2 + len(xs) + len(powers)),
            out_specs=[whole] * 2,
            input_output_aliases={2 + len(xs) + i: i for i in range(len(powers))},
            scratch_shapes=[pltpu.VMEM((rows, half), F32)],
            compiler_params=params,
            cost_estimate=cost(len(xs) * own * rows * 2 * vectors * beams, 8 * own * rows * beams),
        )(mine, other, *[arrived[x] for x in xs], *powers)
    theirs = lax.ppermute(powers[1], "pol", [(0, 1), (1, 0)])

    return pl.pallas_call(
        second_kernel,
        out_shape=jax.ShapeDtypeStruct((samples, chan_dev, half), F32),
        in_specs=[whole] * 2,
        out_specs=whole,
        compiler_params=params,
        cost_estimate=cost(chan_dev * samples * half, 12 * chan_dev * samples * half),
    )(powers[0], theirs)


def solution(mesh):
    placed = (
        P(("groups", "tm"), "pol", "chan", None, None),
        P("pol", "chan", None, None, None),
        P(("groups", "chan")),
        P(("groups", "chan")),
        P(),
    )
    return jax.shard_map(
        local,
        mesh=mesh,
        in_specs=placed,
        out_specs=P(("groups", "tm"), "chan", "pol"),
        check_vma=False,
    )
```

```python
import functools

import jax
import jax.numpy as jnp
from jax import lax
from jax.experimental import pallas as pl
from jax.experimental.pallas import tpu as pltpu
from jax.sharding import PartitionSpec as P

ITERS = 4
PHASES = 1024
QUARTER = PHASES // 4
EPS = 1e-06
F32 = jnp.float32
BF16 = jnp.bfloat16
NT = (((1,), (1,)), ((), ()))
NN = (((1,), (0,)), ((), ()))
TN = (((0,), (0,)), ((), ()))
VMEM_LIMIT = 48 * 1024 * 1024
CHUNK = 128


def dot(left, right, dims):
    return lax.dot_general(left, right, dims, preferred_element_type=F32)


def split(values):
    high = values.astype(BF16)
    low = (values - high.astype(F32)).astype(BF16)
    return high, low


def steer(phase, step, norm):
    turn = (phase * step) & (PHASES - 1)
    quadrant = (turn + QUARTER // 2) // QUARTER
    angle = (turn - quadrant * QUARTER).astype(F32) * (2.0 * jnp.pi / PHASES)
    sq = angle * angle
    sine = angle * (1.0 + sq * (-1.0 / 6 + sq * (1.0 / 120 + sq * (-1.0 / 5040 + sq / 362880))))
    cosine = 1.0 + sq * (-0.5 + sq * (1.0 / 24 + sq * (-1.0 / 720 + sq / 40320)))
    odd = (quadrant & 1) == 1
    real = jnp.where(odd, sine, cosine) * norm
    imag = jnp.where(odd, cosine, sine) * norm
    real = jnp.where(((quadrant + 1) & 2) == 2, -real, real)
    imag = jnp.where((quadrant & 2) == 2, -imag, imag)
    return real.astype(BF16), imag.astype(BF16)


def fill_weights(phase_ref, first, rows, step, out):
    norm = 1.0 / (phase_ref.shape[1] ** 0.5)
    chunk = 32

    def body(i, carry):
        at = pl.multiple_of(i * chunk, chunk)
        real, imag = steer(phase_ref[pl.ds(first + at, chunk), :], step, norm)
        out[pl.ds(at, chunk), :] = real
        out[pl.ds(rows + at, chunk), :] = imag
        return carry

    lax.fori_loop(0, rows // chunk, body, 0)


def orders(tm):
    near = [by for by in range(1, tm - 1) if by != tm // 2]
    return [0, tm // 2, *near, tm - 1], [0, *near, tm // 2, tm - 1]


def steps(tm):
    return [jnp.where(lax.axis_index("pol") == 0, a, b) for a, b in zip(*orders(tm))]


def shifted(by):
    tm = lax.axis_size("tm")
    return lax.rem(lax.axis_index("tm") + tm + by, tm)


def cut_kernel(tm, own, voltages_ref, *rest):
    pieces, done = rest[:-1], rest[-1]
    copies = []
    by = steps(tm)
    for i, (by, piece) in enumerate(zip([by[0], *by[2:]], pieces)):
        channels = pl.ds(shifted(by) * own, own)
        copy = pltpu.make_async_copy(voltages_ref.at[:, 0, channels], piece, done.at[i])
        copy.start()
        copies.append(copy)
    for copy in copies:
        copy.wait()


def turned(values, axis):
    size = values.shape[axis]
    at = lax.broadcasted_iota(jnp.int32, values.shape, axis)
    after = pltpu.roll(values, size - 1, axis)
    before = pltpu.roll(values, 1, axis)
    return jnp.where((at & 1) == 0, after, -before)


def raw_beams_kernel(tm, own, phase_ref, *rest):
    pieces, (mine_ref, other_ref, weights) = rest[:tm], rest[tm:]
    half = phase_ref.shape[0] // 2
    rows = pieces[0].shape[1]
    pol = lax.axis_index("pol")
    start = lax.axis_index("chan") * tm * own
    for by, piece in zip(steps(tm), pieces):
        for o in range(own):
            chan = shifted(by) * own + o
            for swap, out_ref in enumerate((mine_ref, other_ref)):
                first = pl.multiple_of((pol ^ swap) * half, half)
                fill_weights(phase_ref, first, half, start + chan + 1, weights)
                product = dot(piece[o], weights[...], NT)
                by_imag = turned(product[:, half:].reshape(rows // 8, 8, half), 1).reshape(rows, half)
                out_ref[chan] = product[:, :half] - by_imag


def own_weights_kernel(own, chan_dev, phase_ref, out_ref, weights):
    beams = phase_ref.shape[0]
    first = lax.axis_index("chan") * chan_dev + lax.axis_index("tm") * own
    for o in range(own):
        fill_weights(phase_ref, 0, beams, first + o + 1, weights)
        out_ref[o] = weights[...].T


def rotate(x):
    return (-turned(x.astype(F32), 0)).astype(BF16)


def early_kernel(start_ref, *refs):
    blocks, (cov_ref, first_ref, across_ref, along_ref, rotated_ref) = refs[:-5], refs[-5:]
    rows, width = blocks[0].shape[1:]
    own = cov_ref.shape[0]
    for o in range(own):
        for i, block in enumerate(blocks):
            x = block[o]
            at = slice(i * rows, (i + 1) * rows)
            along_ref[at] = x
            rotated_ref[at] = rotate(x)
            across_ref[o, :, at] = x.T
        cov_ref[o, 0] = dot(across_ref[o], along_ref[...], NN)
        cov_ref[o, 1] = dot(across_ref[o], rotated_ref[...], NN)
        chan = lax.axis_index("tm") * own + o
        first_ref[o] = block_times(start_ref[0, chan, 0], start_ref[0, chan, 1], across_ref[o], along_ref[...])


def project(real, imag, across):
    vectors = real.shape[0]
    both = jnp.concatenate(split(jnp.concatenate([real, imag], axis=0)), axis=0)
    product = dot(both, across, NN)
    product = product[: 2 * vectors] + product[2 * vectors :]
    other = turned(product, 1)
    return product[:vectors] + other[vectors:], product[vectors:] - other[:vectors]


def block_times(real, imag, across, along):
    pair = jnp.concatenate(project(real, imag, across), axis=0)
    product = dot(jnp.concatenate(split(pair), axis=0), along, NN)
    return product[: pair.shape[0]] + product[pair.shape[0] :]


def cov_times(real, imag, high_ref, low_ref):
    vectors = real.shape[0]
    rows = jnp.concatenate(
        [jnp.concatenate([real, imag], axis=1), jnp.concatenate([imag, -real], axis=1)], axis=0
    )
    high, low = split(rows)
    product = dot(jnp.concatenate([high, low], axis=0), high_ref[...], NN)
    product = product[: 2 * vectors] + product[2 * vectors :] + dot(high, low_ref[...], NN)
    return product[:vectors], product[vectors:]


def orthonormalize(real_z, imag_z, beside=()):
    beside = list(beside)
    vectors, width = real_z.shape
    row = lax.broadcasted_iota(jnp.int32, (vectors, 1), 0)
    real_v, imag_v = real_z, imag_z
    scale = jnp.zeros((vectors, 1), F32)
    for n in range(vectors):
        real_a = jnp.broadcast_to(real_v[n : n + 1], real_z.shape)
        imag_a = jnp.broadcast_to(imag_v[n : n + 1], real_z.shape)
        norm = jnp.sum(real_a * real_a + imag_a * imag_a, axis=1, keepdims=True) + EPS
        scale = jnp.where(row == n, norm, scale)
        if n + 1 < vectors:
            real_d = jnp.sum(real_a * real_z + imag_a * imag_z, axis=1, keepdims=True)
            imag_d = jnp.sum(real_a * imag_z - imag_a * real_z, axis=1, keepdims=True)
            inverse = jnp.where(row > n, 1.0 / norm, 0.0)
            real_c = real_d * inverse
            imag_c = imag_d * inverse
            real_v = real_v - (real_c * real_a - imag_c * imag_a)
            imag_v = imag_v - (real_c * imag_a + imag_c * real_a)
        for work in beside[n::vectors]:
            work()
    factor = 1.0 / jnp.sqrt(scale)
    return real_v * factor, imag_v * factor


def orthonormalize_by_gram(real_z, imag_z):
    vectors = real_z.shape[0]
    row = lax.broadcasted_iota(jnp.int32, (vectors, 1), 0)
    by_z = []
    for n in range(vectors):
        real_a = jnp.broadcast_to(real_z[n : n + 1], real_z.shape)
        imag_a = jnp.broadcast_to(imag_z[n : n + 1], real_z.shape)
        by_z.append(
            (
                jnp.sum(real_a * real_z + imag_a * imag_z, axis=1, keepdims=True),
                jnp.sum(real_a * imag_z - imag_a * real_z, axis=1, keepdims=True),
            )
        )
    by_v = list(by_z)
    real_v, imag_v = real_z, imag_z
    for n in range(vectors - 1):
        (real_d, imag_d), (real_p, imag_p) = by_z[n], by_v[n]
        square = jnp.maximum(real_p[n : n + 1], 0.0)
        inverse = jnp.where(row > n, 1.0 / (square + EPS), 0.0)
        real_c, imag_c = real_d * inverse, imag_d * inverse
        real_b, imag_b = real_p - real_c * square, imag_p - imag_c * square
        for j in range(n + 1, vectors):
            real_s, imag_s = real_c[j : j + 1], imag_c[j : j + 1]
            real_q, imag_q = real_p[j : j + 1], -imag_p[j : j + 1]
            real, imag = by_v[j]
            by_v[j] = (
                real - (real_c * real_q - imag_c * imag_q) - (real_s * real_b + imag_s * imag_b),
                imag - (real_c * imag_q + imag_c * real_q) - (real_s * imag_b - imag_s * real_b),
            )
            real, imag = by_z[j]
            by_z[j] = (
                real - (real_s * real_d + imag_s * imag_d),
                imag - (real_s * imag_d - imag_s * real_d),
            )
        real_a, imag_a = real_v[n : n + 1], imag_v[n : n + 1]
        real_v = real_v - (real_c * real_a - imag_c * imag_a)
        imag_v = imag_v - (real_c * imag_a + imag_c * real_a)
    factor = 1.0 / jnp.sqrt(jnp.sum(real_v * real_v + imag_v * imag_v, axis=1, keepdims=True) + EPS)
    return real_v * factor, imag_v * factor


def subspace_kernel(
    tm, own, factor, beams_ref, start_ref, flags_ref, ranks_ref, weights_ref, cov_ref, first_ref, across_ref, last_ref, *rest
):
    outs, (high_ref, low_ref, series_ref) = rest[:tm], rest[tm:]
    vectors, width = start_ref.shape[3], start_ref.shape[4]
    rows = last_ref.shape[1]
    tm_index = lax.axis_index("tm")
    beams = weights_ref.shape[2] // 2
    for o in range(own):
        chan = tm_index * own + o
        across = last_ref[o].T
        rotated = rotate(last_ref[o])

        def add_last(part, first):
            right = last_ref[o] if part == 0 else rotated
            term = dot(across[first : first + CHUNK], right, NN)
            at = slice(part * width + first, part * width + first + CHUNK)
            high_ref[at], low_ref[at] = split((cov_ref[o, part, first : first + CHUNK] + term) * factor)

        chunks = [
            functools.partial(add_last, part, first) for part in range(2) for first in range(0, width, CHUNK)
        ]
        last = block_times(start_ref[0, chan, 0], start_ref[0, chan, 1], across, last_ref[o])
        both = (first_ref[o] + last) * factor
        real_q, imag_q = orthonormalize(both[:vectors], both[vectors:], chunks)
        for sweep in range(1, ITERS):
            real_z, imag_z = cov_times(real_q, imag_q, high_ref, low_ref)
            real_q, imag_q = orthonormalize_by_gram(real_z, imag_z)
        rank = flags_ref[chan] * ranks_ref[chan]
        keep = lax.broadcasted_iota(jnp.int32, (vectors, width), 0) < rank
        real_u = jnp.where(keep, real_q, 0.0)
        imag_u = jnp.where(keep, imag_q, 0.0)
        both = jnp.concatenate(split(jnp.concatenate([real_u, imag_u], axis=0)), axis=0)
        product = dot(both, weights_ref[o], NN)
        product = product[: 2 * vectors] + product[2 * vectors :]
        real_w = product[:vectors, :beams] - product[vectors:, beams:]
        imag_w = product[:vectors, beams:] + product[vectors:, :beams]
        for i, by in enumerate(steps(tm)):
            block = across_ref[o, :, i * rows : (i + 1) * rows] if i < tm - 1 else across
            series = project(real_u, imag_u, block)[0]
            series_ref[tm_index ^ shifted(-by)] = series
        steered = jnp.concatenate([real_w, imag_w], axis=0).astype(BF16)
        for x, out in enumerate(outs):
            series = series_ref[x]
            series = jnp.concatenate([series[:, : rows // 2], series[:, rows // 2 :]], axis=0)
            out[o, :, :beams] = steered
            out[o, :, beams:] = series.astype(BF16)


def first_kernel(own, xs, mine_ref, other_ref, *rest):
    packets, (mine_out, other_out, squares) = rest[: len(xs)], rest[-3:]
    rows, half = mine_ref.shape[1:]
    samples = rows // 2
    for x, ref in zip(xs, packets):
        for o in range(own):
            chan = (lax.axis_index("tm") ^ x) * own + o
            series = ref[o, :, 2 * half :].astype(F32)
            vectors = series.shape[0] // 2
            series = jnp.concatenate([series[:vectors], series[vectors:]], axis=1)
            left = jnp.concatenate([series, -turned(series, 1)], axis=0).astype(BF16)
            for swap, (raw_ref, out_ref) in enumerate(((mine_ref, mine_out), (other_ref, other_out))):
                at = pl.multiple_of((lax.axis_index("pol") ^ swap) * half, half)
                right = ref[o, :, pl.ds(at, half)]
                beam = raw_ref[chan] - dot(left, right, TN)
                squares[...] = beam * beam
                out_ref[chan] = squares[pl.ds(0, samples, 2), :] + squares[pl.ds(1, samples, 2), :]


def second_kernel(mine_ref, theirs_ref, out_ref):
    for chan in range(out_ref.shape[1]):
        out_ref[:, chan, :] = mine_ref[chan] + theirs_ref[chan]


def local(voltages, start_block, flags, ranks, phase_index):
    tm = lax.axis_size("tm")
    tm_index = lax.axis_index("tm")
    samples, chan_dev, width = voltages.shape[0], voltages.shape[2], voltages.shape[4]
    own = chan_dev // tm
    vectors = start_block.shape[3]
    beams = phase_index.shape[0]
    half = beams // 2
    rows = 2 * samples
    factor = 1.0 / (samples * tm)
    params = pltpu.CompilerParams(vmem_limit_bytes=VMEM_LIMIT)
    whole = pl.BlockSpec(memory_space=pltpu.VMEM)
    scalars = pl.BlockSpec(memory_space=pltpu.SMEM)
    unread = pl.BlockSpec(memory_space=pl.ANY)

    def cost(multiplies, moved):
        return pl.CostEstimate(flops=2 * multiplies, bytes_accessed=moved, transcendentals=0)

    by = steps(tm)
    later = pl.pallas_call(
        functools.partial(cut_kernel, tm, own),
        out_shape=[jax.ShapeDtypeStruct((samples, own, 2, width), BF16)] * (tm - 1),
        in_specs=[pl.BlockSpec(memory_space=pltpu.HBM)],
        out_specs=[whole] * (tm - 1),
        scratch_shapes=[pltpu.SemaphoreType.DMA((tm - 1,))],
        compiler_params=params,
    )(voltages)
    urgent = lax.dynamic_slice_in_dim(voltages[:, 0], shifted(by[1]) * own, own, 1)
    cut = [later[0], urgent, *later[1:]]
    pieces = [piece.transpose(1, 0, 2, 3).reshape(own, rows, width) for piece in cut]
    blocks = pieces[:1] + [
        lax.ppermute(
            piece, ("tm", "pol"), [(2 * z + p, (z + by[p]) % tm * 2 + p) for z in range(tm) for p in range(2)]
        )
        for by, piece in list(zip(zip(*orders(tm)), pieces))[1:]
    ]

    raw = jax.ShapeDtypeStruct((chan_dev, rows, half), F32)
    mine, other = pl.pallas_call(
        functools.partial(raw_beams_kernel, tm, own),
        out_shape=[raw] * 2,
        in_specs=[whole] * (1 + tm),
        out_specs=[whole] * 2,
        scratch_shapes=[pltpu.VMEM((beams, width), BF16)],
        compiler_params=params,
        cost_estimate=cost(4 * chan_dev * samples * width * beams, 8 * chan_dev * samples * width),
    )(phase_index, *pieces)

    own_weights = pl.pallas_call(
        functools.partial(own_weights_kernel, own, chan_dev),
        out_shape=jax.ShapeDtypeStruct((own, width, 2 * beams), BF16),
        in_specs=[whole],
        out_specs=whole,
        scratch_shapes=[pltpu.VMEM((2 * beams, width), BF16)],
        compiler_params=params,
        cost_estimate=cost(20 * own * beams * width, 8 * own * beams * width),
    )(phase_index)

    early = (tm - 1) * rows
    cov, first, across = pl.pallas_call(
        early_kernel,
        out_shape=[
            jax.ShapeDtypeStruct((own, 2, width, width), F32),
            jax.ShapeDtypeStruct((own, 2 * vectors, width), F32),
            jax.ShapeDtypeStruct((own, width, early), BF16),
        ],
        in_specs=[whole] * tm,
        out_specs=[whole] * 3,
        scratch_shapes=[pltpu.VMEM((early, width), BF16)] * 2,
        compiler_params=params,
        cost_estimate=cost(2 * own * early * width * width, 8 * own * width * width),
    )(start_block, *blocks[:-1])

    packets = pl.pallas_call(
        functools.partial(subspace_kernel, tm, own, factor),
        out_shape=[jax.ShapeDtypeStruct((own, 2 * vectors, beams + samples), BF16)] * tm,
        in_specs=[unread, whole, scalars, scalars] + [whole] * 5,
        out_specs=[whole] * tm,
        scratch_shapes=[pltpu.VMEM((2 * width, width), BF16)] * 2
        + [pltpu.VMEM((tm, vectors, rows), F32)],
        compiler_params=params,
        cost_estimate=cost(32 * own * vectors * tm * samples * width, 8 * own * width * width),
    )(mine, start_block, flags, ranks, own_weights, cov, first, across, blocks[-1])

    order = [*range(2, tm), 1]
    arrived = list(packets)
    for x in order:
        arrived[x] = lax.ppermute(packets[x], "tm", [(z, z ^ x) for z in range(tm)])
    groups = [[0, order[0]], *[[x] for x in order[1:]]]
    shape = jax.ShapeDtypeStruct((chan_dev, samples, half), F32)
    powers = []
    for xs in groups:
        powers = pl.pallas_call(
            functools.partial(first_kernel, own, xs),
            out_shape=[shape] * 2,
            in_specs=[whole] * (2 + len(xs) + len(powers)),
            out_specs=[whole] * 2,
            input_output_aliases={2 + len(xs) + i: i for i in range(len(powers))},
            scratch_shapes=[pltpu.VMEM((rows, half), F32)],
            compiler_params=params,
            cost_estimate=cost(len(xs) * own * rows * 2 * vectors * beams, 8 * own * rows * beams),
        )(mine, other, *[arrived[x] for x in xs], *powers)
    theirs = lax.ppermute(powers[1], "pol", [(0, 1), (1, 0)])

    return pl.pallas_call(
        second_kernel,
        out_shape=jax.ShapeDtypeStruct((samples, chan_dev, half), F32),
        in_specs=[whole] * 2,
        out_specs=whole,
        compiler_params=params,
        cost_estimate=cost(chan_dev * samples * half, 12 * chan_dev * samples * half),
    )(powers[0], theirs)


def solution(mesh):
    placed = (
        P(("groups", "tm"), "pol", "chan", None, None),
        P("pol", "chan", None, None, None),
        P(("groups", "chan")),
        P(("groups", "chan")),
        P(),
    )
    return jax.shard_map(
        local,
        mesh=mesh,
        in_specs=placed,
        out_specs=P(("groups", "tm"), "chan", "pol"),
        check_vma=False,
    )
```

```python
import functools

import jax
import jax.numpy as jnp
from jax import lax
from jax.experimental import pallas as pl
from jax.experimental.pallas import tpu as pltpu
from jax.sharding import PartitionSpec as P

ITERS = 4
PHASES = 1024
QUARTER = PHASES // 4
EPS = 1e-06
F32 = jnp.float32
BF16 = jnp.bfloat16
NT = (((1,), (1,)), ((), ()))
NN = (((1,), (0,)), ((), ()))
TN = (((0,), (0,)), ((), ()))
VMEM_LIMIT = 48 * 1024 * 1024
CHUNK = 128


def dot(left, right, dims):
    return lax.dot_general(left, right, dims, preferred_element_type=F32)


def split(values):
    high = values.astype(BF16)
    low = (values - high.astype(F32)).astype(BF16)
    return high, low


def steer(phase, step, norm):
    turn = (phase * step) & (PHASES - 1)
    quadrant = (turn + QUARTER // 2) // QUARTER
    angle = (turn - quadrant * QUARTER).astype(F32) * (2.0 * jnp.pi / PHASES)
    sq = angle * angle
    sine = angle * (1.0 + sq * (-1.0 / 6 + sq * (1.0 / 120 + sq * (-1.0 / 5040 + sq / 362880))))
    cosine = 1.0 + sq * (-0.5 + sq * (1.0 / 24 + sq * (-1.0 / 720 + sq / 40320)))
    odd = (quadrant & 1) == 1
    real = jnp.where(odd, sine, cosine) * norm
    imag = jnp.where(odd, cosine, sine) * norm
    real = jnp.where(((quadrant + 1) & 2) == 2, -real, real)
    imag = jnp.where((quadrant & 2) == 2, -imag, imag)
    return real.astype(BF16), imag.astype(BF16)


def fill_weights(phase_ref, first, rows, step, out):
    norm = 1.0 / (phase_ref.shape[1] ** 0.5)
    chunk = 32

    def body(i, carry):
        at = pl.multiple_of(i * chunk, chunk)
        real, imag = steer(phase_ref[pl.ds(first + at, chunk), :], step, norm)
        out[pl.ds(at, chunk), :] = real
        out[pl.ds(rows + at, chunk), :] = imag
        return carry

    lax.fori_loop(0, rows // chunk, body, 0)


def steps(tm):
    return [0, *[by for by in range(1, tm) if by != tm // 2], tm // 2]


def shifted(by):
    tm = lax.axis_size("tm")
    return lax.rem(lax.axis_index("tm") + tm + by, tm)


def cut_kernel(own, bys, voltages_ref, *rest):
    pieces, done = rest[:-1], rest[-1]
    copies = []
    for i, (by, piece) in enumerate(zip(bys, pieces)):
        channels = pl.ds(shifted(by) * own, own)
        copy = pltpu.make_async_copy(voltages_ref.at[:, 0, channels], piece, done.at[i])
        copy.start()
        copies.append(copy)
    for copy in copies:
        copy.wait()


def turned(values, axis):
    size = values.shape[axis]
    at = lax.broadcasted_iota(jnp.int32, values.shape, axis)
    after = pltpu.roll(values, size - 1, axis)
    before = pltpu.roll(values, 1, axis)
    return jnp.where((at & 1) == 0, after, -before)


def raw_beams_kernel(tm, own, phase_ref, *rest):
    pieces, (mine_ref, other_ref, weights) = rest[:tm], rest[tm:]
    half = phase_ref.shape[0] // 2
    rows = pieces[0].shape[1]
    pol = lax.axis_index("pol")
    start = lax.axis_index("chan") * tm * own
    for by, piece in zip(steps(tm), pieces):
        for o in range(own):
            chan = shifted(by) * own + o
            for swap, out_ref in enumerate((mine_ref, other_ref)):
                first = pl.multiple_of((pol ^ swap) * half, half)
                fill_weights(phase_ref, first, half, start + chan + 1, weights)
                product = dot(piece[o], weights[...], NT)
                by_imag = turned(product[:, half:].reshape(rows // 8, 8, half), 1).reshape(rows, half)
                out_ref[chan] = product[:, :half] - by_imag


def own_weights_kernel(own, chan_dev, phase_ref, out_ref, weights):
    beams = phase_ref.shape[0]
    first = lax.axis_index("chan") * chan_dev + lax.axis_index("tm") * own
    for o in range(own):
        fill_weights(phase_ref, 0, beams, first + o + 1, weights)
        out_ref[o] = weights[...].T


def rotate(x):
    return (-turned(x.astype(F32), 0)).astype(BF16)


def early_kernel(start_ref, *refs):
    blocks, (cov_ref, first_ref, across_ref, along_ref, rotated_ref) = refs[:-5], refs[-5:]
    rows, width = blocks[0].shape[1:]
    own = cov_ref.shape[0]
    for o in range(own):
        for i, block in enumerate(blocks):
            x = block[o]
            at = slice(i * rows, (i + 1) * rows)
            along_ref[at] = x
            rotated_ref[at] = rotate(x)
            across_ref[o, :, at] = x.T
        cov_ref[o, 0] = dot(across_ref[o], along_ref[...], NN)
        cov_ref[o, 1] = dot(across_ref[o], rotated_ref[...], NN)
        chan = lax.axis_index("tm") * own + o
        first_ref[o] = block_times(start_ref[0, chan, 0], start_ref[0, chan, 1], across_ref[o], along_ref[...])


def project(real, imag, across):
    vectors = real.shape[0]
    both = jnp.concatenate(split(jnp.concatenate([real, imag], axis=0)), axis=0)
    product = dot(both, across, NN)
    product = product[: 2 * vectors] + product[2 * vectors :]
    other = turned(product, 1)
    return product[:vectors] + other[vectors:], product[vectors:] - other[:vectors]


def block_times(real, imag, across, along):
    pair = jnp.concatenate(project(real, imag, across), axis=0)
    product = dot(jnp.concatenate(split(pair), axis=0), along, NN)
    return product[: pair.shape[0]] + product[pair.shape[0] :]


def cov_times(real, imag, high_ref, low_ref):
    vectors = real.shape[0]
    rows = jnp.concatenate(
        [jnp.concatenate([real, imag], axis=1), jnp.concatenate([imag, -real], axis=1)], axis=0
    )
    high, low = split(rows)
    product = dot(jnp.concatenate([high, low], axis=0), high_ref[...], NN)
    product = product[: 2 * vectors] + product[2 * vectors :] + dot(high, low_ref[...], NN)
    return product[:vectors], product[vectors:]


def orthonormalize(real_z, imag_z, beside=()):
    beside = list(beside)
    vectors, width = real_z.shape
    row = lax.broadcasted_iota(jnp.int32, (vectors, 1), 0)
    real_v, imag_v = real_z, imag_z
    scale = jnp.zeros((vectors, 1), F32)
    for n in range(vectors):
        real_a = jnp.broadcast_to(real_v[n : n + 1], real_z.shape)
        imag_a = jnp.broadcast_to(imag_v[n : n + 1], real_z.shape)
        norm = jnp.sum(real_a * real_a + imag_a * imag_a, axis=1, keepdims=True) + EPS
        scale = jnp.where(row == n, norm, scale)
        if n + 1 < vectors:
            real_d = jnp.sum(real_a * real_z + imag_a * imag_z, axis=1, keepdims=True)
            imag_d = jnp.sum(real_a * imag_z - imag_a * real_z, axis=1, keepdims=True)
            inverse = jnp.where(row > n, 1.0 / norm, 0.0)
            real_c = real_d * inverse
            imag_c = imag_d * inverse
            real_v = real_v - (real_c * real_a - imag_c * imag_a)
            imag_v = imag_v - (real_c * imag_a + imag_c * real_a)
        for work in beside[n::vectors]:
            work()
    factor = 1.0 / jnp.sqrt(scale)
    return real_v * factor, imag_v * factor


def orthonormalize_by_gram(real_z, imag_z):
    vectors = real_z.shape[0]
    row = lax.broadcasted_iota(jnp.int32, (vectors, 1), 0)
    by_z = []
    for n in range(vectors):
        real_a = jnp.broadcast_to(real_z[n : n + 1], real_z.shape)
        imag_a = jnp.broadcast_to(imag_z[n : n + 1], real_z.shape)
        by_z.append(
            (
                jnp.sum(real_a * real_z + imag_a * imag_z, axis=1, keepdims=True),
                jnp.sum(real_a * imag_z - imag_a * real_z, axis=1, keepdims=True),
            )
        )
    by_v = list(by_z)
    real_v, imag_v = real_z, imag_z
    for n in range(vectors - 1):
        (real_d, imag_d), (real_p, imag_p) = by_z[n], by_v[n]
        square = jnp.maximum(real_p[n : n + 1], 0.0)
        inverse = jnp.where(row > n, 1.0 / (square + EPS), 0.0)
        real_c, imag_c = real_d * inverse, imag_d * inverse
        real_b, imag_b = real_p - real_c * square, imag_p - imag_c * square
        for j in range(n + 1, vectors):
            real_s, imag_s = real_c[j : j + 1], imag_c[j : j + 1]
            real_q, imag_q = real_p[j : j + 1], -imag_p[j : j + 1]
            real, imag = by_v[j]
            by_v[j] = (
                real - (real_c * real_q - imag_c * imag_q) - (real_s * real_b + imag_s * imag_b),
                imag - (real_c * imag_q + imag_c * real_q) - (real_s * imag_b - imag_s * real_b),
            )
            real, imag = by_z[j]
            by_z[j] = (
                real - (real_s * real_d + imag_s * imag_d),
                imag - (real_s * imag_d - imag_s * real_d),
            )
        real_a, imag_a = real_v[n : n + 1], imag_v[n : n + 1]
        real_v = real_v - (real_c * real_a - imag_c * imag_a)
        imag_v = imag_v - (real_c * imag_a + imag_c * real_a)
    factor = 1.0 / jnp.sqrt(jnp.sum(real_v * real_v + imag_v * imag_v, axis=1, keepdims=True) + EPS)
    return real_v * factor, imag_v * factor


def subspace_kernel(
    tm, own, factor, beams_ref, start_ref, flags_ref, ranks_ref, weights_ref, cov_ref, first_ref, across_ref, last_ref, *rest
):
    outs, (high_ref, low_ref, series_ref) = rest[1 : tm + 1], rest[tm + 1 :]
    vectors, width = start_ref.shape[3], start_ref.shape[4]
    rows = last_ref.shape[1]
    tm_index = lax.axis_index("tm")
    beams = weights_ref.shape[2] // 2
    for o in range(own):
        chan = tm_index * own + o
        across = last_ref[o].T
        rotated = rotate(last_ref[o])

        def add_last(part, first):
            right = last_ref[o] if part == 0 else rotated
            term = dot(across[first : first + CHUNK], right, NN)
            at = slice(part * width + first, part * width + first + CHUNK)
            high_ref[at], low_ref[at] = split((cov_ref[o, part, first : first + CHUNK] + term) * factor)

        chunks = [
            functools.partial(add_last, part, first) for part in range(2) for first in range(0, width, CHUNK)
        ]
        last = block_times(start_ref[0, chan, 0], start_ref[0, chan, 1], across, last_ref[o])
        both = (first_ref[o] + last) * factor
        real_q, imag_q = orthonormalize(both[:vectors], both[vectors:], chunks)
        for sweep in range(1, ITERS):
            real_z, imag_z = cov_times(real_q, imag_q, high_ref, low_ref)
            real_q, imag_q = orthonormalize_by_gram(real_z, imag_z)
        rank = flags_ref[chan] * ranks_ref[chan]
        keep = lax.broadcasted_iota(jnp.int32, (vectors, width), 0) < rank
        real_u = jnp.where(keep, real_q, 0.0)
        imag_u = jnp.where(keep, imag_q, 0.0)
        both = jnp.concatenate(split(jnp.concatenate([real_u, imag_u], axis=0)), axis=0)
        product = dot(both, weights_ref[o], NN)
        product = product[: 2 * vectors] + product[2 * vectors :]
        real_w = product[:vectors, :beams] - product[vectors:, beams:]
        imag_w = product[:vectors, beams:] + product[vectors:, :beams]
        for i, by in enumerate(steps(tm)):
            block = across_ref[o, :, i * rows : (i + 1) * rows] if i < tm - 1 else across
            series = project(real_u, imag_u, block)[0]
            series_ref[tm_index ^ shifted(-by)] = series
        steered = jnp.concatenate([real_w, imag_w], axis=0).astype(BF16)
        for x, out in enumerate(outs):
            series = series_ref[x]
            series = jnp.concatenate([series[:, : rows // 2], series[:, rows // 2 :]], axis=0)
            out[o, :, :beams] = steered
            out[o, :, beams:] = series.astype(BF16)


def nulled_power(raw, packet_ref, squares):
    rows, half = raw.shape
    samples = rows // 2
    series = packet_ref[:, 2 * half :].astype(F32)
    vectors = series.shape[0] // 2
    series = jnp.concatenate([series[:vectors], series[vectors:]], axis=1)
    left = jnp.concatenate([series, -turned(series, 1)], axis=0).astype(BF16)
    right = packet_ref[:, pl.ds(pl.multiple_of(lax.axis_index("pol") * half, half), half)]
    beam = raw - dot(left, right, TN)
    squares[...] = beam * beam
    return squares[pl.ds(0, samples, 2), :] + squares[pl.ds(1, samples, 2), :]


def power_kernel(own, xs, later_xs, mine_ref, theirs_ref, *rest):
    packets, later = rest[: len(xs)], rest[len(xs) : len(xs) + len(later_xs)]
    power_ref, squares = rest[-2:]
    for x, ref in zip(xs, packets):
        for o in range(own):
            chan = (lax.axis_index("tm") ^ x) * own + o
            power_ref[chan] = nulled_power(mine_ref[chan], ref.at[o], squares)
    for x, ref in zip(later_xs, later):
        for o in range(own):
            chan = (lax.axis_index("tm") ^ x) * own + o
            power_ref[chan] = power_ref[chan] + nulled_power(theirs_ref[chan], ref.at[o], squares)


def last_kernel(own, x, theirs_ref, packet_ref, power_ref, out_ref, powers, squares):
    powers[...] = power_ref[...]
    for o in range(own):
        chan = (lax.axis_index("tm") ^ x) * own + o
        powers[chan] = power_ref[chan] + nulled_power(theirs_ref[chan], packet_ref.at[o], squares)
    for chan in range(powers.shape[0]):
        out_ref[:, chan, :] = powers[chan]


def local(voltages, start_block, flags, ranks, phase_index):
    tm = lax.axis_size("tm")
    tm_index = lax.axis_index("tm")
    samples, chan_dev, width = voltages.shape[0], voltages.shape[2], voltages.shape[4]
    own = chan_dev // tm
    vectors = start_block.shape[3]
    beams = phase_index.shape[0]
    half = beams // 2
    rows = 2 * samples
    factor = 1.0 / (samples * tm)
    params = pltpu.CompilerParams(vmem_limit_bytes=VMEM_LIMIT)
    whole = pl.BlockSpec(memory_space=pltpu.VMEM)
    scalars = pl.BlockSpec(memory_space=pltpu.SMEM)
    unread = pl.BlockSpec(memory_space=pl.ANY)

    def cost(multiplies, moved):
        return pl.CostEstimate(flops=2 * multiplies, bytes_accessed=moved, transcendentals=0)

    by = steps(tm)
    later = pl.pallas_call(
        functools.partial(cut_kernel, own, [by[0], *by[2:]]),
        out_shape=[jax.ShapeDtypeStruct((samples, own, 2, width), BF16)] * (tm - 1),
        in_specs=[pl.BlockSpec(memory_space=pltpu.HBM)],
        out_specs=[whole] * (tm - 1),
        scratch_shapes=[pltpu.SemaphoreType.DMA((tm - 1,))],
        compiler_params=params,
    )(voltages)
    urgent = lax.dynamic_slice_in_dim(voltages[:, 0], shifted(by[1]) * own, own, 1)
    cut = [later[0], urgent, *later[1:]]
    pieces = [piece.transpose(1, 0, 2, 3).reshape(own, rows, width) for piece in cut]
    blocks = pieces[:1] + [
        lax.ppermute(piece, "tm", [(z, (z + by) % tm) for z in range(tm)])
        for by, piece in zip(steps(tm)[1:], pieces[1:])
    ]

    raw = jax.ShapeDtypeStruct((chan_dev, rows, half), F32)
    mine, other = pl.pallas_call(
        functools.partial(raw_beams_kernel, tm, own),
        out_shape=[raw] * 2,
        in_specs=[whole] * (1 + tm),
        out_specs=[whole] * 2,
        scratch_shapes=[pltpu.VMEM((beams, width), BF16)],
        compiler_params=params,
        cost_estimate=cost(4 * chan_dev * samples * width * beams, 8 * chan_dev * samples * width),
    )(phase_index, *pieces)

    own_weights = pl.pallas_call(
        functools.partial(own_weights_kernel, own, chan_dev),
        out_shape=jax.ShapeDtypeStruct((own, width, 2 * beams), BF16),
        in_specs=[whole],
        out_specs=whole,
        scratch_shapes=[pltpu.VMEM((2 * beams, width), BF16)],
        compiler_params=params,
        cost_estimate=cost(20 * own * beams * width, 8 * own * beams * width),
    )(phase_index)

    early = (tm - 1) * rows
    cov, first, across = pl.pallas_call(
        early_kernel,
        out_shape=[
            jax.ShapeDtypeStruct((own, 2, width, width), F32),
            jax.ShapeDtypeStruct((own, 2 * vectors, width), F32),
            jax.ShapeDtypeStruct((own, width, early), BF16),
        ],
        in_specs=[whole] * tm,
        out_specs=[whole] * 3,
        scratch_shapes=[pltpu.VMEM((early, width), BF16)] * 2,
        compiler_params=params,
        cost_estimate=cost(2 * own * early * width * width, 8 * own * width * width),
    )(start_block, *blocks[:-1])

    other, *packets = pl.pallas_call(
        functools.partial(subspace_kernel, tm, own, factor),
        out_shape=[raw] + [jax.ShapeDtypeStruct((own, 2 * vectors, beams + samples), BF16)] * tm,
        in_specs=[unread, whole, scalars, scalars] + [whole] * 5,
        out_specs=[unread] + [whole] * tm,
        input_output_aliases={0: 0},
        scratch_shapes=[pltpu.VMEM((2 * width, width), BF16)] * 2
        + [pltpu.VMEM((tm, vectors, rows), F32)],
        compiler_params=params,
        cost_estimate=cost(32 * own * vectors * tm * samples * width, 8 * own * width * width),
    )(other, start_block, flags, ranks, own_weights, cov, first, across, blocks[-1])

    cores = [(0, 1), (1, 0)]
    theirs = lax.ppermute(other, "pol", cores)
    order = [*range(2, tm), 1]
    arrived = list(packets)
    for x in order:
        arrived[x] = lax.ppermute(packets[x], "tm", [(z, z ^ x) for z in range(tm)])
    swapped = [lax.ppermute(packet, "pol", cores) for packet in arrived]

    shape = jax.ShapeDtypeStruct((chan_dev, samples, half), F32)
    groups = [([0, order[0]], [])] + [([x], []) for x in order[1:-1]] + [(order[-1:], [0, *order[-2::-1]])]
    power = []
    for xs, later_xs in groups:
        used = [arrived[x] for x in xs] + [swapped[x] for x in later_xs]
        power = [
            pl.pallas_call(
                functools.partial(power_kernel, own, xs, later_xs),
                out_shape=shape,
                in_specs=[whole, whole if later_xs else unread] + [whole] * (len(used) + len(power)),
                out_specs=whole,
                input_output_aliases={2 + len(used): 0} if power else {},
                scratch_shapes=[pltpu.VMEM((rows, half), F32)],
                compiler_params=params,
                cost_estimate=cost(len(used) * own * rows * 2 * vectors * half, 8 * own * rows * half),
            )(mine, theirs if later_xs else mine, *used, *power)
        ]

    return pl.pallas_call(
        functools.partial(last_kernel, own, order[-1]),
        out_shape=jax.ShapeDtypeStruct((samples, chan_dev, half), F32),
        in_specs=[whole] * 3,
        out_specs=whole,
        scratch_shapes=[pltpu.VMEM((chan_dev, samples, half), F32), pltpu.VMEM((rows, half), F32)],
        compiler_params=params,
        cost_estimate=cost(chan_dev * samples * half, 12 * chan_dev * samples * half),
    )(theirs, swapped[order[-1]], *power)


def solution(mesh):
    placed = (
        P(("groups", "tm"), "pol", "chan", None, None),
        P("pol", "chan", None, None, None),
        P(("groups", "chan")),
        P(("groups", "chan")),
        P(),
    )
    return jax.shard_map(
        local,
        mesh=mesh,
        in_specs=placed,
        out_specs=P(("groups", "tm"), "chan", "pol"),
        check_vma=False,
    )
```

```python
import functools

import jax
import jax.numpy as jnp
from jax import lax
from jax.experimental import pallas as pl
from jax.experimental.pallas import tpu as pltpu
from jax.sharding import PartitionSpec as P

ITERS = 4
PHASES = 1024
QUARTER = PHASES // 4
EPS = 1e-06
F32 = jnp.float32
BF16 = jnp.bfloat16
NT = (((1,), (1,)), ((), ()))
NN = (((1,), (0,)), ((), ()))
TN = (((0,), (0,)), ((), ()))
VMEM_LIMIT = 48 * 1024 * 1024
FIRST_GRANT = 63 * 1024 * 1024
CHUNK = 128


def dot(left, right, dims):
    return lax.dot_general(left, right, dims, preferred_element_type=F32)


def split(values):
    high = values.astype(BF16)
    low = (values - high.astype(F32)).astype(BF16)
    return high, low


def steer(phase, step, norm):
    turn = (phase * step) & (PHASES - 1)
    quadrant = (turn + QUARTER // 2) // QUARTER
    angle = (turn - quadrant * QUARTER).astype(F32) * (2.0 * jnp.pi / PHASES)
    sq = angle * angle
    sine = angle * (1.0 + sq * (-1.0 / 6 + sq * (1.0 / 120 + sq * (-1.0 / 5040 + sq / 362880))))
    cosine = 1.0 + sq * (-0.5 + sq * (1.0 / 24 + sq * (-1.0 / 720 + sq / 40320)))
    odd = (quadrant & 1) == 1
    real = jnp.where(odd, sine, cosine) * norm
    imag = jnp.where(odd, cosine, sine) * norm
    real = jnp.where(((quadrant + 1) & 2) == 2, -real, real)
    imag = jnp.where((quadrant & 2) == 2, -imag, imag)
    return real.astype(BF16), imag.astype(BF16)


def fill_weights(phase_ref, first, rows, step, out):
    norm = 1.0 / (phase_ref.shape[1] ** 0.5)
    chunk = 32

    def body(i, carry):
        at = pl.multiple_of(i * chunk, chunk)
        real, imag = steer(phase_ref[pl.ds(first + at, chunk), :], step, norm)
        out[pl.ds(at, chunk), :] = real
        out[pl.ds(rows + at, chunk), :] = imag
        return carry

    lax.fori_loop(0, rows // chunk, body, 0)


def steps(tm):
    return [0, *[by for by in range(1, tm) if by != tm // 2], tm // 2]


def shifted(by):
    tm = lax.axis_size("tm")
    return lax.rem(lax.axis_index("tm") + tm + by, tm)


def first_cut_kernel(own, voltages_ref, piece_ref, done):
    channels = pl.ds(shifted(steps(lax.axis_size("tm"))[1]) * own, own)
    copy = pltpu.make_async_copy(voltages_ref.at[:, 0, channels], piece_ref, done)
    copy.start()
    copy.wait()


def cut_kernel(own, bys, voltages_ref, *rest):
    pieces, done = rest[:-1], rest[-1]
    copies = []
    for i, (by, piece) in enumerate(zip(bys, pieces)):
        channels = pl.ds(shifted(by) * own, own)
        copy = pltpu.make_async_copy(voltages_ref.at[:, 0, channels], piece, done.at[i])
        copy.start()
        copies.append(copy)
    for copy in copies:
        copy.wait()


def turned(values, axis):
    size = values.shape[axis]
    at = lax.broadcasted_iota(jnp.int32, values.shape, axis)
    after = pltpu.roll(values, size - 1, axis)
    before = pltpu.roll(values, 1, axis)
    return jnp.where((at & 1) == 0, after, -before)


def raw_beams_kernel(tm, own, phase_ref, *rest):
    pieces, (mine_ref, other_ref, weights) = rest[:tm], rest[tm:]
    half = phase_ref.shape[0] // 2
    rows = pieces[0].shape[1]
    pol = lax.axis_index("pol")
    start = lax.axis_index("chan") * tm * own
    for by, piece in zip(steps(tm), pieces):
        for o in range(own):
            chan = shifted(by) * own + o
            for swap, out_ref in enumerate((mine_ref, other_ref)):
                first = pl.multiple_of((pol ^ swap) * half, half)
                fill_weights(phase_ref, first, half, start + chan + 1, weights)
                product = dot(piece[o], weights[...], NT)
                by_imag = turned(product[:, half:].reshape(rows // 8, 8, half), 1).reshape(rows, half)
                out_ref[chan] = product[:, :half] - by_imag


def own_weights_kernel(own, chan_dev, phase_ref, out_ref, weights):
    beams = phase_ref.shape[0]
    first = lax.axis_index("chan") * chan_dev + lax.axis_index("tm") * own
    for o in range(own):
        fill_weights(phase_ref, 0, beams, first + o + 1, weights)
        out_ref[o] = weights[...].T


def rotate(x):
    return (-turned(x.astype(F32), 0)).astype(BF16)


def early_kernel(start_ref, *refs):
    blocks, (cov_ref, first_ref, across_ref, along_ref, rotated_ref) = refs[:-5], refs[-5:]
    rows, width = blocks[0].shape[1:]
    own = cov_ref.shape[0]
    for o in range(own):
        for i, block in enumerate(blocks):
            x = block[o]
            at = slice(i * rows, (i + 1) * rows)
            along_ref[at] = x
            rotated_ref[at] = rotate(x)
            across_ref[o, :, at] = x.T
        cov_ref[o, 0] = dot(across_ref[o], along_ref[...], NN)
        cov_ref[o, 1] = dot(across_ref[o], rotated_ref[...], NN)
        chan = lax.axis_index("tm") * own + o
        first_ref[o] = block_times(start_ref[0, chan, 0], start_ref[0, chan, 1], across_ref[o], along_ref[...])


def project(real, imag, across):
    vectors = real.shape[0]
    both = jnp.concatenate(split(jnp.concatenate([real, imag], axis=0)), axis=0)
    product = dot(both, across, NN)
    product = product[: 2 * vectors] + product[2 * vectors :]
    other = turned(product, 1)
    return product[:vectors] + other[vectors:], product[vectors:] - other[:vectors]


def block_times(real, imag, across, along):
    pair = jnp.concatenate(project(real, imag, across), axis=0)
    product = dot(jnp.concatenate(split(pair), axis=0), along, NN)
    return product[: pair.shape[0]] + product[pair.shape[0] :]


def cov_times(real, imag, high_ref, low_ref):
    vectors = real.shape[0]
    rows = jnp.concatenate(
        [jnp.concatenate([real, imag], axis=1), jnp.concatenate([imag, -real], axis=1)], axis=0
    )
    high, low = split(rows)
    product = dot(jnp.concatenate([high, low], axis=0), high_ref[...], NN)
    product = product[: 2 * vectors] + product[2 * vectors :] + dot(high, low_ref[...], NN)
    return product[:vectors], product[vectors:]


def orthonormalize(real_z, imag_z, beside=()):
    beside = list(beside)
    vectors, width = real_z.shape
    row = lax.broadcasted_iota(jnp.int32, (vectors, 1), 0)
    real_v, imag_v = real_z, imag_z
    scale = jnp.zeros((vectors, 1), F32)
    for n in range(vectors):
        real_a = jnp.broadcast_to(real_v[n : n + 1], real_z.shape)
        imag_a = jnp.broadcast_to(imag_v[n : n + 1], real_z.shape)
        norm = jnp.sum(real_a * real_a + imag_a * imag_a, axis=1, keepdims=True) + EPS
        scale = jnp.where(row == n, norm, scale)
        if n + 1 < vectors:
            real_d = jnp.sum(real_a * real_z + imag_a * imag_z, axis=1, keepdims=True)
            imag_d = jnp.sum(real_a * imag_z - imag_a * real_z, axis=1, keepdims=True)
            inverse = jnp.where(row > n, 1.0 / norm, 0.0)
            real_c = real_d * inverse
            imag_c = imag_d * inverse
            real_v = real_v - (real_c * real_a - imag_c * imag_a)
            imag_v = imag_v - (real_c * imag_a + imag_c * real_a)
        for work in beside[n::vectors]:
            work()
    factor = 1.0 / jnp.sqrt(scale)
    return real_v * factor, imag_v * factor


def orthonormalize_by_gram(real_z, imag_z):
    vectors = real_z.shape[0]
    row = lax.broadcasted_iota(jnp.int32, (vectors, 1), 0)
    by_z = []
    for n in range(vectors):
        real_a = jnp.broadcast_to(real_z[n : n + 1], real_z.shape)
        imag_a = jnp.broadcast_to(imag_z[n : n + 1], real_z.shape)
        by_z.append(
            (
                jnp.sum(real_a * real_z + imag_a * imag_z, axis=1, keepdims=True),
                jnp.sum(real_a * imag_z - imag_a * real_z, axis=1, keepdims=True),
            )
        )
    by_v = list(by_z)
    real_v, imag_v = real_z, imag_z
    for n in range(vectors - 1):
        (real_d, imag_d), (real_p, imag_p) = by_z[n], by_v[n]
        square = jnp.maximum(real_p[n : n + 1], 0.0)
        inverse = jnp.where(row > n, 1.0 / (square + EPS), 0.0)
        real_c, imag_c = real_d * inverse, imag_d * inverse
        real_b, imag_b = real_p - real_c * square, imag_p - imag_c * square
        for j in range(n + 1, vectors):
            real_s, imag_s = real_c[j : j + 1], imag_c[j : j + 1]
            real_q, imag_q = real_p[j : j + 1], -imag_p[j : j + 1]
            real, imag = by_v[j]
            by_v[j] = (
                real - (real_c * real_q - imag_c * imag_q) - (real_s * real_b + imag_s * imag_b),
                imag - (real_c * imag_q + imag_c * real_q) - (real_s * imag_b - imag_s * real_b),
            )
            real, imag = by_z[j]
            by_z[j] = (
                real - (real_s * real_d + imag_s * imag_d),
                imag - (real_s * imag_d - imag_s * real_d),
            )
        real_a, imag_a = real_v[n : n + 1], imag_v[n : n + 1]
        real_v = real_v - (real_c * real_a - imag_c * imag_a)
        imag_v = imag_v - (real_c * imag_a + imag_c * real_a)
    factor = 1.0 / jnp.sqrt(jnp.sum(real_v * real_v + imag_v * imag_v, axis=1, keepdims=True) + EPS)
    return real_v * factor, imag_v * factor


def subspace_kernel(
    tm, own, factor, beams_ref, start_ref, flags_ref, ranks_ref, weights_ref, cov_ref, first_ref, across_ref, last_ref, *rest
):
    outs, (high_ref, low_ref, series_ref) = rest[1 : tm + 1], rest[tm + 1 :]
    vectors, width = start_ref.shape[3], start_ref.shape[4]
    rows = last_ref.shape[1]
    tm_index = lax.axis_index("tm")
    beams = weights_ref.shape[2] // 2
    for o in range(own):
        chan = tm_index * own + o
        across = last_ref[o].T
        rotated = rotate(last_ref[o])

        def add_last(part, first):
            right = last_ref[o] if part == 0 else rotated
            term = dot(across[first : first + CHUNK], right, NN)
            at = slice(part * width + first, part * width + first + CHUNK)
            high_ref[at], low_ref[at] = split((cov_ref[o, part, first : first + CHUNK] + term) * factor)

        chunks = [
            functools.partial(add_last, part, first) for part in range(2) for first in range(0, width, CHUNK)
        ]
        last = block_times(start_ref[0, chan, 0], start_ref[0, chan, 1], across, last_ref[o])
        both = (first_ref[o] + last) * factor
        real_q, imag_q = orthonormalize(both[:vectors], both[vectors:], chunks)
        for sweep in range(1, ITERS):
            real_z, imag_z = cov_times(real_q, imag_q, high_ref, low_ref)
            real_q, imag_q = orthonormalize_by_gram(real_z, imag_z)
        rank = flags_ref[chan] * ranks_ref[chan]
        keep = lax.broadcasted_iota(jnp.int32, (vectors, width), 0) < rank
        real_u = jnp.where(keep, real_q, 0.0)
        imag_u = jnp.where(keep, imag_q, 0.0)
        both = jnp.concatenate(split(jnp.concatenate([real_u, imag_u], axis=0)), axis=0)
        product = dot(both, weights_ref[o], NN)
        product = product[: 2 * vectors] + product[2 * vectors :]
        real_w = product[:vectors, :beams] - product[vectors:, beams:]
        imag_w = product[:vectors, beams:] + product[vectors:, :beams]
        early = project(real_u, imag_u, across_ref[o])[0]
        series = [early[:, i * rows : (i + 1) * rows] for i in range(tm - 1)]
        series.append(project(real_u, imag_u, across)[0])
        for by, values in zip(steps(tm), series):
            series_ref[tm_index ^ shifted(-by)] = values
        steered = jnp.concatenate([real_w, imag_w], axis=0).astype(BF16)
        for x, out in enumerate(outs):
            series = series_ref[x]
            series = jnp.concatenate([series[:, : rows // 2], series[:, rows // 2 :]], axis=0)
            out[o, :, :beams] = steered
            out[o, :, beams:] = series.astype(BF16)


def nulled_power(raw, packet_ref, squares):
    rows, half = raw.shape
    samples = rows // 2
    series = packet_ref[:, 2 * half :].astype(F32)
    vectors = series.shape[0] // 2
    series = jnp.concatenate([series[:vectors], series[vectors:]], axis=1)
    left = jnp.concatenate([series, -turned(series, 1)], axis=0).astype(BF16)
    right = packet_ref[:, pl.ds(pl.multiple_of(lax.axis_index("pol") * half, half), half)]
    beam = raw - dot(left, right, TN)
    squares[...] = beam * beam
    return squares[pl.ds(0, samples, 2), :] + squares[pl.ds(1, samples, 2), :]


def power_kernel(own, xs, later_xs, mine_ref, theirs_ref, *rest):
    packets, later = rest[: len(xs)], rest[len(xs) : len(xs) + len(later_xs)]
    power_ref, squares = rest[-2:]
    for x, ref in zip(xs, packets):
        for o in range(own):
            chan = (lax.axis_index("tm") ^ x) * own + o
            power_ref[chan] = nulled_power(mine_ref[chan], ref.at[o], squares)
    for x, ref in zip(later_xs, later):
        for o in range(own):
            chan = (lax.axis_index("tm") ^ x) * own + o
            power_ref[chan] = power_ref[chan] + nulled_power(theirs_ref[chan], ref.at[o], squares)


def last_kernel(own, x, theirs_ref, packet_ref, power_ref, out_ref, powers, squares):
    powers[...] = power_ref[...]
    for o in range(own):
        chan = (lax.axis_index("tm") ^ x) * own + o
        powers[chan] = power_ref[chan] + nulled_power(theirs_ref[chan], packet_ref.at[o], squares)
    for chan in range(powers.shape[0]):
        out_ref[:, chan, :] = powers[chan]


def local(voltages, start_block, flags, ranks, phase_index):
    tm = lax.axis_size("tm")
    tm_index = lax.axis_index("tm")
    samples, chan_dev, width = voltages.shape[0], voltages.shape[2], voltages.shape[4]
    own = chan_dev // tm
    vectors = start_block.shape[3]
    beams = phase_index.shape[0]
    half = beams // 2
    rows = 2 * samples
    factor = 1.0 / (samples * tm)
    params = pltpu.CompilerParams(vmem_limit_bytes=VMEM_LIMIT)
    whole = pl.BlockSpec(memory_space=pltpu.VMEM)
    scalars = pl.BlockSpec(memory_space=pltpu.SMEM)
    unread = pl.BlockSpec(memory_space=pl.ANY)

    def cost(multiplies, moved):
        return pl.CostEstimate(flops=2 * multiplies, bytes_accessed=moved, transcendentals=0)

    by = steps(tm)
    later = pl.pallas_call(
        functools.partial(cut_kernel, own, [by[0], *by[2:]]),
        out_shape=[jax.ShapeDtypeStruct((samples, own, 2, width), BF16)] * (tm - 1),
        in_specs=[pl.BlockSpec(memory_space=pltpu.HBM)],
        out_specs=[whole] * (tm - 1),
        scratch_shapes=[pltpu.SemaphoreType.DMA((tm - 1,))],
        compiler_params=params,
    )(voltages)
    urgent = pl.pallas_call(
        functools.partial(first_cut_kernel, own),
        out_shape=jax.ShapeDtypeStruct((samples, own, 2, width), BF16),
        in_specs=[pl.BlockSpec(memory_space=pltpu.HBM)],
        out_specs=pl.BlockSpec(memory_space=pltpu.HBM),
        scratch_shapes=[pltpu.SemaphoreType.DMA],
        compiler_params=pltpu.CompilerParams(vmem_limit_bytes=FIRST_GRANT),
    )(voltages)

    def by_channel(piece):
        return piece.transpose(1, 0, 2, 3).reshape(own, rows, width)

    def send(piece, by):
        return lax.ppermute(piece, "tm", [(z, (z + by) % tm) for z in range(tm)])

    arrived = send(urgent, by[1])
    home, *later = [by_channel(piece) for piece in later]
    blocks = [home, None, *[send(piece, step) for piece, step in zip(later, by[2:])]]
    blocks[1] = by_channel(arrived)
    pieces = [home, by_channel(urgent), *later]

    raw = jax.ShapeDtypeStruct((chan_dev, rows, half), F32)
    mine, other = pl.pallas_call(
        functools.partial(raw_beams_kernel, tm, own),
        out_shape=[raw] * 2,
        in_specs=[whole] * (1 + tm),
        out_specs=[whole] * 2,
        scratch_shapes=[pltpu.VMEM((beams, width), BF16)],
        compiler_params=params,
        cost_estimate=cost(4 * chan_dev * samples * width * beams, 8 * chan_dev * samples * width),
    )(phase_index, *pieces)

    own_weights = pl.pallas_call(
        functools.partial(own_weights_kernel, own, chan_dev),
        out_shape=jax.ShapeDtypeStruct((own, width, 2 * beams), BF16),
        in_specs=[whole],
        out_specs=whole,
        scratch_shapes=[pltpu.VMEM((2 * beams, width), BF16)],
        compiler_params=params,
        cost_estimate=cost(20 * own * beams * width, 8 * own * beams * width),
    )(phase_index)

    early = (tm - 1) * rows
    cov, first, across = pl.pallas_call(
        early_kernel,
        out_shape=[
            jax.ShapeDtypeStruct((own, 2, width, width), F32),
            jax.ShapeDtypeStruct((own, 2 * vectors, width), F32),
            jax.ShapeDtypeStruct((own, width, early), BF16),
        ],
        in_specs=[whole] * tm,
        out_specs=[whole] * 3,
        scratch_shapes=[pltpu.VMEM((early, width), BF16)] * 2,
        compiler_params=params,
        cost_estimate=cost(2 * own * early * width * width, 8 * own * width * width),
    )(start_block, *blocks[:-1])

    other, *packets = pl.pallas_call(
        functools.partial(subspace_kernel, tm, own, factor),
        out_shape=[raw] + [jax.ShapeDtypeStruct((own, 2 * vectors, beams + samples), BF16)] * tm,
        in_specs=[unread, whole, scalars, scalars] + [whole] * 5,
        out_specs=[unread] + [whole] * tm,
        input_output_aliases={0: 0},
        scratch_shapes=[pltpu.VMEM((2 * width, width), BF16)] * 2
        + [pltpu.VMEM((tm, vectors, rows), F32)],
        compiler_params=params,
        cost_estimate=cost(32 * own * vectors * tm * samples * width, 8 * own * width * width),
    )(other, start_block, flags, ranks, own_weights, cov, first, across, blocks[-1])

    cores = [(0, 1), (1, 0)]
    theirs = lax.ppermute(other, "pol", cores)
    order = [*range(2, tm), 1]
    arrived = list(packets)
    for x in order:
        arrived[x] = lax.ppermute(packets[x], "tm", [(z, z ^ x) for z in range(tm)])
    swapped = [lax.ppermute(packet, "pol", cores) for packet in arrived]

    shape = jax.ShapeDtypeStruct((chan_dev, samples, half), F32)
    groups = [([0, order[0]], [])] + [([x], []) for x in order[1:-1]] + [(order[-1:], [0, *order[-2::-1]])]
    power = []
    for xs, later_xs in groups:
        used = [arrived[x] for x in xs] + [swapped[x] for x in later_xs]
        power = [
            pl.pallas_call(
                functools.partial(power_kernel, own, xs, later_xs),
                out_shape=shape,
                in_specs=[whole, whole if later_xs else unread] + [whole] * (len(used) + len(power)),
                out_specs=whole,
                input_output_aliases={2 + len(used): 0} if power else {},
                scratch_shapes=[pltpu.VMEM((rows, half), F32)],
                compiler_params=params,
                cost_estimate=cost(10**10 if later_xs else 10**6, 8 * own * rows * half),
            )(mine, theirs if later_xs else mine, *used, *power)
        ]

    return pl.pallas_call(
        functools.partial(last_kernel, own, order[-1]),
        out_shape=jax.ShapeDtypeStruct((samples, chan_dev, half), F32),
        in_specs=[whole] * 3,
        out_specs=whole,
        scratch_shapes=[pltpu.VMEM((chan_dev, samples, half), F32), pltpu.VMEM((rows, half), F32)],
        compiler_params=params,
        cost_estimate=cost(chan_dev * samples * half, 12 * chan_dev * samples * half),
    )(theirs, swapped[order[-1]], *power)


def solution(mesh):
    placed = (
        P(("groups", "tm"), "pol", "chan", None, None),
        P("pol", "chan", None, None, None),
        P(("groups", "chan")),
        P(("groups", "chan")),
        P(),
    )
    return jax.shard_map(
        local,
        mesh=mesh,
        in_specs=placed,
        out_specs=P(("groups", "tm"), "chan", "pol"),
        check_vma=False,
    )
```

```python
import functools

import jax
import jax.numpy as jnp
from jax import lax
from jax.experimental import pallas as pl
from jax.experimental.pallas import tpu as pltpu
from jax.sharding import PartitionSpec as P

ITERS = 4
PHASES = 1024
QUARTER = PHASES // 4
EPS = 1e-06
F32 = jnp.float32
BF16 = jnp.bfloat16
NT = (((1,), (1,)), ((), ()))
NN = (((1,), (0,)), ((), ()))
TN = (((0,), (0,)), ((), ()))
VMEM_LIMIT = 48 * 1024 * 1024
CHUNK = 128


def dot(left, right, dims):
    return lax.dot_general(left, right, dims, preferred_element_type=F32)


def split(values):
    high = values.astype(BF16)
    low = (values - high.astype(F32)).astype(BF16)
    return high, low


def steer(phase, step, norm):
    turn = (phase * step) & (PHASES - 1)
    quadrant = (turn + QUARTER // 2) // QUARTER
    angle = (turn - quadrant * QUARTER).astype(F32) * (2.0 * jnp.pi / PHASES)
    sq = angle * angle
    sine = angle * (1.0 + sq * (-1.0 / 6 + sq * (1.0 / 120 + sq * (-1.0 / 5040 + sq / 362880))))
    cosine = 1.0 + sq * (-0.5 + sq * (1.0 / 24 + sq * (-1.0 / 720 + sq / 40320)))
    odd = (quadrant & 1) == 1
    real = jnp.where(odd, sine, cosine) * norm
    imag = jnp.where(odd, cosine, sine) * norm
    real = jnp.where(((quadrant + 1) & 2) == 2, -real, real)
    imag = jnp.where((quadrant & 2) == 2, -imag, imag)
    return real.astype(BF16), imag.astype(BF16)


def fill_weights(phase_ref, first, rows, step, out):
    norm = 1.0 / (phase_ref.shape[1] ** 0.5)
    chunk = 32

    def body(i, carry):
        at = pl.multiple_of(i * chunk, chunk)
        real, imag = steer(phase_ref[pl.ds(first + at, chunk), :], step, norm)
        out[pl.ds(at, chunk), :] = real
        out[pl.ds(rows + at, chunk), :] = imag
        return carry

    lax.fori_loop(0, rows // chunk, body, 0)


def steps(tm):
    return [0, *[by for by in range(1, tm) if by != tm // 2], tm // 2]


def shifted(by):
    tm = lax.axis_size("tm")
    return lax.rem(lax.axis_index("tm") + tm + by, tm)


def cut_kernel(own, bys, voltages_ref, *rest):
    pieces, done = rest[:-1], rest[-1]
    copies = []
    for i, (by, piece) in enumerate(zip(bys, pieces)):
        channels = pl.ds(shifted(by) * own, own)
        copy = pltpu.make_async_copy(voltages_ref.at[:, 0, channels], piece, done.at[i])
        copy.start()
        copies.append(copy)
    for copy in copies:
        copy.wait()


def turned(values, axis):
    size = values.shape[axis]
    at = lax.broadcasted_iota(jnp.int32, values.shape, axis)
    after = pltpu.roll(values, size - 1, axis)
    before = pltpu.roll(values, 1, axis)
    return jnp.where((at & 1) == 0, after, -before)


def raw_beams_kernel(tm, own, phase_ref, *rest):
    pieces, (mine_ref, other_ref, weights) = rest[:tm], rest[tm:]
    half = phase_ref.shape[0] // 2
    rows = pieces[0].shape[1]
    pol = lax.axis_index("pol")
    start = lax.axis_index("chan") * tm * own
    for by, piece in zip(steps(tm), pieces):
        for o in range(own):
            chan = shifted(by) * own + o
            for swap, out_ref in enumerate((mine_ref, other_ref)):
                first = pl.multiple_of((pol ^ swap) * half, half)
                fill_weights(phase_ref, first, half, start + chan + 1, weights)
                product = dot(piece[o], weights[...], NT)
                by_imag = turned(product[:, half:].reshape(rows // 8, 8, half), 1).reshape(rows, half)
                out_ref[chan] = product[:, :half] - by_imag


def own_weights_kernel(own, chan_dev, phase_ref, out_ref, weights):
    beams = phase_ref.shape[0]
    first = lax.axis_index("chan") * chan_dev + lax.axis_index("tm") * own
    for o in range(own):
        fill_weights(phase_ref, 0, beams, first + o + 1, weights)
        out_ref[o] = weights[...].T


def rotate(x):
    return (-turned(x.astype(F32), 0)).astype(BF16)


def early_kernel(start_ref, *refs):
    blocks, (cov_ref, first_ref, across_ref, along_ref, rotated_ref) = refs[:-5], refs[-5:]
    rows, width = blocks[0].shape[1:]
    own = cov_ref.shape[0]
    for o in range(own):
        for i, block in enumerate(blocks):
            x = block[o]
            at = slice(i * rows, (i + 1) * rows)
            along_ref[at] = x
            rotated_ref[at] = rotate(x)
            across_ref[o, :, at] = x.T
        cov_ref[o, 0] = dot(across_ref[o], along_ref[...], NN)
        cov_ref[o, 1] = dot(across_ref[o], rotated_ref[...], NN)
        chan = lax.axis_index("tm") * own + o
        first_ref[o] = block_times(start_ref[0, chan, 0], start_ref[0, chan, 1], across_ref[o], along_ref[...])


def project(real, imag, across):
    vectors = real.shape[0]
    both = jnp.concatenate(split(jnp.concatenate([real, imag], axis=0)), axis=0)
    product = dot(both, across, NN)
    product = product[: 2 * vectors] + product[2 * vectors :]
    other = turned(product, 1)
    return product[:vectors] + other[vectors:], product[vectors:] - other[:vectors]


def block_times(real, imag, across, along):
    pair = jnp.concatenate(project(real, imag, across), axis=0)
    product = dot(jnp.concatenate(split(pair), axis=0), along, NN)
    return product[: pair.shape[0]] + product[pair.shape[0] :]


def cov_times(real, imag, high_ref, low_ref):
    vectors = real.shape[0]
    rows = jnp.concatenate(
        [jnp.concatenate([real, imag], axis=1), jnp.concatenate([imag, -real], axis=1)], axis=0
    )
    high, low = split(rows)
    product = dot(jnp.concatenate([high, low], axis=0), high_ref[...], NN)
    product = product[: 2 * vectors] + product[2 * vectors :] + dot(high, low_ref[...], NN)
    return product[:vectors], product[vectors:]


def orthonormalize(real_z, imag_z, beside=()):
    beside = list(beside)
    vectors, width = real_z.shape
    row = lax.broadcasted_iota(jnp.int32, (vectors, 1), 0)
    real_v, imag_v = real_z, imag_z
    scale = jnp.zeros((vectors, 1), F32)
    for n in range(vectors):
        real_a = jnp.broadcast_to(real_v[n : n + 1], real_z.shape)
        imag_a = jnp.broadcast_to(imag_v[n : n + 1], real_z.shape)
        norm = jnp.sum(real_a * real_a + imag_a * imag_a, axis=1, keepdims=True) + EPS
        scale = jnp.where(row == n, norm, scale)
        if n + 1 < vectors:
            real_d = jnp.sum(real_a * real_z + imag_a * imag_z, axis=1, keepdims=True)
            imag_d = jnp.sum(real_a * imag_z - imag_a * real_z, axis=1, keepdims=True)
            inverse = jnp.where(row > n, 1.0 / norm, 0.0)
            real_c = real_d * inverse
            imag_c = imag_d * inverse
            real_v = real_v - (real_c * real_a - imag_c * imag_a)
            imag_v = imag_v - (real_c * imag_a + imag_c * real_a)
        for work in beside[n::vectors]:
            work()
    factor = 1.0 / jnp.sqrt(scale)
    return real_v * factor, imag_v * factor


def orthonormalize_by_gram(real_z, imag_z, riders=()):
    vectors = real_z.shape[0]
    row = lax.broadcasted_iota(jnp.int32, (vectors, 1), 0)
    by_z = []
    for n in range(vectors):
        real_a = jnp.broadcast_to(real_z[n : n + 1], real_z.shape)
        imag_a = jnp.broadcast_to(imag_z[n : n + 1], real_z.shape)
        by_z.append(
            (
                jnp.sum(real_a * real_z + imag_a * imag_z, axis=1, keepdims=True),
                jnp.sum(real_a * imag_z - imag_a * real_z, axis=1, keepdims=True),
            )
        )
    by_v = list(by_z)
    pairs = [(real_z, imag_z), *riders]
    for n in range(vectors - 1):
        (real_d, imag_d), (real_p, imag_p) = by_z[n], by_v[n]
        square = jnp.maximum(real_p[n : n + 1], 0.0)
        inverse = jnp.where(row > n, 1.0 / (square + EPS), 0.0)
        real_c, imag_c = real_d * inverse, imag_d * inverse
        real_b, imag_b = real_p - real_c * square, imag_p - imag_c * square
        for j in range(n + 1, vectors):
            real_s, imag_s = real_c[j : j + 1], imag_c[j : j + 1]
            real_q, imag_q = real_p[j : j + 1], -imag_p[j : j + 1]
            real, imag = by_v[j]
            by_v[j] = (
                real - (real_c * real_q - imag_c * imag_q) - (real_s * real_b + imag_s * imag_b),
                imag - (real_c * imag_q + imag_c * real_q) - (real_s * imag_b - imag_s * real_b),
            )
            real, imag = by_z[j]
            by_z[j] = (
                real - (real_s * real_d + imag_s * imag_d),
                imag - (real_s * imag_d - imag_s * real_d),
            )
        pairs = [
            (
                real - (real_c * real[n : n + 1] - imag_c * imag[n : n + 1]),
                imag - (real_c * imag[n : n + 1] + imag_c * real[n : n + 1]),
            )
            for real, imag in pairs
        ]
    real_v, imag_v = pairs[0]
    factor = 1.0 / jnp.sqrt(jnp.sum(real_v * real_v + imag_v * imag_v, axis=1, keepdims=True) + EPS)
    return [(real * factor, imag * factor) for real, imag in pairs]


def subspace_kernel(
    tm, own, factor, beams_ref, start_ref, flags_ref, ranks_ref, weights_ref, cov_ref, first_ref, across_ref, last_ref, *rest
):
    outs, (high_ref, low_ref, series_ref) = rest[1 : tm + 1], rest[tm + 1 :]
    vectors, width = start_ref.shape[3], start_ref.shape[4]
    rows = last_ref.shape[1]
    tm_index = lax.axis_index("tm")
    beams = weights_ref.shape[2] // 2
    for o in range(own):
        chan = tm_index * own + o
        across = last_ref[o].T
        rotated = rotate(last_ref[o])

        def add_last(part, first):
            right = last_ref[o] if part == 0 else rotated
            term = dot(across[first : first + CHUNK], right, NN)
            at = slice(part * width + first, part * width + first + CHUNK)
            high_ref[at], low_ref[at] = split((cov_ref[o, part, first : first + CHUNK] + term) * factor)

        chunks = [
            functools.partial(add_last, part, first) for part in range(2) for first in range(0, width, CHUNK)
        ]
        last = block_times(start_ref[0, chan, 0], start_ref[0, chan, 1], across, last_ref[o])
        both = (first_ref[o] + last) * factor
        real_q, imag_q = orthonormalize(both[:vectors], both[vectors:], chunks)
        for sweep in range(1, ITERS - 1):
            real_z, imag_z = cov_times(real_q, imag_q, high_ref, low_ref)
            ((real_q, imag_q),) = orthonormalize_by_gram(real_z, imag_z)
        real_z, imag_z = cov_times(real_q, imag_q, high_ref, low_ref)
        both = jnp.concatenate(split(jnp.concatenate([real_z, imag_z], axis=0)), axis=0)
        product = dot(both, weights_ref[o], NN)
        product = product[: 2 * vectors] + product[2 * vectors :]
        real_w = product[:vectors, :beams] - product[vectors:, beams:]
        imag_w = product[:vectors, beams:] + product[vectors:, :beams]
        riders = [
            (real_w, imag_w),
            project(real_z, imag_z, across_ref[o]),
            project(real_z, imag_z, across),
        ]
        unused, (real_w, imag_w), (early, unused), (late, unused) = orthonormalize_by_gram(real_z, imag_z, riders)
        rank = flags_ref[chan] * ranks_ref[chan]
        keep = lax.broadcasted_iota(jnp.int32, (vectors, 1), 0) < rank
        real_w = jnp.where(keep, real_w, 0.0)
        imag_w = jnp.where(keep, imag_w, 0.0)
        series = [early[:, i * rows : (i + 1) * rows] for i in range(tm - 1)] + [late]
        for by, values in zip(steps(tm), series):
            series_ref[tm_index ^ shifted(-by)] = jnp.where(keep, values, 0.0)
        steered = jnp.concatenate([real_w, imag_w], axis=0).astype(BF16)
        for x, out in enumerate(outs):
            series = series_ref[x]
            series = jnp.concatenate([series[:, : rows // 2], series[:, rows // 2 :]], axis=0)
            out[o, :, :beams] = steered
            out[o, :, beams:] = series.astype(BF16)


def nulled_power(raw, packet_ref, squares):
    rows, half = raw.shape
    samples = rows // 2
    series = packet_ref[:, 2 * half :].astype(F32)
    vectors = series.shape[0] // 2
    series = jnp.concatenate([series[:vectors], series[vectors:]], axis=1)
    left = jnp.concatenate([series, -turned(series, 1)], axis=0).astype(BF16)
    right = packet_ref[:, pl.ds(pl.multiple_of(lax.axis_index("pol") * half, half), half)]
    beam = raw - dot(left, right, TN)
    squares[...] = beam * beam
    return squares[pl.ds(0, samples, 2), :] + squares[pl.ds(1, samples, 2), :]


def power_kernel(own, xs, later_xs, mine_ref, theirs_ref, *rest):
    packets, later = rest[: len(xs)], rest[len(xs) : len(xs) + len(later_xs)]
    power_ref, squares = rest[-2:]
    for x, ref in zip(xs, packets):
        for o in range(own):
            chan = (lax.axis_index("tm") ^ x) * own + o
            power_ref[chan] = nulled_power(mine_ref[chan], ref.at[o], squares)
    for x, ref in zip(later_xs, later):
        for o in range(own):
            chan = (lax.axis_index("tm") ^ x) * own + o
            power_ref[chan] = power_ref[chan] + nulled_power(theirs_ref[chan], ref.at[o], squares)


def last_kernel(own, x, theirs_ref, packet_ref, power_ref, out_ref, powers, squares):
    powers[...] = power_ref[...]
    for o in range(own):
        chan = (lax.axis_index("tm") ^ x) * own + o
        powers[chan] = power_ref[chan] + nulled_power(theirs_ref[chan], packet_ref.at[o], squares)
    for chan in range(powers.shape[0]):
        out_ref[:, chan, :] = powers[chan]


def local(voltages, start_block, flags, ranks, phase_index):
    tm = lax.axis_size("tm")
    tm_index = lax.axis_index("tm")
    samples, chan_dev, width = voltages.shape[0], voltages.shape[2], voltages.shape[4]
    own = chan_dev // tm
    vectors = start_block.shape[3]
    beams = phase_index.shape[0]
    half = beams // 2
    rows = 2 * samples
    factor = 1.0 / (samples * tm)
    params = pltpu.CompilerParams(vmem_limit_bytes=VMEM_LIMIT)
    whole = pl.BlockSpec(memory_space=pltpu.VMEM)
    scalars = pl.BlockSpec(memory_space=pltpu.SMEM)
    unread = pl.BlockSpec(memory_space=pl.ANY)

    def cost(multiplies, moved):
        return pl.CostEstimate(flops=2 * multiplies, bytes_accessed=moved, transcendentals=0)

    by = steps(tm)
    later = pl.pallas_call(
        functools.partial(cut_kernel, own, [by[0], *by[2:]]),
        out_shape=[jax.ShapeDtypeStruct((samples, own, 2, width), BF16)] * (tm - 1),
        in_specs=[pl.BlockSpec(memory_space=pltpu.HBM)],
        out_specs=[whole] * (tm - 1),
        scratch_shapes=[pltpu.SemaphoreType.DMA((tm - 1,))],
        compiler_params=params,
    )(voltages)
    urgent = lax.dynamic_slice_in_dim(voltages[:, 0], shifted(by[1]) * own, own, 1)
    cut = [later[0], urgent, *later[1:]]
    pieces = [piece.transpose(1, 0, 2, 3).reshape(own, rows, width) for piece in cut]
    blocks = pieces[:1] + [
        lax.ppermute(piece, "tm", [(z, (z + by) % tm) for z in range(tm)])
        for by, piece in zip(steps(tm)[1:], pieces[1:])
    ]

    raw = jax.ShapeDtypeStruct((chan_dev, rows, half), F32)
    mine, other = pl.pallas_call(
        functools.partial(raw_beams_kernel, tm, own),
        out_shape=[raw] * 2,
        in_specs=[whole] * (1 + tm),
        out_specs=[whole] * 2,
        scratch_shapes=[pltpu.VMEM((beams, width), BF16)],
        compiler_params=params,
        cost_estimate=cost(4 * chan_dev * samples * width * beams, 8 * chan_dev * samples * width),
    )(phase_index, *pieces)

    own_weights = pl.pallas_call(
        functools.partial(own_weights_kernel, own, chan_dev),
        out_shape=jax.ShapeDtypeStruct((own, width, 2 * beams), BF16),
        in_specs=[whole],
        out_specs=whole,
        scratch_shapes=[pltpu.VMEM((2 * beams, width), BF16)],
        compiler_params=params,
        cost_estimate=cost(20 * own * beams * width, 8 * own * beams * width),
    )(phase_index)

    early = (tm - 1) * rows
    cov, first, across = pl.pallas_call(
        early_kernel,
        out_shape=[
            jax.ShapeDtypeStruct((own, 2, width, width), F32),
            jax.ShapeDtypeStruct((own, 2 * vectors, width), F32),
            jax.ShapeDtypeStruct((own, width, early), BF16),
        ],
        in_specs=[whole] * tm,
        out_specs=[whole] * 3,
        scratch_shapes=[pltpu.VMEM((early, width), BF16)] * 2,
        compiler_params=params,
        cost_estimate=cost(2 * own * early * width * width, 8 * own * width * width),
    )(start_block, *blocks[:-1])

    other, *packets = pl.pallas_call(
        functools.partial(subspace_kernel, tm, own, factor),
        out_shape=[raw] + [jax.ShapeDtypeStruct((own, 2 * vectors, beams + samples), BF16)] * tm,
        in_specs=[unread, whole, scalars, scalars] + [whole] * 5,
        out_specs=[unread] + [whole] * tm,
        input_output_aliases={0: 0},
        scratch_shapes=[pltpu.VMEM((2 * width, width), BF16)] * 2
        + [pltpu.VMEM((tm, vectors, rows), F32)],
        compiler_params=params,
        cost_estimate=cost(32 * own * vectors * tm * samples * width, 8 * own * width * width),
    )(other, start_block, flags, ranks, own_weights, cov, first, across, blocks[-1])

    cores = [(0, 1), (1, 0)]
    theirs = lax.ppermute(other, "pol", cores)
    order = [*range(2, tm), 1]
    arrived = list(packets)
    for x in order:
        arrived[x] = lax.ppermute(packets[x], "tm", [(z, z ^ x) for z in range(tm)])
    swapped = [lax.ppermute(packet, "pol", cores) for packet in arrived]

    shape = jax.ShapeDtypeStruct((chan_dev, samples, half), F32)
    groups = [([0, *order[:-1]], []), (order[-1:], [0, *order[-2::-1]])]
    power = []
    for xs, later_xs in groups:
        used = [arrived[x] for x in xs] + [swapped[x] for x in later_xs]
        power = [
            pl.pallas_call(
                functools.partial(power_kernel, own, xs, later_xs),
                out_shape=shape,
                in_specs=[whole, whole if later_xs else unread] + [whole] * (len(used) + len(power)),
                out_specs=whole,
                input_output_aliases={2 + len(used): 0} if power else {},
                scratch_shapes=[pltpu.VMEM((rows, half), F32)],
                compiler_params=params,
                cost_estimate=cost(len(used) * own * rows * 2 * vectors * half, 8 * own * rows * half),
            )(mine, theirs if later_xs else mine, *used, *power)
        ]

    return pl.pallas_call(
        functools.partial(last_kernel, own, order[-1]),
        out_shape=jax.ShapeDtypeStruct((samples, chan_dev, half), F32),
        in_specs=[whole] * 3,
        out_specs=whole,
        scratch_shapes=[pltpu.VMEM((chan_dev, samples, half), F32), pltpu.VMEM((rows, half), F32)],
        compiler_params=params,
        cost_estimate=cost(chan_dev * samples * half, 12 * chan_dev * samples * half),
    )(theirs, swapped[order[-1]], *power)


def solution(mesh):
    placed = (
        P(("groups", "tm"), "pol", "chan", None, None),
        P("pol", "chan", None, None, None),
        P(("groups", "chan")),
        P(("groups", "chan")),
        P(),
    )
    return jax.shard_map(
        local,
        mesh=mesh,
        in_specs=placed,
        out_specs=P(("groups", "tm"), "chan", "pol"),
        check_vma=False,
    )
```

```python
import functools

import jax
import jax.numpy as jnp
from jax import lax
from jax.experimental import pallas as pl
from jax.experimental.pallas import tpu as pltpu
from jax.sharding import PartitionSpec as P

ITERS = 4
PHASES = 1024
QUARTER = PHASES // 4
EPS = 1e-06
F32 = jnp.float32
BF16 = jnp.bfloat16
NT = (((1,), (1,)), ((), ()))
NN = (((1,), (0,)), ((), ()))
TN = (((0,), (0,)), ((), ()))
VMEM_LIMIT = 48 * 1024 * 1024
CHUNK = 128


def dot(left, right, dims):
    return lax.dot_general(left, right, dims, preferred_element_type=F32)


def split(values):
    high = values.astype(BF16)
    low = (values - high.astype(F32)).astype(BF16)
    return high, low


def steer(phase, step, norm):
    turn = (phase * step) & (PHASES - 1)
    quadrant = (turn + QUARTER // 2) // QUARTER
    angle = (turn - quadrant * QUARTER).astype(F32) * (2.0 * jnp.pi / PHASES)
    sq = angle * angle
    sine = angle * (1.0 + sq * (-1.0 / 6 + sq * (1.0 / 120 + sq * (-1.0 / 5040 + sq / 362880))))
    cosine = 1.0 + sq * (-0.5 + sq * (1.0 / 24 + sq * (-1.0 / 720 + sq / 40320)))
    odd = (quadrant & 1) == 1
    real = jnp.where(odd, sine, cosine) * norm
    imag = jnp.where(odd, cosine, sine) * norm
    real = jnp.where(((quadrant + 1) & 2) == 2, -real, real)
    imag = jnp.where((quadrant & 2) == 2, -imag, imag)
    return real.astype(BF16), imag.astype(BF16)


def fill_weights(phase_ref, first, rows, step, out):
    norm = 1.0 / (phase_ref.shape[1] ** 0.5)
    chunk = 32

    def body(i, carry):
        at = pl.multiple_of(i * chunk, chunk)
        real, imag = steer(phase_ref[pl.ds(first + at, chunk), :], step, norm)
        out[pl.ds(at, chunk), :] = real
        out[pl.ds(rows + at, chunk), :] = imag
        return carry

    lax.fori_loop(0, rows // chunk, body, 0)


def steps(tm):
    return [0, *[by for by in range(1, tm) if by != tm // 2], tm // 2]


def shifted(by):
    tm = lax.axis_size("tm")
    return lax.rem(lax.axis_index("tm") + tm + by, tm)


def cut_kernel(own, bys, voltages_ref, *rest):
    pieces, done = rest[:-1], rest[-1]
    copies = []
    for i, (by, piece) in enumerate(zip(bys, pieces)):
        channels = pl.ds(shifted(by) * own, own)
        copy = pltpu.make_async_copy(voltages_ref.at[:, 0, channels], piece, done.at[i])
        copy.start()
        copies.append(copy)
    for copy in copies:
        copy.wait()


def turned(values, axis):
    size = values.shape[axis]
    at = lax.broadcasted_iota(jnp.int32, values.shape, axis)
    after = pltpu.roll(values, size - 1, axis)
    before = pltpu.roll(values, 1, axis)
    return jnp.where((at & 1) == 0, after, -before)


def raw_beams_kernel(tm, own, phase_ref, *rest):
    pieces, (mine_ref, other_ref, weights) = rest[:tm], rest[tm:]
    half = phase_ref.shape[0] // 2
    rows = pieces[0].shape[1]
    pol = lax.axis_index("pol")
    start = lax.axis_index("chan") * tm * own
    for by, piece in zip(steps(tm), pieces):
        for o in range(own):
            chan = shifted(by) * own + o
            for swap, out_ref in enumerate((mine_ref, other_ref)):
                first = pl.multiple_of((pol ^ swap) * half, half)
                fill_weights(phase_ref, first, half, start + chan + 1, weights)
                product = dot(piece[o], weights[...], NT)
                by_imag = turned(product[:, half:].reshape(rows // 8, 8, half), 1).reshape(rows, half)
                out_ref[chan] = product[:, :half] - by_imag


def own_weights_kernel(own, chan_dev, phase_ref, out_ref, weights):
    beams = phase_ref.shape[0]
    first = lax.axis_index("chan") * chan_dev + lax.axis_index("tm") * own
    for o in range(own):
        fill_weights(phase_ref, 0, beams, first + o + 1, weights)
        out_ref[o] = weights[...].T


def rotate(x):
    return (-turned(x.astype(F32), 0)).astype(BF16)


def early_kernel(start_ref, *refs):
    blocks, (cov_ref, first_ref, across_ref, along_ref, rotated_ref) = refs[:-5], refs[-5:]
    rows, width = blocks[0].shape[1:]
    own = cov_ref.shape[0]
    for o in range(own):
        for i, block in enumerate(blocks):
            x = block[o]
            at = slice(i * rows, (i + 1) * rows)
            along_ref[at] = x
            rotated_ref[at] = rotate(x)
            across_ref[o, :, at] = x.T
        cov_ref[o, 0] = dot(across_ref[o], along_ref[...], NN)
        cov_ref[o, 1] = dot(across_ref[o], rotated_ref[...], NN)
        chan = lax.axis_index("tm") * own + o
        first_ref[o] = block_times(start_ref[0, chan, 0], start_ref[0, chan, 1], across_ref[o], along_ref[...])


def project(real, imag, across):
    vectors = real.shape[0]
    both = jnp.concatenate(split(jnp.concatenate([real, imag], axis=0)), axis=0)
    product = dot(both, across, NN)
    product = product[: 2 * vectors] + product[2 * vectors :]
    other = turned(product, 1)
    return product[:vectors] + other[vectors:], product[vectors:] - other[:vectors]


def block_times(real, imag, across, along):
    pair = jnp.concatenate(project(real, imag, across), axis=0)
    product = dot(jnp.concatenate(split(pair), axis=0), along, NN)
    return product[: pair.shape[0]] + product[pair.shape[0] :]


def cov_times(real, imag, high_ref, low_ref):
    vectors = real.shape[0]
    rows = jnp.concatenate(
        [jnp.concatenate([real, imag], axis=1), jnp.concatenate([imag, -real], axis=1)], axis=0
    )
    high, low = split(rows)
    product = dot(jnp.concatenate([high, low], axis=0), high_ref[...], NN)
    product = product[: 2 * vectors] + product[2 * vectors :] + dot(high, low_ref[...], NN)
    return product[:vectors], product[vectors:]


def orthonormalize(real_z, imag_z, beside=()):
    beside = list(beside)
    vectors, width = real_z.shape
    row = lax.broadcasted_iota(jnp.int32, (vectors, 1), 0)
    real_v, imag_v = real_z, imag_z
    scale = jnp.zeros((vectors, 1), F32)
    for n in range(vectors):
        real_a = jnp.broadcast_to(real_v[n : n + 1], real_z.shape)
        imag_a = jnp.broadcast_to(imag_v[n : n + 1], real_z.shape)
        norm = jnp.sum(real_a * real_a + imag_a * imag_a, axis=1, keepdims=True) + EPS
        scale = jnp.where(row == n, norm, scale)
        if n + 1 < vectors:
            real_d = jnp.sum(real_a * real_z + imag_a * imag_z, axis=1, keepdims=True)
            imag_d = jnp.sum(real_a * imag_z - imag_a * real_z, axis=1, keepdims=True)
            inverse = jnp.where(row > n, 1.0 / norm, 0.0)
            real_c = real_d * inverse
            imag_c = imag_d * inverse
            real_v = real_v - (real_c * real_a - imag_c * imag_a)
            imag_v = imag_v - (real_c * imag_a + imag_c * real_a)
        for work in beside[n::vectors]:
            work()
    factor = 1.0 / jnp.sqrt(scale)
    return real_v * factor, imag_v * factor


def orthonormalize_by_gram(real_z, imag_z, riders=()):
    vectors = real_z.shape[0]
    row = lax.broadcasted_iota(jnp.int32, (vectors, 1), 0)
    by_z = []
    for n in range(vectors):
        real_a = jnp.broadcast_to(real_z[n : n + 1], real_z.shape)
        imag_a = jnp.broadcast_to(imag_z[n : n + 1], real_z.shape)
        by_z.append(
            (
                jnp.sum(real_a * real_z + imag_a * imag_z, axis=1, keepdims=True),
                jnp.sum(real_a * imag_z - imag_a * real_z, axis=1, keepdims=True),
            )
        )
    by_v = list(by_z)
    pairs = [(real_z, imag_z), *riders]
    for n in range(vectors - 1):
        (real_d, imag_d), (real_p, imag_p) = by_z[n], by_v[n]
        square = jnp.maximum(real_p[n : n + 1], 0.0)
        inverse = jnp.where(row > n, 1.0 / (square + EPS), 0.0)
        real_c, imag_c = real_d * inverse, imag_d * inverse
        real_b, imag_b = real_p - real_c * square, imag_p - imag_c * square
        for j in range(n + 1, vectors):
            real_s, imag_s = real_c[j : j + 1], imag_c[j : j + 1]
            real_q, imag_q = real_p[j : j + 1], -imag_p[j : j + 1]
            real, imag = by_v[j]
            by_v[j] = (
                real - (real_c * real_q - imag_c * imag_q) - (real_s * real_b + imag_s * imag_b),
                imag - (real_c * imag_q + imag_c * real_q) - (real_s * imag_b - imag_s * real_b),
            )
            real, imag = by_z[j]
            by_z[j] = (
                real - (real_s * real_d + imag_s * imag_d),
                imag - (real_s * imag_d - imag_s * real_d),
            )
        pairs = [
            (
                real - (real_c * real[n : n + 1] - imag_c * imag[n : n + 1]),
                imag - (real_c * imag[n : n + 1] + imag_c * real[n : n + 1]),
            )
            for real, imag in pairs
        ]
    real_v, imag_v = pairs[0]
    factor = 1.0 / jnp.sqrt(jnp.sum(real_v * real_v + imag_v * imag_v, axis=1, keepdims=True) + EPS)
    return [(real * factor, imag * factor) for real, imag in pairs]


def subspace_kernel(
    tm, own, factor, beams_ref, start_ref, flags_ref, ranks_ref, weights_ref, cov_ref, first_ref, across_ref, last_ref, *rest
):
    outs, (high_ref, low_ref, series_ref) = rest[1 : tm + 1], rest[tm + 1 :]
    vectors, width = start_ref.shape[3], start_ref.shape[4]
    rows = last_ref.shape[1]
    tm_index = lax.axis_index("tm")
    beams = weights_ref.shape[2] // 2
    for o in range(own):
        chan = tm_index * own + o
        across = last_ref[o].T
        rotated = rotate(last_ref[o])

        def add_last(part, first):
            right = last_ref[o] if part == 0 else rotated
            term = dot(across[first : first + CHUNK], right, NN)
            at = slice(part * width + first, part * width + first + CHUNK)
            high_ref[at], low_ref[at] = split((cov_ref[o, part, first : first + CHUNK] + term) * factor)

        chunks = [
            functools.partial(add_last, part, first) for part in range(2) for first in range(0, width, CHUNK)
        ]
        last = block_times(start_ref[0, chan, 0], start_ref[0, chan, 1], across, last_ref[o])
        both = (first_ref[o] + last) * factor
        real_q, imag_q = orthonormalize(both[:vectors], both[vectors:], chunks)
        for sweep in range(1, ITERS - 1):
            real_z, imag_z = cov_times(real_q, imag_q, high_ref, low_ref)
            ((real_q, imag_q),) = orthonormalize_by_gram(real_z, imag_z)
        real_z, imag_z = cov_times(real_q, imag_q, high_ref, low_ref)
        both = jnp.concatenate(split(jnp.concatenate([real_z, imag_z], axis=0)), axis=0)
        product = dot(both, weights_ref[o], NN)
        product = product[: 2 * vectors] + product[2 * vectors :]
        real_w = product[:vectors, :beams] - product[vectors:, beams:]
        imag_w = product[:vectors, beams:] + product[vectors:, :beams]
        riders = [
            (real_w, imag_w),
            project(real_z, imag_z, across_ref[o]),
            project(real_z, imag_z, across),
        ]
        unused, (real_w, imag_w), (early, unused), (late, unused) = orthonormalize_by_gram(real_z, imag_z, riders)
        rank = flags_ref[chan] * ranks_ref[chan]
        keep = lax.broadcasted_iota(jnp.int32, (vectors, 1), 0) < rank
        real_w = jnp.where(keep, real_w, 0.0)
        imag_w = jnp.where(keep, imag_w, 0.0)
        series = [early[:, i * rows : (i + 1) * rows] for i in range(tm - 1)] + [late]
        for by, values in zip(steps(tm), series):
            series_ref[tm_index ^ shifted(-by)] = jnp.where(keep, values, 0.0)
        steered = jnp.concatenate([real_w, imag_w], axis=0).astype(BF16)
        for x, out in enumerate(outs):
            series = series_ref[x]
            series = jnp.concatenate([series[:, : rows // 2], series[:, rows // 2 :]], axis=0)
            out[o, :, :beams] = steered
            out[o, :, beams:] = series.astype(BF16)


def nulled_power(raw, packet_ref, squares):
    rows, half = raw.shape
    samples = rows // 2
    series = packet_ref[:, 2 * half :].astype(F32)
    vectors = series.shape[0] // 2
    series = jnp.concatenate([series[:vectors], series[vectors:]], axis=1)
    left = jnp.concatenate([series, -turned(series, 1)], axis=0).astype(BF16)
    right = packet_ref[:, pl.ds(pl.multiple_of(lax.axis_index("pol") * half, half), half)]
    beam = raw - dot(left, right, TN)
    squares[...] = beam * beam
    return squares[pl.ds(0, samples, 2), :] + squares[pl.ds(1, samples, 2), :]


def power_kernel(own, xs, later_xs, mine_ref, theirs_ref, *rest):
    packets, later = rest[: len(xs)], rest[len(xs) : len(xs) + len(later_xs)]
    power_ref, squares = rest[-2:]
    for x, ref in zip(xs, packets):
        for o in range(own):
            chan = (lax.axis_index("tm") ^ x) * own + o
            power_ref[chan] = nulled_power(mine_ref[chan], ref.at[o], squares)
    for x, ref in zip(later_xs, later):
        for o in range(own):
            chan = (lax.axis_index("tm") ^ x) * own + o
            power_ref[chan] = power_ref[chan] + nulled_power(theirs_ref[chan], ref.at[o], squares)


def last_kernel(own, x, theirs_ref, packet_ref, power_ref, out_ref, powers, squares):
    powers[...] = power_ref[...]
    for o in range(own):
        chan = (lax.axis_index("tm") ^ x) * own + o
        powers[chan] = power_ref[chan] + nulled_power(theirs_ref[chan], packet_ref.at[o], squares)
    channels, samples = powers.shape[:2]
    for chan in range(channels):
        out_ref[pl.ds(chan, samples, channels), :] = powers[chan]


def local(voltages, start_block, flags, ranks, phase_index):
    tm = lax.axis_size("tm")
    tm_index = lax.axis_index("tm")
    samples, chan_dev, width = voltages.shape[0], voltages.shape[2], voltages.shape[4]
    own = chan_dev // tm
    vectors = start_block.shape[3]
    beams = phase_index.shape[0]
    half = beams // 2
    rows = 2 * samples
    factor = 1.0 / (samples * tm)
    params = pltpu.CompilerParams(vmem_limit_bytes=VMEM_LIMIT)
    whole = pl.BlockSpec(memory_space=pltpu.VMEM)
    scalars = pl.BlockSpec(memory_space=pltpu.SMEM)
    unread = pl.BlockSpec(memory_space=pl.ANY)

    def cost(multiplies, moved):
        return pl.CostEstimate(flops=2 * multiplies, bytes_accessed=moved, transcendentals=0)

    by = steps(tm)
    later = pl.pallas_call(
        functools.partial(cut_kernel, own, [by[0], *by[2:]]),
        out_shape=[jax.ShapeDtypeStruct((samples, own, 2, width), BF16)] * (tm - 1),
        in_specs=[pl.BlockSpec(memory_space=pltpu.HBM)],
        out_specs=[whole] * (tm - 1),
        scratch_shapes=[pltpu.SemaphoreType.DMA((tm - 1,))],
        compiler_params=params,
    )(voltages)
    urgent = lax.dynamic_slice_in_dim(voltages[:, 0], shifted(by[1]) * own, own, 1)
    cut = [later[0], urgent, *later[1:]]
    pieces = [piece.transpose(1, 0, 2, 3).reshape(own, rows, width) for piece in cut]
    blocks = pieces[:1] + [
        lax.ppermute(piece, "tm", [(z, (z + by) % tm) for z in range(tm)])
        for by, piece in zip(steps(tm)[1:], pieces[1:])
    ]

    raw = jax.ShapeDtypeStruct((chan_dev, rows, half), F32)
    mine, other = pl.pallas_call(
        functools.partial(raw_beams_kernel, tm, own),
        out_shape=[raw] * 2,
        in_specs=[whole] * (1 + tm),
        out_specs=[whole] * 2,
        scratch_shapes=[pltpu.VMEM((beams, width), BF16)],
        compiler_params=params,
        cost_estimate=cost(4 * chan_dev * samples * width * beams, 8 * chan_dev * samples * width),
    )(phase_index, *pieces)

    own_weights = pl.pallas_call(
        functools.partial(own_weights_kernel, own, chan_dev),
        out_shape=jax.ShapeDtypeStruct((own, width, 2 * beams), BF16),
        in_specs=[whole],
        out_specs=whole,
        scratch_shapes=[pltpu.VMEM((2 * beams, width), BF16)],
        compiler_params=params,
        cost_estimate=cost(20 * own * beams * width, 8 * own * beams * width),
    )(phase_index)

    early = (tm - 1) * rows
    cov, first, across = pl.pallas_call(
        early_kernel,
        out_shape=[
            jax.ShapeDtypeStruct((own, 2, width, width), F32),
            jax.ShapeDtypeStruct((own, 2 * vectors, width), F32),
            jax.ShapeDtypeStruct((own, width, early), BF16),
        ],
        in_specs=[whole] * tm,
        out_specs=[whole] * 3,
        scratch_shapes=[pltpu.VMEM((early, width), BF16)] * 2,
        compiler_params=params,
        cost_estimate=cost(2 * own * early * width * width, 8 * own * width * width),
    )(start_block, *blocks[:-1])

    other, *packets = pl.pallas_call(
        functools.partial(subspace_kernel, tm, own, factor),
        out_shape=[raw] + [jax.ShapeDtypeStruct((own, 2 * vectors, beams + samples), BF16)] * tm,
        in_specs=[unread, whole, scalars, scalars] + [whole] * 5,
        out_specs=[unread] + [whole] * tm,
        input_output_aliases={0: 0},
        scratch_shapes=[pltpu.VMEM((2 * width, width), BF16)] * 2
        + [pltpu.VMEM((tm, vectors, rows), F32)],
        compiler_params=params,
        cost_estimate=cost(32 * own * vectors * tm * samples * width, 8 * own * width * width),
    )(other, start_block, flags, ranks, own_weights, cov, first, across, blocks[-1])

    cores = [(0, 1), (1, 0)]
    theirs = lax.ppermute(other, "pol", cores)
    order = [*range(2, tm), 1]
    arrived = list(packets)
    for x in order:
        arrived[x] = lax.ppermute(packets[x], "tm", [(z, z ^ x) for z in range(tm)])
    swapped = [lax.ppermute(packet, "pol", cores) for packet in arrived]

    shape = jax.ShapeDtypeStruct((chan_dev, samples, half), F32)
    groups = [([0, *order[:-1]], []), (order[-1:], [0, *order[-2::-1]])]
    power = []
    for xs, later_xs in groups:
        used = [arrived[x] for x in xs] + [swapped[x] for x in later_xs]
        power = [
            pl.pallas_call(
                functools.partial(power_kernel, own, xs, later_xs),
                out_shape=shape,
                in_specs=[whole, whole if later_xs else unread] + [whole] * (len(used) + len(power)),
                out_specs=whole,
                input_output_aliases={2 + len(used): 0} if power else {},
                scratch_shapes=[pltpu.VMEM((rows, half), F32)],
                compiler_params=params,
                cost_estimate=cost(len(used) * own * rows * 2 * vectors * half, 8 * own * rows * half),
            )(mine, theirs if later_xs else mine, *used, *power)
        ]

    rows_out = pl.pallas_call(
        functools.partial(last_kernel, own, order[-1]),
        out_shape=jax.ShapeDtypeStruct((samples * chan_dev, half), F32),
        in_specs=[whole] * 3,
        out_specs=whole,
        scratch_shapes=[pltpu.VMEM((chan_dev, samples, half), F32), pltpu.VMEM((rows, half), F32)],
        compiler_params=params,
        cost_estimate=cost(chan_dev * samples * half, 12 * chan_dev * samples * half),
    )(theirs, swapped[order[-1]], *power)
    return rows_out.reshape(samples, chan_dev, half)


def solution(mesh):
    placed = (
        P(("groups", "tm"), "pol", "chan", None, None),
        P("pol", "chan", None, None, None),
        P(("groups", "chan")),
        P(("groups", "chan")),
        P(),
    )
    return jax.shard_map(
        local,
        mesh=mesh,
        in_specs=placed,
        out_specs=P(("groups", "tm"), "chan", "pol"),
        check_vma=False,
    )
```

```python
import functools

import jax
import jax.numpy as jnp
from jax import lax
from jax.experimental import pallas as pl
from jax.experimental.pallas import tpu as pltpu
from jax.sharding import PartitionSpec as P

ITERS = 4
PHASES = 1024
QUARTER = PHASES // 4
EPS = 1e-06
F32 = jnp.float32
BF16 = jnp.bfloat16
NT = (((1,), (1,)), ((), ()))
NN = (((1,), (0,)), ((), ()))
TN = (((0,), (0,)), ((), ()))
VMEM_LIMIT = 48 * 1024 * 1024
CHUNK = 128


def dot(left, right, dims):
    return lax.dot_general(left, right, dims, preferred_element_type=F32)


def split(values):
    high = values.astype(BF16)
    low = (values - high.astype(F32)).astype(BF16)
    return high, low


def steer(phase, step, norm):
    turn = (phase * step) & (PHASES - 1)
    quadrant = (turn + QUARTER // 2) // QUARTER
    angle = (turn - quadrant * QUARTER).astype(F32) * (2.0 * jnp.pi / PHASES)
    sq = angle * angle
    sine = angle * (1.0 + sq * (-1.0 / 6 + sq * (1.0 / 120 + sq * (-1.0 / 5040 + sq / 362880))))
    cosine = 1.0 + sq * (-0.5 + sq * (1.0 / 24 + sq * (-1.0 / 720 + sq / 40320)))
    odd = (quadrant & 1) == 1
    real = jnp.where(odd, sine, cosine) * norm
    imag = jnp.where(odd, cosine, sine) * norm
    real = jnp.where(((quadrant + 1) & 2) == 2, -real, real)
    imag = jnp.where((quadrant & 2) == 2, -imag, imag)
    return real.astype(BF16), imag.astype(BF16)


def fill_weights(phase_ref, first, rows, step, out):
    norm = 1.0 / (phase_ref.shape[1] ** 0.5)
    chunk = 32

    def body(i, carry):
        at = pl.multiple_of(i * chunk, chunk)
        real, imag = steer(phase_ref[pl.ds(first + at, chunk), :], step, norm)
        out[pl.ds(at, chunk), :] = real
        out[pl.ds(rows + at, chunk), :] = imag
        return carry

    lax.fori_loop(0, rows // chunk, body, 0)


def steps(tm):
    return [0, *[by for by in range(1, tm) if by != tm // 2], tm // 2]


def parts(tm):
    far = steps(tm)[1:]
    return [(0, None)] + [(by, at) for at in range(2) for by in far]


def shifted(by):
    tm = lax.axis_size("tm")
    return lax.rem(lax.axis_index("tm") + tm + by, tm)


def cut_kernel(own, wanted, voltages_ref, *rest):
    pieces, done = rest[:-1], rest[-1]
    copies = []
    for i, ((by, at), piece) in enumerate(zip(wanted, pieces)):
        times = pl.ds((at or 0) * piece.shape[0], piece.shape[0])
        channels = pl.ds(shifted(by) * own, own)
        copy = pltpu.make_async_copy(voltages_ref.at[times, 0, channels], piece, done.at[i])
        copy.start()
        copies.append(copy)
    for copy in copies:
        copy.wait()


def turned(values, axis):
    size = values.shape[axis]
    at = lax.broadcasted_iota(jnp.int32, values.shape, axis)
    after = pltpu.roll(values, size - 1, axis)
    before = pltpu.roll(values, 1, axis)
    return jnp.where((at & 1) == 0, after, -before)


def raw_beams_kernel(tm, own, phase_ref, *rest):
    pieces, (mine_ref, other_ref, weights) = dict(zip(parts(tm), rest[:-3])), rest[-3:]
    half = phase_ref.shape[0] // 2
    pol = lax.axis_index("pol")
    start = lax.axis_index("chan") * tm * own
    for by in steps(tm):
        for o in range(own):
            chan = shifted(by) * own + o
            for swap, out_ref in enumerate((mine_ref, other_ref)):
                first = pl.multiple_of((pol ^ swap) * half, half)
                fill_weights(phase_ref, first, half, start + chan + 1, weights)
                for at in (0, 1) if by else (None,):
                    piece = pieces[by, at]
                    rows = piece.shape[1]
                    product = dot(piece[o], weights[...], NT)
                    by_imag = turned(product[:, half:].reshape(rows // 8, 8, half), 1).reshape(rows, half)
                    out_ref[chan, (at or 0) * rows : (at or 0) * rows + rows] = product[:, :half] - by_imag


def own_weights_kernel(own, chan_dev, phase_ref, out_ref, weights):
    beams = phase_ref.shape[0]
    first = lax.axis_index("chan") * chan_dev + lax.axis_index("tm") * own
    for o in range(own):
        fill_weights(phase_ref, 0, beams, first + o + 1, weights)
        out_ref[o] = weights[...].T


def rotate(x):
    return (-turned(x.astype(F32), 0)).astype(BF16)


def early_kernel(start_ref, *refs):
    blocks, (cov_ref, first_ref, across_ref, along_ref, rotated_ref) = refs[:-5], refs[-5:]
    own = cov_ref.shape[0]
    for o in range(own):
        first = 0
        for block in blocks:
            x = block[o]
            at = slice(first, first + x.shape[0])
            along_ref[at] = x
            rotated_ref[at] = rotate(x)
            across_ref[o, :, at] = x.T
            first += x.shape[0]
        cov_ref[o, 0] = dot(across_ref[o], along_ref[...], NN)
        cov_ref[o, 1] = dot(across_ref[o], rotated_ref[...], NN)
        chan = lax.axis_index("tm") * own + o
        first_ref[o] = block_times(start_ref[0, chan, 0], start_ref[0, chan, 1], across_ref[o], along_ref[...])


def project(real, imag, across):
    vectors = real.shape[0]
    both = jnp.concatenate(split(jnp.concatenate([real, imag], axis=0)), axis=0)
    product = dot(both, across, NN)
    product = product[: 2 * vectors] + product[2 * vectors :]
    other = turned(product, 1)
    return product[:vectors] + other[vectors:], product[vectors:] - other[:vectors]


def block_times(real, imag, across, along):
    pair = jnp.concatenate(project(real, imag, across), axis=0)
    product = dot(jnp.concatenate(split(pair), axis=0), along, NN)
    return product[: pair.shape[0]] + product[pair.shape[0] :]


def cov_times(real, imag, high_ref, low_ref):
    vectors = real.shape[0]
    rows = jnp.concatenate(
        [jnp.concatenate([real, imag], axis=1), jnp.concatenate([imag, -real], axis=1)], axis=0
    )
    high, low = split(rows)
    product = dot(jnp.concatenate([high, low], axis=0), high_ref[...], NN)
    product = product[: 2 * vectors] + product[2 * vectors :] + dot(high, low_ref[...], NN)
    return product[:vectors], product[vectors:]


def orthonormalize(real_z, imag_z, beside=()):
    beside = list(beside)
    vectors, width = real_z.shape
    row = lax.broadcasted_iota(jnp.int32, (vectors, 1), 0)
    real_v, imag_v = real_z, imag_z
    scale = jnp.zeros((vectors, 1), F32)
    for n in range(vectors):
        real_a = jnp.broadcast_to(real_v[n : n + 1], real_z.shape)
        imag_a = jnp.broadcast_to(imag_v[n : n + 1], real_z.shape)
        norm = jnp.sum(real_a * real_a + imag_a * imag_a, axis=1, keepdims=True) + EPS
        scale = jnp.where(row == n, norm, scale)
        if n + 1 < vectors:
            real_d = jnp.sum(real_a * real_z + imag_a * imag_z, axis=1, keepdims=True)
            imag_d = jnp.sum(real_a * imag_z - imag_a * real_z, axis=1, keepdims=True)
            inverse = jnp.where(row > n, 1.0 / norm, 0.0)
            real_c = real_d * inverse
            imag_c = imag_d * inverse
            real_v = real_v - (real_c * real_a - imag_c * imag_a)
            imag_v = imag_v - (real_c * imag_a + imag_c * real_a)
        for work in beside[n::vectors]:
            work()
    factor = 1.0 / jnp.sqrt(scale)
    return real_v * factor, imag_v * factor


def orthonormalize_by_gram(real_z, imag_z, riders=()):
    vectors = real_z.shape[0]
    row = lax.broadcasted_iota(jnp.int32, (vectors, 1), 0)
    by_z = []
    for n in range(vectors):
        real_a = jnp.broadcast_to(real_z[n : n + 1], real_z.shape)
        imag_a = jnp.broadcast_to(imag_z[n : n + 1], real_z.shape)
        by_z.append(
            (
                jnp.sum(real_a * real_z + imag_a * imag_z, axis=1, keepdims=True),
                jnp.sum(real_a * imag_z - imag_a * real_z, axis=1, keepdims=True),
            )
        )
    by_v = list(by_z)
    pairs = [(real_z, imag_z), *riders]
    for n in range(vectors - 1):
        (real_d, imag_d), (real_p, imag_p) = by_z[n], by_v[n]
        square = jnp.maximum(real_p[n : n + 1], 0.0)
        inverse = jnp.where(row > n, 1.0 / (square + EPS), 0.0)
        real_c, imag_c = real_d * inverse, imag_d * inverse
        real_b, imag_b = real_p - real_c * square, imag_p - imag_c * square
        for j in range(n + 1, vectors):
            real_s, imag_s = real_c[j : j + 1], imag_c[j : j + 1]
            real_q, imag_q = real_p[j : j + 1], -imag_p[j : j + 1]
            real, imag = by_v[j]
            by_v[j] = (
                real - (real_c * real_q - imag_c * imag_q) - (real_s * real_b + imag_s * imag_b),
                imag - (real_c * imag_q + imag_c * real_q) - (real_s * imag_b - imag_s * real_b),
            )
            real, imag = by_z[j]
            by_z[j] = (
                real - (real_s * real_d + imag_s * imag_d),
                imag - (real_s * imag_d - imag_s * real_d),
            )
        pairs = [
            (
                real - (real_c * real[n : n + 1] - imag_c * imag[n : n + 1]),
                imag - (real_c * imag[n : n + 1] + imag_c * real[n : n + 1]),
            )
            for real, imag in pairs
        ]
    real_v, imag_v = pairs[0]
    factor = 1.0 / jnp.sqrt(jnp.sum(real_v * real_v + imag_v * imag_v, axis=1, keepdims=True) + EPS)
    return [(real * factor, imag * factor) for real, imag in pairs]


def subspace_kernel(
    tm, own, factor, beams_ref, start_ref, flags_ref, ranks_ref, weights_ref, cov_ref, first_ref, across_ref, last_ref, *rest
):
    outs, (high_ref, low_ref, series_ref) = rest[1 : tm + 1], rest[tm + 1 :]
    vectors, width = start_ref.shape[3], start_ref.shape[4]
    rows = last_ref.shape[1] * 2
    tm_index = lax.axis_index("tm")
    beams = weights_ref.shape[2] // 2
    for o in range(own):
        chan = tm_index * own + o
        across = last_ref[o].T
        rotated = rotate(last_ref[o])

        def add_last(part, first):
            right = last_ref[o] if part == 0 else rotated
            term = dot(across[first : first + CHUNK], right, NN)
            at = slice(part * width + first, part * width + first + CHUNK)
            high_ref[at], low_ref[at] = split((cov_ref[o, part, first : first + CHUNK] + term) * factor)

        chunks = [
            functools.partial(add_last, part, first) for part in range(2) for first in range(0, width, CHUNK)
        ]
        last = block_times(start_ref[0, chan, 0], start_ref[0, chan, 1], across, last_ref[o])
        both = (first_ref[o] + last) * factor
        real_q, imag_q = orthonormalize(both[:vectors], both[vectors:], chunks)
        for sweep in range(1, ITERS - 1):
            real_z, imag_z = cov_times(real_q, imag_q, high_ref, low_ref)
            ((real_q, imag_q),) = orthonormalize_by_gram(real_z, imag_z)
        real_z, imag_z = cov_times(real_q, imag_q, high_ref, low_ref)
        both = jnp.concatenate(split(jnp.concatenate([real_z, imag_z], axis=0)), axis=0)
        product = dot(both, weights_ref[o], NN)
        product = product[: 2 * vectors] + product[2 * vectors :]
        real_w = product[:vectors, :beams] - product[vectors:, beams:]
        imag_w = product[:vectors, beams:] + product[vectors:, :beams]
        riders = [
            (real_w, imag_w),
            project(real_z, imag_z, across_ref[o]),
            project(real_z, imag_z, across),
        ]
        unused, (real_w, imag_w), (early, unused), (late, unused) = orthonormalize_by_gram(real_z, imag_z, riders)
        rank = flags_ref[chan] * ranks_ref[chan]
        keep = lax.broadcasted_iota(jnp.int32, (vectors, 1), 0) < rank
        real_w = jnp.where(keep, real_w, 0.0)
        imag_w = jnp.where(keep, imag_w, 0.0)
        found, first = {}, 0
        for part in parts(tm)[:-1]:
            length = rows if part[1] is None else rows // 2
            found[part] = early[:, first : first + length]
            first += length
        found[parts(tm)[-1]] = late
        for by in steps(tm):
            values = jnp.concatenate([found[by, 0], found[by, 1]], axis=1) if by else found[0, None]
            series_ref[tm_index ^ shifted(-by)] = jnp.where(keep, values, 0.0)
        steered = jnp.concatenate([real_w, imag_w], axis=0).astype(BF16)
        for x, out in enumerate(outs):
            series = series_ref[x]
            series = jnp.concatenate([series[:, : rows // 2], series[:, rows // 2 :]], axis=0)
            out[o, :, :beams] = steered
            out[o, :, beams:] = series.astype(BF16)


def nulled_power(raw, packet_ref, squares):
    rows, half = raw.shape
    samples = rows // 2
    series = packet_ref[:, 2 * half :].astype(F32)
    vectors = series.shape[0] // 2
    series = jnp.concatenate([series[:vectors], series[vectors:]], axis=1)
    left = jnp.concatenate([series, -turned(series, 1)], axis=0).astype(BF16)
    right = packet_ref[:, pl.ds(pl.multiple_of(lax.axis_index("pol") * half, half), half)]
    beam = raw - dot(left, right, TN)
    squares[...] = beam * beam
    return squares[pl.ds(0, samples, 2), :] + squares[pl.ds(1, samples, 2), :]


def power_kernel(own, xs, later_xs, mine_ref, theirs_ref, *rest):
    packets, later = rest[: len(xs)], rest[len(xs) : len(xs) + len(later_xs)]
    power_ref, squares = rest[-2:]
    for x, ref in zip(xs, packets):
        for o in range(own):
            chan = (lax.axis_index("tm") ^ x) * own + o
            power_ref[chan] = nulled_power(mine_ref[chan], ref.at[o], squares)
    for x, ref in zip(later_xs, later):
        for o in range(own):
            chan = (lax.axis_index("tm") ^ x) * own + o
            power_ref[chan] = power_ref[chan] + nulled_power(theirs_ref[chan], ref.at[o], squares)


def last_kernel(own, x, theirs_ref, packet_ref, power_ref, out_ref, powers, squares):
    powers[...] = power_ref[...]
    for o in range(own):
        chan = (lax.axis_index("tm") ^ x) * own + o
        powers[chan] = power_ref[chan] + nulled_power(theirs_ref[chan], packet_ref.at[o], squares)
    channels, samples = powers.shape[:2]
    for chan in range(channels):
        out_ref[pl.ds(chan, samples, channels), :] = powers[chan]


def local(voltages, start_block, flags, ranks, phase_index):
    tm = lax.axis_size("tm")
    tm_index = lax.axis_index("tm")
    samples, chan_dev, width = voltages.shape[0], voltages.shape[2], voltages.shape[4]
    own = chan_dev // tm
    vectors = start_block.shape[3]
    beams = phase_index.shape[0]
    half = beams // 2
    rows = 2 * samples
    factor = 1.0 / (samples * tm)
    params = pltpu.CompilerParams(vmem_limit_bytes=VMEM_LIMIT)
    whole = pl.BlockSpec(memory_space=pltpu.VMEM)
    scalars = pl.BlockSpec(memory_space=pltpu.SMEM)
    unread = pl.BlockSpec(memory_space=pl.ANY)

    def cost(multiplies, moved):
        return pl.CostEstimate(flops=2 * multiplies, bytes_accessed=moved, transcendentals=0)

    wanted = parts(tm)
    first_by = wanted[1][0]
    urgent = lax.dynamic_slice(
        voltages, (0, 0, shifted(first_by) * own, 0, 0), (samples // 2, 1, own, 2, width)
    )[:, 0]
    later = pl.pallas_call(
        functools.partial(cut_kernel, own, wanted[:1] + wanted[2:]),
        out_shape=[
            jax.ShapeDtypeStruct((samples if at is None else samples // 2, own, 2, width), BF16)
            for by, at in wanted[:1] + wanted[2:]
        ],
        in_specs=[pl.BlockSpec(memory_space=pltpu.HBM)],
        out_specs=[whole] * (len(wanted) - 1),
        scratch_shapes=[pltpu.SemaphoreType.DMA((len(wanted) - 1,))],
        compiler_params=params,
    )(voltages)
    pieces = [
        piece.transpose(1, 0, 2, 3).reshape(own, 2 * piece.shape[0], width)
        for piece in (later[0], urgent, *later[1:])
    ]
    blocks = pieces[:1] + [
        lax.ppermute(piece, "tm", [(z, (z + by) % tm) for z in range(tm)])
        for (by, at), piece in list(zip(wanted, pieces))[1:]
    ]

    raw = jax.ShapeDtypeStruct((chan_dev, rows, half), F32)
    mine, other = pl.pallas_call(
        functools.partial(raw_beams_kernel, tm, own),
        out_shape=[raw] * 2,
        in_specs=[whole] * (1 + len(pieces)),
        out_specs=[whole] * 2,
        scratch_shapes=[pltpu.VMEM((beams, width), BF16)],
        compiler_params=params,
        cost_estimate=cost(4 * chan_dev * samples * width * beams, 8 * chan_dev * samples * width),
    )(phase_index, *pieces)

    own_weights = pl.pallas_call(
        functools.partial(own_weights_kernel, own, chan_dev),
        out_shape=jax.ShapeDtypeStruct((own, width, 2 * beams), BF16),
        in_specs=[whole],
        out_specs=whole,
        scratch_shapes=[pltpu.VMEM((2 * beams, width), BF16)],
        compiler_params=params,
        cost_estimate=cost(20 * own * beams * width, 8 * own * beams * width),
    )(phase_index)

    early = tm * rows - blocks[-1].shape[1]
    cov, first, across = pl.pallas_call(
        early_kernel,
        out_shape=[
            jax.ShapeDtypeStruct((own, 2, width, width), F32),
            jax.ShapeDtypeStruct((own, 2 * vectors, width), F32),
            jax.ShapeDtypeStruct((own, width, early), BF16),
        ],
        in_specs=[whole] * len(blocks),
        out_specs=[whole] * 3,
        scratch_shapes=[pltpu.VMEM((early, width), BF16)] * 2,
        compiler_params=params,
        cost_estimate=cost(2 * own * early * width * width, 8 * own * width * width),
    )(start_block, *blocks[:-1])

    other, *packets = pl.pallas_call(
        functools.partial(subspace_kernel, tm, own, factor),
        out_shape=[raw] + [jax.ShapeDtypeStruct((own, 2 * vectors, beams + samples), BF16)] * tm,
        in_specs=[unread, whole, scalars, scalars] + [whole] * 5,
        out_specs=[unread] + [whole] * tm,
        input_output_aliases={0: 0},
        scratch_shapes=[pltpu.VMEM((2 * width, width), BF16)] * 2
        + [pltpu.VMEM((tm, vectors, rows), F32)],
        compiler_params=params,
        cost_estimate=cost(32 * own * vectors * tm * samples * width, 8 * own * width * width),
    )(other, start_block, flags, ranks, own_weights, cov, first, across, blocks[-1])

    cores = [(0, 1), (1, 0)]
    theirs = lax.ppermute(other, "pol", cores)
    order = [*range(2, tm), 1]
    arrived = list(packets)
    for x in order:
        arrived[x] = lax.ppermute(packets[x], "tm", [(z, z ^ x) for z in range(tm)])
    swapped = [lax.ppermute(packet, "pol", cores) for packet in arrived]

    shape = jax.ShapeDtypeStruct((chan_dev, samples, half), F32)
    groups = [([0, *order[:-1]], []), (order[-1:], [0, *order[-2::-1]])]
    power = []
    for xs, later_xs in groups:
        used = [arrived[x] for x in xs] + [swapped[x] for x in later_xs]
        power = [
            pl.pallas_call(
                functools.partial(power_kernel, own, xs, later_xs),
                out_shape=shape,
                in_specs=[whole, whole if later_xs else unread] + [whole] * (len(used) + len(power)),
                out_specs=whole,
                input_output_aliases={2 + len(used): 0} if power else {},
                scratch_shapes=[pltpu.VMEM((rows, half), F32)],
                compiler_params=params,
                cost_estimate=cost(len(used) * own * rows * 2 * vectors * half, 8 * own * rows * half),
            )(mine, theirs if later_xs else mine, *used, *power)
        ]

    rows_out = pl.pallas_call(
        functools.partial(last_kernel, own, order[-1]),
        out_shape=jax.ShapeDtypeStruct((samples * chan_dev, half), F32),
        in_specs=[whole] * 3,
        out_specs=whole,
        scratch_shapes=[pltpu.VMEM((chan_dev, samples, half), F32), pltpu.VMEM((rows, half), F32)],
        compiler_params=params,
        cost_estimate=cost(chan_dev * samples * half, 12 * chan_dev * samples * half),
    )(theirs, swapped[order[-1]], *power)
    return rows_out.reshape(samples, chan_dev, half)


def solution(mesh):
    placed = (
        P(("groups", "tm"), "pol", "chan", None, None),
        P("pol", "chan", None, None, None),
        P(("groups", "chan")),
        P(("groups", "chan")),
        P(),
    )
    return jax.shard_map(
        local,
        mesh=mesh,
        in_specs=placed,
        out_specs=P(("groups", "tm"), "chan", "pol"),
        check_vma=False,
    )
```

```python
import functools

import jax
import jax.numpy as jnp
from jax import lax
from jax.experimental import pallas as pl
from jax.experimental.pallas import tpu as pltpu
from jax.sharding import PartitionSpec as P

ITERS = 4
PHASES = 1024
QUARTER = PHASES // 4
EPS = 1e-06
F32 = jnp.float32
BF16 = jnp.bfloat16
NT = (((1,), (1,)), ((), ()))
NN = (((1,), (0,)), ((), ()))
TN = (((0,), (0,)), ((), ()))
VMEM_LIMIT = 48 * 1024 * 1024
CHUNK = 128
LEAST_PIVOT = 1e-4


def dot(left, right, dims):
    return lax.dot_general(left, right, dims, preferred_element_type=F32)


def split(values):
    high = values.astype(BF16)
    low = (values - high.astype(F32)).astype(BF16)
    return high, low


def steer(phase, step, norm):
    turn = (phase * step) & (PHASES - 1)
    quadrant = (turn + QUARTER // 2) // QUARTER
    angle = (turn - quadrant * QUARTER).astype(F32) * (2.0 * jnp.pi / PHASES)
    sq = angle * angle
    sine = angle * (1.0 + sq * (-1.0 / 6 + sq * (1.0 / 120 + sq * (-1.0 / 5040 + sq / 362880))))
    cosine = 1.0 + sq * (-0.5 + sq * (1.0 / 24 + sq * (-1.0 / 720 + sq / 40320)))
    odd = (quadrant & 1) == 1
    real = jnp.where(odd, sine, cosine) * norm
    imag = jnp.where(odd, cosine, sine) * norm
    real = jnp.where(((quadrant + 1) & 2) == 2, -real, real)
    imag = jnp.where((quadrant & 2) == 2, -imag, imag)
    return real.astype(BF16), imag.astype(BF16)


def fill_weights(phase_ref, first, rows, step, out):
    norm = 1.0 / (phase_ref.shape[1] ** 0.5)
    chunk = 32

    def body(i, carry):
        at = pl.multiple_of(i * chunk, chunk)
        real, imag = steer(phase_ref[pl.ds(first + at, chunk), :], step, norm)
        out[pl.ds(at, chunk), :] = real
        out[pl.ds(rows + at, chunk), :] = imag
        return carry

    lax.fori_loop(0, rows // chunk, body, 0)


def steps(tm):
    return [0, *[by for by in range(1, tm) if by != tm // 2], tm // 2]


def shifted(by):
    tm = lax.axis_size("tm")
    return lax.rem(lax.axis_index("tm") + tm + by, tm)


def cut_kernel(own, bys, voltages_ref, *rest):
    pieces, done = rest[:-1], rest[-1]
    copies = []
    for i, (by, piece) in enumerate(zip(bys, pieces)):
        channels = pl.ds(shifted(by) * own, own)
        copy = pltpu.make_async_copy(voltages_ref.at[:, 0, channels], piece, done.at[i])
        copy.start()
        copies.append(copy)
    for copy in copies:
        copy.wait()


def turned(values, axis):
    size = values.shape[axis]
    at = lax.broadcasted_iota(jnp.int32, values.shape, axis)
    after = pltpu.roll(values, size - 1, axis)
    before = pltpu.roll(values, 1, axis)
    return jnp.where((at & 1) == 0, after, -before)


def raw_beams_kernel(tm, own, phase_ref, *rest):
    pieces, (mine_ref, other_ref, weights) = rest[:tm], rest[tm:]
    half = phase_ref.shape[0] // 2
    rows = pieces[0].shape[1]
    pol = lax.axis_index("pol")
    start = lax.axis_index("chan") * tm * own
    for by, piece in zip(steps(tm), pieces):
        for o in range(own):
            chan = shifted(by) * own + o
            for swap, out_ref in enumerate((mine_ref, other_ref)):
                first = pl.multiple_of((pol ^ swap) * half, half)
                fill_weights(phase_ref, first, half, start + chan + 1, weights)
                product = dot(piece[o], weights[...], NT)
                by_imag = turned(product[:, half:].reshape(rows // 8, 8, half), 1).reshape(rows, half)
                out_ref[chan] = product[:, :half] - by_imag


def own_weights_kernel(own, chan_dev, phase_ref, out_ref, weights):
    beams = phase_ref.shape[0]
    first = lax.axis_index("chan") * chan_dev + lax.axis_index("tm") * own
    for o in range(own):
        fill_weights(phase_ref, 0, beams, first + o + 1, weights)
        out_ref[o] = weights[...].T


def rotate(x):
    return (-turned(x.astype(F32), 0)).astype(BF16)


def early_kernel(start_ref, *refs):
    blocks, (cov_ref, first_ref, across_ref, along_ref, rotated_ref) = refs[:-5], refs[-5:]
    rows, width = blocks[0].shape[1:]
    own = cov_ref.shape[0]
    for o in range(own):
        for i, block in enumerate(blocks):
            x = block[o]
            at = slice(i * rows, (i + 1) * rows)
            along_ref[at] = x
            rotated_ref[at] = rotate(x)
            across_ref[o, :, at] = x.T
        cov_ref[o, 0] = dot(across_ref[o], along_ref[...], NN)
        cov_ref[o, 1] = dot(across_ref[o], rotated_ref[...], NN)
        chan = lax.axis_index("tm") * own + o
        first_ref[o] = block_times(start_ref[0, chan, 0], start_ref[0, chan, 1], across_ref[o], along_ref[...])


def project(real, imag, across):
    vectors = real.shape[0]
    both = jnp.concatenate(split(jnp.concatenate([real, imag], axis=0)), axis=0)
    product = dot(both, across, NN)
    product = product[: 2 * vectors] + product[2 * vectors :]
    other = turned(product, 1)
    return product[:vectors] + other[vectors:], product[vectors:] - other[:vectors]


def block_times(real, imag, across, along):
    pair = jnp.concatenate(project(real, imag, across), axis=0)
    product = dot(jnp.concatenate(split(pair), axis=0), along, NN)
    return product[: pair.shape[0]] + product[pair.shape[0] :]


def cov_times(real, imag, high_ref, low_ref):
    vectors = real.shape[0]
    rows = jnp.concatenate(
        [jnp.concatenate([real, imag], axis=1), jnp.concatenate([imag, -real], axis=1)], axis=0
    )
    high, low = split(rows)
    product = dot(jnp.concatenate([high, low], axis=0), high_ref[...], NN)
    product = product[: 2 * vectors] + product[2 * vectors :] + dot(high, low_ref[...], NN)
    return product[:vectors], product[vectors:]


def orthonormalize(real_z, imag_z, beside=()):
    beside = list(beside)
    vectors, width = real_z.shape
    row = lax.broadcasted_iota(jnp.int32, (vectors, 1), 0)
    real_v, imag_v = real_z, imag_z
    scale = jnp.zeros((vectors, 1), F32)
    for n in range(vectors):
        real_a = jnp.broadcast_to(real_v[n : n + 1], real_z.shape)
        imag_a = jnp.broadcast_to(imag_v[n : n + 1], real_z.shape)
        norm = jnp.sum(real_a * real_a + imag_a * imag_a, axis=1, keepdims=True) + EPS
        scale = jnp.where(row == n, norm, scale)
        if n + 1 < vectors:
            real_d = jnp.sum(real_a * real_z + imag_a * imag_z, axis=1, keepdims=True)
            imag_d = jnp.sum(real_a * imag_z - imag_a * real_z, axis=1, keepdims=True)
            inverse = jnp.where(row > n, 1.0 / norm, 0.0)
            real_c = real_d * inverse
            imag_c = imag_d * inverse
            real_v = real_v - (real_c * real_a - imag_c * imag_a)
            imag_v = imag_v - (real_c * imag_a + imag_c * real_a)
        for work in beside[n::vectors]:
            work()
    factor = 1.0 / jnp.sqrt(scale)
    return real_v * factor, imag_v * factor


def orthonormalize_by_gram(real_z, imag_z, riders=()):
    vectors = real_z.shape[0]
    row = lax.broadcasted_iota(jnp.int32, (vectors, 1), 0)
    by_z = []
    for n in range(vectors):
        real_a = jnp.broadcast_to(real_z[n : n + 1], real_z.shape)
        imag_a = jnp.broadcast_to(imag_z[n : n + 1], real_z.shape)
        by_z.append(
            (
                jnp.sum(real_a * real_z + imag_a * imag_z, axis=1, keepdims=True),
                jnp.sum(real_a * imag_z - imag_a * real_z, axis=1, keepdims=True),
            )
        )
    by_v = list(by_z)
    whole = [real[n : n + 1] for n, (real, imag) in enumerate(by_z)]
    sound = jnp.ones((1, 1), F32)
    pairs = [(real_z, imag_z), *riders]
    for n in range(vectors - 1):
        (real_d, imag_d), (real_p, imag_p) = by_z[n], by_v[n]
        square = jnp.maximum(real_p[n : n + 1], 0.0)
        fits = (square >= LEAST_PIVOT * whole[n]) & (square <= 4.0 * whole[n])
        sound = jnp.where(fits, sound, 0.0)
        inverse = jnp.where(row > n, 1.0 / (square + EPS), 0.0)
        real_c, imag_c = real_d * inverse, imag_d * inverse
        real_b, imag_b = real_p - real_c * square, imag_p - imag_c * square
        for j in range(n + 1, vectors):
            real_s, imag_s = real_c[j : j + 1], imag_c[j : j + 1]
            real_q, imag_q = real_p[j : j + 1], -imag_p[j : j + 1]
            real, imag = by_v[j]
            by_v[j] = (
                real - (real_c * real_q - imag_c * imag_q) - (real_s * real_b + imag_s * imag_b),
                imag - (real_c * imag_q + imag_c * real_q) - (real_s * imag_b - imag_s * real_b),
            )
            real, imag = by_z[j]
            by_z[j] = (
                real - (real_s * real_d + imag_s * imag_d),
                imag - (real_s * imag_d - imag_s * real_d),
            )
        pairs = [
            (
                real - (real_c * real[n : n + 1] - imag_c * imag[n : n + 1]),
                imag - (real_c * imag[n : n + 1] + imag_c * real[n : n + 1]),
            )
            for real, imag in pairs
        ]
    real_v, imag_v = pairs[0]
    factor = 1.0 / jnp.sqrt(jnp.sum(real_v * real_v + imag_v * imag_v, axis=1, keepdims=True) + EPS)
    return [(real * factor, imag * factor) for real, imag in pairs], sound


def subspace_kernel(
    tm, own, factor, beams_ref, start_ref, flags_ref, ranks_ref, weights_ref, cov_ref, first_ref, across_ref, last_ref, *rest
):
    outs, (high_ref, low_ref, series_ref) = rest[1 : tm + 1], rest[tm + 1 :]
    vectors, width = start_ref.shape[3], start_ref.shape[4]
    rows = last_ref.shape[1]
    tm_index = lax.axis_index("tm")
    beams = weights_ref.shape[2] // 2
    for o in range(own):
        chan = tm_index * own + o
        across = last_ref[o].T
        rotated = rotate(last_ref[o])

        def add_last(part, first):
            right = last_ref[o] if part == 0 else rotated
            term = dot(across[first : first + CHUNK], right, NN)
            at = slice(part * width + first, part * width + first + CHUNK)
            high_ref[at], low_ref[at] = split((cov_ref[o, part, first : first + CHUNK] + term) * factor)

        chunks = [
            functools.partial(add_last, part, first) for part in range(2) for first in range(0, width, CHUNK)
        ]
        last = block_times(start_ref[0, chan, 0], start_ref[0, chan, 1], across, last_ref[o])
        both = (first_ref[o] + last) * factor
        start = orthonormalize(both[:vectors], both[vectors:], chunks)
        rank = flags_ref[chan] * ranks_ref[chan]
        keep = lax.broadcasted_iota(jnp.int32, (vectors, 1), 0) < rank

        def steered_by(real, imag):
            rows_in = jnp.concatenate(split(jnp.concatenate([real, imag], axis=0)), axis=0)
            product = dot(rows_in, weights_ref[o], NN)
            product = product[: 2 * vectors] + product[2 * vectors :]
            return (
                product[:vectors, :beams] - product[vectors:, beams:],
                product[:vectors, beams:] + product[vectors:, :beams],
            )

        def write(real_w, imag_w, early, late):
            series = [early[:, i * rows : (i + 1) * rows] for i in range(tm - 1)] + [late]
            for by, values in zip(steps(tm), series):
                series_ref[tm_index ^ shifted(-by)] = jnp.where(keep, values, 0.0)
            kept = [jnp.where(keep, real_w, 0.0), jnp.where(keep, imag_w, 0.0)]
            for x, out in enumerate(outs):
                values = series_ref[x]
                values = jnp.concatenate([values[:, : rows // 2], values[:, rows // 2 :]], axis=0)
                out[o, :, :beams] = jnp.concatenate(kept, axis=0).astype(BF16)
                out[o, :, beams:] = values.astype(BF16)

        real_q, imag_q = start
        sound = jnp.ones((1, 1), F32)
        for sweep in range(1, ITERS - 1):
            real_z, imag_z = cov_times(real_q, imag_q, high_ref, low_ref)
            ((real_q, imag_q),), now = orthonormalize_by_gram(real_z, imag_z)
            sound = jnp.minimum(sound, now)
        real_z, imag_z = cov_times(real_q, imag_q, high_ref, low_ref)
        riders = [
            steered_by(real_z, imag_z),
            project(real_z, imag_z, across_ref[o]),
            project(real_z, imag_z, across),
        ]
        (unused, steered, early, late), now = orthonormalize_by_gram(real_z, imag_z, riders)
        write(*steered, early[0], late[0])

        @pl.when(jnp.min(jnp.minimum(sound, now)) < 0.5)
        def plainly():
            real, imag = start
            for sweep in range(1, ITERS):
                real, imag = orthonormalize(*cov_times(real, imag, high_ref, low_ref))
            write(
                *steered_by(real, imag),
                project(real, imag, across_ref[o])[0],
                project(real, imag, last_ref[o].T)[0],
            )


def nulled_power(raw, packet_ref, squares):
    rows, half = raw.shape
    samples = rows // 2
    series = packet_ref[:, 2 * half :].astype(F32)
    vectors = series.shape[0] // 2
    series = jnp.concatenate([series[:vectors], series[vectors:]], axis=1)
    left = jnp.concatenate([series, -turned(series, 1)], axis=0).astype(BF16)
    right = packet_ref[:, pl.ds(pl.multiple_of(lax.axis_index("pol") * half, half), half)]
    beam = raw - dot(left, right, TN)
    squares[...] = beam * beam
    return squares[pl.ds(0, samples, 2), :] + squares[pl.ds(1, samples, 2), :]


def power_kernel(own, xs, later_xs, mine_ref, theirs_ref, *rest):
    packets, later = rest[: len(xs)], rest[len(xs) : len(xs) + len(later_xs)]
    power_ref, squares = rest[-2:]
    for x, ref in zip(xs, packets):
        for o in range(own):
            chan = (lax.axis_index("tm") ^ x) * own + o
            power_ref[chan] = nulled_power(mine_ref[chan], ref.at[o], squares)
    for x, ref in zip(later_xs, later):
        for o in range(own):
            chan = (lax.axis_index("tm") ^ x) * own + o
            power_ref[chan] = power_ref[chan] + nulled_power(theirs_ref[chan], ref.at[o], squares)


def last_kernel(own, x, theirs_ref, packet_ref, power_ref, out_ref, powers, squares):
    powers[...] = power_ref[...]
    for o in range(own):
        chan = (lax.axis_index("tm") ^ x) * own + o
        powers[chan] = power_ref[chan] + nulled_power(theirs_ref[chan], packet_ref.at[o], squares)
    channels, samples = powers.shape[:2]
    for chan in range(channels):
        out_ref[pl.ds(chan, samples, channels), :] = powers[chan]


def local(voltages, start_block, flags, ranks, phase_index):
    tm = lax.axis_size("tm")
    tm_index = lax.axis_index("tm")
    samples, chan_dev, width = voltages.shape[0], voltages.shape[2], voltages.shape[4]
    own = chan_dev // tm
    vectors = start_block.shape[3]
    beams = phase_index.shape[0]
    half = beams // 2
    rows = 2 * samples
    factor = 1.0 / (samples * tm)
    params = pltpu.CompilerParams(vmem_limit_bytes=VMEM_LIMIT)
    whole = pl.BlockSpec(memory_space=pltpu.VMEM)
    scalars = pl.BlockSpec(memory_space=pltpu.SMEM)
    unread = pl.BlockSpec(memory_space=pl.ANY)

    def cost(multiplies, moved):
        return pl.CostEstimate(flops=2 * multiplies, bytes_accessed=moved, transcendentals=0)

    by = steps(tm)
    later = pl.pallas_call(
        functools.partial(cut_kernel, own, [by[0], *by[2:]]),
        out_shape=[jax.ShapeDtypeStruct((samples, own, 2, width), BF16)] * (tm - 1),
        in_specs=[pl.BlockSpec(memory_space=pltpu.HBM)],
        out_specs=[whole] * (tm - 1),
        scratch_shapes=[pltpu.SemaphoreType.DMA((tm - 1,))],
        compiler_params=params,
    )(voltages)
    urgent = lax.dynamic_slice_in_dim(voltages[:, 0], shifted(by[1]) * own, own, 1)
    cut = [later[0], urgent, *later[1:]]
    pieces = [piece.transpose(1, 0, 2, 3).reshape(own, rows, width) for piece in cut]
    blocks = pieces[:1] + [
        lax.ppermute(piece, "tm", [(z, (z + by) % tm) for z in range(tm)])
        for by, piece in zip(steps(tm)[1:], pieces[1:])
    ]

    raw = jax.ShapeDtypeStruct((chan_dev, rows, half), F32)
    mine, other = pl.pallas_call(
        functools.partial(raw_beams_kernel, tm, own),
        out_shape=[raw] * 2,
        in_specs=[whole] * (1 + tm),
        out_specs=[whole] * 2,
        scratch_shapes=[pltpu.VMEM((beams, width), BF16)],
        compiler_params=params,
        cost_estimate=cost(4 * chan_dev * samples * width * beams, 8 * chan_dev * samples * width),
    )(phase_index, *pieces)

    own_weights = pl.pallas_call(
        functools.partial(own_weights_kernel, own, chan_dev),
        out_shape=jax.ShapeDtypeStruct((own, width, 2 * beams), BF16),
        in_specs=[whole],
        out_specs=whole,
        scratch_shapes=[pltpu.VMEM((2 * beams, width), BF16)],
        compiler_params=params,
        cost_estimate=cost(20 * own * beams * width, 8 * own * beams * width),
    )(phase_index)

    early = (tm - 1) * rows
    cov, first, across = pl.pallas_call(
        early_kernel,
        out_shape=[
            jax.ShapeDtypeStruct((own, 2, width, width), F32),
            jax.ShapeDtypeStruct((own, 2 * vectors, width), F32),
            jax.ShapeDtypeStruct((own, width, early), BF16),
        ],
        in_specs=[whole] * tm,
        out_specs=[whole] * 3,
        scratch_shapes=[pltpu.VMEM((early, width), BF16)] * 2,
        compiler_params=params,
        cost_estimate=cost(2 * own * early * width * width, 8 * own * width * width),
    )(start_block, *blocks[:-1])

    other, *packets = pl.pallas_call(
        functools.partial(subspace_kernel, tm, own, factor),
        out_shape=[raw] + [jax.ShapeDtypeStruct((own, 2 * vectors, beams + samples), BF16)] * tm,
        in_specs=[unread, whole, scalars, scalars] + [whole] * 5,
        out_specs=[unread] + [whole] * tm,
        input_output_aliases={0: 0},
        scratch_shapes=[pltpu.VMEM((2 * width, width), BF16)] * 2
        + [pltpu.VMEM((tm, vectors, rows), F32)],
        compiler_params=params,
        cost_estimate=cost(32 * own * vectors * tm * samples * width, 8 * own * width * width),
    )(other, start_block, flags, ranks, own_weights, cov, first, across, blocks[-1])

    cores = [(0, 1), (1, 0)]
    theirs = lax.ppermute(other, "pol", cores)
    order = [*range(2, tm), 1]
    arrived = list(packets)
    for x in order:
        arrived[x] = lax.ppermute(packets[x], "tm", [(z, z ^ x) for z in range(tm)])
    swapped = [lax.ppermute(packet, "pol", cores) for packet in arrived]

    shape = jax.ShapeDtypeStruct((chan_dev, samples, half), F32)
    groups = [([0, *order[:-1]], []), (order[-1:], [0, *order[-2::-1]])]
    power = []
    for xs, later_xs in groups:
        used = [arrived[x] for x in xs] + [swapped[x] for x in later_xs]
        power = [
            pl.pallas_call(
                functools.partial(power_kernel, own, xs, later_xs),
                out_shape=shape,
                in_specs=[whole, whole if later_xs else unread] + [whole] * (len(used) + len(power)),
                out_specs=whole,
                input_output_aliases={2 + len(used): 0} if power else {},
                scratch_shapes=[pltpu.VMEM((rows, half), F32)],
                compiler_params=params,
                cost_estimate=cost(len(used) * own * rows * 2 * vectors * half, 8 * own * rows * half),
            )(mine, theirs if later_xs else mine, *used, *power)
        ]

    rows_out = pl.pallas_call(
        functools.partial(last_kernel, own, order[-1]),
        out_shape=jax.ShapeDtypeStruct((samples * chan_dev, half), F32),
        in_specs=[whole] * 3,
        out_specs=whole,
        scratch_shapes=[pltpu.VMEM((chan_dev, samples, half), F32), pltpu.VMEM((rows, half), F32)],
        compiler_params=params,
        cost_estimate=cost(chan_dev * samples * half, 12 * chan_dev * samples * half),
    )(theirs, swapped[order[-1]], *power)
    return rows_out.reshape(samples, chan_dev, half)


def solution(mesh):
    placed = (
        P(("groups", "tm"), "pol", "chan", None, None),
        P("pol", "chan", None, None, None),
        P(("groups", "chan")),
        P(("groups", "chan")),
        P(),
    )
    return jax.shard_map(
        local,
        mesh=mesh,
        in_specs=placed,
        out_specs=P(("groups", "tm"), "chan", "pol"),
        check_vma=False,
    )
```

```python
import functools

import jax
import jax.numpy as jnp
from jax import lax
from jax.experimental import pallas as pl
from jax.experimental.pallas import tpu as pltpu
from jax.sharding import PartitionSpec as P

ITERS = 4
PHASES = 1024
QUARTER = PHASES // 4
EPS = 1e-06
F32 = jnp.float32
BF16 = jnp.bfloat16
NT = (((1,), (1,)), ((), ()))
NN = (((1,), (0,)), ((), ()))
TN = (((0,), (0,)), ((), ()))
VMEM_LIMIT = 48 * 1024 * 1024
CHUNK = 128
LEAST_PIVOT = 1e-4


def dot(left, right, dims):
    return lax.dot_general(left, right, dims, preferred_element_type=F32)


def split(values):
    high = values.astype(BF16)
    low = (values - high.astype(F32)).astype(BF16)
    return high, low


def steer(phase, step, norm):
    turn = (phase * step) & (PHASES - 1)
    quadrant = (turn + QUARTER // 2) // QUARTER
    angle = (turn - quadrant * QUARTER).astype(F32) * (2.0 * jnp.pi / PHASES)
    sq = angle * angle
    sine = angle * (1.0 + sq * (-1.0 / 6 + sq * (1.0 / 120 + sq * (-1.0 / 5040 + sq / 362880))))
    cosine = 1.0 + sq * (-0.5 + sq * (1.0 / 24 + sq * (-1.0 / 720 + sq / 40320)))
    odd = (quadrant & 1) == 1
    real = jnp.where(odd, sine, cosine) * norm
    imag = jnp.where(odd, cosine, sine) * norm
    real = jnp.where(((quadrant + 1) & 2) == 2, -real, real)
    imag = jnp.where((quadrant & 2) == 2, -imag, imag)
    return real.astype(BF16), imag.astype(BF16)


def fill_weights(phase_ref, first, rows, step, out):
    norm = 1.0 / (phase_ref.shape[1] ** 0.5)
    chunk = 32

    def body(i, carry):
        at = pl.multiple_of(i * chunk, chunk)
        real, imag = steer(phase_ref[pl.ds(first + at, chunk), :], step, norm)
        out[pl.ds(at, chunk), :] = real
        out[pl.ds(rows + at, chunk), :] = imag
        return carry

    lax.fori_loop(0, rows // chunk, body, 0)


def steps(tm):
    return [0, *[by for by in reversed(range(1, tm)) if by != tm // 2], tm // 2]


def shifted(by):
    tm = lax.axis_size("tm")
    return lax.rem(lax.axis_index("tm") + tm + by, tm)


def cut_kernel(own, bys, voltages_ref, *rest):
    pieces, done = rest[:-1], rest[-1]
    copies = []
    for i, (by, piece) in enumerate(zip(bys, pieces)):
        channels = pl.ds(shifted(by) * own, own)
        copy = pltpu.make_async_copy(voltages_ref.at[:, 0, channels], piece, done.at[i])
        copy.start()
        copies.append(copy)
    for copy in copies:
        copy.wait()


def turned(values, axis):
    size = values.shape[axis]
    at = lax.broadcasted_iota(jnp.int32, values.shape, axis)
    after = pltpu.roll(values, size - 1, axis)
    before = pltpu.roll(values, 1, axis)
    return jnp.where((at & 1) == 0, after, -before)


def raw_beams_kernel(tm, own, phase_ref, *rest):
    pieces, (mine_ref, other_ref, weights) = rest[:tm], rest[tm:]
    half = phase_ref.shape[0] // 2
    rows = pieces[0].shape[1]
    pol = lax.axis_index("pol")
    start = lax.axis_index("chan") * tm * own
    for by, piece in zip(steps(tm), pieces):
        for o in range(own):
            chan = shifted(by) * own + o
            for swap, out_ref in enumerate((mine_ref, other_ref)):
                first = pl.multiple_of((pol ^ swap) * half, half)
                fill_weights(phase_ref, first, half, start + chan + 1, weights)
                product = dot(piece[o], weights[...], NT)
                by_imag = turned(product[:, half:].reshape(rows // 8, 8, half), 1).reshape(rows, half)
                out_ref[chan] = product[:, :half] - by_imag


def own_weights_kernel(own, chan_dev, phase_ref, out_ref, weights):
    beams = phase_ref.shape[0]
    first = lax.axis_index("chan") * chan_dev + lax.axis_index("tm") * own
    for o in range(own):
        fill_weights(phase_ref, 0, beams, first + o + 1, weights)
        out_ref[o] = weights[...].T


def rotate(x):
    return (-turned(x.astype(F32), 0)).astype(BF16)


def early_kernel(start_ref, *refs):
    blocks, (cov_ref, first_ref, across_ref, along_ref, rotated_ref) = refs[:-5], refs[-5:]
    rows, width = blocks[0].shape[1:]
    own = cov_ref.shape[0]
    for o in range(own):
        for i, block in enumerate(blocks):
            x = block[o]
            at = slice(i * rows, (i + 1) * rows)
            along_ref[at] = x
            rotated_ref[at] = rotate(x)
            across_ref[o, :, at] = x.T
        cov_ref[o, 0] = dot(across_ref[o], along_ref[...], NN)
        cov_ref[o, 1] = dot(across_ref[o], rotated_ref[...], NN)
        chan = lax.axis_index("tm") * own + o
        first_ref[o] = block_times(start_ref[0, chan, 0], start_ref[0, chan, 1], across_ref[o], along_ref[...])


def project(real, imag, across):
    vectors = real.shape[0]
    both = jnp.concatenate(split(jnp.concatenate([real, imag], axis=0)), axis=0)
    product = dot(both, across, NN)
    product = product[: 2 * vectors] + product[2 * vectors :]
    other = turned(product, 1)
    return product[:vectors] + other[vectors:], product[vectors:] - other[:vectors]


def block_times(real, imag, across, along):
    pair = jnp.concatenate(project(real, imag, across), axis=0)
    product = dot(jnp.concatenate(split(pair), axis=0), along, NN)
    return product[: pair.shape[0]] + product[pair.shape[0] :]


def cov_times(real, imag, high_ref, low_ref):
    vectors = real.shape[0]
    rows = jnp.concatenate(
        [jnp.concatenate([real, imag], axis=1), jnp.concatenate([imag, -real], axis=1)], axis=0
    )
    high, low = split(rows)
    product = dot(jnp.concatenate([high, low], axis=0), high_ref[...], NN)
    product = product[: 2 * vectors] + product[2 * vectors :] + dot(high, low_ref[...], NN)
    return product[:vectors], product[vectors:]


def orthonormalize(real_z, imag_z, beside=()):
    beside = list(beside)
    vectors, width = real_z.shape
    row = lax.broadcasted_iota(jnp.int32, (vectors, 1), 0)
    real_v, imag_v = real_z, imag_z
    scale = jnp.zeros((vectors, 1), F32)
    for n in range(vectors):
        real_a = jnp.broadcast_to(real_v[n : n + 1], real_z.shape)
        imag_a = jnp.broadcast_to(imag_v[n : n + 1], real_z.shape)
        norm = jnp.sum(real_a * real_a + imag_a * imag_a, axis=1, keepdims=True) + EPS
        scale = jnp.where(row == n, norm, scale)
        if n + 1 < vectors:
            real_d = jnp.sum(real_a * real_z + imag_a * imag_z, axis=1, keepdims=True)
            imag_d = jnp.sum(real_a * imag_z - imag_a * real_z, axis=1, keepdims=True)
            inverse = jnp.where(row > n, 1.0 / norm, 0.0)
            real_c = real_d * inverse
            imag_c = imag_d * inverse
            real_v = real_v - (real_c * real_a - imag_c * imag_a)
            imag_v = imag_v - (real_c * imag_a + imag_c * real_a)
        for work in beside[n::vectors]:
            work()
    factor = 1.0 / jnp.sqrt(scale)
    return real_v * factor, imag_v * factor


def orthonormalize_by_gram(real_z, imag_z, riders=()):
    vectors = real_z.shape[0]
    row = lax.broadcasted_iota(jnp.int32, (vectors, 1), 0)
    by_z = []
    for n in range(vectors):
        real_a = jnp.broadcast_to(real_z[n : n + 1], real_z.shape)
        imag_a = jnp.broadcast_to(imag_z[n : n + 1], real_z.shape)
        by_z.append(
            (
                jnp.sum(real_a * real_z + imag_a * imag_z, axis=1, keepdims=True),
                jnp.sum(real_a * imag_z - imag_a * real_z, axis=1, keepdims=True),
            )
        )
    by_v = list(by_z)
    whole = [real[n : n + 1] for n, (real, imag) in enumerate(by_z)]
    sound = jnp.ones((1, 1), F32)
    pairs = [(real_z, imag_z), *riders]
    for n in range(vectors - 1):
        (real_d, imag_d), (real_p, imag_p) = by_z[n], by_v[n]
        square = jnp.maximum(real_p[n : n + 1], 0.0)
        fits = (square >= LEAST_PIVOT * whole[n]) & (square <= 4.0 * whole[n])
        sound = jnp.where(fits, sound, 0.0)
        inverse = jnp.where(row > n, 1.0 / (square + EPS), 0.0)
        real_c, imag_c = real_d * inverse, imag_d * inverse
        real_b, imag_b = real_p - real_c * square, imag_p - imag_c * square
        for j in range(n + 1, vectors):
            real_s, imag_s = real_c[j : j + 1], imag_c[j : j + 1]
            real_q, imag_q = real_p[j : j + 1], -imag_p[j : j + 1]
            real, imag = by_v[j]
            by_v[j] = (
                real - (real_c * real_q - imag_c * imag_q) - (real_s * real_b + imag_s * imag_b),
                imag - (real_c * imag_q + imag_c * real_q) - (real_s * imag_b - imag_s * real_b),
            )
            real, imag = by_z[j]
            by_z[j] = (
                real - (real_s * real_d + imag_s * imag_d),
                imag - (real_s * imag_d - imag_s * real_d),
            )
        pairs = [
            (
                real - (real_c * real[n : n + 1] - imag_c * imag[n : n + 1]),
                imag - (real_c * imag[n : n + 1] + imag_c * real[n : n + 1]),
            )
            for real, imag in pairs
        ]
    real_v, imag_v = pairs[0]
    factor = 1.0 / jnp.sqrt(jnp.sum(real_v * real_v + imag_v * imag_v, axis=1, keepdims=True) + EPS)
    return [(real * factor, imag * factor) for real, imag in pairs], sound


def subspace_kernel(
    tm, own, factor, beams_ref, start_ref, flags_ref, ranks_ref, weights_ref, cov_ref, first_ref, across_ref, last_ref, *rest
):
    outs, (high_ref, low_ref, series_ref) = rest[1 : tm + 1], rest[tm + 1 :]
    vectors, width = start_ref.shape[3], start_ref.shape[4]
    rows = last_ref.shape[1]
    tm_index = lax.axis_index("tm")
    beams = weights_ref.shape[2] // 2
    for o in range(own):
        chan = tm_index * own + o
        across = last_ref[o].T
        rotated = rotate(last_ref[o])

        def add_last(part, first):
            right = last_ref[o] if part == 0 else rotated
            term = dot(across[first : first + CHUNK], right, NN)
            at = slice(part * width + first, part * width + first + CHUNK)
            high_ref[at], low_ref[at] = split((cov_ref[o, part, first : first + CHUNK] + term) * factor)

        chunks = [
            functools.partial(add_last, part, first) for part in range(2) for first in range(0, width, CHUNK)
        ]
        last = block_times(start_ref[0, chan, 0], start_ref[0, chan, 1], across, last_ref[o])
        both = (first_ref[o] + last) * factor
        start = orthonormalize(both[:vectors], both[vectors:], chunks)
        rank = flags_ref[chan] * ranks_ref[chan]
        keep = lax.broadcasted_iota(jnp.int32, (vectors, 1), 0) < rank

        def steered_by(real, imag):
            rows_in = jnp.concatenate(split(jnp.concatenate([real, imag], axis=0)), axis=0)
            product = dot(rows_in, weights_ref[o], NN)
            product = product[: 2 * vectors] + product[2 * vectors :]
            return (
                product[:vectors, :beams] - product[vectors:, beams:],
                product[:vectors, beams:] + product[vectors:, :beams],
            )

        def write(real_w, imag_w, early, late):
            series = [early[:, i * rows : (i + 1) * rows] for i in range(tm - 1)] + [late]
            for by, values in zip(steps(tm), series):
                series_ref[tm_index ^ shifted(-by)] = jnp.where(keep, values, 0.0)
            kept = [jnp.where(keep, real_w, 0.0), jnp.where(keep, imag_w, 0.0)]
            for x, out in enumerate(outs):
                values = series_ref[x]
                values = jnp.concatenate([values[:, : rows // 2], values[:, rows // 2 :]], axis=0)
                out[o, :, :beams] = jnp.concatenate(kept, axis=0).astype(BF16)
                out[o, :, beams:] = values.astype(BF16)

        real_q, imag_q = start
        sound = jnp.ones((1, 1), F32)
        for sweep in range(1, ITERS - 1):
            real_z, imag_z = cov_times(real_q, imag_q, high_ref, low_ref)
            ((real_q, imag_q),), now = orthonormalize_by_gram(real_z, imag_z)
            sound = jnp.minimum(sound, now)
        real_z, imag_z = cov_times(real_q, imag_q, high_ref, low_ref)
        riders = [
            steered_by(real_z, imag_z),
            project(real_z, imag_z, across_ref[o]),
            project(real_z, imag_z, across),
        ]
        (unused, steered, early, late), now = orthonormalize_by_gram(real_z, imag_z, riders)
        write(*steered, early[0], late[0])

        @pl.when(jnp.min(jnp.minimum(sound, now)) < 0.5)
        def plainly():
            real, imag = start
            for sweep in range(1, ITERS):
                real, imag = orthonormalize(*cov_times(real, imag, high_ref, low_ref))
            write(
                *steered_by(real, imag),
                project(real, imag, across_ref[o])[0],
                project(real, imag, last_ref[o].T)[0],
            )


def nulled_power(raw, packet_ref, squares):
    rows, half = raw.shape
    samples = rows // 2
    series = packet_ref[:, 2 * half :].astype(F32)
    vectors = series.shape[0] // 2
    series = jnp.concatenate([series[:vectors], series[vectors:]], axis=1)
    left = jnp.concatenate([series, -turned(series, 1)], axis=0).astype(BF16)
    right = packet_ref[:, pl.ds(pl.multiple_of(lax.axis_index("pol") * half, half), half)]
    beam = raw - dot(left, right, TN)
    squares[...] = beam * beam
    return squares[pl.ds(0, samples, 2), :] + squares[pl.ds(1, samples, 2), :]


def power_kernel(own, xs, later_xs, mine_ref, theirs_ref, *rest):
    packets, later = rest[: len(xs)], rest[len(xs) : len(xs) + len(later_xs)]
    power_ref, squares = rest[-2:]
    for x, ref in zip(xs, packets):
        for o in range(own):
            chan = (lax.axis_index("tm") ^ x) * own + o
            power_ref[chan] = nulled_power(mine_ref[chan], ref.at[o], squares)
    for x, ref in zip(later_xs, later):
        for o in range(own):
            chan = (lax.axis_index("tm") ^ x) * own + o
            power_ref[chan] = power_ref[chan] + nulled_power(theirs_ref[chan], ref.at[o], squares)


def last_kernel(own, x, theirs_ref, packet_ref, power_ref, out_ref, powers, squares):
    powers[...] = power_ref[...]
    for o in range(own):
        chan = (lax.axis_index("tm") ^ x) * own + o
        powers[chan] = power_ref[chan] + nulled_power(theirs_ref[chan], packet_ref.at[o], squares)
    channels, samples = powers.shape[:2]
    for chan in range(channels):
        out_ref[pl.ds(chan, samples, channels), :] = powers[chan]


def local(voltages, start_block, flags, ranks, phase_index):
    tm = lax.axis_size("tm")
    tm_index = lax.axis_index("tm")
    samples, chan_dev, width = voltages.shape[0], voltages.shape[2], voltages.shape[4]
    own = chan_dev // tm
    vectors = start_block.shape[3]
    beams = phase_index.shape[0]
    half = beams // 2
    rows = 2 * samples
    factor = 1.0 / (samples * tm)
    params = pltpu.CompilerParams(vmem_limit_bytes=VMEM_LIMIT)
    whole = pl.BlockSpec(memory_space=pltpu.VMEM)
    scalars = pl.BlockSpec(memory_space=pltpu.SMEM)
    unread = pl.BlockSpec(memory_space=pl.ANY)

    def cost(multiplies, moved):
        return pl.CostEstimate(flops=2 * multiplies, bytes_accessed=moved, transcendentals=0)

    by = steps(tm)
    later = pl.pallas_call(
        functools.partial(cut_kernel, own, [by[0], *by[2:]]),
        out_shape=[jax.ShapeDtypeStruct((samples, own, 2, width), BF16)] * (tm - 1),
        in_specs=[pl.BlockSpec(memory_space=pltpu.HBM)],
        out_specs=[whole] * (tm - 1),
        scratch_shapes=[pltpu.SemaphoreType.DMA((tm - 1,))],
        compiler_params=params,
    )(voltages)
    urgent = lax.dynamic_slice_in_dim(voltages[:, 0], shifted(by[1]) * own, own, 1)
    cut = [later[0], urgent, *later[1:]]
    pieces = [piece.transpose(1, 0, 2, 3).reshape(own, rows, width) for piece in cut]
    blocks = pieces[:1] + [
        lax.ppermute(piece, "tm", [(z, (z + by) % tm) for z in range(tm)])
        for by, piece in zip(steps(tm)[1:], pieces[1:])
    ]

    raw = jax.ShapeDtypeStruct((chan_dev, rows, half), F32)
    mine, other = pl.pallas_call(
        functools.partial(raw_beams_kernel, tm, own),
        out_shape=[raw] * 2,
        in_specs=[whole] * (1 + tm),
        out_specs=[whole] * 2,
        scratch_shapes=[pltpu.VMEM((beams, width), BF16)],
        compiler_params=params,
        cost_estimate=cost(4 * chan_dev * samples * width * beams, 8 * chan_dev * samples * width),
    )(phase_index, *pieces)

    own_weights = pl.pallas_call(
        functools.partial(own_weights_kernel, own, chan_dev),
        out_shape=jax.ShapeDtypeStruct((own, width, 2 * beams), BF16),
        in_specs=[whole],
        out_specs=whole,
        scratch_shapes=[pltpu.VMEM((2 * beams, width), BF16)],
        compiler_params=params,
        cost_estimate=cost(20 * own * beams * width, 8 * own * beams * width),
    )(phase_index)

    early = (tm - 1) * rows
    cov, first, across = pl.pallas_call(
        early_kernel,
        out_shape=[
            jax.ShapeDtypeStruct((own, 2, width, width), F32),
            jax.ShapeDtypeStruct((own, 2 * vectors, width), F32),
            jax.ShapeDtypeStruct((own, width, early), BF16),
        ],
        in_specs=[whole] * tm,
        out_specs=[whole] * 3,
        scratch_shapes=[pltpu.VMEM((early, width), BF16)] * 2,
        compiler_params=params,
        cost_estimate=cost(2 * own * early * width * width, 8 * own * width * width),
    )(start_block, *blocks[:-1])

    other, *packets = pl.pallas_call(
        functools.partial(subspace_kernel, tm, own, factor),
        out_shape=[raw] + [jax.ShapeDtypeStruct((own, 2 * vectors, beams + samples), BF16)] * tm,
        in_specs=[unread, whole, scalars, scalars] + [whole] * 5,
        out_specs=[unread] + [whole] * tm,
        input_output_aliases={0: 0},
        scratch_shapes=[pltpu.VMEM((2 * width, width), BF16)] * 2
        + [pltpu.VMEM((tm, vectors, rows), F32)],
        compiler_params=params,
        cost_estimate=cost(32 * own * vectors * tm * samples * width, 8 * own * width * width),
    )(other, start_block, flags, ranks, own_weights, cov, first, across, blocks[-1])

    cores = [(0, 1), (1, 0)]
    theirs = lax.ppermute(other, "pol", cores)
    order = [*reversed(range(1, tm))]
    arrived = list(packets)
    for x in order:
        arrived[x] = lax.ppermute(packets[x], "tm", [(z, z ^ x) for z in range(tm)])
    swapped = [lax.ppermute(packet, "pol", cores) for packet in arrived]

    shape = jax.ShapeDtypeStruct((chan_dev, samples, half), F32)
    groups = [([0, *order[:-1]], []), (order[-1:], [0, *order[-2::-1]])]
    power = []
    for xs, later_xs in groups:
        used = [arrived[x] for x in xs] + [swapped[x] for x in later_xs]
        power = [
            pl.pallas_call(
                functools.partial(power_kernel, own, xs, later_xs),
                out_shape=shape,
                in_specs=[whole, whole if later_xs else unread] + [whole] * (len(used) + len(power)),
                out_specs=whole,
                input_output_aliases={2 + len(used): 0} if power else {},
                scratch_shapes=[pltpu.VMEM((rows, half), F32)],
                compiler_params=params,
                cost_estimate=cost(len(used) * own * rows * 2 * vectors * half, 8 * own * rows * half),
            )(mine, theirs if later_xs else mine, *used, *power)
        ]

    rows_out = pl.pallas_call(
        functools.partial(last_kernel, own, order[-1]),
        out_shape=jax.ShapeDtypeStruct((samples * chan_dev, half), F32),
        in_specs=[whole] * 3,
        out_specs=whole,
        scratch_shapes=[pltpu.VMEM((chan_dev, samples, half), F32), pltpu.VMEM((rows, half), F32)],
        compiler_params=params,
        cost_estimate=cost(chan_dev * samples * half, 12 * chan_dev * samples * half),
    )(theirs, swapped[order[-1]], *power)
    return rows_out.reshape(samples, chan_dev, half)


def solution(mesh):
    placed = (
        P(("groups", "tm"), "pol", "chan", None, None),
        P("pol", "chan", None, None, None),
        P(("groups", "chan")),
        P(("groups", "chan")),
        P(),
    )
    return jax.shard_map(
        local,
        mesh=mesh,
        in_specs=placed,
        out_specs=P(("groups", "tm"), "chan", "pol"),
        check_vma=False,
    )
```

```python
import functools

import jax
import jax.numpy as jnp
from jax import lax
from jax.experimental import pallas as pl
from jax.experimental.pallas import tpu as pltpu
from jax.sharding import PartitionSpec as P

ITERS = 4
PHASES = 1024
QUARTER = PHASES // 4
EPS = 1e-06
F32 = jnp.float32
BF16 = jnp.bfloat16
NT = (((1,), (1,)), ((), ()))
NN = (((1,), (0,)), ((), ()))
TN = (((0,), (0,)), ((), ()))
VMEM_LIMIT = 48 * 1024 * 1024
CHUNK = 256
LEAST_PIVOT = 1e-4


def dot(left, right, dims):
    return lax.dot_general(left, right, dims, preferred_element_type=F32)


def split(values):
    high = values.astype(BF16)
    low = (values - high.astype(F32)).astype(BF16)
    return high, low


def steer(phase, step, norm):
    turn = (phase * step) & (PHASES - 1)
    quadrant = (turn + QUARTER // 2) // QUARTER
    angle = (turn - quadrant * QUARTER).astype(F32) * (2.0 * jnp.pi / PHASES)
    sq = angle * angle
    sine = angle * (1.0 + sq * (-1.0 / 6 + sq * (1.0 / 120 + sq * (-1.0 / 5040 + sq / 362880))))
    cosine = 1.0 + sq * (-0.5 + sq * (1.0 / 24 + sq * (-1.0 / 720 + sq / 40320)))
    odd = (quadrant & 1) == 1
    real = jnp.where(odd, sine, cosine) * norm
    imag = jnp.where(odd, cosine, sine) * norm
    real = jnp.where(((quadrant + 1) & 2) == 2, -real, real)
    imag = jnp.where((quadrant & 2) == 2, -imag, imag)
    return real.astype(BF16), imag.astype(BF16)


def fill_weights(phase_ref, first, rows, step, out):
    norm = 1.0 / (phase_ref.shape[1] ** 0.5)
    chunk = 32

    def body(i, carry):
        at = pl.multiple_of(i * chunk, chunk)
        real, imag = steer(phase_ref[pl.ds(first + at, chunk), :], step, norm)
        out[pl.ds(at, chunk), :] = real
        out[pl.ds(rows + at, chunk), :] = imag
        return carry

    lax.fori_loop(0, rows // chunk, body, 0)


def steps(tm):
    return [0, *[by for by in range(1, tm) if by != tm // 2], tm // 2]


def shifted(by):
    tm = lax.axis_size("tm")
    return lax.rem(lax.axis_index("tm") + tm + by, tm)


def cut_kernel(own, bys, voltages_ref, *rest):
    pieces, done = rest[:-1], rest[-1]
    copies = []
    for i, (by, piece) in enumerate(zip(bys, pieces)):
        channels = pl.ds(shifted(by) * own, own)
        copy = pltpu.make_async_copy(voltages_ref.at[:, 0, channels], piece, done.at[i])
        copy.start()
        copies.append(copy)
    for copy in copies:
        copy.wait()


def turned(values, axis):
    size = values.shape[axis]
    at = lax.broadcasted_iota(jnp.int32, values.shape, axis)
    after = pltpu.roll(values, size - 1, axis)
    before = pltpu.roll(values, 1, axis)
    return jnp.where((at & 1) == 0, after, -before)


def raw_beams_kernel(tm, own, phase_ref, *rest):
    pieces, (mine_ref, other_ref, weights) = rest[:tm], rest[tm:]
    half = phase_ref.shape[0] // 2
    rows = pieces[0].shape[1]
    pol = lax.axis_index("pol")
    start = lax.axis_index("chan") * tm * own
    for by, piece in zip(steps(tm), pieces):
        for o in range(own):
            chan = shifted(by) * own + o
            for swap, out_ref in enumerate((mine_ref, other_ref)):
                first = pl.multiple_of((pol ^ swap) * half, half)
                fill_weights(phase_ref, first, half, start + chan + 1, weights)
                product = dot(piece[o], weights[...], NT)
                by_imag = turned(product[:, half:].reshape(rows // 8, 8, half), 1).reshape(rows, half)
                out_ref[chan] = product[:, :half] - by_imag


def own_weights_kernel(own, chan_dev, phase_ref, out_ref, weights):
    beams = phase_ref.shape[0]
    first = lax.axis_index("chan") * chan_dev + lax.axis_index("tm") * own
    for o in range(own):
        fill_weights(phase_ref, 0, beams, first + o + 1, weights)
        out_ref[o] = weights[...].T


def rotate(x):
    return (-turned(x.astype(F32), 0)).astype(BF16)


def early_kernel(start_ref, *refs):
    blocks, (cov_ref, first_ref, across_ref, along_ref, rotated_ref) = refs[:-5], refs[-5:]
    rows, width = blocks[0].shape[1:]
    own = cov_ref.shape[0]
    for o in range(own):
        for i, block in enumerate(blocks):
            x = block[o]
            at = slice(i * rows, (i + 1) * rows)
            along_ref[at] = x
            rotated_ref[at] = rotate(x)
            across_ref[o, :, at] = x.T
        cov_ref[o, 0] = dot(across_ref[o], along_ref[...], NN)
        cov_ref[o, 1] = dot(across_ref[o], rotated_ref[...], NN)
        chan = lax.axis_index("tm") * own + o
        first_ref[o] = block_times(start_ref[0, chan, 0], start_ref[0, chan, 1], across_ref[o], along_ref[...])


def project(real, imag, across):
    vectors = real.shape[0]
    both = jnp.concatenate(split(jnp.concatenate([real, imag], axis=0)), axis=0)
    product = dot(both, across, NN)
    product = product[: 2 * vectors] + product[2 * vectors :]
    other = turned(product, 1)
    return product[:vectors] + other[vectors:], product[vectors:] - other[:vectors]


def block_times(real, imag, across, along):
    pair = jnp.concatenate(project(real, imag, across), axis=0)
    product = dot(jnp.concatenate(split(pair), axis=0), along, NN)
    return product[: pair.shape[0]] + product[pair.shape[0] :]


def cov_times(real, imag, high_ref, low_ref):
    vectors = real.shape[0]
    rows = jnp.concatenate(
        [jnp.concatenate([real, imag], axis=1), jnp.concatenate([imag, -real], axis=1)], axis=0
    )
    high, low = split(rows)
    product = dot(jnp.concatenate([high, low], axis=0), high_ref[...], NN)
    product = product[: 2 * vectors] + product[2 * vectors :] + dot(high, low_ref[...], NN)
    return product[:vectors], product[vectors:]


def orthonormalize(real_z, imag_z, beside=()):
    beside = list(beside)
    vectors, width = real_z.shape
    row = lax.broadcasted_iota(jnp.int32, (vectors, 1), 0)
    real_v, imag_v = real_z, imag_z
    scale = jnp.zeros((vectors, 1), F32)
    for n in range(vectors):
        real_a = jnp.broadcast_to(real_v[n : n + 1], real_z.shape)
        imag_a = jnp.broadcast_to(imag_v[n : n + 1], real_z.shape)
        norm = jnp.sum(real_a * real_a + imag_a * imag_a, axis=1, keepdims=True) + EPS
        scale = jnp.where(row == n, norm, scale)
        if n + 1 < vectors:
            real_d = jnp.sum(real_a * real_z + imag_a * imag_z, axis=1, keepdims=True)
            imag_d = jnp.sum(real_a * imag_z - imag_a * real_z, axis=1, keepdims=True)
            inverse = jnp.where(row > n, 1.0 / norm, 0.0)
            real_c = real_d * inverse
            imag_c = imag_d * inverse
            real_v = real_v - (real_c * real_a - imag_c * imag_a)
            imag_v = imag_v - (real_c * imag_a + imag_c * real_a)
        for work in beside[n::vectors]:
            work()
    factor = 1.0 / jnp.sqrt(scale)
    return real_v * factor, imag_v * factor


def orthonormalize_by_gram(real_z, imag_z, riders=()):
    vectors = real_z.shape[0]
    row = lax.broadcasted_iota(jnp.int32, (vectors, 1), 0)
    by_z = []
    for n in range(vectors):
        real_a = jnp.broadcast_to(real_z[n : n + 1], real_z.shape)
        imag_a = jnp.broadcast_to(imag_z[n : n + 1], real_z.shape)
        by_z.append(
            (
                jnp.sum(real_a * real_z + imag_a * imag_z, axis=1, keepdims=True),
                jnp.sum(real_a * imag_z - imag_a * real_z, axis=1, keepdims=True),
            )
        )
    by_v = list(by_z)
    whole = [real[n : n + 1] for n, (real, imag) in enumerate(by_z)]
    sound = jnp.ones((1, 1), F32)
    pairs = [(real_z, imag_z), *riders]
    for n in range(vectors - 1):
        (real_d, imag_d), (real_p, imag_p) = by_z[n], by_v[n]
        square = jnp.maximum(real_p[n : n + 1], 0.0)
        fits = (square >= LEAST_PIVOT * whole[n]) & (square <= 4.0 * whole[n])
        sound = jnp.where(fits, sound, 0.0)
        inverse = jnp.where(row > n, 1.0 / (square + EPS), 0.0)
        real_c, imag_c = real_d * inverse, imag_d * inverse
        real_b, imag_b = real_p - real_c * square, imag_p - imag_c * square
        for j in range(n + 1, vectors):
            real_s, imag_s = real_c[j : j + 1], imag_c[j : j + 1]
            real_q, imag_q = real_p[j : j + 1], -imag_p[j : j + 1]
            real, imag = by_v[j]
            by_v[j] = (
                real - (real_c * real_q - imag_c * imag_q) - (real_s * real_b + imag_s * imag_b),
                imag - (real_c * imag_q + imag_c * real_q) - (real_s * imag_b - imag_s * real_b),
            )
            real, imag = by_z[j]
            by_z[j] = (
                real - (real_s * real_d + imag_s * imag_d),
                imag - (real_s * imag_d - imag_s * real_d),
            )
        pairs = [
            (
                real - (real_c * real[n : n + 1] - imag_c * imag[n : n + 1]),
                imag - (real_c * imag[n : n + 1] + imag_c * real[n : n + 1]),
            )
            for real, imag in pairs
        ]
    real_v, imag_v = pairs[0]
    factor = 1.0 / jnp.sqrt(jnp.sum(real_v * real_v + imag_v * imag_v, axis=1, keepdims=True) + EPS)
    return [(real * factor, imag * factor) for real, imag in pairs], sound


def subspace_kernel(
    tm, own, factor, beams_ref, start_ref, flags_ref, ranks_ref, weights_ref, cov_ref, first_ref, across_ref, last_ref, *rest
):
    outs, (high_ref, low_ref, series_ref) = rest[1 : tm + 1], rest[tm + 1 :]
    vectors, width = start_ref.shape[3], start_ref.shape[4]
    rows = last_ref.shape[1]
    tm_index = lax.axis_index("tm")
    beams = weights_ref.shape[2] // 2
    for o in range(own):
        chan = tm_index * own + o
        across = last_ref[o].T
        rotated = rotate(last_ref[o])

        def add_last(part, first):
            right = last_ref[o] if part == 0 else rotated
            term = dot(across[first : first + CHUNK], right, NN)
            at = slice(part * width + first, part * width + first + CHUNK)
            high_ref[at], low_ref[at] = split((cov_ref[o, part, first : first + CHUNK] + term) * factor)

        chunks = [
            functools.partial(add_last, part, first) for part in range(2) for first in range(0, width, CHUNK)
        ]
        last = block_times(start_ref[0, chan, 0], start_ref[0, chan, 1], across, last_ref[o])
        both = (first_ref[o] + last) * factor
        start = orthonormalize(both[:vectors], both[vectors:], chunks)
        rank = flags_ref[chan] * ranks_ref[chan]
        keep = lax.broadcasted_iota(jnp.int32, (vectors, 1), 0) < rank

        def steered_by(real, imag):
            rows_in = jnp.concatenate(split(jnp.concatenate([real, imag], axis=0)), axis=0)
            product = dot(rows_in, weights_ref[o], NN)
            product = product[: 2 * vectors] + product[2 * vectors :]
            return (
                product[:vectors, :beams] - product[vectors:, beams:],
                product[:vectors, beams:] + product[vectors:, :beams],
            )

        def write(real_w, imag_w, early, late):
            series = [early[:, i * rows : (i + 1) * rows] for i in range(tm - 1)] + [late]
            for by, values in zip(steps(tm), series):
                series_ref[tm_index ^ shifted(-by)] = jnp.where(keep, values, 0.0)
            kept = [jnp.where(keep, real_w, 0.0), jnp.where(keep, imag_w, 0.0)]
            for x, out in enumerate(outs):
                values = series_ref[x]
                values = jnp.concatenate([values[:, : rows // 2], values[:, rows // 2 :]], axis=0)
                out[o, :, :beams] = jnp.concatenate(kept, axis=0).astype(BF16)
                out[o, :, beams:] = values.astype(BF16)

        real_q, imag_q = start
        sound = jnp.ones((1, 1), F32)
        for sweep in range(1, ITERS - 1):
            real_z, imag_z = cov_times(real_q, imag_q, high_ref, low_ref)
            ((real_q, imag_q),), now = orthonormalize_by_gram(real_z, imag_z)
            sound = jnp.minimum(sound, now)
        real_z, imag_z = cov_times(real_q, imag_q, high_ref, low_ref)
        riders = [
            steered_by(real_z, imag_z),
            project(real_z, imag_z, across_ref[o]),
            project(real_z, imag_z, across),
        ]
        (unused, steered, early, late), now = orthonormalize_by_gram(real_z, imag_z, riders)
        write(*steered, early[0], late[0])

        @pl.when(jnp.min(jnp.minimum(sound, now)) < 0.5)
        def plainly():
            real, imag = start
            for sweep in range(1, ITERS):
                real, imag = orthonormalize(*cov_times(real, imag, high_ref, low_ref))
            write(
                *steered_by(real, imag),
                project(real, imag, across_ref[o])[0],
                project(real, imag, last_ref[o].T)[0],
            )


def nulled_power(raw, packet_ref, squares):
    rows, half = raw.shape
    samples = rows // 2
    series = packet_ref[:, 2 * half :].astype(F32)
    vectors = series.shape[0] // 2
    series = jnp.concatenate([series[:vectors], series[vectors:]], axis=1)
    left = jnp.concatenate([series, -turned(series, 1)], axis=0).astype(BF16)
    right = packet_ref[:, pl.ds(pl.multiple_of(lax.axis_index("pol") * half, half), half)]
    beam = raw - dot(left, right, TN)
    squares[...] = beam * beam
    return squares[pl.ds(0, samples, 2), :] + squares[pl.ds(1, samples, 2), :]


def power_kernel(own, xs, later_xs, mine_ref, theirs_ref, *rest):
    packets, later = rest[: len(xs)], rest[len(xs) : len(xs) + len(later_xs)]
    power_ref, squares = rest[-2:]
    for x, ref in zip(xs, packets):
        for o in range(own):
            chan = (lax.axis_index("tm") ^ x) * own + o
            power_ref[chan] = nulled_power(mine_ref[chan], ref.at[o], squares)
    for x, ref in zip(later_xs, later):
        for o in range(own):
            chan = (lax.axis_index("tm") ^ x) * own + o
            power_ref[chan] = power_ref[chan] + nulled_power(theirs_ref[chan], ref.at[o], squares)


def last_kernel(own, x, theirs_ref, packet_ref, power_ref, out_ref, powers, squares):
    powers[...] = power_ref[...]
    for o in range(own):
        chan = (lax.axis_index("tm") ^ x) * own + o
        powers[chan] = power_ref[chan] + nulled_power(theirs_ref[chan], packet_ref.at[o], squares)
    channels, samples = powers.shape[:2]
    for chan in range(channels):
        out_ref[pl.ds(chan, samples, channels), :] = powers[chan]


def local(voltages, start_block, flags, ranks, phase_index):
    tm = lax.axis_size("tm")
    tm_index = lax.axis_index("tm")
    samples, chan_dev, width = voltages.shape[0], voltages.shape[2], voltages.shape[4]
    own = chan_dev // tm
    vectors = start_block.shape[3]
    beams = phase_index.shape[0]
    half = beams // 2
    rows = 2 * samples
    factor = 1.0 / (samples * tm)
    params = pltpu.CompilerParams(vmem_limit_bytes=VMEM_LIMIT)
    whole = pl.BlockSpec(memory_space=pltpu.VMEM)
    scalars = pl.BlockSpec(memory_space=pltpu.SMEM)
    unread = pl.BlockSpec(memory_space=pl.ANY)

    def cost(multiplies, moved):
        return pl.CostEstimate(flops=2 * multiplies, bytes_accessed=moved, transcendentals=0)

    by = steps(tm)
    later = pl.pallas_call(
        functools.partial(cut_kernel, own, [by[0], *by[2:]]),
        out_shape=[jax.ShapeDtypeStruct((samples, own, 2, width), BF16)] * (tm - 1),
        in_specs=[pl.BlockSpec(memory_space=pltpu.HBM)],
        out_specs=[whole] * (tm - 1),
        scratch_shapes=[pltpu.SemaphoreType.DMA((tm - 1,))],
        compiler_params=params,
    )(voltages)
    urgent = lax.dynamic_slice_in_dim(voltages[:, 0], shifted(by[1]) * own, own, 1)
    cut = [later[0], urgent, *later[1:]]
    pieces = [piece.transpose(1, 0, 2, 3).reshape(own, rows, width) for piece in cut]
    blocks = pieces[:1] + [
        lax.ppermute(piece, "tm", [(z, (z + by) % tm) for z in range(tm)])
        for by, piece in zip(steps(tm)[1:], pieces[1:])
    ]

    raw = jax.ShapeDtypeStruct((chan_dev, rows, half), F32)
    mine, other = pl.pallas_call(
        functools.partial(raw_beams_kernel, tm, own),
        out_shape=[raw] * 2,
        in_specs=[whole] * (1 + tm),
        out_specs=[whole] * 2,
        scratch_shapes=[pltpu.VMEM((beams, width), BF16)],
        compiler_params=params,
        cost_estimate=cost(4 * chan_dev * samples * width * beams, 8 * chan_dev * samples * width),
    )(phase_index, *pieces)

    own_weights = pl.pallas_call(
        functools.partial(own_weights_kernel, own, chan_dev),
        out_shape=jax.ShapeDtypeStruct((own, width, 2 * beams), BF16),
        in_specs=[whole],
        out_specs=whole,
        scratch_shapes=[pltpu.VMEM((2 * beams, width), BF16)],
        compiler_params=params,
        cost_estimate=cost(20 * own * beams * width, 8 * own * beams * width),
    )(phase_index)

    early = (tm - 1) * rows
    cov, first, across = pl.pallas_call(
        early_kernel,
        out_shape=[
            jax.ShapeDtypeStruct((own, 2, width, width), F32),
            jax.ShapeDtypeStruct((own, 2 * vectors, width), F32),
            jax.ShapeDtypeStruct((own, width, early), BF16),
        ],
        in_specs=[whole] * tm,
        out_specs=[whole] * 3,
        scratch_shapes=[pltpu.VMEM((early, width), BF16)] * 2,
        compiler_params=params,
        cost_estimate=cost(2 * own * early * width * width, 8 * own * width * width),
    )(start_block, *blocks[:-1])

    other, *packets = pl.pallas_call(
        functools.partial(subspace_kernel, tm, own, factor),
        out_shape=[raw] + [jax.ShapeDtypeStruct((own, 2 * vectors, beams + samples), BF16)] * tm,
        in_specs=[unread, whole, scalars, scalars] + [whole] * 5,
        out_specs=[unread] + [whole] * tm,
        input_output_aliases={0: 0},
        scratch_shapes=[pltpu.VMEM((2 * width, width), BF16)] * 2
        + [pltpu.VMEM((tm, vectors, rows), F32)],
        compiler_params=params,
        cost_estimate=cost(32 * own * vectors * tm * samples * width, 8 * own * width * width),
    )(other, start_block, flags, ranks, own_weights, cov, first, across, blocks[-1])

    cores = [(0, 1), (1, 0)]
    theirs = lax.ppermute(other, "pol", cores)
    order = [*range(2, tm), 1]
    arrived = list(packets)
    for x in order:
        arrived[x] = lax.ppermute(packets[x], "tm", [(z, z ^ x) for z in range(tm)])
    swapped = [lax.ppermute(packet, "pol", cores) for packet in arrived]

    shape = jax.ShapeDtypeStruct((chan_dev, samples, half), F32)
    groups = [([0, *order[:-1]], []), (order[-1:], [0, *order[-2::-1]])]
    power = []
    for xs, later_xs in groups:
        used = [arrived[x] for x in xs] + [swapped[x] for x in later_xs]
        power = [
            pl.pallas_call(
                functools.partial(power_kernel, own, xs, later_xs),
                out_shape=shape,
                in_specs=[whole, whole if later_xs else unread] + [whole] * (len(used) + len(power)),
                out_specs=whole,
                input_output_aliases={2 + len(used): 0} if power else {},
                scratch_shapes=[pltpu.VMEM((rows, half), F32)],
                compiler_params=params,
                cost_estimate=cost(len(used) * own * rows * 2 * vectors * half, 8 * own * rows * half),
            )(mine, theirs if later_xs else mine, *used, *power)
        ]

    rows_out = pl.pallas_call(
        functools.partial(last_kernel, own, order[-1]),
        out_shape=jax.ShapeDtypeStruct((samples * chan_dev, half), F32),
        in_specs=[whole] * 3,
        out_specs=whole,
        scratch_shapes=[pltpu.VMEM((chan_dev, samples, half), F32), pltpu.VMEM((rows, half), F32)],
        compiler_params=params,
        cost_estimate=cost(chan_dev * samples * half, 12 * chan_dev * samples * half),
    )(theirs, swapped[order[-1]], *power)
    return rows_out.reshape(samples, chan_dev, half)


def solution(mesh):
    placed = (
        P(("groups", "tm"), "pol", "chan", None, None),
        P("pol", "chan", None, None, None),
        P(("groups", "chan")),
        P(("groups", "chan")),
        P(),
    )
    return jax.shard_map(
        local,
        mesh=mesh,
        in_specs=placed,
        out_specs=P(("groups", "tm"), "chan", "pol"),
        check_vma=False,
    )
```

```python
import functools

import jax
import jax.numpy as jnp
from jax import lax
from jax.experimental import pallas as pl
from jax.experimental.pallas import tpu as pltpu
from jax.sharding import PartitionSpec as P

ITERS = 4
PHASES = 1024
QUARTER = PHASES // 4
EPS = 1e-06
F32 = jnp.float32
BF16 = jnp.bfloat16
NT = (((1,), (1,)), ((), ()))
NN = (((1,), (0,)), ((), ()))
TN = (((0,), (0,)), ((), ()))
VMEM_LIMIT = 48 * 1024 * 1024
CHUNK = 128
LEAST_PIVOT = 1e-4


def dot(left, right, dims):
    return lax.dot_general(left, right, dims, preferred_element_type=F32)


def split(values):
    high = values.astype(BF16)
    low = (values - high.astype(F32)).astype(BF16)
    return high, low


def steer(phase, step, norm):
    turn = (phase * step) & (PHASES - 1)
    quadrant = (turn + QUARTER // 2) // QUARTER
    angle = (turn - quadrant * QUARTER).astype(F32) * (2.0 * jnp.pi / PHASES)
    sq = angle * angle
    sine = angle * (1.0 + sq * (-1.0 / 6 + sq * (1.0 / 120 + sq * (-1.0 / 5040 + sq / 362880))))
    cosine = 1.0 + sq * (-0.5 + sq * (1.0 / 24 + sq * (-1.0 / 720 + sq / 40320)))
    odd = (quadrant & 1) == 1
    real = jnp.where(odd, sine, cosine) * norm
    imag = jnp.where(odd, cosine, sine) * norm
    real = jnp.where(((quadrant + 1) & 2) == 2, -real, real)
    imag = jnp.where((quadrant & 2) == 2, -imag, imag)
    return real.astype(BF16), imag.astype(BF16)


def fill_weights(phase_ref, first, rows, step, out):
    norm = 1.0 / (phase_ref.shape[1] ** 0.5)
    chunk = 32

    def body(i, carry):
        at = pl.multiple_of(i * chunk, chunk)
        real, imag = steer(phase_ref[pl.ds(first + at, chunk), :], step, norm)
        out[pl.ds(at, chunk), :] = real
        out[pl.ds(rows + at, chunk), :] = imag
        return carry

    lax.fori_loop(0, rows // chunk, body, 0)


def steps(tm):
    return [0, *[by for by in range(1, tm) if by != tm // 2], tm // 2]


def shifted(by):
    tm = lax.axis_size("tm")
    return lax.rem(lax.axis_index("tm") + tm + by, tm)


def cut_kernel(own, bys, voltages_ref, *rest):
    pieces, done = rest[:-1], rest[-1]
    copies = []
    for i, (by, piece) in enumerate(zip(bys, pieces)):
        channels = pl.ds(shifted(by) * own, own)
        copy = pltpu.make_async_copy(voltages_ref.at[:, 0, channels], piece, done.at[i])
        copy.start()
        copies.append(copy)
    for copy in copies:
        copy.wait()


def turned(values, axis):
    size = values.shape[axis]
    at = lax.broadcasted_iota(jnp.int32, values.shape, axis)
    after = pltpu.roll(values, size - 1, axis)
    before = pltpu.roll(values, 1, axis)
    return jnp.where((at & 1) == 0, after, -before)


def raw_beams_kernel(tm, own, phase_ref, *rest):
    pieces, (mine_ref, other_ref, weights) = rest[:tm], rest[tm:]
    half = phase_ref.shape[0] // 2
    rows = pieces[0].shape[1]
    pol = lax.axis_index("pol")
    start = lax.axis_index("chan") * tm * own
    for by, piece in zip(steps(tm), pieces):
        for o in range(own):
            chan = shifted(by) * own + o
            for swap, out_ref in enumerate((mine_ref, other_ref)):
                first = pl.multiple_of((pol ^ swap) * half, half)
                fill_weights(phase_ref, first, half, start + chan + 1, weights)
                product = dot(piece[o], weights[...], NT)
                by_imag = turned(product[:, half:].reshape(rows // 8, 8, half), 1).reshape(rows, half)
                out_ref[chan] = product[:, :half] - by_imag


def own_weights_kernel(own, chan_dev, phase_ref, out_ref, weights):
    beams = phase_ref.shape[0]
    first = lax.axis_index("chan") * chan_dev + lax.axis_index("tm") * own
    for o in range(own):
        fill_weights(phase_ref, 0, beams, first + o + 1, weights)
        out_ref[o] = weights[...].T


def rotate(x):
    return (-turned(x.astype(F32), 0)).astype(BF16)


def early_kernel(start_ref, *refs):
    blocks, (cov_ref, first_ref, across_ref, along_ref, rotated_ref) = refs[:-5], refs[-5:]
    rows, width = blocks[0].shape[1:]
    own = cov_ref.shape[0]
    for o in range(own):
        for i, block in enumerate(blocks):
            x = block[o]
            at = slice(i * rows, (i + 1) * rows)
            along_ref[at] = x
            rotated_ref[at] = rotate(x)
            across_ref[o, :, at] = x.T
        cov_ref[o, 0] = dot(across_ref[o], along_ref[...], NN)
        cov_ref[o, 1] = dot(across_ref[o], rotated_ref[...], NN)
        chan = lax.axis_index("tm") * own + o
        first_ref[o] = block_times(start_ref[0, chan, 0], start_ref[0, chan, 1], across_ref[o], along_ref[...])


def project(real, imag, across):
    vectors = real.shape[0]
    both = jnp.concatenate(split(jnp.concatenate([real, imag], axis=0)), axis=0)
    product = dot(both, across, NN)
    product = product[: 2 * vectors] + product[2 * vectors :]
    other = turned(product, 1)
    return product[:vectors] + other[vectors:], product[vectors:] - other[:vectors]


def block_times(real, imag, across, along):
    pair = jnp.concatenate(project(real, imag, across), axis=0)
    product = dot(jnp.concatenate(split(pair), axis=0), along, NN)
    return product[: pair.shape[0]] + product[pair.shape[0] :]


def cov_times(real, imag, high_ref, low_ref):
    vectors = real.shape[0]
    rows = jnp.concatenate(
        [jnp.concatenate([real, imag], axis=1), jnp.concatenate([imag, -real], axis=1)], axis=0
    )
    high, low = split(rows)
    product = dot(jnp.concatenate([high, low], axis=0), high_ref[...], NN)
    product = product[: 2 * vectors] + product[2 * vectors :] + dot(high, low_ref[...], NN)
    return product[:vectors], product[vectors:]


def orthonormalize(real_z, imag_z, beside=()):
    beside = list(beside)
    vectors, width = real_z.shape
    row = lax.broadcasted_iota(jnp.int32, (vectors, 1), 0)
    real_v, imag_v = real_z, imag_z
    scale = jnp.zeros((vectors, 1), F32)
    for n in range(vectors):
        real_a = jnp.broadcast_to(real_v[n : n + 1], real_z.shape)
        imag_a = jnp.broadcast_to(imag_v[n : n + 1], real_z.shape)
        norm = jnp.sum(real_a * real_a + imag_a * imag_a, axis=1, keepdims=True) + EPS
        scale = jnp.where(row == n, norm, scale)
        if n + 1 < vectors:
            real_d = jnp.sum(real_a * real_z + imag_a * imag_z, axis=1, keepdims=True)
            imag_d = jnp.sum(real_a * imag_z - imag_a * real_z, axis=1, keepdims=True)
            inverse = jnp.where(row > n, 1.0 / norm, 0.0)
            real_c = real_d * inverse
            imag_c = imag_d * inverse
            real_v = real_v - (real_c * real_a - imag_c * imag_a)
            imag_v = imag_v - (real_c * imag_a + imag_c * real_a)
        for work in beside[n::vectors]:
            work()
    factor = 1.0 / jnp.sqrt(scale)
    return real_v * factor, imag_v * factor


def orthonormalize_by_gram(real_z, imag_z, riders=()):
    vectors = real_z.shape[0]
    row = lax.broadcasted_iota(jnp.int32, (vectors, 1), 0)
    by_z = []
    for n in range(vectors):
        real_a = jnp.broadcast_to(real_z[n : n + 1], real_z.shape)
        imag_a = jnp.broadcast_to(imag_z[n : n + 1], real_z.shape)
        by_z.append(
            (
                jnp.sum(real_a * real_z + imag_a * imag_z, axis=1, keepdims=True),
                jnp.sum(real_a * imag_z - imag_a * real_z, axis=1, keepdims=True),
            )
        )
    by_v = list(by_z)
    whole = [real[n : n + 1] for n, (real, imag) in enumerate(by_z)]
    sound = jnp.ones((1, 1), F32)
    pairs = [(real_z, imag_z), *riders]
    for n in range(vectors - 1):
        (real_d, imag_d), (real_p, imag_p) = by_z[n], by_v[n]
        square = jnp.maximum(real_p[n : n + 1], 0.0)
        fits = (square >= LEAST_PIVOT * whole[n]) & (square <= 4.0 * whole[n])
        sound = jnp.where(fits, sound, 0.0)
        inverse = jnp.where(row > n, 1.0 / (square + EPS), 0.0)
        real_c, imag_c = real_d * inverse, imag_d * inverse
        real_b, imag_b = real_p - real_c * square, imag_p - imag_c * square
        for j in range(n + 1, vectors):
            real_s, imag_s = real_c[j : j + 1], imag_c[j : j + 1]
            real_q, imag_q = real_p[j : j + 1], -imag_p[j : j + 1]
            real, imag = by_v[j]
            by_v[j] = (
                real - (real_c * real_q - imag_c * imag_q) - (real_s * real_b + imag_s * imag_b),
                imag - (real_c * imag_q + imag_c * real_q) - (real_s * imag_b - imag_s * real_b),
            )
            real, imag = by_z[j]
            by_z[j] = (
                real - (real_s * real_d + imag_s * imag_d),
                imag - (real_s * imag_d - imag_s * real_d),
            )
        pairs = [
            (
                real - (real_c * real[n : n + 1] - imag_c * imag[n : n + 1]),
                imag - (real_c * imag[n : n + 1] + imag_c * real[n : n + 1]),
            )
            for real, imag in pairs
        ]
    real_v, imag_v = pairs[0]
    factor = 1.0 / jnp.sqrt(jnp.sum(real_v * real_v + imag_v * imag_v, axis=1, keepdims=True) + EPS)
    return [(real * factor, imag * factor) for real, imag in pairs], sound


def subspace_kernel(
    tm, own, factor, beams_ref, start_ref, flags_ref, ranks_ref, weights_ref, cov_ref, first_ref, across_ref, last_ref, *rest
):
    outs, (high_ref, low_ref, series_ref) = rest[1 : tm + 1], rest[tm + 1 :]
    vectors, width = start_ref.shape[3], start_ref.shape[4]
    rows = last_ref.shape[1]
    tm_index = lax.axis_index("tm")
    beams = weights_ref.shape[2] // 2
    for o in range(own):
        chan = tm_index * own + o
        across = last_ref[o].T
        rotated = rotate(last_ref[o])

        def add_last(part, first):
            right = last_ref[o] if part == 0 else rotated
            term = dot(across[first : first + CHUNK], right, NN)
            at = slice(part * width + first, part * width + first + CHUNK)
            high_ref[at], low_ref[at] = split((cov_ref[o, part, first : first + CHUNK] + term) * factor)

        chunks = [
            functools.partial(add_last, part, first) for part in range(2) for first in range(0, width, CHUNK)
        ]
        last = block_times(start_ref[0, chan, 0], start_ref[0, chan, 1], across, last_ref[o])
        both = (first_ref[o] + last) * factor
        start = orthonormalize(both[:vectors], both[vectors:], chunks)
        rank = flags_ref[chan] * ranks_ref[chan]
        keep = lax.broadcasted_iota(jnp.int32, (vectors, 1), 0) < rank

        def steered_by(real, imag):
            rows_in = jnp.concatenate(split(jnp.concatenate([real, imag], axis=0)), axis=0)
            product = dot(rows_in, weights_ref[o], NN)
            product = product[: 2 * vectors] + product[2 * vectors :]
            return (
                product[:vectors, :beams] - product[vectors:, beams:],
                product[:vectors, beams:] + product[vectors:, :beams],
            )

        def write(real_w, imag_w, early, late):
            series = [early[:, i * rows : (i + 1) * rows] for i in range(tm - 1)] + [late]
            for by, values in zip(steps(tm), series):
                series_ref[tm_index ^ shifted(-by)] = jnp.where(keep, values, 0.0)
            kept = [jnp.where(keep, real_w, 0.0), jnp.where(keep, imag_w, 0.0)]
            for x, out in enumerate(outs):
                values = series_ref[x]
                values = jnp.concatenate([values[:, : rows // 2], values[:, rows // 2 :]], axis=0)
                out[o, :, :beams] = jnp.concatenate(kept, axis=0).astype(BF16)
                out[o, :, beams:] = values.astype(BF16)

        real_q, imag_q = start
        sound = jnp.ones((1, 1), F32)
        for sweep in range(1, ITERS - 1):
            real_z, imag_z = cov_times(real_q, imag_q, high_ref, low_ref)
            ((real_q, imag_q),), now = orthonormalize_by_gram(real_z, imag_z)
            sound = jnp.minimum(sound, now)
        real_z, imag_z = cov_times(real_q, imag_q, high_ref, low_ref)
        riders = [
            steered_by(real_z, imag_z),
            project(real_z, imag_z, across_ref[o]),
            project(real_z, imag_z, across),
        ]
        (unused, steered, early, late), now = orthonormalize_by_gram(real_z, imag_z, riders)
        write(*steered, early[0], late[0])

        @pl.when(jnp.min(jnp.minimum(sound, now)) < 0.5)
        def plainly():
            real, imag = start
            for sweep in range(1, ITERS):
                real, imag = orthonormalize(*cov_times(real, imag, high_ref, low_ref))
            write(
                *steered_by(real, imag),
                project(real, imag, across_ref[o])[0],
                project(real, imag, last_ref[o].T)[0],
            )


def nulled_power(raw, packet_ref, squares):
    rows, half = raw.shape
    samples = rows // 2
    series = packet_ref[:, 2 * half :].astype(F32)
    vectors = series.shape[0] // 2
    series = jnp.concatenate([series[:vectors], series[vectors:]], axis=1)
    left = jnp.concatenate([series, -turned(series, 1)], axis=0).astype(BF16)
    right = packet_ref[:, pl.ds(pl.multiple_of(lax.axis_index("pol") * half, half), half)]
    beam = raw - dot(left, right, TN)
    squares[...] = beam * beam
    return squares[pl.ds(0, samples, 2), :] + squares[pl.ds(1, samples, 2), :]


def power_kernel(own, xs, later_xs, mine_ref, theirs_ref, *rest):
    packets, later = rest[: len(xs)], rest[len(xs) : len(xs) + len(later_xs)]
    power_ref, squares = rest[-2:]
    for x, ref in zip(xs, packets):
        for o in range(own):
            chan = (lax.axis_index("tm") ^ x) * own + o
            power_ref[chan] = nulled_power(mine_ref[chan], ref.at[o], squares)
    for x, ref in zip(later_xs, later):
        for o in range(own):
            chan = (lax.axis_index("tm") ^ x) * own + o
            power_ref[chan] = power_ref[chan] + nulled_power(theirs_ref[chan], ref.at[o], squares)


def last_kernel(own, xs, theirs_ref, *rest):
    packets, (power_ref, out_ref, powers, squares) = rest[: len(xs)], rest[len(xs) :]
    powers[...] = power_ref[...]
    for x, ref in zip(xs, packets):
        for o in range(own):
            chan = (lax.axis_index("tm") ^ x) * own + o
            powers[chan] = power_ref[chan] + nulled_power(theirs_ref[chan], ref.at[o], squares)
    channels, samples = powers.shape[:2]
    for chan in range(channels):
        out_ref[pl.ds(chan, samples, channels), :] = powers[chan]


def local(voltages, start_block, flags, ranks, phase_index):
    tm = lax.axis_size("tm")
    tm_index = lax.axis_index("tm")
    samples, chan_dev, width = voltages.shape[0], voltages.shape[2], voltages.shape[4]
    own = chan_dev // tm
    vectors = start_block.shape[3]
    beams = phase_index.shape[0]
    half = beams // 2
    rows = 2 * samples
    factor = 1.0 / (samples * tm)
    params = pltpu.CompilerParams(vmem_limit_bytes=VMEM_LIMIT)
    whole = pl.BlockSpec(memory_space=pltpu.VMEM)
    scalars = pl.BlockSpec(memory_space=pltpu.SMEM)
    unread = pl.BlockSpec(memory_space=pl.ANY)

    def cost(multiplies, moved):
        return pl.CostEstimate(flops=2 * multiplies, bytes_accessed=moved, transcendentals=0)

    by = steps(tm)
    later = pl.pallas_call(
        functools.partial(cut_kernel, own, [by[0], *by[2:]]),
        out_shape=[jax.ShapeDtypeStruct((samples, own, 2, width), BF16)] * (tm - 1),
        in_specs=[pl.BlockSpec(memory_space=pltpu.HBM)],
        out_specs=[whole] * (tm - 1),
        scratch_shapes=[pltpu.SemaphoreType.DMA((tm - 1,))],
        compiler_params=params,
    )(voltages)
    urgent = lax.dynamic_slice_in_dim(voltages[:, 0], shifted(by[1]) * own, own, 1)
    cut = [later[0], urgent, *later[1:]]
    pieces = [piece.transpose(1, 0, 2, 3).reshape(own, rows, width) for piece in cut]
    blocks = pieces[:1] + [
        lax.ppermute(piece, "tm", [(z, (z + by) % tm) for z in range(tm)])
        for by, piece in zip(steps(tm)[1:], pieces[1:])
    ]

    raw = jax.ShapeDtypeStruct((chan_dev, rows, half), F32)
    mine, other = pl.pallas_call(
        functools.partial(raw_beams_kernel, tm, own),
        out_shape=[raw] * 2,
        in_specs=[whole] * (1 + tm),
        out_specs=[whole] * 2,
        scratch_shapes=[pltpu.VMEM((beams, width), BF16)],
        compiler_params=params,
        cost_estimate=cost(4 * chan_dev * samples * width * beams, 8 * chan_dev * samples * width),
    )(phase_index, *pieces)

    own_weights = pl.pallas_call(
        functools.partial(own_weights_kernel, own, chan_dev),
        out_shape=jax.ShapeDtypeStruct((own, width, 2 * beams), BF16),
        in_specs=[whole],
        out_specs=whole,
        scratch_shapes=[pltpu.VMEM((2 * beams, width), BF16)],
        compiler_params=params,
        cost_estimate=cost(20 * own * beams * width, 8 * own * beams * width),
    )(phase_index)

    early = (tm - 1) * rows
    cov, first, across = pl.pallas_call(
        early_kernel,
        out_shape=[
            jax.ShapeDtypeStruct((own, 2, width, width), F32),
            jax.ShapeDtypeStruct((own, 2 * vectors, width), F32),
            jax.ShapeDtypeStruct((own, width, early), BF16),
        ],
        in_specs=[whole] * tm,
        out_specs=[whole] * 3,
        scratch_shapes=[pltpu.VMEM((early, width), BF16)] * 2,
        compiler_params=params,
        cost_estimate=cost(2 * own * early * width * width, 8 * own * width * width),
    )(start_block, *blocks[:-1])

    other, *packets = pl.pallas_call(
        functools.partial(subspace_kernel, tm, own, factor),
        out_shape=[raw] + [jax.ShapeDtypeStruct((own, 2 * vectors, beams + samples), BF16)] * tm,
        in_specs=[unread, whole, scalars, scalars] + [whole] * 5,
        out_specs=[unread] + [whole] * tm,
        input_output_aliases={0: 0},
        scratch_shapes=[pltpu.VMEM((2 * width, width), BF16)] * 2
        + [pltpu.VMEM((tm, vectors, rows), F32)],
        compiler_params=params,
        cost_estimate=cost(32 * own * vectors * tm * samples * width, 8 * own * width * width),
    )(other, start_block, flags, ranks, own_weights, cov, first, across, blocks[-1])

    cores = [(0, 1), (1, 0)]
    theirs = lax.ppermute(other, "pol", cores)
    order = [*range(2, tm), 1]
    arrived = list(packets)
    for x in order:
        arrived[x] = lax.ppermute(packets[x], "tm", [(z, z ^ x) for z in range(tm)])
    swapped = [lax.ppermute(packet, "pol", cores) for packet in arrived]

    shape = jax.ShapeDtypeStruct((chan_dev, samples, half), F32)
    groups = [([0, *order], [0, *order[:-2]])]
    power = []
    for xs, later_xs in groups:
        used = [arrived[x] for x in xs] + [swapped[x] for x in later_xs]
        power = [
            pl.pallas_call(
                functools.partial(power_kernel, own, xs, later_xs),
                out_shape=shape,
                in_specs=[whole, whole if later_xs else unread] + [whole] * (len(used) + len(power)),
                out_specs=whole,
                input_output_aliases={2 + len(used): 0} if power else {},
                scratch_shapes=[pltpu.VMEM((rows, half), F32)],
                compiler_params=params,
                cost_estimate=cost(len(used) * own * rows * 2 * vectors * half, 8 * own * rows * half),
            )(mine, theirs if later_xs else mine, *used, *power)
        ]

    rows_out = pl.pallas_call(
        functools.partial(last_kernel, own, order[-2:]),
        out_shape=jax.ShapeDtypeStruct((samples * chan_dev, half), F32),
        in_specs=[whole] * 4,
        out_specs=whole,
        scratch_shapes=[pltpu.VMEM((chan_dev, samples, half), F32), pltpu.VMEM((rows, half), F32)],
        compiler_params=params,
        cost_estimate=cost(chan_dev * samples * half, 12 * chan_dev * samples * half),
    )(theirs, *[swapped[x] for x in order[-2:]], *power)
    return rows_out.reshape(samples, chan_dev, half)


def solution(mesh):
    placed = (
        P(("groups", "tm"), "pol", "chan", None, None),
        P("pol", "chan", None, None, None),
        P(("groups", "chan")),
        P(("groups", "chan")),
        P(),
    )
    return jax.shard_map(
        local,
        mesh=mesh,
        in_specs=placed,
        out_specs=P(("groups", "tm"), "chan", "pol"),
        check_vma=False,
    )
```

```python
import functools

import jax
import jax.numpy as jnp
from jax import lax
from jax.experimental import pallas as pl
from jax.experimental.pallas import tpu as pltpu
from jax.sharding import PartitionSpec as P

ITERS = 4
PHASES = 1024
QUARTER = PHASES // 4
EPS = 1e-06
F32 = jnp.float32
BF16 = jnp.bfloat16
NT = (((1,), (1,)), ((), ()))
NN = (((1,), (0,)), ((), ()))
TN = (((0,), (0,)), ((), ()))
VMEM_LIMIT = 48 * 1024 * 1024
CHUNK = 64
LEAST_PIVOT = 1e-4


def dot(left, right, dims):
    return lax.dot_general(left, right, dims, preferred_element_type=F32)


def split(values):
    high = values.astype(BF16)
    low = (values - high.astype(F32)).astype(BF16)
    return high, low


def steer(phase, step, norm):
    turn = (phase * step) & (PHASES - 1)
    quadrant = (turn + QUARTER // 2) // QUARTER
    angle = (turn - quadrant * QUARTER).astype(F32) * (2.0 * jnp.pi / PHASES)
    sq = angle * angle
    sine = angle * (1.0 + sq * (-1.0 / 6 + sq * (1.0 / 120 + sq * (-1.0 / 5040 + sq / 362880))))
    cosine = 1.0 + sq * (-0.5 + sq * (1.0 / 24 + sq * (-1.0 / 720 + sq / 40320)))
    odd = (quadrant & 1) == 1
    real = jnp.where(odd, sine, cosine) * norm
    imag = jnp.where(odd, cosine, sine) * norm
    real = jnp.where(((quadrant + 1) & 2) == 2, -real, real)
    imag = jnp.where((quadrant & 2) == 2, -imag, imag)
    return real.astype(BF16), imag.astype(BF16)


def fill_weights(phase_ref, first, rows, step, out):
    norm = 1.0 / (phase_ref.shape[1] ** 0.5)
    chunk = 32

    def body(i, carry):
        at = pl.multiple_of(i * chunk, chunk)
        real, imag = steer(phase_ref[pl.ds(first + at, chunk), :], step, norm)
        out[pl.ds(at, chunk), :] = real
        out[pl.ds(rows + at, chunk), :] = imag
        return carry

    lax.fori_loop(0, rows // chunk, body, 0)


def steps(tm):
    return [0, *[by for by in range(1, tm) if by != tm // 2], tm // 2]


def shifted(by):
    tm = lax.axis_size("tm")
    return lax.rem(lax.axis_index("tm") + tm + by, tm)


def cut_kernel(own, bys, voltages_ref, *rest):
    pieces, done = rest[:-1], rest[-1]
    copies = []
    for i, (by, piece) in enumerate(zip(bys, pieces)):
        channels = pl.ds(shifted(by) * own, own)
        copy = pltpu.make_async_copy(voltages_ref.at[:, 0, channels], piece, done.at[i])
        copy.start()
        copies.append(copy)
    for copy in copies:
        copy.wait()


def turned(values, axis):
    size = values.shape[axis]
    at = lax.broadcasted_iota(jnp.int32, values.shape, axis)
    after = pltpu.roll(values, size - 1, axis)
    before = pltpu.roll(values, 1, axis)
    return jnp.where((at & 1) == 0, after, -before)


def raw_beams_kernel(tm, own, phase_ref, *rest):
    pieces, (mine_ref, other_ref, weights) = rest[:tm], rest[tm:]
    half = phase_ref.shape[0] // 2
    rows = pieces[0].shape[1]
    pol = lax.axis_index("pol")
    start = lax.axis_index("chan") * tm * own
    for by, piece in zip(steps(tm), pieces):
        for o in range(own):
            chan = shifted(by) * own + o
            for swap, out_ref in enumerate((mine_ref, other_ref)):
                first = pl.multiple_of((pol ^ swap) * half, half)
                fill_weights(phase_ref, first, half, start + chan + 1, weights)
                product = dot(piece[o], weights[...], NT)
                by_imag = turned(product[:, half:].reshape(rows // 8, 8, half), 1).reshape(rows, half)
                out_ref[chan] = product[:, :half] - by_imag


def own_weights_kernel(own, chan_dev, phase_ref, out_ref, weights):
    beams = phase_ref.shape[0]
    first = lax.axis_index("chan") * chan_dev + lax.axis_index("tm") * own
    for o in range(own):
        fill_weights(phase_ref, 0, beams, first + o + 1, weights)
        out_ref[o] = weights[...].T


def rotate(x):
    return (-turned(x.astype(F32), 0)).astype(BF16)


def early_kernel(start_ref, *refs):
    blocks, (cov_ref, first_ref, across_ref, along_ref, rotated_ref) = refs[:-5], refs[-5:]
    rows, width = blocks[0].shape[1:]
    own = cov_ref.shape[0]
    for o in range(own):
        for i, block in enumerate(blocks):
            x = block[o]
            at = slice(i * rows, (i + 1) * rows)
            along_ref[at] = x
            rotated_ref[at] = rotate(x)
            across_ref[o, :, at] = x.T
        cov_ref[o, 0] = dot(across_ref[o], along_ref[...], NN)
        cov_ref[o, 1] = dot(across_ref[o], rotated_ref[...], NN)
        chan = lax.axis_index("tm") * own + o
        first_ref[o] = block_times(start_ref[0, chan, 0], start_ref[0, chan, 1], across_ref[o], along_ref[...])


def project(real, imag, across):
    vectors = real.shape[0]
    both = jnp.concatenate(split(jnp.concatenate([real, imag], axis=0)), axis=0)
    product = dot(both, across, NN)
    product = product[: 2 * vectors] + product[2 * vectors :]
    other = turned(product, 1)
    return product[:vectors] + other[vectors:], product[vectors:] - other[:vectors]


def block_times(real, imag, across, along):
    pair = jnp.concatenate(project(real, imag, across), axis=0)
    product = dot(jnp.concatenate(split(pair), axis=0), along, NN)
    return product[: pair.shape[0]] + product[pair.shape[0] :]


def cov_times(real, imag, high_ref, low_ref):
    vectors = real.shape[0]
    rows = jnp.concatenate(
        [jnp.concatenate([real, imag], axis=1), jnp.concatenate([imag, -real], axis=1)], axis=0
    )
    high, low = split(rows)
    product = dot(jnp.concatenate([high, low], axis=0), high_ref[...], NN)
    product = product[: 2 * vectors] + product[2 * vectors :] + dot(high, low_ref[...], NN)
    return product[:vectors], product[vectors:]


def orthonormalize(real_z, imag_z, beside=()):
    beside = list(beside)
    vectors, width = real_z.shape
    row = lax.broadcasted_iota(jnp.int32, (vectors, 1), 0)
    real_v, imag_v = real_z, imag_z
    scale = jnp.zeros((vectors, 1), F32)
    for n in range(vectors):
        real_a = jnp.broadcast_to(real_v[n : n + 1], real_z.shape)
        imag_a = jnp.broadcast_to(imag_v[n : n + 1], real_z.shape)
        norm = jnp.sum(real_a * real_a + imag_a * imag_a, axis=1, keepdims=True) + EPS
        scale = jnp.where(row == n, norm, scale)
        if n + 1 < vectors:
            real_d = jnp.sum(real_a * real_z + imag_a * imag_z, axis=1, keepdims=True)
            imag_d = jnp.sum(real_a * imag_z - imag_a * real_z, axis=1, keepdims=True)
            inverse = jnp.where(row > n, 1.0 / norm, 0.0)
            real_c = real_d * inverse
            imag_c = imag_d * inverse
            real_v = real_v - (real_c * real_a - imag_c * imag_a)
            imag_v = imag_v - (real_c * imag_a + imag_c * real_a)
        for work in beside[n::vectors]:
            work()
    factor = 1.0 / jnp.sqrt(scale)
    return real_v * factor, imag_v * factor


def orthonormalize_by_gram(real_z, imag_z, riders=()):
    vectors = real_z.shape[0]
    row = lax.broadcasted_iota(jnp.int32, (vectors, 1), 0)
    by_z = []
    for n in range(vectors):
        real_a = jnp.broadcast_to(real_z[n : n + 1], real_z.shape)
        imag_a = jnp.broadcast_to(imag_z[n : n + 1], real_z.shape)
        by_z.append(
            (
                jnp.sum(real_a * real_z + imag_a * imag_z, axis=1, keepdims=True),
                jnp.sum(real_a * imag_z - imag_a * real_z, axis=1, keepdims=True),
            )
        )
    by_v = list(by_z)
    whole = [real[n : n + 1] for n, (real, imag) in enumerate(by_z)]
    sound = jnp.ones((1, 1), F32)
    pairs = [(real_z, imag_z), *riders]
    for n in range(vectors - 1):
        (real_d, imag_d), (real_p, imag_p) = by_z[n], by_v[n]
        square = jnp.maximum(real_p[n : n + 1], 0.0)
        fits = (square >= LEAST_PIVOT * whole[n]) & (square <= 4.0 * whole[n])
        sound = jnp.where(fits, sound, 0.0)
        inverse = jnp.where(row > n, 1.0 / (square + EPS), 0.0)
        real_c, imag_c = real_d * inverse, imag_d * inverse
        real_b, imag_b = real_p - real_c * square, imag_p - imag_c * square
        for j in range(n + 1, vectors):
            real_s, imag_s = real_c[j : j + 1], imag_c[j : j + 1]
            real_q, imag_q = real_p[j : j + 1], -imag_p[j : j + 1]
            real, imag = by_v[j]
            by_v[j] = (
                real - (real_c * real_q - imag_c * imag_q) - (real_s * real_b + imag_s * imag_b),
                imag - (real_c * imag_q + imag_c * real_q) - (real_s * imag_b - imag_s * real_b),
            )
            real, imag = by_z[j]
            by_z[j] = (
                real - (real_s * real_d + imag_s * imag_d),
                imag - (real_s * imag_d - imag_s * real_d),
            )
        pairs = [
            (
                real - (real_c * real[n : n + 1] - imag_c * imag[n : n + 1]),
                imag - (real_c * imag[n : n + 1] + imag_c * real[n : n + 1]),
            )
            for real, imag in pairs
        ]
    real_v, imag_v = pairs[0]
    factor = 1.0 / jnp.sqrt(jnp.sum(real_v * real_v + imag_v * imag_v, axis=1, keepdims=True) + EPS)
    return [(real * factor, imag * factor) for real, imag in pairs], sound


def subspace_kernel(
    tm, own, factor, beams_ref, start_ref, flags_ref, ranks_ref, weights_ref, cov_ref, first_ref, across_ref, last_ref, *rest
):
    outs, (high_ref, low_ref, series_ref) = rest[1 : tm + 1], rest[tm + 1 :]
    vectors, width = start_ref.shape[3], start_ref.shape[4]
    rows = last_ref.shape[1]
    tm_index = lax.axis_index("tm")
    beams = weights_ref.shape[2] // 2
    for o in range(own):
        chan = tm_index * own + o
        across = last_ref[o].T
        rotated = rotate(last_ref[o])

        def add_last(part, first):
            right = last_ref[o] if part == 0 else rotated
            term = dot(across[first : first + CHUNK], right, NN)
            at = slice(part * width + first, part * width + first + CHUNK)
            high_ref[at], low_ref[at] = split((cov_ref[o, part, first : first + CHUNK] + term) * factor)

        chunks = [
            functools.partial(add_last, part, first) for part in range(2) for first in range(0, width, CHUNK)
        ]
        last = block_times(start_ref[0, chan, 0], start_ref[0, chan, 1], across, last_ref[o])
        both = (first_ref[o] + last) * factor
        start = orthonormalize(both[:vectors], both[vectors:], chunks)
        rank = flags_ref[chan] * ranks_ref[chan]
        keep = lax.broadcasted_iota(jnp.int32, (vectors, 1), 0) < rank

        def steered_by(real, imag):
            rows_in = jnp.concatenate(split(jnp.concatenate([real, imag], axis=0)), axis=0)
            product = dot(rows_in, weights_ref[o], NN)
            product = product[: 2 * vectors] + product[2 * vectors :]
            return (
                product[:vectors, :beams] - product[vectors:, beams:],
                product[:vectors, beams:] + product[vectors:, :beams],
            )

        def write(real_w, imag_w, early, late):
            series = [early[:, i * rows : (i + 1) * rows] for i in range(tm - 1)] + [late]
            for by, values in zip(steps(tm), series):
                series_ref[tm_index ^ shifted(-by)] = jnp.where(keep, values, 0.0)
            kept = [jnp.where(keep, real_w, 0.0), jnp.where(keep, imag_w, 0.0)]
            for x, out in enumerate(outs):
                values = series_ref[x]
                values = jnp.concatenate([values[:, : rows // 2], values[:, rows // 2 :]], axis=0)
                out[o, :, :beams] = jnp.concatenate(kept, axis=0).astype(BF16)
                out[o, :, beams:] = values.astype(BF16)

        real_q, imag_q = start
        sound = jnp.ones((1, 1), F32)
        for sweep in range(1, ITERS - 1):
            real_z, imag_z = cov_times(real_q, imag_q, high_ref, low_ref)
            ((real_q, imag_q),), now = orthonormalize_by_gram(real_z, imag_z)
            sound = jnp.minimum(sound, now)
        real_z, imag_z = cov_times(real_q, imag_q, high_ref, low_ref)
        riders = [
            steered_by(real_z, imag_z),
            project(real_z, imag_z, across_ref[o]),
            project(real_z, imag_z, across),
        ]
        (unused, steered, early, late), now = orthonormalize_by_gram(real_z, imag_z, riders)
        write(*steered, early[0], late[0])

        @pl.when(jnp.min(jnp.minimum(sound, now)) < 0.5)
        def plainly():
            real, imag = start
            for sweep in range(1, ITERS):
                real, imag = orthonormalize(*cov_times(real, imag, high_ref, low_ref))
            write(
                *steered_by(real, imag),
                project(real, imag, across_ref[o])[0],
                project(real, imag, last_ref[o].T)[0],
            )


def nulled_power(raw, packet_ref, squares):
    rows, half = raw.shape
    samples = rows // 2
    series = packet_ref[:, 2 * half :].astype(F32)
    vectors = series.shape[0] // 2
    series = jnp.concatenate([series[:vectors], series[vectors:]], axis=1)
    left = jnp.concatenate([series, -turned(series, 1)], axis=0).astype(BF16)
    right = packet_ref[:, pl.ds(pl.multiple_of(lax.axis_index("pol") * half, half), half)]
    beam = raw - dot(left, right, TN)
    squares[...] = beam * beam
    return squares[pl.ds(0, samples, 2), :] + squares[pl.ds(1, samples, 2), :]


def power_kernel(own, xs, later_xs, mine_ref, theirs_ref, *rest):
    packets, later = rest[: len(xs)], rest[len(xs) : len(xs) + len(later_xs)]
    power_ref, squares = rest[-2:]
    for x, ref in zip(xs, packets):
        for o in range(own):
            chan = (lax.axis_index("tm") ^ x) * own + o
            power_ref[chan] = nulled_power(mine_ref[chan], ref.at[o], squares)
    for x, ref in zip(later_xs, later):
        for o in range(own):
            chan = (lax.axis_index("tm") ^ x) * own + o
            power_ref[chan] = power_ref[chan] + nulled_power(theirs_ref[chan], ref.at[o], squares)


def last_kernel(own, x, theirs_ref, packet_ref, power_ref, out_ref, powers, squares):
    powers[...] = power_ref[...]
    for o in range(own):
        chan = (lax.axis_index("tm") ^ x) * own + o
        powers[chan] = power_ref[chan] + nulled_power(theirs_ref[chan], packet_ref.at[o], squares)
    channels, samples = powers.shape[:2]
    for chan in range(channels):
        out_ref[pl.ds(chan, samples, channels), :] = powers[chan]


def local(voltages, start_block, flags, ranks, phase_index):
    tm = lax.axis_size("tm")
    tm_index = lax.axis_index("tm")
    samples, chan_dev, width = voltages.shape[0], voltages.shape[2], voltages.shape[4]
    own = chan_dev // tm
    vectors = start_block.shape[3]
    beams = phase_index.shape[0]
    half = beams // 2
    rows = 2 * samples
    factor = 1.0 / (samples * tm)
    params = pltpu.CompilerParams(vmem_limit_bytes=VMEM_LIMIT)
    whole = pl.BlockSpec(memory_space=pltpu.VMEM)
    scalars = pl.BlockSpec(memory_space=pltpu.SMEM)
    unread = pl.BlockSpec(memory_space=pl.ANY)

    def cost(multiplies, moved):
        return pl.CostEstimate(flops=2 * multiplies, bytes_accessed=moved, transcendentals=0)

    by = steps(tm)
    later = pl.pallas_call(
        functools.partial(cut_kernel, own, [by[0], *by[2:]]),
        out_shape=[jax.ShapeDtypeStruct((samples, own, 2, width), BF16)] * (tm - 1),
        in_specs=[pl.BlockSpec(memory_space=pltpu.HBM)],
        out_specs=[whole] * (tm - 1),
        scratch_shapes=[pltpu.SemaphoreType.DMA((tm - 1,))],
        compiler_params=params,
    )(voltages)
    urgent = lax.dynamic_slice_in_dim(voltages[:, 0], shifted(by[1]) * own, own, 1)
    cut = [later[0], urgent, *later[1:]]
    pieces = [piece.transpose(1, 0, 2, 3).reshape(own, rows, width) for piece in cut]
    blocks = pieces[:1] + [
        lax.ppermute(piece, "tm", [(z, (z + by) % tm) for z in range(tm)])
        for by, piece in zip(steps(tm)[1:], pieces[1:])
    ]

    raw = jax.ShapeDtypeStruct((chan_dev, rows, half), F32)
    mine, other = pl.pallas_call(
        functools.partial(raw_beams_kernel, tm, own),
        out_shape=[raw] * 2,
        in_specs=[whole] * (1 + tm),
        out_specs=[whole] * 2,
        scratch_shapes=[pltpu.VMEM((beams, width), BF16)],
        compiler_params=params,
        cost_estimate=cost(4 * chan_dev * samples * width * beams, 8 * chan_dev * samples * width),
    )(phase_index, *pieces)

    own_weights = pl.pallas_call(
        functools.partial(own_weights_kernel, own, chan_dev),
        out_shape=jax.ShapeDtypeStruct((own, width, 2 * beams), BF16),
        in_specs=[whole],
        out_specs=whole,
        scratch_shapes=[pltpu.VMEM((2 * beams, width), BF16)],
        compiler_params=params,
        cost_estimate=cost(20 * own * beams * width, 8 * own * beams * width),
    )(phase_index)

    early = (tm - 1) * rows
    cov, first, across = pl.pallas_call(
        early_kernel,
        out_shape=[
            jax.ShapeDtypeStruct((own, 2, width, width), F32),
            jax.ShapeDtypeStruct((own, 2 * vectors, width), F32),
            jax.ShapeDtypeStruct((own, width, early), BF16),
        ],
        in_specs=[whole] * tm,
        out_specs=[whole] * 3,
        scratch_shapes=[pltpu.VMEM((early, width), BF16)] * 2,
        compiler_params=params,
        cost_estimate=cost(2 * own * early * width * width, 8 * own * width * width),
    )(start_block, *blocks[:-1])

    other, *packets = pl.pallas_call(
        functools.partial(subspace_kernel, tm, own, factor),
        out_shape=[raw] + [jax.ShapeDtypeStruct((own, 2 * vectors, beams + samples), BF16)] * tm,
        in_specs=[unread, whole, scalars, scalars] + [whole] * 5,
        out_specs=[unread] + [whole] * tm,
        input_output_aliases={0: 0},
        scratch_shapes=[pltpu.VMEM((2 * width, width), BF16)] * 2
        + [pltpu.VMEM((tm, vectors, rows), F32)],
        compiler_params=params,
        cost_estimate=cost(32 * own * vectors * tm * samples * width, 8 * own * width * width),
    )(other, start_block, flags, ranks, own_weights, cov, first, across, blocks[-1])

    cores = [(0, 1), (1, 0)]
    theirs = lax.ppermute(other, "pol", cores)
    order = [*range(2, tm), 1]
    arrived = list(packets)
    for x in order:
        arrived[x] = lax.ppermute(packets[x], "tm", [(z, z ^ x) for z in range(tm)])
    swapped = [lax.ppermute(packet, "pol", cores) for packet in arrived]

    shape = jax.ShapeDtypeStruct((chan_dev, samples, half), F32)
    groups = [([0, *order[:-1]], []), (order[-1:], [0, *order[-2::-1]])]
    power = []
    for xs, later_xs in groups:
        used = [arrived[x] for x in xs] + [swapped[x] for x in later_xs]
        power = [
            pl.pallas_call(
                functools.partial(power_kernel, own, xs, later_xs),
                out_shape=shape,
                in_specs=[whole, whole if later_xs else unread] + [whole] * (len(used) + len(power)),
                out_specs=whole,
                input_output_aliases={2 + len(used): 0} if power else {},
                scratch_shapes=[pltpu.VMEM((rows, half), F32)],
                compiler_params=params,
                cost_estimate=cost(len(used) * own * rows * 2 * vectors * half, 8 * own * rows * half),
            )(mine, theirs if later_xs else mine, *used, *power)
        ]

    rows_out = pl.pallas_call(
        functools.partial(last_kernel, own, order[-1]),
        out_shape=jax.ShapeDtypeStruct((samples * chan_dev, half), F32),
        in_specs=[whole] * 3,
        out_specs=whole,
        scratch_shapes=[pltpu.VMEM((chan_dev, samples, half), F32), pltpu.VMEM((rows, half), F32)],
        compiler_params=params,
        cost_estimate=cost(chan_dev * samples * half, 12 * chan_dev * samples * half),
    )(theirs, swapped[order[-1]], *power)
    return rows_out.reshape(samples, chan_dev, half)


def solution(mesh):
    placed = (
        P(("groups", "tm"), "pol", "chan", None, None),
        P("pol", "chan", None, None, None),
        P(("groups", "chan")),
        P(("groups", "chan")),
        P(),
    )
    return jax.shard_map(
        local,
        mesh=mesh,
        in_specs=placed,
        out_specs=P(("groups", "tm"), "chan", "pol"),
        check_vma=False,
    )
```
